32 devices in a mesh: dp: 8 (over z, y), tensor: 4 (over x, core).
Axes of the slice: x: 2, y: 2, z: 4, core: 2. Of those that a mesh axis runs over, the one named last changes fastest.
Arguments:
- clean_latents: bfloat16 [64, 256, 16], P('dp'), may hold values from -6 to 6
- noise_draw: bfloat16 [64, 256, 16], P('dp'), may hold values from -6 to 6
- timesteps: float32 [64], P('dp'), may hold values from 0 to 1, as said below
- labels: int32 [64], P('dp'), may hold values from 0 to 31
- col_weights: float32 [768, 4, 2880], P('dp', 'tensor'), may hold values from -0.21875 to 0.21875
- col_moments: float32 [768, 4, 2880], P('dp', 'tensor'), may hold values from -0.015625 to 0.015625
- col_errors: float32 [8, 4, 768, 2880], P('dp', 'tensor'), may hold values from -0.00030517578 to 0.00030517578
- row_weights: float32 [4, 960, 768], P('tensor', None, 'dp'), may hold values from -0.21875 to 0.21875
- row_moments: float32 [4, 960, 768], P('tensor', None, 'dp'), may hold values from -0.015625 to 0.015625
- row_errors: float32 [8, 4, 960, 768], P('dp', 'tensor'), may hold values from -0.00030517578 to 0.00030517578
- bias_weights: float32 [4, 2880], P('tensor'), may hold values from -4 to 4
- bias_moments: float32 [4, 2880], P('tensor'), may hold values from -0.046875 to 0.046875
- small_weights: float32 [1093, 768], P(None, 'dp'), may hold values from -4 to 4
- small_moments: float32 [1093, 768], P(None, 'dp'), may hold values from -0.046875 to 0.046875
- head_bias: float32 [16], replicated, may hold values from -6 to 6
- head_moments: float32 [16], replicated, may hold values from -0.00030517578 to 0.00030517578
- right_factors: float32 [4, 8, 4416], P('tensor'), may hold values from -6 to 6
Outputs:
- loss_value: float32 [], replicated
- col_new: float32 [768, 4, 2880], P('dp', 'tensor')
- col_momentum: float32 [768, 4, 2880], P('dp', 'tensor')
- col_residue: float32 [8, 4, 768, 2880], P('dp', 'tensor')
- row_new: float32 [4, 960, 768], P('tensor', None, 'dp')
- row_momentum: float32 [4, 960, 768], P('tensor', None, 'dp')
- row_residue: float32 [8, 4, 960, 768], P('dp', 'tensor')
- bias_new: float32 [4, 2880], P('tensor')
- bias_momentum: float32 [4, 2880], P('tensor')
- small_new: float32 [1093, 768], P(None, 'dp')
- small_momentum: float32 [1093, 768], P(None, 'dp')
- head_new: float32 [16], replicated
- head_momentum: float32 [16], replicated
- left_factors: float32 [4, 8, 3264], P('tensor')
- right_new: float32 [4, 8, 4416], P('tensor')
The draws below stay inside these ranges and needn't reach their ends.
Inputs may be any that keep to these rules, and one draw needn't show every extreme that they name: `timesteps`: each is (k + 0.5) / 1000 for a whole number k.
All inputs are finite; a program needn't handle non-finite values.
Results may differ from the reference program's by a relative error of at most 0.012.
The reference program's roundings to bfloat16 on the way count: a program that leaves them out, or rounds other values in their place, can miss the bound.
Values may be sent and summed in bfloat16 or wider, within the bound.
A program may use at most 256 MiB of HBM per device.

```python
import math
import jax
import jax.numpy as jnp
from jax import lax

D = 768
HEADS = 12
HEAD_DIM = 64
FF = 3072
FREQ = 256
GRID = 16
PATCH_IN = 16
CLASSES = 32
RANK = 8
LAT_DEV = 8
SEQ = 256
LATENTS = 64
COLW = 2880
ROWW = 960
QW = 4416
SMALLR = 1093
N_DP = 8
N_TENSOR = 4


def draw_timesteps(key, part):
    grid_index = jax.random.randint(key, (LATENTS,), 0, 1000)
    return (grid_index.astype(jnp.float32) + 0.5) / 1000.0


def draw_small_weights(key, part):
    counts = [PATCH_IN, 1, FREQ, 1, D, 1, CLASSES, PATCH_IN, 1, 1]
    scales = [PATCH_IN ** (-0.5), 0.3, FREQ ** (-0.5), 0.3, D ** (-0.5), 0.3, 1.0, D ** (-0.5), 0.3, 0.3]
    row_scale = jnp.concatenate([jnp.full((amount,), scale_value, jnp.float32) for amount, scale_value in zip(counts, scales)])
    normals = jnp.clip(jax.random.normal(key, (SMALLR, D), jnp.float32), -4.0, 4.0)
    return normals * row_scale[:, None]


def touch_ends(result, stream_key, low, top_value):
    longest = result.shape.index(max(result.shape))
    spots = []
    for shift in (0, 1):
        where = [jax.random.randint(jax.random.fold_in(stream_key, axis), (), 0, length) for axis, length in enumerate(result.shape)]
        where[longest] = (where[longest] + shift) % result.shape[longest]
        spots.append(tuple(where))
    return result.at[spots[0]].set(low).at[spots[1]].set(top_value)


def steps_of(stream_key, dims, split, smallest, top_value):
    gain, own = 1.0, jax.random.fold_in(stream_key, 6)
    for dim, blocks in split:
        draws = jnp.exp(jax.random.uniform(jax.random.fold_in(own, dim), (blocks,), jnp.float32, smallest / len(split), top_value / len(split)))
        gain = gain * jnp.repeat(draws, dims[dim] // blocks).reshape([-1 if axis == dim else 1 for axis in range(len(dims))])
    return gain


def normal_values(key, dims, scale, reach, shards=(), kind=jnp.bfloat16):
    drawn = jax.random.normal(key, dims, jnp.float32) * scale
    if len(shards) > 0:
        drawn = steps_of(key, dims, shards, -0.22, 0.18) * drawn
    return jnp.clip(drawn, min=-reach, max=reach).astype(kind)


def setup_inputs(seed: int = 0) -> dict:
    key_list = jax.random.split(jax.random.key(seed), 18)
    return {
        "clean_latents": normal_values(key_list[0], (LATENTS, SEQ, PATCH_IN), 1.0, 6.0, ((0, 8),)),
        "noise_draw": normal_values(key_list[1], (LATENTS, SEQ, PATCH_IN), 1.0, 6.0, ((0, 8),)),
        "timesteps": draw_timesteps(jax.random.fold_in(key_list[17], 71), 0),
        "labels": touch_ends(jax.random.randint(key_list[3], (LATENTS,), 0, CLASSES), jax.random.fold_in(key_list[3], 1), 0, CLASSES - 1).astype(jnp.int32),
        "col_weights": normal_values(key_list[4], (D, N_TENSOR, COLW), D ** -0.5, 0.21875, ((0, 8), (1, 4)), jnp.float32),
        "col_moments": normal_values(key_list[5], (D, N_TENSOR, COLW), (1e-3), 0.015625, ((0, 8), (1, 4)), jnp.float32),
        "col_errors": normal_values(key_list[6], (N_DP, N_TENSOR, D, COLW), (2e-5), 0.00030517578, ((0, 8), (1, 4)), jnp.float32),
        "row_weights": normal_values(key_list[7], (N_TENSOR, ROWW, D), D ** -0.5, 0.21875, ((0, 4), (2, 8)), jnp.float32),
        "row_moments": normal_values(key_list[8], (N_TENSOR, ROWW, D), (1e-3), 0.015625, ((0, 4), (2, 8)), jnp.float32),
        "row_errors": normal_values(key_list[9], (N_DP, N_TENSOR, ROWW, D), (2e-5), 0.00030517578, ((0, 8), (1, 4)), jnp.float32),
        "bias_weights": normal_values(key_list[10], (N_TENSOR, COLW), 0.3, 4.0, ((0, 4),), jnp.float32),
        "bias_moments": normal_values(key_list[11], (N_TENSOR, COLW), (3e-3), 0.046875, ((0, 4),), jnp.float32),
        "small_weights": draw_small_weights(jax.random.fold_in(key_list[17], 71), 0),
        "small_moments": normal_values(key_list[13], (SMALLR, D), (3e-3), 0.046875, ((1, 8),), jnp.float32),
        "head_bias": normal_values(key_list[14], (PATCH_IN,), 0.5, 6.0, (), jnp.float32),
        "head_moments": normal_values(key_list[15], (PATCH_IN,), (2e-5), 0.00030517578, (), jnp.float32),
        "right_factors": normal_values(key_list[16], (N_TENSOR, RANK, QW), 1.0, 6.0, ((0, 4),), jnp.float32),
    }


@jax.custom_vjp
def low(v):
    return lax.optimization_barrier(v.astype(jnp.bfloat16)).astype(jnp.float32)

@jax.custom_vjp
def low_back(v):
    return v

def low_keep(v):
    return (low(v), None)

def low_pass(kept, grad):
    return (grad,)

def back_keep(v):
    return (v, None)

def back_low(kept, grad):
    return (low(grad),)
low.defvjp(low_keep, low_pass)
low_back.defvjp(back_keep, back_low)
EPSILON = 1e-06
TINY = 1e-30
DECAY = 0.9
LEARN_RATE = 100.0
TIME_OFFSET = 0.25

def exact_mul(left, right):
    return jnp.matmul(left, right, precision=lax.Precision.HIGHEST, preferred_element_type=jnp.float32)

def exact_tdot(left, right):
    return lax.dot_general(left, right, (((0,), (0,)), ((), ())), precision=lax.Precision.HIGHEST, preferred_element_type=jnp.float32)

def exact_ndot(left, right):
    return lax.dot_general(left, right, (((1,), (1,)), ((), ())), precision=lax.Precision.HIGHEST, preferred_element_type=jnp.float32)

def to_compute(values):
    return lax.optimization_barrier(values.astype(jnp.bfloat16)).astype(jnp.float32)

def layer_norm(hidden):
    center = hidden - lax.optimization_barrier(jnp.mean(hidden, axis=-1, keepdims=True))
    spread = lax.optimization_barrier(jnp.mean(center * center, axis=-1, keepdims=True))
    return center * lax.rsqrt(spread + EPSILON)

def modulate(hidden, shift_rows, scale_rows):
    return layer_norm(hidden) * (1.0 + scale_rows) + shift_rows

def position_rows(token_ids):
    quarter = D // 4
    omega = 1.0 / 10000.0 ** (jnp.arange(quarter, dtype=jnp.float32) / quarter)
    row_pos = (token_ids // GRID).astype(jnp.float32)[:, None] * omega[None, :]
    col_pos = (token_ids % GRID).astype(jnp.float32)[:, None] * omega[None, :]
    return jnp.concatenate([jnp.sin(row_pos), jnp.cos(row_pos), jnp.sin(col_pos), jnp.cos(col_pos)], axis=1)

def time_features(times):
    half = FREQ // 2
    freqs = jnp.exp(-math.log(10000.0) * jnp.arange(half, dtype=jnp.float32) / half)
    angles = 1000.0 * times[:, None] * freqs[None, :]
    return jnp.concatenate([jnp.cos(angles), jnp.sin(angles)], axis=1)

def small_starts():
    counts = [PATCH_IN, 1, FREQ, 1, D, 1, CLASSES, PATCH_IN, 1, 1]
    starts = [0]
    for amount in counts:
        starts.append(starts[-1] + amount)
    return starts

def cut_parts(array, widths, axis):
    pieces = []
    offset = 0
    for width in widths:
        pieces.append(lax.slice_in_dim(array, offset, offset + width, axis=axis))
        offset = offset + width
    return pieces

def local_widths():
    return (8 * D // N_TENSOR, 3 * D // N_TENSOR, FF // N_TENSOR, D // N_TENSOR)

def unpack(col_exact, row_exact, bias_exact, small_exact, head_exact):
    mod_width, qkv_width, ffn_width, proj_rows = local_widths()
    w_mod, w_qkv, w_fc1 = cut_parts(col_exact, [mod_width, qkv_width, ffn_width], 2)
    b_mod, b_qkv, b_fc1 = cut_parts(bias_exact, [mod_width, qkv_width, ffn_width], 1)
    w_proj, w_fc2 = cut_parts(row_exact, [proj_rows, ffn_width], 1)
    starts = small_starts()
    pieces = [small_exact[starts[index]:starts[index + 1]] for index in range(10)]
    return (w_mod.reshape(D, 8 * D), b_mod.reshape(8 * D), w_qkv.reshape(D, 3 * D), b_qkv.reshape(3 * D), w_fc1.reshape(D, FF), b_fc1.reshape(FF), w_proj.reshape(D, D), w_fc2.reshape(FF, D), pieces[0], pieces[1][0], pieces[2], pieces[3][0], pieces[4], pieces[5][0], pieces[6], pieces[7], pieces[8][0], pieces[9][0], head_exact)

def pack_grads(grads):
    g_mod, g_bmod, g_qkv, g_bqkv, g_fc1, g_bfc1, g_proj, g_fc2, g_patch, g_bpatch, g_tin, g_btin, g_tout, g_btout, g_table, g_head, g_bproj, g_bfc2, g_bhead = grads
    mod_width, qkv_width, ffn_width, proj_rows = local_widths()
    col_grad = jnp.concatenate([g_mod.reshape(D, N_TENSOR, mod_width), g_qkv.reshape(D, N_TENSOR, qkv_width), g_fc1.reshape(D, N_TENSOR, ffn_width)], axis=2).transpose(1, 0, 2)
    row_grad = jnp.concatenate([g_proj.reshape(N_TENSOR, proj_rows, D), g_fc2.reshape(N_TENSOR, ffn_width, D)], axis=1)
    bias_grad = jnp.concatenate([g_bmod.reshape(N_TENSOR, mod_width), g_bqkv.reshape(N_TENSOR, qkv_width), g_bfc1.reshape(N_TENSOR, ffn_width)], axis=1)
    small_grad = jnp.concatenate([g_patch, g_bpatch[None], g_tin, g_btin[None], g_tout, g_btout[None], g_table, g_head, g_bproj[None], g_bfc2[None]], axis=0)
    return (col_grad, row_grad, bias_grad, small_grad, g_bhead)

def forward(params, clean, noise, times, labels):
    w_mod, b_mod, w_qkv, b_qkv, w_fc1, b_fc1, w_proj, w_fc2, w_patch, b_patch, w_time_in, b_time_in, w_time_out, b_time_out, table, w_head, b_proj, b_fc2, b_head = params
    count = clean.shape[0]
    mixed = times[:, None, None] * clean + (1.0 - times)[:, None, None] * noise
    target = clean - noise
    time_act = jax.nn.silu(exact_mul(time_features(times), w_time_in) + b_time_in)
    onehot = (labels[:, None] == jnp.arange(CLASSES, dtype=jnp.int32)[None, :]).astype(jnp.float32)
    condition = exact_mul(time_act, w_time_out) + b_time_out + exact_mul(onehot, table)
    modulation = exact_mul(jax.nn.silu(condition), w_mod) + b_mod

    def span(which):
        return modulation[:, None, which * D:(which + 1) * D]
    positions = position_rows(jnp.arange(SEQ, dtype=jnp.int32))
    hidden0 = low_back(exact_mul(low(mixed), w_patch)) + b_patch + positions[None]
    attn_in = low(modulate(hidden0, span(0), span(1)))
    qkv = low(low_back(exact_mul(attn_in, w_qkv)) + b_qkv).reshape(count, SEQ, HEADS, 3, HEAD_DIM)
    query = qkv[:, :, :, 0]
    keys = qkv[:, :, :, 1]
    values = qkv[:, :, :, 2]
    scale_factor = 1.0 / math.sqrt(HEAD_DIM)
    scores = low_back(jnp.einsum('bqhd,bkhd->bhqk', query, keys, precision=lax.Precision.HIGHEST) * scale_factor)
    probs = jax.nn.softmax(scores, axis=-1)
    attended = low(low_back(jnp.einsum('bhqk,bkhd->bqhd', low(probs), values, precision=lax.Precision.HIGHEST)))
    attended = attended.reshape(count, SEQ, D)
    attn_out = low_back(exact_mul(attended, w_proj)) + b_proj
    hidden1 = hidden0 + span(2) * attn_out
    mlp_in = low(modulate(hidden1, span(3), span(4)))
    pre_act = low_back(exact_mul(mlp_in, w_fc1)) + b_fc1
    mlp_act = low(jax.nn.gelu(pre_act, approximate=True))
    mlp_out = low_back(exact_mul(mlp_act, w_fc2)) + b_fc2
    hidden2 = hidden1 + span(5) * mlp_out
    final_in = low(modulate(hidden2, span(6), span(7)))
    predicted = low_back(exact_mul(final_in, w_head.T)) + b_head
    weighting = 1.0 / (1.0 - times + TIME_OFFSET)
    error_sq = (predicted - target) * (predicted - target)
    return jnp.sum(weighting[:, None, None] * error_sq) / (LATENTS * SEQ * PATCH_IN)

def orthonormal(block):
    basis = []
    for index in range(block.shape[0]):
        vector = block[index]
        for earlier in basis:
            vector = vector - jnp.sum(vector * earlier) * earlier
        vector = vector * lax.rsqrt(jnp.sum(vector * vector) + TINY)
        basis.append(vector)
    return jnp.stack(basis)

def matrix_parts(col_total, row_total):
    mod_width, qkv_width, ffn_width, proj_rows = local_widths()
    return cut_parts(col_total, [mod_width, qkv_width, ffn_width], 1) + cut_parts(row_total, [proj_rows, ffn_width], 0)

def right_parts(right):
    mod_width, qkv_width, ffn_width, proj_rows = local_widths()
    return cut_parts(right, [mod_width, qkv_width, ffn_width, D, D], 1)

def left_parts(left):
    mod_width, qkv_width, ffn_width, proj_rows = local_widths()
    return cut_parts(left, [D, D, D, proj_rows, ffn_width], 1)

def project(col_total, row_total, right):
    matrices = matrix_parts(col_total, row_total)
    pieces = right_parts(right)
    return jnp.concatenate([exact_ndot(pieces[index], matrices[index]) for index in range(5)], axis=1)

def orthonormal_all(left):
    return jnp.concatenate([orthonormal(part) for part in left_parts(left)], axis=1)

def expand(col_total, row_total, bases):
    matrices = matrix_parts(col_total, row_total)
    pieces = left_parts(bases)
    return jnp.concatenate([exact_mul(pieces[index], matrices[index]) for index in range(5)], axis=1)

def approximate(bases, right):
    lefts = left_parts(bases)
    rights = right_parts(right)
    approx = [exact_tdot(lefts[index], rights[index]) for index in range(5)]
    return (jnp.concatenate(approx[:3], axis=1), jnp.concatenate(approx[3:], axis=0))

def reference(clean_latents, noise_draw, timesteps, labels, col_weights, col_moments, col_errors, row_weights, row_moments, row_errors, bias_weights, bias_moments, small_weights, small_moments, head_bias, head_moments, right_factors):
    clean_exact = clean_latents.astype(jnp.float32)
    noise_exact = noise_draw.astype(jnp.float32)
    params = unpack(to_compute(col_weights), to_compute(row_weights), to_compute(bias_weights), to_compute(small_weights), to_compute(head_bias))

    def one_worker(index):
        start = index * LAT_DEV

        def take(array):
            return lax.dynamic_slice_in_dim(array, start, LAT_DEV, 0)
        value, pull = jax.vjp(lambda weights: forward(weights, take(clean_exact), take(noise_exact), take(timesteps), take(labels)), params)
        grads = pull(jnp.ones((), jnp.float32))[0]
        return (value,) + pack_grads(grads)
    loss_parts, col_grads, row_grads, bias_grads, small_grads, head_grads = lax.map(one_worker, jnp.arange(N_DP, dtype=jnp.int32))
    loss_value = jnp.sum(loss_parts)
    bias_sum = lax.optimization_barrier(jnp.sum(bias_grads, axis=0))
    small_sum = lax.optimization_barrier(jnp.sum(small_grads, axis=0))
    head_sum = lax.optimization_barrier(jnp.sum(head_grads, axis=0))
    col_total = col_grads + col_errors
    row_total = row_grads + row_errors
    left_sum = lax.optimization_barrier(jnp.sum(jax.vmap(jax.vmap(project), in_axes=(0, 0, None))(col_total, row_total, right_factors), axis=0))
    bases = jax.vmap(orthonormal_all)(left_sum)
    right_sum = lax.optimization_barrier(jnp.sum(jax.vmap(jax.vmap(expand), in_axes=(0, 0, None))(col_total, row_total, bases), axis=0))
    col_hat, row_hat = jax.vmap(approximate)(bases, right_sum)
    col_residue = col_total - col_hat[None] / N_DP
    row_residue = row_total - row_hat[None] / N_DP
    col_momentum = DECAY * col_moments + col_hat.transpose(1, 0, 2)
    col_new = col_weights - LEARN_RATE * col_momentum
    row_momentum = DECAY * row_moments + row_hat
    row_new = row_weights - LEARN_RATE * row_momentum
    bias_momentum = DECAY * bias_moments + bias_sum
    bias_new = bias_weights - LEARN_RATE * bias_momentum
    small_momentum = DECAY * small_moments + small_sum
    small_new = small_weights - LEARN_RATE * small_momentum
    head_momentum = DECAY * head_moments + head_sum
    head_new = head_bias - LEARN_RATE * head_momentum
    return (loss_value, col_new, col_momentum, col_residue, row_new, row_momentum, row_residue, bias_new, bias_momentum, small_new, small_momentum, head_new, head_momentum, bases, right_sum)
```

```python
import functools
import math

import jax
import jax.numpy as jnp
from jax import lax
from jax.experimental import pallas as pl
from jax.experimental.pallas import tpu as pltpu
from jax.sharding import PartitionSpec as P

D = 768
HEADS = 12
HEAD_DIM = 64
FF = 3072
FREQ = 256
GRID = 16
PATCH_IN = 16
CLASSES = 32
SEQ = 256

EPSILON = 1e-06
TINY = 1e-30
DECAY = 0.9
LEARN_RATE = 100.0
TIME_OFFSET = 0.25
F32 = jnp.float32
BF = jnp.bfloat16
SCALE = 1.0 / math.sqrt(HEAD_DIM)
GELU_C = math.sqrt(2.0 / math.pi)


def exact_dot(left, right):
    return jnp.dot(left, right, precision=lax.Precision.HIGHEST, preferred_element_type=F32)


def exact_tdot(left, right):
    return lax.dot_general(left, right, (((0,), (0,)), ((), ())), precision=lax.Precision.HIGHEST, preferred_element_type=F32)


def exact_ndot(left, right):
    return lax.dot_general(left, right, (((1,), (1,)), ((), ())), precision=lax.Precision.HIGHEST, preferred_element_type=F32)


def dot(a,b): return lax.dot_general(a,b,(((1,),(0,)),((),())),preferred_element_type=F32)
def ndot(a,b): return lax.dot_general(a,b,(((1,),(1,)),((),())),preferred_element_type=F32)
def tdot(a,b): return lax.dot_general(a,b,(((0,),(0,)),((),())),preferred_element_type=F32)

def ln(h):
    c=h-jnp.mean(h,axis=-1,keepdims=True)
    v=jnp.mean(c*c,axis=-1,keepdims=True)
    r=lax.rsqrt(v+EPSILON)
    return c*r,r

def ln_back(dout,xh,r,scale):
    dx=dout*(1.0+scale)
    return r*(dx-jnp.mean(dx,axis=-1,keepdims=True)-xh*jnp.mean(dx*xh,axis=-1,keepdims=True))

def colsum(v): return jnp.sum(v,axis=0,keepdims=True)

def block_kernel(base_ref,times_ref,clean_ref,noise_ref,mod_ref,wall_ref,pe_ref,wp_ref,bp_ref,wh_ref,bh_ref,bo_ref,b2_ref,bq_ref,b1_ref,
           a_ref,m_ref,dy_ref,dz_ref,o_ref,dq_ref,g_ref,du_ref,dmod_ref,small_ref,dbq_ref,db1_ref,dbh_ref,loss_ref,
           r_s,p_s,gp_s,xh1_s,xh2_s,y_s,z_s,h_s,acc_s,r1_s,r2_s,*,count_all):
    step=pl.program_id(0)
    base=base_ref[0]
    t=times_ref[step]
    lo=lax.broadcasted_iota(jnp.int32,(1,128),1)<64
    @pl.when(step==0)
    def _():
        small_ref[...]=jnp.zeros_like(small_ref); dbq_ref[...]=jnp.zeros_like(dbq_ref); db1_ref[...]=jnp.zeros_like(db1_ref)
        dbh_ref[...]=jnp.zeros_like(dbh_ref); loss_ref[...]=jnp.zeros_like(loss_ref)
    clean=clean_ref[0].astype(F32); noise=noise_ref[0].astype(F32)
    mixed=(t*clean+(1.0-t)*noise).astype(BF)
    mod=lambda i: mod_ref[0,i:i+1,:]
    h0=dot(mixed,wp_ref[...])+bp_ref[...]+pe_ref[...]
    h_s[...]=h0
    xh,r=ln(h0)
    xh1_s[...]=xh; r1_s[...]=r
    a_ref[0]=(xh*(1.0+mod(1))+mod(0)).astype(BF)
    y_s[...]=jnp.zeros_like(y_s)
    zero=jnp.zeros((),BF)
    roll=lambda v: pltpu.roll(v.astype(F32),64,1).astype(BF)
    def softmax_store(s,idx):
        s=s*SCALE
        e=jnp.exp(s-jnp.max(s,axis=-1,keepdims=True))
        p=e/jnp.sum(e,axis=-1,keepdims=True)
        p_s[idx]=p
        return p.astype(BF)
    @pl.loop(0,4)
    def _(jj):
        j=lax.rem(base+jj,4)
        r_s[jj]=(dot(a_ref[0],wall_ref[j,:,0:768])+bq_ref[j]).astype(BF)
        blk=lambda i: r_s[jj,:,128*i:128*(i+1)]
        b0,b1,b2,b3,b4=[blk(i) for i in range(5)]
        p0=softmax_store(ndot(jnp.where(lo,b0,zero),roll(b0)),3*jj)
        p1=softmax_store(ndot(jnp.where(lo,zero,b1),roll(b2)),3*jj+1)
        p2=softmax_store(ndot(jnp.where(lo,b3,zero),roll(b3)),3*jj+2)
        o01=jnp.where(lo,dot(p0,b1),dot(p1,b2)).astype(BF)
        o2=jnp.where(lo,dot(p2,b4),0.0).astype(BF)
        @pl.when(jj<2)
        def _():
            o_ref[jj,0,:,0:128]=o01; o_ref[jj,0,:,128:256]=o2
        ro=roll(o01)
        ob4=jnp.where(lo,zero,ro)
        ob5=jnp.where(lo,ro,roll(o2))
        y_s[...]+=ndot(jnp.concatenate([ob4,ob5],axis=1),wall_ref[j,:,512:768])
    y=y_s[...]+bo_ref[...]
    y_s[...]=y
    h1=h_s[...]+mod(2)*y
    h_s[...]=h1
    xh,r=ln(h1)
    xh2_s[...]=xh; r2_s[...]=r
    m_ref[0]=(xh*(1.0+mod(4))+mod(3)).astype(BF)
    z_s[...]=jnp.zeros_like(z_s)
    @pl.loop(0,4)
    def _(jj):
        j=lax.rem(base+jj,4)
        u=dot(m_ref[0],wall_ref[j,:,768:1536])+b1_ref[j]
        uu=u*u
        th=jnp.tanh(GELU_C*(u+0.044715*(uu*u)))
        cdf=0.5*(1.0+th)
        g=(u*cdf).astype(BF)
        gp_s[jj]=cdf+0.5*u*(1.0-th*th)*(GELU_C*(1.0+3.0*0.044715*uu))
        @pl.when(jj<2)
        def _(): g_ref[jj,0]=g
        z_s[...]+=ndot(g,wall_ref[j,:,1536:2304])
    z=z_s[...]+b2_ref[...]
    z_s[...]=z
    h2=h_s[...]+mod(5)*z
    xh,r=ln(h2)
    fi=(xh*(1.0+mod(7))+mod(6)).astype(BF)
    pred=ndot(fi,wh_ref[...])+bh_ref[...]
    diff=pred-(clean-noise)
    weight=1.0/(1.0-t+0.25)
    loss_ref[...]+=jnp.sum(colsum(weight*diff*diff),axis=1,keepdims=True)*(1.0/count_all)
    dpred=2.0*weight*diff*(1.0/count_all)
    dbh_ref[...]+=colsum(dpred)
    dpl=dpred.astype(BF)
    small_ref[16:32]+=tdot(dpl,fi)
    dfi=dot(dpl,wh_ref[...])
    dmod_ref[0,6:7]=colsum(dfi); dmod_ref[0,7:8]=colsum(dfi*xh)
    dh=ln_back(dfi,xh,r,mod(7))
    h_s[...]=dh
    dmod_ref[0,5:6]=colsum(dh*z_s[...])
    dzf=dh*mod(5)
    small_ref[34:35]+=colsum(dzf)
    dz_ref[0]=dzf.astype(BF)
    acc_s[...]=jnp.zeros_like(acc_s)
    @pl.loop(0,4)
    def _(jj):
        j=lax.rem(base+jj,4)
        du=dot(dz_ref[0],wall_ref[j,:,1536:2304])*gp_s[jj]
        dul=du.astype(BF)
        @pl.when(jj<2)
        def _():
            du_ref[jj,0]=dul
            db1_ref[jj]+=colsum(du)
        acc_s[...]+=ndot(dul,wall_ref[j,:,768:1536])
    dm=acc_s[...]
    xh=xh2_s[...]
    dmod_ref[0,3:4]=colsum(dm); dmod_ref[0,4:5]=colsum(dm*xh)
    dh=h_s[...]+ln_back(dm,xh,r2_s[...],mod(4))
    h_s[...]=dh
    dmod_ref[0,2:3]=colsum(dh*y_s[...])
    dyf=dh*mod(2)
    small_ref[33:34]+=colsum(dyf)
    dy_ref[0]=dyf.astype(BF)
    acc_s[...]=jnp.zeros_like(acc_s)
    @pl.loop(0,4)
    def _(jj):
        j=lax.rem(base+jj,4)
        do=dot(dy_ref[0],wall_ref[j,:,512:768]).astype(BF)
        r4=roll(do[:,0:128]); r5=roll(do[:,128:256])
        do0=jnp.where(lo,r4,zero); do1=jnp.where(lo,zero,r5); do2=jnp.where(lo,r5,zero)
        blk=lambda i: r_s[jj,:,128*i:128*(i+1)]
        b0,b1,b2,b3,b4=[blk(i) for i in range(5)]
        def head(h,doh,v,):
            p=p_s[3*jj+h]
            dv=tdot(p.astype(BF),doh)
            dp=ndot(doh,v)
            ds=(p*(dp-jnp.sum(p*dp,axis=-1,keepdims=True))).astype(BF)
            return dv,ds
        dv0,ds0=head(0,do0,b1)
        dv1,ds1=head(1,do1,b2)
        dv2,ds2=head(2,do2,b4)
        rb0=roll(b0); rb3=roll(b3)
        n0=jnp.where(lo,dot(ds0,rb0),tdot(ds0,rb0))*SCALE
        dq1=dot(ds1,roll(b2))*SCALE; dk1=tdot(ds1,roll(b1))*SCALE
        n1=jnp.where(lo,dv0,dq1); n2=jnp.where(lo,dk1,dv1)
        n3=jnp.where(lo,dot(ds2,rb3),tdot(ds2,rb3))*SCALE
        n4=jnp.where(lo,dv2,0.0)
        dqkv=jnp.concatenate([n0,n1,n2,n3,n4],axis=1)
        dl=dqkv.astype(BF)
        @pl.when(jj<2)
        def _():
            dq_ref[jj,0]=dl
            dbq_ref[jj]+=colsum(dqkv)
        acc_s[...]+=ndot(dl,wall_ref[j,:,0:640])
    da=acc_s[...]
    xh=xh1_s[...]
    dmod_ref[0,0:1]=colsum(da); dmod_ref[0,1:2]=colsum(da*xh)
    dh=h_s[...]+ln_back(da,xh,r1_s[...],mod(1))
    small_ref[32:33]+=colsum(dh)
    small_ref[0:16]+=tdot(mixed,dh.astype(BF))

def run_block(base,times,clean,noise,mod,wall,pe,wp,bp,wh,bh,bo,b2,bq,b1,count_all):
    L=clean.shape[0]
    full=lambda a: pl.BlockSpec(a.shape,lambda i,*_: (0,)*a.ndim,pipeline_mode=pl.Buffered(1))
    lat=lambda *s: pl.BlockSpec((1,)+s,lambda i,*_:(i,)+(0,)*len(s))
    pair=lambda w: pl.BlockSpec((2,1,SEQ,w),lambda i,*_:(0,i,0,0))
    const=lambda *s: pl.BlockSpec(s,lambda i,*_:(0,)*len(s))
    S=jax.ShapeDtypeStruct
    outs=[S((L,SEQ,D),BF)]*4+[S((2,L,SEQ,256),BF),S((2,L,SEQ,640),BF),S((2,L,SEQ,768),BF),S((2,L,SEQ,768),BF),
        S((L,8,D),F32),S((40,D),F32),S((2,1,640),F32),S((2,1,768),F32),S((1,PATCH_IN),F32),S((1,1),F32)]
    ospecs=[lat(SEQ,D)]*4+[pair(256),pair(640),pair(768),pair(768),lat(8,D),const(40,D),const(2,1,640),const(2,1,768),const(1,PATCH_IN),const(1,1)]
    V=pltpu.VMEM
    f=lambda: V((SEQ,D),F32)
    return pl.pallas_call(functools.partial(block_kernel,count_all=count_all),
        grid_spec=pltpu.PrefetchScalarGridSpec(num_scalar_prefetch=2,grid=(L,),
            in_specs=[lat(SEQ,PATCH_IN),lat(SEQ,PATCH_IN),lat(8,D)]+[full(v) for v in (wall,pe,wp,bp,wh,bh,bo,b2,bq,b1)],
            out_specs=ospecs,
            scratch_shapes=[V((4,SEQ,768),BF),V((12,SEQ,SEQ),F32),V((4,SEQ,768),F32),f(),f(),f(),f(),f(),f(),V((SEQ,1),F32),V((SEQ,1),F32)]),
        out_shape=outs,
        compiler_params=pltpu.CompilerParams(vmem_limit_bytes=60*1024*1024),
        name="block",
    )(base,times,clean,noise,mod,wall,pe,wp,bp,wh,bh,bo,b2,bq,b1)


def position_rows(token_ids):
    quarter = D // 4
    omega = 1.0 / 10000.0 ** (jnp.arange(quarter, dtype=jnp.float32) / quarter)
    row_pos = (token_ids // GRID).astype(jnp.float32)[:, None] * omega[None, :]
    col_pos = (token_ids % GRID).astype(jnp.float32)[:, None] * omega[None, :]
    return jnp.concatenate(
        [jnp.sin(row_pos), jnp.cos(row_pos), jnp.sin(col_pos), jnp.cos(col_pos)], axis=1
    )


def time_features(times):
    half = FREQ // 2
    freqs = jnp.exp(-math.log(10000.0) * jnp.arange(half, dtype=jnp.float32) / half)
    angles = 1000.0 * times[:, None] * freqs[None, :]
    return jnp.concatenate([jnp.cos(angles), jnp.sin(angles)], axis=1)


def small_starts():
    counts = [PATCH_IN, 1, FREQ, 1, D, 1, CLASSES, PATCH_IN, 1, 1]
    starts = [0]
    for amount in counts:
        starts.append(starts[-1] + amount)
    return starts


def cut_parts(array, widths, axis):
    pieces = []
    offset = 0
    for width in widths:
        pieces.append(lax.slice_in_dim(array, offset, offset + width, axis=axis))
        offset = offset + width
    return pieces


def ortho_kernel(x_ref, o_ref):
    count = x_ref.shape[0]
    rows = [x_ref[index] for index in range(count)]
    for index in range(count):
        vector = rows[index]
        vector = vector * lax.rsqrt(jnp.sum(vector * vector, axis=-1, keepdims=True) + TINY)
        o_ref[index] = vector
        for later in range(index + 1, count):
            rows[later] = rows[later] - jnp.sum(rows[later] * vector, axis=-1, keepdims=True) * vector


def orthonormal_all(parts):
    stacked = jnp.stack([jnp.pad(part, ((0, 0), (0, D - part.shape[1]))) for part in parts], axis=1)
    stacked = jnp.pad(stacked, ((0, 0), (0, 8 - len(parts)), (0, 0)))
    out = pl.pallas_call(ortho_kernel, out_shape=jax.ShapeDtypeStruct(stacked.shape, F32), name="ortho")(stacked)
    return [out[:, index, : part.shape[1]] for index, part in enumerate(parts)]


def rounded(values):
    return lax.optimization_barrier(values.astype(BF)).astype(F32)


def silu_slope(values):
    gate = jax.nn.sigmoid(values)
    return gate * (1.0 + values * (1.0 - gate))


def shards(
    clean_latents,
    noise_draw,
    timesteps,
    labels,
    col_weights,
    col_moments,
    col_errors,
    row_weights,
    row_moments,
    row_errors,
    bias_weights,
    bias_moments,
    small_weights,
    small_moments,
    head_bias,
    head_moments,
    right_factors,
):
    tensor_size = lax.axis_size("tensor")
    data_size = lax.axis_size("dp")
    tensor_rank = lax.axis_index("tensor")
    data_rank = lax.axis_index("dp")
    batch = clean_latents.shape[0]
    half = batch // 2
    share = D // data_size
    mod_width = 8 * D // tensor_size
    qkv_width = 3 * D // tensor_size
    ffn_width = FF // tensor_size
    proj_rows = D // tensor_size
    count_all = data_size * batch * SEQ * PATCH_IN
    col_widths = [mod_width, qkv_width, ffn_width]
    core = lax.rem(tensor_rank, 2)
    base = tensor_rank - core
    pair = [(index, index + 1 - 2 * (index % 2)) for index in range(tensor_size)]

    def swap(values):
        return lax.ppermute(values, "tensor", pair)

    col_low = col_weights[:, 0, :].astype(BF)
    row_low = row_weights[0].astype(BF).T
    packed = jnp.concatenate(
        [
            col_low[:, mod_width : mod_width + qkv_width],
            row_low[:, :proj_rows],
            col_low[:, mod_width + qkv_width :],
            row_low[:, proj_rows:],
        ],
        axis=1,
    )
    wall = lax.all_gather(lax.all_gather(packed, "dp", axis=0, tiled=True), "tensor", axis=0)
    starts = small_starts()
    small_low = small_weights.astype(BF)
    small_exact = rounded(small_weights)
    picked = jnp.concatenate([small_low[: starts[2]], small_low[starts[7] :]], axis=0)
    emb = lax.all_gather(picked.astype(F32), "dp", axis=1, tiled=True)
    w_patch = emb[:16].astype(BF)
    b_patch = emb[16:17]
    w_head = emb[17:33].astype(BF)
    b_proj = emb[33:34]
    b_fc2 = emb[34:35]
    w_tin = small_exact[starts[2] : starts[3]]
    b_tin = small_exact[starts[3]]
    w_tout = small_exact[starts[4] : starts[5]]
    b_tout = small_exact[starts[5]]
    table = small_exact[starts[6] : starts[7]]
    bias_exact = rounded(bias_weights[0])
    head_exact = rounded(head_bias)
    w_mod = rounded(col_weights[:, 0, :mod_width])
    bias_all = lax.all_gather(bias_exact, "tensor", axis=0)
    times_all = lax.all_gather(timesteps, "dp", axis=0, tiled=True)
    labels_all = lax.all_gather(labels, "dp", axis=0, tiled=True)
    time_feat = time_features(times_all)
    time_hidden = exact_dot(time_feat, w_tin) + b_tin
    time_act = lax.all_gather(jax.nn.silu(time_hidden), "dp", axis=1, tiled=True)
    onehot = (labels_all[:, None] == jnp.arange(CLASSES, dtype=jnp.int32)[None, :]).astype(F32)
    condition = exact_dot(time_act, w_tout) + b_tout + exact_dot(onehot, table)
    cond_act = jax.nn.silu(condition)
    mod_part = exact_dot(cond_act, w_mod)
    mod_own = lax.psum_scatter(mod_part, "dp", scatter_dimension=0, tiled=True) + bias_exact[:mod_width]
    mod_full = lax.all_gather(mod_own, "tensor", axis=1, tiled=True).reshape(batch, 8, D)
    cond_rows = lax.all_to_all(cond_act, "dp", split_axis=0, concat_axis=1, tiled=True)

    def mine(values):
        return lax.dynamic_slice_in_dim(values, core * half, half, 0)

    bq = jnp.pad(bias_all[:, mod_width : mod_width + qkv_width], ((0, 0), (0, 768 - qkv_width)))[:, None]
    b1 = bias_all[:, mod_width + qkv_width :][:, None]
    positions = position_rows(jnp.arange(SEQ, dtype=jnp.int32))
    (a, m, dy, dz, o, dq, g, du, dmod, small, dbq, db1, dbh, loss) = run_block(
        base.reshape(1),
        mine(timesteps),
        mine(clean_latents),
        mine(noise_draw),
        mine(mod_full),
        wall,
        positions,
        w_patch,
        b_patch,
        w_head,
        head_exact[None],
        b_proj,
        b_fc2,
        bq,
        b1,
        count_all,
    )
    rows = half * SEQ

    def flat(values):
        return values.reshape(rows, values.shape[-1])

    def pick(values, which):
        return lax.dynamic_index_in_dim(values, which, 0, keepdims=False)

    def gradients(which):
        return (
            tdot(flat(a), flat(pick(dq, which))[:, :qkv_width]),
            tdot(flat(m), flat(pick(du, which))),
            tdot(flat(pick(o, which))[:, :proj_rows], flat(dy)),
            tdot(flat(pick(g, which)), flat(dz)),
            pick(dbq, which)[0, :qkv_width],
            pick(db1, which)[0],
        )

    other = swap(gradients(1 - core))
    own = gradients(core)
    g_qkv, g_fc1, g_proj, g_fc2, g_bqkv, g_bfc1 = [left + right for left, right in zip(own, other)]
    dmod_own = dmod.reshape(half, 8 * D)
    dmod_other = swap(dmod_own)
    dmod_group = jnp.where(
        core == 0,
        jnp.concatenate([dmod_own, dmod_other], axis=0),
        jnp.concatenate([dmod_other, dmod_own], axis=0),
    )
    d_mod = lax.dynamic_slice_in_dim(dmod_group, tensor_rank * mod_width, mod_width, 1)
    g_bmod = jnp.sum(d_mod, axis=0)
    g_mod = exact_tdot(cond_rows, d_mod)
    d_mod_all = lax.all_gather(d_mod, "dp", axis=0, tiled=True)
    d_cond = lax.psum(exact_ndot(d_mod_all, w_mod), "tensor") * silu_slope(condition)
    g_table = exact_tdot(onehot, d_cond)
    g_btout = jnp.sum(d_cond, axis=0)
    g_tout = exact_tdot(time_act, d_cond)
    d_time = lax.psum_scatter(exact_ndot(d_cond, w_tout), "dp", scatter_dimension=1, tiled=True)
    d_time = d_time * silu_slope(time_hidden)
    g_btin = jnp.sum(d_time, axis=0)
    g_tin = exact_tdot(time_feat, d_time)
    small_own = lax.psum(lax.psum_scatter(small, "dp", scatter_dimension=1, tiled=True), "tensor") * 0.5
    head_sum, loss_value = lax.psum((dbh[0] * 0.5, loss[0, 0] * 0.5), ("dp", "tensor"))
    small_step = jnp.concatenate(
        [
            small_own[:16],
            small_own[32:33],
            g_tin,
            g_btin[None],
            g_tout,
            g_btout[None],
            g_table,
            small_own[16:32],
            small_own[33:34],
            small_own[34:35],
        ],
        axis=0,
    )
    bias_sum = lax.psum(jnp.concatenate([g_bmod, g_bqkv, g_bfc1], axis=0), "dp")
    col_cuts = cut_parts(col_errors[0, 0], col_widths, 1)
    row_cuts = cut_parts(row_errors[0, 0], [proj_rows, ffn_width], 0)
    matrices = [
        g_mod + col_cuts[0],
        g_qkv + col_cuts[1],
        g_fc1 + col_cuts[2],
        g_proj + row_cuts[0],
        g_fc2 + row_cuts[1],
    ]
    right_pieces = cut_parts(right_factors[0], col_widths + [D, D], 1)
    left_local = jnp.concatenate([exact_ndot(right_pieces[i], matrices[i]) for i in range(5)], axis=1)
    left_sum = lax.psum(left_local, "dp")
    bases = orthonormal_all(cut_parts(left_sum, [D, D, D, proj_rows, ffn_width], 1))
    right_local = jnp.concatenate([exact_dot(bases[i], matrices[i]) for i in range(5)], axis=1)
    right_sum = lax.psum(right_local, "dp")
    right_split = cut_parts(right_sum, col_widths + [D, D], 1)
    approx = [exact_tdot(bases[i], right_split[i]) for i in range(5)]
    rest = [matrices[i] - approx[i] / data_size for i in range(5)]
    col_residue = jnp.concatenate(rest[:3], axis=1)[None, None]
    row_residue = jnp.concatenate(rest[3:], axis=0)[None, None]

    def own_columns(values):
        return lax.dynamic_slice_in_dim(values, data_rank * share, share, 1)

    col_step = jnp.concatenate(
        [exact_tdot(own_columns(bases[i]), right_split[i]) for i in range(3)], axis=1
    )[:, None, :]
    row_step = jnp.concatenate(
        [exact_tdot(bases[i], own_columns(right_split[i])) for i in (3, 4)], axis=0
    )[None]
    col_momentum = DECAY * col_moments + col_step
    col_new = col_weights - LEARN_RATE * col_momentum
    row_momentum = DECAY * row_moments + row_step
    row_new = row_weights - LEARN_RATE * row_momentum
    small_momentum = DECAY * small_moments + small_step
    small_new = small_weights - LEARN_RATE * small_momentum
    bias_momentum = DECAY * bias_moments + bias_sum[None]
    bias_new = bias_weights - LEARN_RATE * bias_momentum
    head_momentum = DECAY * head_moments + head_sum
    head_new = head_bias - LEARN_RATE * head_momentum
    left_factors = jnp.concatenate(bases, axis=1)[None]
    right_new = right_sum[None]
    return (
        loss_value,
        col_new,
        col_momentum,
        col_residue,
        row_new,
        row_momentum,
        row_residue,
        bias_new,
        bias_momentum,
        small_new,
        small_momentum,
        head_new,
        head_momentum,
        left_factors,
        right_new,
    )


def solution(mesh):
    placed = (
        P("dp", None, None),
        P("dp", None, None),
        P("dp"),
        P("dp"),
        P("dp", "tensor", None),
        P("dp", "tensor", None),
        P("dp", "tensor", None, None),
        P("tensor", None, "dp"),
        P("tensor", None, "dp"),
        P("dp", "tensor", None, None),
        P("tensor", None),
        P("tensor", None),
        P(None, "dp"),
        P(None, "dp"),
        P(),
        P(),
        P("tensor", None, None),
    )
    return jax.shard_map(
        shards,
        mesh=mesh,
        in_specs=placed,
        out_specs=(
            P(),
            P("dp", "tensor", None),
            P("dp", "tensor", None),
            P("dp", "tensor", None, None),
            P("tensor", None, "dp"),
            P("tensor", None, "dp"),
            P("dp", "tensor", None, None),
            P("tensor", None),
            P("tensor", None),
            P(None, "dp"),
            P(None, "dp"),
            P(),
            P(),
            P("tensor", None, None),
            P("tensor", None, None),
        ),
        check_vma=False,
    )
```

```python
import functools
import math

import jax
import jax.numpy as jnp
from jax import lax
from jax.experimental import pallas as pl
from jax.experimental.pallas import tpu as pltpu
from jax.sharding import PartitionSpec as P

D = 768
HEADS = 12
HEAD_DIM = 64
FF = 3072
FREQ = 256
GRID = 16
PATCH_IN = 16
CLASSES = 32
SEQ = 256

EPSILON = 1e-06
TINY = 1e-30
DECAY = 0.9
LEARN_RATE = 100.0
TIME_OFFSET = 0.25
F32 = jnp.float32
BF = jnp.bfloat16
SCALE = 1.0 / math.sqrt(HEAD_DIM)
GELU_C = math.sqrt(2.0 / math.pi)


def exact_dot(left, right):
    return jnp.dot(left, right, precision=lax.Precision.HIGHEST, preferred_element_type=F32)


def exact_tdot(left, right):
    return lax.dot_general(left, right, (((0,), (0,)), ((), ())), precision=lax.Precision.HIGHEST, preferred_element_type=F32)


def exact_ndot(left, right):
    return lax.dot_general(left, right, (((1,), (1,)), ((), ())), precision=lax.Precision.HIGHEST, preferred_element_type=F32)


def dot(a,b): return lax.dot_general(a,b,(((1,),(0,)),((),())),preferred_element_type=F32)
def ndot(a,b): return lax.dot_general(a,b,(((1,),(1,)),((),())),preferred_element_type=F32)
def tdot(a,b): return lax.dot_general(a,b,(((0,),(0,)),((),())),preferred_element_type=F32)

def ln(h):
    c=h-jnp.mean(h,axis=-1,keepdims=True)
    v=jnp.mean(c*c,axis=-1,keepdims=True)
    r=lax.rsqrt(v+EPSILON)
    return c*r,r

def ln_back(dout,xh,r,scale):
    dx=dout*(1.0+scale)
    return r*(dx-jnp.mean(dx,axis=-1,keepdims=True)-xh*jnp.mean(dx*xh,axis=-1,keepdims=True))

def colsum(v): return jnp.sum(v,axis=0,keepdims=True)

def block_kernel(base_ref,times_ref,clean_ref,noise_ref,mod_ref,wall_ref,pe_ref,wp_ref,bp_ref,wh_ref,bh_ref,bo_ref,b2_ref,bq_ref,b1_ref,
           a_ref,m_ref,dy_ref,dz_ref,o_ref,x_ref,g_ref,dmod_ref,small_ref,dbias_ref,
           r_s,p_s,gp_s,xh1_s,xh2_s,y_s,z_s,h_s,acc_s,r1_s,r2_s,*,count_all):
    step=pl.program_id(0)
    base=base_ref[0]
    t=times_ref[step]
    lo=lax.broadcasted_iota(jnp.int32,(1,128),1)<64
    @pl.when(step==0)
    def _():
        small_ref[...]=jnp.zeros_like(small_ref); dbias_ref[...]=jnp.zeros_like(dbias_ref)
    clean=clean_ref[0].astype(F32); noise=noise_ref[0].astype(F32)
    mixed=(t*clean+(1.0-t)*noise).astype(BF)
    mod=lambda i: mod_ref[0,i:i+1,:]
    h0=dot(mixed,wp_ref[...])+bp_ref[...]+pe_ref[...]
    h_s[...]=h0
    xh,r=ln(h0)
    xh1_s[...]=xh; r1_s[...]=r
    a_ref[0]=(xh*(1.0+mod(1))+mod(0)).astype(BF)
    y_s[...]=jnp.zeros_like(y_s)
    zero=jnp.zeros((),BF)
    roll=lambda v: pltpu.roll(v.astype(F32),64,1).astype(BF)
    def softmax_store(s,idx):
        s=s*SCALE
        e=jnp.exp(s-jnp.max(s,axis=-1,keepdims=True))
        p=e/jnp.sum(e,axis=-1,keepdims=True)
        p_s[idx]=p
        return p.astype(BF)
    @pl.loop(0,4)
    def _(j):
        own=(j>=base)&(j<base+2)
        k=j-base
        r_s[j]=(dot(a_ref[0],wall_ref[j,:,0:768])+bq_ref[j]).astype(BF)
        blk=lambda i: r_s[j,:,128*i:128*(i+1)]
        b0,b1,b2,b3,b4=[blk(i) for i in range(5)]
        p0=softmax_store(ndot(jnp.where(lo,b0,zero),roll(b0)),3*j)
        p1=softmax_store(ndot(jnp.where(lo,zero,b1),roll(b2)),3*j+1)
        p2=softmax_store(ndot(jnp.where(lo,b3,zero),roll(b3)),3*j+2)
        o01=jnp.where(lo,dot(p0,b1),dot(p1,b2)).astype(BF)
        o2=jnp.where(lo,dot(p2,b4),0.0).astype(BF)
        @pl.when(own)
        def _():
            o_ref[k,0,:,0:128]=o01; o_ref[k,0,:,128:256]=o2
        ro=roll(o01)
        ob4=jnp.where(lo,zero,ro)
        ob5=jnp.where(lo,ro,roll(o2))
        y_s[...]+=ndot(jnp.concatenate([ob4,ob5],axis=1),wall_ref[j,:,512:768])
    y=y_s[...]+bo_ref[...]
    y_s[...]=y
    h1=h_s[...]+mod(2)*y
    h_s[...]=h1
    xh,r=ln(h1)
    xh2_s[...]=xh; r2_s[...]=r
    m_ref[0]=(xh*(1.0+mod(4))+mod(3)).astype(BF)
    z_s[...]=jnp.zeros_like(z_s)
    @pl.loop(0,4)
    def _(j):
        own=(j>=base)&(j<base+2)
        k=j-base
        u=dot(m_ref[0],wall_ref[j,:,768:1536])+b1_ref[j]
        uu=u*u
        th=jnp.tanh(GELU_C*(u+0.044715*(uu*u)))
        cdf=0.5*(1.0+th)
        g=(u*cdf).astype(BF)
        gp_s[j]=cdf+0.5*u*(1.0-th*th)*(GELU_C*(1.0+3.0*0.044715*uu))
        @pl.when(own)
        def _(): g_ref[k,0]=g
        z_s[...]+=ndot(g,wall_ref[j,:,1536:2304])
    z=z_s[...]+b2_ref[...]
    z_s[...]=z
    h2=h_s[...]+mod(5)*z
    xh,r=ln(h2)
    fi=(xh*(1.0+mod(7))+mod(6)).astype(BF)
    pred=ndot(fi,wh_ref[...])+bh_ref[...]
    diff=pred-(clean-noise)
    weight=1.0/(1.0-t+0.25)
    small_ref[36:37,0:1]+=jnp.sum(colsum(weight*diff*diff),axis=1,keepdims=True)*(1.0/count_all)
    dpred=2.0*weight*diff*(1.0/count_all)
    small_ref[35:36,0:PATCH_IN]+=colsum(dpred)
    dpl=dpred.astype(BF)
    small_ref[16:32]+=tdot(dpl,fi)
    dfi=dot(dpl,wh_ref[...])
    dmod_ref[0,6:7]=colsum(dfi); dmod_ref[0,7:8]=colsum(dfi*xh)
    dh=ln_back(dfi,xh,r,mod(7))
    h_s[...]=dh
    dmod_ref[0,5:6]=colsum(dh*z_s[...])
    dzf=dh*mod(5)
    small_ref[34:35]+=colsum(dzf)
    dz_ref[0]=dzf.astype(BF)
    def store_x(k):
        def put(start,width,values): x_ref[k,0,:,start:start+width]=values.astype(BF)
        return put
    def add_bias(k):
        def put(start,width,values): dbias_ref[k,:,start:start+width]+=values
        return put
    acc_s[...]=jnp.zeros_like(acc_s)
    @pl.loop(0,4)
    def _(j):
        own=(j>=base)&(j<base+2)
        k=j-base
        du=dot(dz_ref[0],wall_ref[j,:,1536:2304])*gp_s[j]
        dul=du.astype(BF)
        @pl.when(own)
        def _():
            for values,put in ((du,store_x(k)),(colsum(du),add_bias(k))):
                turned=pltpu.roll(values,64,1)
                put(512,128,jnp.where(lo,0.0,turned[:,0:128]))
                put(640,640,turned[:,128:768])
                put(1280,128,jnp.where(lo,turned[:,0:128],0.0))
        acc_s[...]+=ndot(dul,wall_ref[j,:,768:1536])
    dm=acc_s[...]
    xh=xh2_s[...]
    dmod_ref[0,3:4]=colsum(dm); dmod_ref[0,4:5]=colsum(dm*xh)
    dh=h_s[...]+ln_back(dm,xh,r2_s[...],mod(4))
    h_s[...]=dh
    dmod_ref[0,2:3]=colsum(dh*y_s[...])
    dyf=dh*mod(2)
    small_ref[33:34]+=colsum(dyf)
    dy_ref[0]=dyf.astype(BF)
    acc_s[...]=jnp.zeros_like(acc_s)
    @pl.loop(0,4)
    def _(j):
        own=(j>=base)&(j<base+2)
        k=j-base
        do=dot(dy_ref[0],wall_ref[j,:,512:768]).astype(BF)
        r4=roll(do[:,0:128]); r5=roll(do[:,128:256])
        do0=jnp.where(lo,r4,zero); do1=jnp.where(lo,zero,r5); do2=jnp.where(lo,r5,zero)
        blk=lambda i: r_s[j,:,128*i:128*(i+1)]
        b0,b1,b2,b3,b4=[blk(i) for i in range(5)]
        def head(h,doh,v,):
            p=p_s[3*j+h]
            dv=tdot(p.astype(BF),doh)
            dp=ndot(doh,v)
            ds=(p*(dp-jnp.sum(p*dp,axis=-1,keepdims=True))).astype(BF)
            return dv,ds
        dv0,ds0=head(0,do0,b1)
        dv1,ds1=head(1,do1,b2)
        dv2,ds2=head(2,do2,b4)
        rb0=roll(b0); rb3=roll(b3)
        n0=jnp.where(lo,dot(ds0,rb0),tdot(ds0,rb0))*SCALE
        dq1=dot(ds1,roll(b2))*SCALE; dk1=tdot(ds1,roll(b1))*SCALE
        n1=jnp.where(lo,dv0,dq1); n2=jnp.where(lo,dk1,dv1)
        n3=jnp.where(lo,dot(ds2,rb3),tdot(ds2,rb3))*SCALE
        n4=jnp.where(lo,dv2,0.0)
        dqkv=jnp.concatenate([n0,n1,n2,n3,n4],axis=1)
        dl=dqkv.astype(BF)
        @pl.when(own)
        def _():
            x_ref[k,0,:,0:512]=dl[:,0:512]
            x_ref[k,0,:,512:640]=jnp.where(lo,dl[:,512:640],x_ref[k,0,:,512:640])
            dbias_ref[k,:,0:640]+=colsum(dqkv)
        acc_s[...]+=ndot(dl,wall_ref[j,:,0:640])
    da=acc_s[...]
    xh=xh1_s[...]
    dmod_ref[0,0:1]=colsum(da); dmod_ref[0,1:2]=colsum(da*xh)
    dh=h_s[...]+ln_back(da,xh,r1_s[...],mod(1))
    small_ref[32:33]+=colsum(dh)
    small_ref[0:16]+=tdot(mixed,dh.astype(BF))

def run_block(base,times,clean,noise,mod,wall,pe,wp,bp,wh,bh,bo,b2,bq,b1,count_all):
    L=clean.shape[0]
    full=lambda a: pl.BlockSpec(a.shape,lambda i,*_: (0,)*a.ndim,pipeline_mode=pl.Buffered(1))
    lat=lambda *s: pl.BlockSpec((1,)+s,lambda i,*_:(i,)+(0,)*len(s))
    pair=lambda w: pl.BlockSpec((2,1,SEQ,w),lambda i,*_:(0,i,0,0))
    const=lambda *s: pl.BlockSpec(s,lambda i,*_:(0,)*len(s))
    S=jax.ShapeDtypeStruct
    outs=[S((L,SEQ,D),BF)]*4+[S((2,L,SEQ,256),BF),S((2,L,SEQ,1408),BF),S((2,L,SEQ,768),BF),
        S((L,8,D),F32),S((40,D),F32),S((2,1,1408),F32)]
    ospecs=[lat(SEQ,D)]*4+[pair(256),pair(1408),pair(768),lat(8,D),const(40,D),const(2,1,1408)]
    V=pltpu.VMEM
    f=lambda: V((SEQ,D),F32)
    return pl.pallas_call(functools.partial(block_kernel,count_all=count_all),
        grid_spec=pltpu.PrefetchScalarGridSpec(num_scalar_prefetch=2,grid=(L,),
            in_specs=[lat(SEQ,PATCH_IN),lat(SEQ,PATCH_IN),lat(8,D)]+[full(v) for v in (wall,pe,wp,bp,wh,bh,bo,b2,bq,b1)],
            out_specs=ospecs,
            scratch_shapes=[V((4,SEQ,768),BF),V((12,SEQ,SEQ),F32),V((4,SEQ,768),F32),f(),f(),f(),f(),f(),f(),V((SEQ,1),F32),V((SEQ,1),F32)]),
        out_shape=outs,
        compiler_params=pltpu.CompilerParams(vmem_limit_bytes=60*1024*1024),
        name="block",
    )(base,times,clean,noise,mod,wall,pe,wp,bp,wh,bh,bo,b2,bq,b1)


MESH = pl.DeviceIdType.MESH
HI = lax.Precision.HIGHEST


def hdot(a, b):
    return lax.dot_general(a, b, (((1,), (0,)), ((), ())), precision=HI, preferred_element_type=F32)


def hndot(a, b):
    return lax.dot_general(a, b, (((1,), (1,)), ((), ())), precision=HI, preferred_element_type=F32)


def htdot(a, b):
    return lax.dot_general(a, b, (((0,), (0,)), ((), ())), precision=HI, preferred_element_type=F32)


def split2(values):
    first = values.astype(BF)
    return first, (values - first.astype(F32)).astype(BF)


def split3(values):
    first, rest = values.astype(BF), values
    rest = rest - first.astype(F32)
    second = rest.astype(BF)
    return first, second, (rest - second.astype(F32)).astype(BF)


def silu_slope_k(values):
    gate = 1.0 / (1.0 + jnp.exp(-values))
    return gate * (1.0 + values * (1.0 - gate))


class Peers:
    def __init__(self, send_sem, recv_sem):
        self.w = lax.axis_index("dp")
        self.t = lax.axis_index("tensor")
        self.n = lax.axis_size("dp")
        self.tn = lax.axis_size("tensor")
        self.c = lax.rem(self.t, 2)
        self.sib = self.t + 1 - 2 * self.c
        self.send_sem, self.recv_sem = send_sem, recv_sem
        self.pending = []

    def barrier(self):
        bar = pltpu.get_barrier_semaphore()
        for i in range(1, self.n):
            pl.semaphore_signal(bar, inc=1, device_id=(lax.rem(self.w + i, self.n), self.t), device_id_type=MESH)
        for i in range(1, self.tn):
            pl.semaphore_signal(bar, inc=1, device_id=(self.w, lax.rem(self.t + i, self.tn)), device_id_type=MESH)
        pl.semaphore_wait(bar, self.n - 1 + self.tn - 1)

    def copy(self, src, dst, index, device):
        op = pltpu.make_async_remote_copy(
            src_ref=src,
            dst_ref=dst,
            send_sem=self.send_sem.at[index],
            recv_sem=self.recv_sem.at[index],
            device_id=device,
            device_id_type=MESH,
        )
        op.start()
        self.pending.append(op)
        return op

    def dp_push(self, src_of, dst, base):
        ops = []
        for i in range(1, self.n):
            peer = lax.rem(self.w + i, self.n)
            ops.append(self.copy(src_of(peer), dst, base + i - 1, (peer, self.t)))
        return ops

    def tensor_push(self, src, dst, base):
        ops = []
        for i in range(1, self.tn):
            ops.append(self.copy(src, dst, base + i - 1, (self.w, lax.rem(self.t + i, self.tn))))
        return ops

    def core_push(self, src, dst, index):
        return self.copy(src, dst, index, (self.w, self.sib))

    def finish(self):
        for op in self.pending:
            op.wait_send()


def wait_all(ops):
    for op in ops:
        op.wait_recv()


P_TILES = (6, 6, 6, 2, 6)
P_COUNT = 32
Q_COUNT = 40
QKV0, FC0 = 1536, 2112
COLS, PAIRW = 2880, 1344


def gram_schmidt(block):
    rows = lax.broadcasted_iota(jnp.int32, (8, 1), 0)
    for index in range(8):
        row = block[index : index + 1]
        row = row * lax.rsqrt(jnp.sum(row * row, axis=-1, keepdims=True) + TINY)
        inner = jnp.sum(block * row, axis=-1, keepdims=True)
        inner = jnp.where(rows > index, inner, 0.0)
        block = jnp.where(rows == index, row, block - inner * row)
    return block


def grad_kernel(
    a_ref, m_ref, dy_ref, dz_ref, o_ref, x_ref, g_ref, cerr_ref, rerr_ref,
    dmod_ref, small_ref, dbias_ref, right_ref, cs_ref, c_ref, t1_ref, a1t_ref, tf_ref, hot_ref, wmod_ref, wto_ref,
    mcol_ref, mrow_ref, left_ref, rightn_ref, ps_ref, pr_ref, qs_ref, qrs_ref, misc_ref, gtin_ref, gtout_ref, gtab_ref, gtok_ref, gvec_ref,
    mc, mr, sc, sr, rc, rr, av, mv, dyv, dzv, ov, xv, gv,
    dmo, smo, dbo, dm8, dma, dsc, dss, dts, dtl, tks, tkl, px, pland, py, qx, qland, qy,
    load_sem, send_sem, recv_sem,
):
    net = Peers(send_sem, recv_sem)
    w, t, c = net.w, net.t, net.c
    n = net.n
    share = D // n
    lo = lax.broadcasted_iota(jnp.int32, (1, 128), 1) < 64
    loads = {}

    def load(name, src, dst, index):
        op = pltpu.make_async_copy(src, dst, load_sem.at[index])
        op.start()
        loads[name] = op

    load("x", x_ref, xv, 0)
    load("a", a_ref, av, 1)
    load("m", m_ref, mv, 2)
    load("g", g_ref, gv, 3)
    load("dz", dz_ref, dzv, 4)
    load("o", o_ref, ov, 5)
    load("dy", dy_ref, dyv, 6)
    load("ce", cerr_ref, mc, 7)
    load("re", rerr_ref, mr, 8)
    net.barrier()
    side = [
        net.core_push(dmod_ref, dmo, 0),
        net.core_push(small_ref, smo, 1),
        net.core_push(dbias_ref.at[1 - c], dbo, 2),
    ]

    def chunk(i, size=256):
        return pl.ds(pl.multiple_of(i * size, size), size)

    def col_part(which, i):
        left = av[:, chunk(i)]
        first = tdot(left, xv[which, :, 0:640])
        second = tdot(mv[:, chunk(i)], xv[which, :, 512:1408])
        edge = jnp.where(lo, first[:, 512:640], second[:, 0:128])
        return first[:, 0:512], edge, second[:, 128:832]

    for name in ("x", "a", "m"):
        loads[name].wait()
    col_ops, row_ops = [], []

    @pl.loop(0, 3)
    def _(i):
        first, edge, second = col_part(1 - c, i)
        sc[chunk(i), 0:512] = first
        sc[chunk(i), 512:640] = edge
        sc[chunk(i), 640:1344] = second

    for i in range(3):
        col_ops.append(net.core_push(sc.at[256 * i : 256 * i + 256], rc.at[256 * i : 256 * i + 256], 3 + i))
    wait_all(side)
    for lat in range(4):
        for piece in range(2):
            span = slice(D * piece, D * piece + D)
            dm8[pl.ds(4 * c + lat, 1), span] = dmod_ref[lat, pl.ds(2 * t + piece, 1), :]
            dm8[pl.ds(4 * (1 - c) + lat, 1), span] = dmo[lat, pl.ds(2 * t + piece, 1), :]
    dma[w] = dm8[...]
    dm_ops = net.dp_push(lambda peer: dm8, dma.at[w], 16)
    for name in ("g", "dz", "o", "dy"):
        loads[name].wait()

    @pl.loop(0, 3)
    def _(i):
        sr[pl.ds(pl.multiple_of(192 + 256 * i, 64), 256), :] = tdot(gv[1 - c, :, chunk(i)], dzv[...])

    sr[0:192, :] = tdot(ov[1 - c], dyv[...])[0:192]
    for i in range(3):
        row_ops.append(net.core_push(sr.at[320 * i : 320 * i + 320], rr.at[320 * i : 320 * i + 320], 6 + i))
    total = small_ref[...] + smo[...]
    for k in range(n):
        tks[k, :, 0:share] = total[:, share * k : share * k + share]
    tkl[w] = tks[w]
    tok_ops = net.dp_push(lambda peer: tks.at[peer], tkl.at[w], 24)
    loads["ce"].wait()
    dms = split3(dm8[...])
    right_side = jnp.concatenate([dms[0], dms[1], dms[0], dms[2], dms[1], dms[0]], axis=0)
    for k in range(n):
        cs = split3(cs_ref[k])
        left_side = jnp.concatenate([cs[0], cs[0], cs[1], cs[0], cs[1], cs[2]], axis=0)
        mc[share * k : share * k + share, 0:QKV0] += tdot(left_side, right_side)[0:share]
    wait_all(col_ops)

    @pl.loop(0, 3)
    def _(i):
        first, edge, second = col_part(c, i)
        rows = chunk(i)
        mc[rows, 1536:2048] += first + rc[rows, 0:512]
        mc[rows, 2048:2176] += edge + rc[rows, 512:640]
        mc[rows, 2176:2880] += second + rc[rows, 640:1344]

    out_col = pltpu.make_async_copy(mc, mcol_ref, load_sem.at[0])
    out_col.start()
    wait_all(dm_ops)
    dmx = dma[...].reshape(8 * n, QKV0)
    part = sum(ndot(piece, wmod_ref[...]) for piece in split3(dmx))
    dss[...] = part
    dsc[t] = part
    ds_ops = net.tensor_push(dss, dsc.at[t], 32)
    loads["re"].wait()
    wait_all(row_ops)

    @pl.loop(0, 3)
    def _(i):
        rows = pl.ds(pl.multiple_of(192 + 256 * i, 64), 256)
        mr[rows, :] += tdot(gv[c, :, chunk(i)], dzv[...]) + rr[rows, :]

    mr[0:192, :] += tdot(ov[c], dyv[...])[0:192] + rr[0:192, :]
    out_row = pltpu.make_async_copy(mr, mrow_ref, load_sem.at[1])
    out_row.start()
    right = right_ref[...]
    lanes = lax.broadcasted_iota(jnp.int32, (8, COLS), 1)
    zero = jnp.zeros((8, COLS), F32)
    col_right = right[:, 0:COLS]
    stack = []
    for first, last in ((0, QKV0), (QKV0, FC0), (FC0, COLS)):
        cut = jnp.where((lanes >= first) & (lanes < last), col_right, zero)
        high = cut.astype(BF).astype(F32)
        stack += [high, cut - high]
    col_side = jnp.concatenate(stack + [jnp.zeros((80, COLS), F32)], axis=0).T.astype(BF)
    stack = []
    for first in (COLS, COLS + D):
        cut = right[:, first : first + D]
        high = cut.astype(BF).astype(F32)
        stack += [high, cut - high]
    row_side = jnp.concatenate(stack + [jnp.zeros((96, D), F32)], axis=0).T.astype(BF)

    def left_chunk(values, side):
        high, low = split2(values)
        return dot(high, side) + dot(low, side)

    for i in range(6):
        got = left_chunk(mc[128 * i : 128 * i + 128, :], col_side).T
        for k in range(3):
            px[6 * k + i] = got[16 * k : 16 * k + 8] + got[16 * k + 8 : 16 * k + 16]
    got = left_chunk(mr[0:192, :], row_side)
    got = jnp.concatenate([got, jnp.zeros((64, 128), F32)], axis=0).T
    for i in range(2):
        px[18 + i] = got[0:8, 128 * i : 128 * i + 128] + got[8:16, 128 * i : 128 * i + 128]
    for i in range(6):
        got = left_chunk(mr[192 + 128 * i : 320 + 128 * i, :], row_side).T
        px[20 + i] = got[16:24] + got[24:32]
    bmod = colsum(dm8[...])
    brest = dbias_ref[c] + dbo[...]
    for i in range(12):
        px[26 + i // 8, i % 8 : i % 8 + 1, :] = bmod[:, 128 * i : 128 * i + 128]
    for i in range(11):
        k = 12 + i
        px[26 + k // 8, k % 8 : k % 8 + 1, :] = brest[:, 128 * i : 128 * i + 128]
    px[28, 7:8, :] = jnp.zeros((1, 128), F32)
    px[29] = total[32:40, 0:128]
    px[30] = jnp.zeros((8, 128), F32)
    px[31] = jnp.zeros((8, 128), F32)

    def scatter(x, land, per, base):
        own = pl.ds(w * per, per)
        land[w] = x[own]
        return net.dp_push(lambda peer: x.at[pl.ds(peer * per, per)], land.at[w], base)

    def collect(land, y, per, base, ops):
        wait_all(ops)
        own = pl.ds(w * per, per)
        y[own] = sum(land[k] for k in range(1, n)) + land[0]
        return net.dp_push(lambda peer: y.at[own], y.at[own], base)

    ops = scatter(px, pland, P_COUNT // n, 40)
    wait_all(ds_ops)
    dcond = (dsc[0] + dsc[1] + dsc[2] + dsc[3]) * silu_slope_k(c_ref[...])
    gtout_ref[...] = hdot(a1t_ref[...], dcond)
    gtab_ref[...] = htdot(hot_ref[...], dcond)
    gvec_ref[...] = jnp.zeros_like(gvec_ref)
    gvec_ref[0:1] = colsum(dcond)
    dtime = sum(ndot(piece, wto_ref[...]) for piece in split3(dcond))
    for k in range(n):
        dts[k, :, 0:share] = dtime[:, share * k : share * k + share]
    dtl[w] = dts[w]
    dt_ops = net.dp_push(lambda peer: dts.at[peer], dtl.at[w], 56)
    ops = collect(pland, py, P_COUNT // n, 48, ops)
    wait_all(tok_ops)
    gtok_ref[...] = sum(tkl[k] for k in range(1, n)) + tkl[0]
    wait_all(ops)
    base = 0
    bases = []
    for index, count in enumerate(P_TILES):
        block = gram_schmidt(jnp.concatenate([py[base + k] for k in range(count)], axis=1))
        bases.append(block)
        base += count
    offset = 0
    for block, width in zip(bases, (D, D, D, 192, D)):
        left_ref[:, offset : offset + width] = block[:, 0:width]
        offset += width
    misc_ref[...] = py[26:30]

    def halves(block):
        high = block.astype(BF).astype(F32)
        return [high, block - high]

    col_left = jnp.concatenate(halves(bases[0]) + halves(bases[1]) + halves(bases[2]), axis=0).astype(BF)

    def right_part(values, left):
        high, low = split2(values)
        return dot(left, high) + dot(left, low)

    for i in range(23):
        width = 128 if i < 22 else 64
        got = right_part(mc[:, 128 * i : 128 * i + width], col_left)
        got = [got[16 * k : 16 * k + 8] + got[16 * k + 8 : 16 * k + 16] for k in range(3)]
        if i < 12:
            qx[i] = got[0]
        elif i < 16:
            qx[i] = got[1]
        elif i == 16:
            qx[i] = jnp.where(lo, got[1], got[2])
        elif i < 22:
            qx[i] = got[2]
        else:
            qx[i] = jnp.concatenate([got[2], jnp.zeros((8, 64), F32)], axis=1)
    proj_left = jnp.concatenate(halves(bases[3][:, 0:192]), axis=0).astype(BF)
    fc_left = jnp.concatenate(halves(bases[4]), axis=0).astype(BF)
    for k, (rows, left) in enumerate(((slice(0, 192), proj_left), (slice(192, 960), fc_left))):
        got = right_part(mr[rows, :], left)
        got = got[0:8] + got[8:16]
        for i in range(6):
            qx[23 + 6 * k + i] = got[:, 128 * i : 128 * i + 128]
    for i in range(35, Q_COUNT):
        qx[i] = jnp.zeros((8, 128), F32)
    ops = scatter(qx, qland, Q_COUNT // n, 64)
    wait_all(dt_ops)
    dtime = (sum(dtl[k] for k in range(1, n)) + dtl[0]) * silu_slope_k(t1_ref[...])
    gtin_ref[...] = htdot(tf_ref[...], dtime)
    gvec_ref[1:2] = colsum(dtime)
    ops = collect(qland, qy, Q_COUNT // n, 72, ops)
    wait_all(ops)
    def stack_left(blocks):
        rows = []
        for block in blocks:
            high, low = halves(block)
            rows += [high, low, high]
        rows.append(jnp.zeros((128 - 8 * len(rows), rows[0].shape[1]), F32))
        return jnp.concatenate(rows, axis=0).T.astype(BF)

    def stack_right(blocks):
        rows = []
        for block in blocks:
            high, low = halves(block)
            rows += [high, high, low]
        rows.append(jnp.zeros((128 - 8 * len(rows), rows[0].shape[1]), F32))
        return jnp.concatenate(rows, axis=0).astype(BF)

    ps_ref[...] = stack_left(bases[:3])
    pr_ref[...] = jnp.zeros_like(pr_ref)
    pr_ref[0:192, :] = stack_left([bases[3]])[0:192]
    fc_stack = stack_left([bases[4]])
    pr_ref[192:960, :] = jnp.concatenate([jnp.zeros((D, 24), BF), fc_stack[:, 0:104]], axis=1)
    qc = jnp.concatenate([qy[i] for i in range(23)], axis=1)
    span = lax.broadcasted_iota(jnp.int32, (8, 2944), 1)
    cuts = [
        jnp.where((span >= first) & (span < last), qc, 0.0) for first, last in ((0, QKV0), (QKV0, FC0), (FC0, COLS))
    ]
    qs_ref[...] = stack_right(cuts)
    qr = [jnp.concatenate([qy[23 + 6 * k + i] for i in range(6)], axis=1) for k in range(2)]
    qrs_ref[...] = stack_right(qr)
    rightn_ref[:, 0:COLS] = qc[:, 0:COLS]
    rightn_ref[:, COLS : COLS + D] = qr[0]
    rightn_ref[:, COLS + D : COLS + 2 * D] = qr[1]
    net.finish()
    out_col.wait()
    out_row.wait()


def run_grad(a, m, dy, dz, o, x, g, cerr, rerr, dmod, small, dbias, right, cs, cond, t1, a1t, tf, hot, wmod, wto, n):
    S = jax.ShapeDtypeStruct
    V = pltpu.VMEM
    rows = a.shape[0]
    lat = 8 * n
    share = D // n
    any_spec = pl.BlockSpec(memory_space=pl.ANY)
    vm = pl.BlockSpec(memory_space=pltpu.VMEM)
    outs = [
        S((D, COLS), F32), S((960, D), F32), S((8, 3264), F32), S((8, 4416), F32),
        S((D, 128), BF), S((960, 128), BF), S((128, 2944), BF), S((128, D), BF), S((4, 8, 128), F32),
        S((FREQ, 128), F32), S((D, 128), F32), S((128, 128), F32), S((40, 128), F32), S((8, 128), F32),
    ]
    scratch = [
        V((D, COLS), F32), V((960, D), F32), V((D, PAIRW), F32), V((960, D), F32), V((D, PAIRW), F32), V((960, D), F32),
        V((rows, D), BF), V((rows, D), BF), V((rows, D), BF), V((rows, D), BF),
        V((2, rows, 256), BF), V((2, rows, 1408), BF), V((2, rows, D), BF),
        V((4, 8, D), F32), V((40, D), F32), V((1, 1408), F32), V((8, QKV0), F32), V((n, 8, QKV0), F32),
        V((4, lat, 128), F32), V((lat, 128), F32), V((n, lat, 128), F32), V((n, lat, 128), F32),
        V((n, 40, 128), F32), V((n, 40, 128), F32),
        V((P_COUNT, 8, 128), F32), V((n, P_COUNT // n, 8, 128), F32), V((P_COUNT, 8, 128), F32),
        V((Q_COUNT, 8, 128), F32), V((n, Q_COUNT // n, 8, 128), F32), V((Q_COUNT, 8, 128), F32),
        pltpu.SemaphoreType.DMA((9,)), pltpu.SemaphoreType.DMA((80,)), pltpu.SemaphoreType.DMA((80,)),
    ]
    return pl.pallas_call(
        grad_kernel,
        out_shape=outs,
        in_specs=[any_spec] * 9 + [vm] * 12,
        out_specs=[any_spec] * 2 + [vm] * 12,
        scratch_shapes=scratch,
        compiler_params=pltpu.CompilerParams(collective_id=1, has_side_effects=True, vmem_limit_bytes=60 * 1024 * 1024),
        name="grad",
    )(a, m, dy, dz, o, x, g, cerr, rerr, dmod, small, dbias, right, cs, cond, t1, a1t, tf, hot, wmod, wto)


def apply_kernel(
    w_ref, mcol_ref, mrow_ref, pbt_ref, pr_ref, qc_ref, qr_ref, cw_ref, cm_ref, rw_ref, rm_ref,
    cres_ref, rres_ref, cn_ref, cmn_ref, rn_ref, rmn_ref, *, n
):
    step = pl.program_id(0)
    mine = w_ref[0]
    hat = dot(pbt_ref[...], qc_ref[...])
    cres_ref[...] = mcol_ref[...] - hat[:, 0:COLS] * (1.0 / n)

    @pl.when(step == mine)
    def _():
        mom = DECAY * cm_ref[...] + hat[:, 0:COLS]
        cmn_ref[...] = mom
        cn_ref[...] = cw_ref[...] - LEARN_RATE * mom

    rhat = dot(pr_ref[...], qr_ref[...])
    rres_ref[...] = mrow_ref[...] - rhat * (1.0 / n)

    pick = lax.broadcasted_iota(jnp.int32, (D, 128), 0) == mine * (D // n) + lax.broadcasted_iota(jnp.int32, (D, 128), 1)
    own = dot(qr_ref[...], jnp.where(pick, 1.0, 0.0).astype(BF)).astype(BF)
    part = dot(pr_ref[...], own)[:, 0 : D // n]
    mom = DECAY * rm_ref[...] + part
    rmn_ref[...] = mom
    rn_ref[...] = rw_ref[...] - LEARN_RATE * mom


def run_apply(w, mcol, mrow, pbt, pr, qcs, qrs, cw, cm, rw, rm, n):
    share = D // n
    S = jax.ShapeDtypeStruct
    rowc = 960 // n
    blk = lambda r, cc: pl.BlockSpec((r, cc), lambda i, *_: (i, 0))
    full = lambda r, cc: pl.BlockSpec((r, cc), lambda i, *_: (0, 0))
    return pl.pallas_call(
        functools.partial(apply_kernel, n=n),
        grid_spec=pltpu.PrefetchScalarGridSpec(
            num_scalar_prefetch=1,
            grid=(n,),
            in_specs=[blk(share, COLS), blk(rowc, D), blk(share, 128), blk(rowc, 128), full(128, 2944), full(128, D),
                full(share, COLS), full(share, COLS), blk(rowc, share), blk(rowc, share)],
            out_specs=[blk(share, COLS), blk(rowc, D), full(share, COLS), full(share, COLS), blk(rowc, share), blk(rowc, share)],
        ),
        out_shape=[S((D, COLS), F32), S((960, D), F32), S((share, COLS), F32), S((share, COLS), F32), S((960, share), F32), S((960, share), F32)],
        compiler_params=pltpu.CompilerParams(vmem_limit_bytes=48 * 1024 * 1024),
        name="apply",
    )(w, mcol, mrow, pbt, pr, qcs, qrs, cw, cm, rw, rm)


def position_rows(token_ids):
    quarter = D // 4
    omega = 1.0 / 10000.0 ** (jnp.arange(quarter, dtype=jnp.float32) / quarter)
    row_pos = (token_ids // GRID).astype(jnp.float32)[:, None] * omega[None, :]
    col_pos = (token_ids % GRID).astype(jnp.float32)[:, None] * omega[None, :]
    return jnp.concatenate(
        [jnp.sin(row_pos), jnp.cos(row_pos), jnp.sin(col_pos), jnp.cos(col_pos)], axis=1
    )


def time_features(times):
    half = FREQ // 2
    freqs = jnp.exp(-math.log(10000.0) * jnp.arange(half, dtype=jnp.float32) / half)
    angles = 1000.0 * times[:, None] * freqs[None, :]
    return jnp.concatenate([jnp.cos(angles), jnp.sin(angles)], axis=1)


def small_starts():
    counts = [PATCH_IN, 1, FREQ, 1, D, 1, CLASSES, PATCH_IN, 1, 1]
    starts = [0]
    for amount in counts:
        starts.append(starts[-1] + amount)
    return starts


def cut_parts(array, widths, axis):
    pieces = []
    offset = 0
    for width in widths:
        pieces.append(lax.slice_in_dim(array, offset, offset + width, axis=axis))
        offset = offset + width
    return pieces


def ortho_kernel(x_ref, o_ref):
    count = x_ref.shape[0]
    rows = [x_ref[index] for index in range(count)]
    for index in range(count):
        vector = rows[index]
        vector = vector * lax.rsqrt(jnp.sum(vector * vector, axis=-1, keepdims=True) + TINY)
        o_ref[index] = vector
        for later in range(index + 1, count):
            rows[later] = rows[later] - jnp.sum(rows[later] * vector, axis=-1, keepdims=True) * vector


def orthonormal_all(parts):
    stacked = jnp.stack([jnp.pad(part, ((0, 0), (0, D - part.shape[1]))) for part in parts], axis=1)
    stacked = jnp.pad(stacked, ((0, 0), (0, 8 - len(parts)), (0, 0)))
    out = pl.pallas_call(ortho_kernel, out_shape=jax.ShapeDtypeStruct(stacked.shape, F32), name="ortho")(stacked)
    return [out[:, index, : part.shape[1]] for index, part in enumerate(parts)]


def rounded(values):
    return lax.optimization_barrier(values.astype(BF)).astype(F32)


def silu_slope(values):
    gate = jax.nn.sigmoid(values)
    return gate * (1.0 + values * (1.0 - gate))


def shards_general(
    clean_latents,
    noise_draw,
    timesteps,
    labels,
    col_weights,
    col_moments,
    col_errors,
    row_weights,
    row_moments,
    row_errors,
    bias_weights,
    bias_moments,
    small_weights,
    small_moments,
    head_bias,
    head_moments,
    right_factors,
):
    tensor_size = lax.axis_size("tensor")
    data_size = lax.axis_size("dp")
    tensor_rank = lax.axis_index("tensor")
    data_rank = lax.axis_index("dp")
    batch = clean_latents.shape[0]
    half = batch // 2
    share = D // data_size
    mod_width = 8 * D // tensor_size
    qkv_width = 3 * D // tensor_size
    ffn_width = FF // tensor_size
    proj_rows = D // tensor_size
    count_all = data_size * batch * SEQ * PATCH_IN
    col_widths = [mod_width, qkv_width, ffn_width]
    core = lax.rem(tensor_rank, 2)
    base = tensor_rank - core
    pair = [(index, index + 1 - 2 * (index % 2)) for index in range(tensor_size)]

    def swap(values):
        return lax.ppermute(values, "tensor", pair)

    col_low = col_weights[:, 0, :].astype(BF)
    row_low = row_weights[0].astype(BF).T
    packed = jnp.concatenate(
        [
            col_low[:, mod_width : mod_width + qkv_width],
            row_low[:, :proj_rows],
            col_low[:, mod_width + qkv_width :],
            row_low[:, proj_rows:],
        ],
        axis=1,
    )
    wall = lax.all_gather(lax.all_gather(packed, "dp", axis=0, tiled=True), "tensor", axis=0)
    starts = small_starts()
    small_low = small_weights.astype(BF)
    small_exact = rounded(small_weights)
    picked = jnp.concatenate([small_low[: starts[2]], small_low[starts[7] :]], axis=0)
    emb = lax.all_gather(picked.astype(F32), "dp", axis=1, tiled=True)
    w_patch = emb[:16].astype(BF)
    b_patch = emb[16:17]
    w_head = emb[17:33].astype(BF)
    b_proj = emb[33:34]
    b_fc2 = emb[34:35]
    w_tin = small_exact[starts[2] : starts[3]]
    b_tin = small_exact[starts[3]]
    w_tout = small_exact[starts[4] : starts[5]]
    b_tout = small_exact[starts[5]]
    table = small_exact[starts[6] : starts[7]]
    bias_exact = rounded(bias_weights[0])
    head_exact = rounded(head_bias)
    w_mod = rounded(col_weights[:, 0, :mod_width])
    bias_all = lax.all_gather(bias_exact, "tensor", axis=0)
    times_all = lax.all_gather(timesteps, "dp", axis=0, tiled=True)
    labels_all = lax.all_gather(labels, "dp", axis=0, tiled=True)
    time_feat = time_features(times_all)
    time_hidden = exact_dot(time_feat, w_tin) + b_tin
    time_act = lax.all_gather(jax.nn.silu(time_hidden), "dp", axis=1, tiled=True)
    onehot = (labels_all[:, None] == jnp.arange(CLASSES, dtype=jnp.int32)[None, :]).astype(F32)
    condition = exact_dot(time_act, w_tout) + b_tout + exact_dot(onehot, table)
    cond_act = jax.nn.silu(condition)
    mod_part = exact_dot(cond_act, w_mod)
    mod_own = lax.psum_scatter(mod_part, "dp", scatter_dimension=0, tiled=True) + bias_exact[:mod_width]
    mod_full = lax.all_gather(mod_own, "tensor", axis=1, tiled=True).reshape(batch, 8, D)
    cond_rows = lax.all_to_all(cond_act, "dp", split_axis=0, concat_axis=1, tiled=True)

    def mine(values):
        return lax.dynamic_slice_in_dim(values, core * half, half, 0)

    bq = jnp.pad(bias_all[:, mod_width : mod_width + qkv_width], ((0, 0), (0, 768 - qkv_width)))[:, None]
    b1 = bias_all[:, mod_width + qkv_width :][:, None]
    positions = position_rows(jnp.arange(SEQ, dtype=jnp.int32))
    (a, m, dy, dz, o, x, g, dmod, small, dbias) = run_block(
        base.reshape(1),
        mine(timesteps),
        mine(clean_latents),
        mine(noise_draw),
        mine(mod_full),
        wall,
        positions,
        w_patch,
        b_patch,
        w_head,
        head_exact[None],
        b_proj,
        b_fc2,
        bq,
        b1,
        count_all,
    )
    rows = half * SEQ

    def flat(values):
        return values.reshape(rows, values.shape[-1])

    def pick(values, which):
        return lax.dynamic_index_in_dim(values, which, 0, keepdims=False)

    def gradients(which):
        return (
            tdot(flat(a), flat(pick(x, which))[:, :qkv_width]),
            tdot(flat(m), flat(pick(x, which))[:, qkv_width : qkv_width + ffn_width]),
            tdot(flat(pick(o, which))[:, :proj_rows], flat(dy)),
            tdot(flat(pick(g, which)), flat(dz)),
            pick(dbias, which)[0, :qkv_width],
            pick(dbias, which)[0, qkv_width : qkv_width + ffn_width],
        )

    other = swap(gradients(1 - core))
    own = gradients(core)
    g_qkv, g_fc1, g_proj, g_fc2, g_bqkv, g_bfc1 = [left + right for left, right in zip(own, other)]
    dmod_own = dmod.reshape(half, 8 * D)
    dmod_other = swap(dmod_own)
    dmod_group = jnp.where(
        core == 0,
        jnp.concatenate([dmod_own, dmod_other], axis=0),
        jnp.concatenate([dmod_other, dmod_own], axis=0),
    )
    d_mod = lax.dynamic_slice_in_dim(dmod_group, tensor_rank * mod_width, mod_width, 1)
    g_bmod = jnp.sum(d_mod, axis=0)
    g_mod = exact_tdot(cond_rows, d_mod)
    d_mod_all = lax.all_gather(d_mod, "dp", axis=0, tiled=True)
    d_cond = lax.psum(exact_ndot(d_mod_all, w_mod), "tensor") * silu_slope(condition)
    g_table = exact_tdot(onehot, d_cond)
    g_btout = jnp.sum(d_cond, axis=0)
    g_tout = exact_tdot(time_act, d_cond)
    d_time = lax.psum_scatter(exact_ndot(d_cond, w_tout), "dp", scatter_dimension=1, tiled=True)
    d_time = d_time * silu_slope(time_hidden)
    g_btin = jnp.sum(d_time, axis=0)
    g_tin = exact_tdot(time_feat, d_time)
    small_own = lax.psum(lax.psum_scatter(small, "dp", scatter_dimension=1, tiled=True), "tensor") * 0.5
    head_sum, loss_value = lax.psum((small[35, :PATCH_IN] * 0.5, small[36, 0] * 0.5), ("dp", "tensor"))
    small_step = jnp.concatenate(
        [
            small_own[:16],
            small_own[32:33],
            g_tin,
            g_btin[None],
            g_tout,
            g_btout[None],
            g_table,
            small_own[16:32],
            small_own[33:34],
            small_own[34:35],
        ],
        axis=0,
    )
    bias_sum = lax.psum(jnp.concatenate([g_bmod, g_bqkv, g_bfc1], axis=0), "dp")
    col_cuts = cut_parts(col_errors[0, 0], col_widths, 1)
    row_cuts = cut_parts(row_errors[0, 0], [proj_rows, ffn_width], 0)
    matrices = [
        g_mod + col_cuts[0],
        g_qkv + col_cuts[1],
        g_fc1 + col_cuts[2],
        g_proj + row_cuts[0],
        g_fc2 + row_cuts[1],
    ]
    right_pieces = cut_parts(right_factors[0], col_widths + [D, D], 1)
    left_local = jnp.concatenate([exact_ndot(right_pieces[i], matrices[i]) for i in range(5)], axis=1)
    left_sum = lax.psum(left_local, "dp")
    bases = orthonormal_all(cut_parts(left_sum, [D, D, D, proj_rows, ffn_width], 1))
    right_local = jnp.concatenate([exact_dot(bases[i], matrices[i]) for i in range(5)], axis=1)
    right_sum = lax.psum(right_local, "dp")
    right_split = cut_parts(right_sum, col_widths + [D, D], 1)
    approx = [exact_tdot(bases[i], right_split[i]) for i in range(5)]
    rest = [matrices[i] - approx[i] / data_size for i in range(5)]
    col_residue = jnp.concatenate(rest[:3], axis=1)[None, None]
    row_residue = jnp.concatenate(rest[3:], axis=0)[None, None]

    def own_columns(values):
        return lax.dynamic_slice_in_dim(values, data_rank * share, share, 1)

    col_step = jnp.concatenate(
        [exact_tdot(own_columns(bases[i]), right_split[i]) for i in range(3)], axis=1
    )[:, None, :]
    row_step = jnp.concatenate(
        [exact_tdot(bases[i], own_columns(right_split[i])) for i in (3, 4)], axis=0
    )[None]
    col_momentum = DECAY * col_moments + col_step
    col_new = col_weights - LEARN_RATE * col_momentum
    row_momentum = DECAY * row_moments + row_step
    row_new = row_weights - LEARN_RATE * row_momentum
    small_momentum = DECAY * small_moments + small_step
    small_new = small_weights - LEARN_RATE * small_momentum
    bias_momentum = DECAY * bias_moments + bias_sum[None]
    bias_new = bias_weights - LEARN_RATE * bias_momentum
    head_momentum = DECAY * head_moments + head_sum
    head_new = head_bias - LEARN_RATE * head_momentum
    left_factors = jnp.concatenate(bases, axis=1)[None]
    right_new = right_sum[None]
    return (
        loss_value,
        col_new,
        col_momentum,
        col_residue,
        row_new,
        row_momentum,
        row_residue,
        bias_new,
        bias_momentum,
        small_new,
        small_momentum,
        head_new,
        head_momentum,
        left_factors,
        right_new,
    )


def shards(
    clean_latents,
    noise_draw,
    timesteps,
    labels,
    col_weights,
    col_moments,
    col_errors,
    row_weights,
    row_moments,
    row_errors,
    bias_weights,
    bias_moments,
    small_weights,
    small_moments,
    head_bias,
    head_moments,
    right_factors,
):
    tensor_size = lax.axis_size("tensor")
    data_size = lax.axis_size("dp")
    tensor_rank = lax.axis_index("tensor")
    data_rank = lax.axis_index("dp")
    batch = clean_latents.shape[0]
    half = batch // 2
    share = D // data_size
    mod_width = 8 * D // tensor_size
    qkv_width = 3 * D // tensor_size
    ffn_width = FF // tensor_size
    proj_rows = D // tensor_size
    count_all = data_size * batch * SEQ * PATCH_IN
    col_widths = [mod_width, qkv_width, ffn_width]
    core = lax.rem(tensor_rank, 2)
    base = tensor_rank - core
    pair = [(index, index + 1 - 2 * (index % 2)) for index in range(tensor_size)]

    def swap(values):
        return lax.ppermute(values, "tensor", pair)

    col_low = col_weights[:, 0, :].astype(BF)
    row_low = row_weights[0].astype(BF).T
    packed = jnp.concatenate(
        [
            col_low[:, mod_width : mod_width + qkv_width],
            row_low[:, :proj_rows],
            col_low[:, mod_width + qkv_width :],
            row_low[:, proj_rows:],
        ],
        axis=1,
    )
    wall = lax.all_gather(lax.all_gather(packed, "dp", axis=0, tiled=True), "tensor", axis=0)
    starts = small_starts()
    small_low = small_weights.astype(BF)
    small_exact = rounded(small_weights)
    picked = jnp.concatenate([small_low[: starts[2]], small_low[starts[7] :]], axis=0)
    emb = lax.all_gather(picked.astype(F32), "dp", axis=1, tiled=True)
    w_patch = emb[:16].astype(BF)
    b_patch = emb[16:17]
    w_head = emb[17:33].astype(BF)
    b_proj = emb[33:34]
    b_fc2 = emb[34:35]
    w_tin = small_exact[starts[2] : starts[3]]
    b_tin = small_exact[starts[3]]
    w_tout = small_exact[starts[4] : starts[5]]
    b_tout = small_exact[starts[5]]
    table = small_exact[starts[6] : starts[7]]
    bias_exact = rounded(bias_weights[0])
    head_exact = rounded(head_bias)
    w_mod = rounded(col_weights[:, 0, :mod_width])
    bias_all = lax.all_gather(bias_exact, "tensor", axis=0)
    times_all = lax.all_gather(timesteps, "dp", axis=0, tiled=True)
    labels_all = lax.all_gather(labels, "dp", axis=0, tiled=True)
    time_feat = time_features(times_all)
    time_hidden = exact_dot(time_feat, w_tin) + b_tin
    time_act = lax.all_gather(jax.nn.silu(time_hidden), "dp", axis=1, tiled=True)
    onehot = (labels_all[:, None] == jnp.arange(CLASSES, dtype=jnp.int32)[None, :]).astype(F32)
    condition = exact_dot(time_act, w_tout) + b_tout + exact_dot(onehot, table)
    cond_act = jax.nn.silu(condition)
    mod_part = exact_dot(cond_act, w_mod)
    mod_own = lax.psum_scatter(mod_part, "dp", scatter_dimension=0, tiled=True) + bias_exact[:mod_width]
    mod_full = lax.all_gather(mod_own, "tensor", axis=1, tiled=True).reshape(batch, 8, D)
    cond_rows = lax.all_to_all(cond_act, "dp", split_axis=0, concat_axis=1, tiled=True)

    def mine(values):
        return lax.dynamic_slice_in_dim(values, core * half, half, 0)

    bq = jnp.pad(bias_all[:, mod_width : mod_width + qkv_width], ((0, 0), (0, 768 - qkv_width)))[:, None]
    b1 = bias_all[:, mod_width + qkv_width :][:, None]
    positions = position_rows(jnp.arange(SEQ, dtype=jnp.int32))
    (a, m, dy, dz, o, x, g, dmod, small, dbias) = run_block(
        base.reshape(1),
        mine(timesteps),
        mine(clean_latents),
        mine(noise_draw),
        mine(mod_full),
        wall,
        positions,
        w_patch,
        b_patch,
        w_head,
        head_exact[None],
        b_proj,
        b_fc2,
        bq,
        b1,
        count_all,
    )
    rows = half * SEQ

    def flat(values):
        return values.reshape(values.shape[:-3] + (rows, values.shape[-1]))

    def wide(values):
        return jnp.pad(values, ((0, 0), (0, 128 - values.shape[1])))

    act_t = lax.transpose(time_act, (1, 0))
    conds = jnp.pad(cond_rows.reshape(batch, data_size, share).transpose(1, 0, 2), ((0, 0), (0, 0), (0, 128 - share)))
    mcol, mrow, left_all, right_sum, ps, pr, qs, qrs, misc, g_tin, g_tout, g_table, g_tok, g_vec = run_grad(
        flat(a), flat(m), flat(dy), flat(dz), flat(o), flat(x), flat(g),
        col_errors[0, 0], row_errors[0, 0], dmod, small, dbias, right_factors[0],
        conds, wide(condition), wide(time_hidden), act_t, time_feat, wide(onehot),
        jnp.pad(col_low[:, :mod_width], ((0, 128 - share), (0, 0))), wide(small_low[starts[4] : starts[5]]), data_size,
    )
    cres, rres, cn, cmn, rn, rmn = run_apply(
        data_rank.reshape(1), mcol, mrow, ps, pr, qs, qrs,
        col_weights[:, 0], col_moments[:, 0], row_weights[0], row_moments[0], data_size,
    )
    small_step = jnp.concatenate(
        [g_tok[:16], g_tok[32:33], g_tin, g_vec[1:2], g_tout, g_vec[0:1], g_table[:CLASSES], g_tok[16:32], g_tok[33:35]],
        axis=0,
    )[:, :share]
    col_new, col_momentum, col_residue = cn[:, None], cmn[:, None], cres[None, None]
    row_new, row_momentum, row_residue = rn[None], rmn[None], rres[None, None]
    small_momentum = DECAY * small_moments + small_step
    small_new = small_weights - LEARN_RATE * small_momentum
    bias_sum = misc[:3].reshape(3 * 8 * 128)[: bias_weights.shape[1]]
    head_sum = misc[3, 3, :PATCH_IN]
    loss_value = misc[3, 4, 0]
    bias_momentum = DECAY * bias_moments + bias_sum[None]
    bias_new = bias_weights - LEARN_RATE * bias_momentum
    head_momentum = DECAY * head_moments + head_sum
    head_new = head_bias - LEARN_RATE * head_momentum
    left_factors = left_all[None]
    right_new = right_sum[None]
    return (
        loss_value,
        col_new,
        col_momentum,
        col_residue,
        row_new,
        row_momentum,
        row_residue,
        bias_new,
        bias_momentum,
        small_new,
        small_momentum,
        head_new,
        head_momentum,
        left_factors,
        right_new,
    )


def solution(mesh):
    fits = mesh.shape["dp"] == 8 and mesh.shape["tensor"] == 4
    placed = (
        P("dp", None, None),
        P("dp", None, None),
        P("dp"),
        P("dp"),
        P("dp", "tensor", None),
        P("dp", "tensor", None),
        P("dp", "tensor", None, None),
        P("tensor", None, "dp"),
        P("tensor", None, "dp"),
        P("dp", "tensor", None, None),
        P("tensor", None),
        P("tensor", None),
        P(None, "dp"),
        P(None, "dp"),
        P(),
        P(),
        P("tensor", None, None),
    )
    return jax.shard_map(
        shards if fits else shards_general,
        mesh=mesh,
        in_specs=placed,
        out_specs=(
            P(),
            P("dp", "tensor", None),
            P("dp", "tensor", None),
            P("dp", "tensor", None, None),
            P("tensor", None, "dp"),
            P("tensor", None, "dp"),
            P("dp", "tensor", None, None),
            P("tensor", None),
            P("tensor", None),
            P(None, "dp"),
            P(None, "dp"),
            P(),
            P(),
            P("tensor", None, None),
            P("tensor", None, None),
        ),
        check_vma=False,
    )
```

```python
import functools
import math

import jax
import jax.numpy as jnp
from jax import lax
from jax.experimental import pallas as pl
from jax.experimental.pallas import tpu as pltpu
from jax.sharding import PartitionSpec as P

D = 768
HEADS = 12
HEAD_DIM = 64
FF = 3072
FREQ = 256
GRID = 16
PATCH_IN = 16
CLASSES = 32
SEQ = 256

EPSILON = 1e-06
TINY = 1e-30
DECAY = 0.9
LEARN_RATE = 100.0
TIME_OFFSET = 0.25
F32 = jnp.float32
BF = jnp.bfloat16
SCALE = 1.0 / math.sqrt(HEAD_DIM)
GELU_C = math.sqrt(2.0 / math.pi)


def exact_dot(left, right):
    return jnp.dot(left, right, precision=lax.Precision.HIGHEST, preferred_element_type=F32)


def exact_tdot(left, right):
    return lax.dot_general(left, right, (((0,), (0,)), ((), ())), precision=lax.Precision.HIGHEST, preferred_element_type=F32)


def exact_ndot(left, right):
    return lax.dot_general(left, right, (((1,), (1,)), ((), ())), precision=lax.Precision.HIGHEST, preferred_element_type=F32)


def dot(a,b): return lax.dot_general(a,b,(((1,),(0,)),((),())),preferred_element_type=F32)
def ndot(a,b): return lax.dot_general(a,b,(((1,),(1,)),((),())),preferred_element_type=F32)
def tdot(a,b): return lax.dot_general(a,b,(((0,),(0,)),((),())),preferred_element_type=F32)

def ln(h):
    c=h-jnp.mean(h,axis=-1,keepdims=True)
    v=jnp.mean(c*c,axis=-1,keepdims=True)
    r=lax.rsqrt(v+EPSILON)
    return c*r,r

def ln_back(dout,xh,r,scale):
    dx=dout*(1.0+scale)
    return r*(dx-jnp.mean(dx,axis=-1,keepdims=True)-xh*jnp.mean(dx*xh,axis=-1,keepdims=True))

def colsum(v): return jnp.sum(v,axis=0,keepdims=True)

def block_kernel(base_ref,times_ref,clean_ref,noise_ref,mod_ref,wall_ref,pe_ref,emb_ref,bh_ref,ball_ref,
           a_ref,m_ref,dy_ref,dz_ref,o_ref,dq_ref,du_ref,g_ref,dmod_ref,small_ref,dbq_ref,db1_ref,hb_ref,
           pe_s,r_s,p_s,gp_s,xh1_s,xh2_s,y_s,z_s,h_s,acc_s,r1_s,r2_s,*,count_all):
    step=pl.program_id(0)
    base=base_ref[0]
    t=times_ref[step]
    lo=lax.broadcasted_iota(jnp.int32,(1,128),1)<64
    @pl.when(step==0)
    def _():
        small_ref[...]=jnp.zeros_like(small_ref); dbq_ref[...]=jnp.zeros_like(dbq_ref); db1_ref[...]=jnp.zeros_like(db1_ref)
        hb_ref[...]=jnp.zeros_like(hb_ref)
        for i in range(GRID):
            pe_s[16*i:16*i+16,0:384]=jnp.broadcast_to(pe_ref[i:i+1,:],(16,384))
            pe_s[16*i:16*i+16,384:768]=pe_ref[...]
    clean=clean_ref[0].astype(F32); noise=noise_ref[0].astype(F32)
    mixed=(t*clean+(1.0-t)*noise).astype(BF)
    mod=lambda i: mod_ref[0,i:i+1,:]
    wp=emb_ref[0:16].astype(BF); wh=emb_ref[16:32].astype(BF)
    h0=tdot(mixed,wp)+emb_ref[32:33]+pe_s[...]
    h_s[...]=h0
    xh,r=ln(h0)
    xh1_s[...]=xh; r1_s[...]=r
    a_ref[0]=(xh*(1.0+mod(1))+mod(0)).astype(BF)
    y_s[...]=jnp.zeros_like(y_s)
    zero=jnp.zeros((),BF)
    roll=lambda v: pltpu.roll(v.astype(F32),64,1).astype(BF)
    def softmax_store(s,idx):
        s=s*SCALE
        e=jnp.exp(s-jnp.max(s,axis=-1,keepdims=True))
        p=e/jnp.sum(e,axis=-1,keepdims=True)
        p_s[idx]=p
        return p.astype(BF)
    @pl.loop(0,4)
    def _(j):
        own=(j>=base)&(j<base+2)
        k=j-base
        r_s[j]=(dot(a_ref[0],wall_ref[0,j])+ball_ref[j,:,0:768]).astype(BF)
        blk=lambda i: r_s[j,:,128*i:128*(i+1)]
        b0,b1,b2,b3,b4=[blk(i) for i in range(5)]
        p0=softmax_store(ndot(jnp.where(lo,b0,zero),roll(b0)),3*j)
        p1=softmax_store(ndot(jnp.where(lo,zero,b1),roll(b2)),3*j+1)
        p2=softmax_store(ndot(jnp.where(lo,b3,zero),roll(b3)),3*j+2)
        o01=jnp.where(lo,dot(p0,b1),dot(p1,b2)).astype(BF)
        o2=jnp.where(lo,dot(p2,b4),0.0).astype(BF)
        @pl.when(own)
        def _():
            o_ref[k,0,:,0:128]=o01; o_ref[k,0,:,128:256]=o2
        ro=roll(o01)
        ob4=jnp.where(lo,zero,ro)
        ob5=jnp.where(lo,ro,roll(o2))
        y_s[...]+=ndot(jnp.concatenate([ob4,ob5],axis=1),wall_ref[0,j,:,512:768])
    y=y_s[...]+emb_ref[33:34]
    y_s[...]=y
    h1=h_s[...]+mod(2)*y
    h_s[...]=h1
    xh,r=ln(h1)
    xh2_s[...]=xh; r2_s[...]=r
    m_ref[0]=(xh*(1.0+mod(4))+mod(3)).astype(BF)
    z_s[...]=jnp.zeros_like(z_s)
    @pl.loop(0,4)
    def _(j):
        own=(j>=base)&(j<base+2)
        k=j-base
        u=dot(m_ref[0],wall_ref[1,j])+ball_ref[j,:,768:1536]
        uu=u*u
        th=jnp.tanh(GELU_C*(u+0.044715*(uu*u)))
        cdf=0.5*(1.0+th)
        g=(u*cdf).astype(BF)
        gp_s[j]=cdf+0.5*u*(1.0-th*th)*(GELU_C*(1.0+3.0*0.044715*uu))
        @pl.when(own)
        def _(): g_ref[k,0]=g
        z_s[...]+=ndot(g,wall_ref[2,j])
    z=z_s[...]+emb_ref[34:35]
    z_s[...]=z
    h2=h_s[...]+mod(5)*z
    xh,r=ln(h2)
    fi=(xh*(1.0+mod(7))+mod(6)).astype(BF)
    pred=ndot(wh,fi)+bh_ref[...]
    diff=pred-(clean-noise)
    weight=1.0/(1.0-t+0.25)
    hb_ref[0:1,1:2]+=jnp.sum(colsum(weight*diff*diff),axis=1,keepdims=True)*(1.0/count_all)
    dpred=2.0*weight*diff*(1.0/count_all)
    hb_ref[:,0:1]+=jnp.sum(dpred,axis=1,keepdims=True)
    dpl=dpred.astype(BF)
    small_ref[16:32]+=dot(dpl,fi)
    dfi=tdot(dpl,wh)
    dmod_ref[0,6:7]=colsum(dfi); dmod_ref[0,7:8]=colsum(dfi*xh)
    dh=ln_back(dfi,xh,r,mod(7))
    h_s[...]=dh
    dmod_ref[0,5:6]=colsum(dh*z_s[...])
    dzf=dh*mod(5)
    small_ref[34:35]+=colsum(dzf)
    dz_ref[0]=dzf.astype(BF)
    acc_s[...]=jnp.zeros_like(acc_s)
    @pl.loop(0,4)
    def _(j):
        own=(j>=base)&(j<base+2)
        k=j-base
        du=dot(dz_ref[0],wall_ref[2,j])*gp_s[j]
        dul=du.astype(BF)
        @pl.when(own)
        def _():
            du_ref[k,0]=dul
            db1_ref[k]+=colsum(du)
        acc_s[...]+=ndot(dul,wall_ref[1,j])
    dm=acc_s[...]
    xh=xh2_s[...]
    dmod_ref[0,3:4]=colsum(dm); dmod_ref[0,4:5]=colsum(dm*xh)
    dh=h_s[...]+ln_back(dm,xh,r2_s[...],mod(4))
    h_s[...]=dh
    dmod_ref[0,2:3]=colsum(dh*y_s[...])
    dyf=dh*mod(2)
    small_ref[33:34]+=colsum(dyf)
    dy_ref[0]=dyf.astype(BF)
    acc_s[...]=jnp.zeros_like(acc_s)
    @pl.loop(0,4)
    def _(j):
        own=(j>=base)&(j<base+2)
        k=j-base
        do=dot(dy_ref[0],wall_ref[0,j,:,512:768]).astype(BF)
        r4=roll(do[:,0:128]); r5=roll(do[:,128:256])
        do0=jnp.where(lo,r4,zero); do1=jnp.where(lo,zero,r5); do2=jnp.where(lo,r5,zero)
        blk=lambda i: r_s[j,:,128*i:128*(i+1)]
        b0,b1,b2,b3,b4=[blk(i) for i in range(5)]
        def head(h,doh,v,):
            p=p_s[3*j+h]
            dv=tdot(p.astype(BF),doh)
            dp=ndot(doh,v)
            ds=(p*(dp-jnp.sum(p*dp,axis=-1,keepdims=True))).astype(BF)
            return dv,ds
        dv0,ds0=head(0,do0,b1)
        dv1,ds1=head(1,do1,b2)
        dv2,ds2=head(2,do2,b4)
        rb0=roll(b0); rb3=roll(b3)
        n0=jnp.where(lo,dot(ds0,rb0),tdot(ds0,rb0))*SCALE
        dq1=dot(ds1,roll(b2))*SCALE; dk1=tdot(ds1,roll(b1))*SCALE
        n1=jnp.where(lo,dv0,dq1); n2=jnp.where(lo,dk1,dv1)
        n3=jnp.where(lo,dot(ds2,rb3),tdot(ds2,rb3))*SCALE
        n4=jnp.where(lo,dv2,0.0)
        dqkv=jnp.concatenate([n0,n1,n2,n3,n4],axis=1)
        dl=dqkv.astype(BF)
        @pl.when(own)
        def _():
            dq_ref[k,0]=dl
            dbq_ref[k]+=colsum(dqkv)
        acc_s[...]+=ndot(dl,wall_ref[0,j,:,0:640])
    da=acc_s[...]
    xh=xh1_s[...]
    dmod_ref[0,0:1]=colsum(da); dmod_ref[0,1:2]=colsum(da*xh)
    dh=h_s[...]+ln_back(da,xh,r1_s[...],mod(1))
    small_ref[32:33]+=colsum(dh)
    small_ref[0:16]+=dot(mixed,dh.astype(BF))

def run_block(base,times,clean,noise,mod,wall,pe,emb,bh,ball,count_all):
    L=clean.shape[0]
    full=lambda a: pl.BlockSpec(a.shape,lambda i,*_: (0,)*a.ndim,pipeline_mode=pl.Buffered(1))
    lat=lambda *s: pl.BlockSpec((1,)+s,lambda i,*_:(i,)+(0,)*len(s))
    pair=lambda w: pl.BlockSpec((2,1,SEQ,w),lambda i,*_:(0,i,0,0))
    const=lambda *s: pl.BlockSpec(s,lambda i,*_:(0,)*len(s))
    S=jax.ShapeDtypeStruct
    outs=[S((L,SEQ,D),BF)]*4+[S((2,L,SEQ,256),BF),S((2,L,SEQ,640),BF),S((2,L,SEQ,768),BF),S((2,L,SEQ,768),BF),
        S((L,8,D),F32),S((40,D),F32),S((2,1,640),F32),S((2,1,768),F32),S((PATCH_IN,128),F32)]
    ospecs=[lat(SEQ,D)]*4+[pair(256),pair(640),pair(768),pair(768),lat(8,D),const(40,D),const(2,1,640),const(2,1,768),const(PATCH_IN,128)]
    V=pltpu.VMEM
    f=lambda: V((SEQ,D),F32)
    return pl.pallas_call(functools.partial(block_kernel,count_all=count_all),
        grid_spec=pltpu.PrefetchScalarGridSpec(num_scalar_prefetch=2,grid=(L,),
            in_specs=[lat(PATCH_IN,SEQ),lat(PATCH_IN,SEQ),lat(8,D)]+[full(v) for v in (wall,pe,emb,bh,ball)],
            out_specs=ospecs,
            scratch_shapes=[f(),V((4,SEQ,768),BF),V((12,SEQ,SEQ),F32),V((4,SEQ,768),F32),f(),f(),f(),f(),f(),f(),V((SEQ,1),F32),V((SEQ,1),F32)]),
        out_shape=outs,
        compiler_params=pltpu.CompilerParams(vmem_limit_bytes=60*1024*1024),
        name="block",
    )(base,times,clean,noise,mod,wall,pe,emb,bh,ball)


MESH = pl.DeviceIdType.MESH
HI = lax.Precision.HIGHEST


def hdot(a, b):
    return lax.dot_general(a, b, (((1,), (0,)), ((), ())), precision=HI, preferred_element_type=F32)


def hndot(a, b):
    return lax.dot_general(a, b, (((1,), (1,)), ((), ())), precision=HI, preferred_element_type=F32)


def htdot(a, b):
    return lax.dot_general(a, b, (((0,), (0,)), ((), ())), precision=HI, preferred_element_type=F32)


def split2(values):
    first = values.astype(BF)
    return first, (values - first.astype(F32)).astype(BF)


def split3(values):
    first, rest = values.astype(BF), values
    rest = rest - first.astype(F32)
    second = rest.astype(BF)
    return first, second, (rest - second.astype(F32)).astype(BF)


def silu_slope_k(values):
    gate = 1.0 / (1.0 + jnp.exp(-values))
    return gate * (1.0 + values * (1.0 - gate))


class Peers:
    def __init__(self, send_sem, recv_sem):
        self.w = lax.axis_index("dp")
        self.t = lax.axis_index("tensor")
        self.n = lax.axis_size("dp")
        self.tn = lax.axis_size("tensor")
        self.c = lax.rem(self.t, 2)
        self.sib = self.t + 1 - 2 * self.c
        self.send_sem, self.recv_sem = send_sem, recv_sem
        self.pending = []

    def barrier(self):
        bar = pltpu.get_barrier_semaphore()
        for i in range(1, self.n):
            pl.semaphore_signal(bar, inc=1, device_id=(lax.rem(self.w + i, self.n), self.t), device_id_type=MESH)
        for i in range(1, self.tn):
            pl.semaphore_signal(bar, inc=1, device_id=(self.w, lax.rem(self.t + i, self.tn)), device_id_type=MESH)
        pl.semaphore_wait(bar, self.n - 1 + self.tn - 1)

    def copy(self, src, dst, index, device):
        op = pltpu.make_async_remote_copy(
            src_ref=src,
            dst_ref=dst,
            send_sem=self.send_sem.at[index],
            recv_sem=self.recv_sem.at[index],
            device_id=device,
            device_id_type=MESH,
        )
        op.start()
        self.pending.append(op)
        return op

    def dp_push(self, src_of, dst, base):
        ops = []
        for i in range(1, self.n):
            peer = lax.rem(self.w + i, self.n)
            ops.append(self.copy(src_of(peer), dst, base + i - 1, (peer, self.t)))
        return ops

    def tensor_push(self, src, dst, base):
        ops = []
        for i in range(1, self.tn):
            ops.append(self.copy(src, dst, base + i - 1, (self.w, lax.rem(self.t + i, self.tn))))
        return ops

    def core_push(self, src, dst, index):
        return self.copy(src, dst, index, (self.w, self.sib))

    def finish(self):
        for op in self.pending:
            op.wait_send()


def wait_all(ops):
    for op in ops:
        op.wait_recv()


P_TILES = (6, 6, 6, 2, 6)
P_COUNT = 32
Q_COUNT = 40
QKV0, FC0 = 1536, 2112
COLS = 2880


def halves(block):
    high = block.astype(BF).astype(F32)
    return [high, block - high]


def fill(rows, total):
    used = sum(row.shape[0] for row in rows)
    return jnp.concatenate(rows + [jnp.zeros((total - used, rows[0].shape[1]), F32)], axis=0)


def gather_kernel(
    pack_ref, pk_ref, smt_ref, wmod_ref, brow_ref, bmod_ref,
    wall_ref, mod_ref, emb_ref, ball_ref, cs_ref, ct_ref, t1_ref, a1_ref, tf_ref, hot_ref, wto_ref,
    pkl, ems, eml, a1s, a1l, css, csl, mps, mpl_, mos, mol, bal,
    local_sem, wsend, wrecv, send_sem, recv_sem,
):
    net = Peers(send_sem, recv_sem)
    w, t, c, n = net.w, net.t, net.c, net.n
    share = D // n
    half = share // 2
    x, z, y = t // 2, w // 2, lax.rem(w, 2)
    own = []
    for q in range(3):
        op = pltpu.make_async_copy(pack_ref.at[q], wall_ref.at[q, t, w], local_sem.at[q])
        op.start()
        own.append(op)
    net.barrier()
    pkl[w] = pk_ref[...]
    pk_ops = net.dp_push(lambda peer: pk_ref, pkl.at[w], 0)
    rest = smt_ref.shape[1]
    emb = jnp.concatenate(
        [smt_ref[:, 0:16], smt_ref[:, rest - 18 : rest - 2], smt_ref[:, 16:17], smt_ref[:, rest - 2 : rest], jnp.zeros((share, 5), F32)],
        axis=1,
    )
    third = share // 3
    emb = jnp.concatenate([emb[0:third], emb[third : 2 * third], emb[2 * third : share], jnp.zeros((third, 8), F32)], axis=1)
    ems[...] = emb.astype(BF)
    eml[w] = ems[...]
    em_ops = net.dp_push(lambda peer: ems, eml.at[w], 7)
    bal[t] = brow_ref[...]
    ba_ops = net.tensor_push(brow_ref, bal.at[t], 14)

    zs = [z, z + 1 - 2 * lax.rem(z, 2), lax.rem(z + 2, 4), 3 - z]
    xo = 1 - x
    mine, across = 2 * x + c, 2 * xo + c
    wy = lambda k: 2 * zs[k] + y
    wo = lambda k: 2 * zs[k] + (1 - y)
    to_z = lambda k: (2 * zs[k] + y, t)
    to_x, to_y, to_core = (w, across), (2 * z + (1 - y), t), (w, net.sib)
    sends = []

    def send(q, j, v, device, src=None):
        slot = wall_ref.at[q, j, v]
        op = pltpu.make_async_remote_copy(
            src_ref=slot if src is None else src, dst_ref=slot, send_sem=wsend.at[len(sends)],
            recv_sem=wrecv.at[q, j, v], device_id=device, device_id_type=MESH,
        )
        op.start()
        sends.append(op)

    def arrived(q, j, v):
        slot = wall_ref.at[q, j, v]
        pltpu.make_async_remote_copy(
            src_ref=slot, dst_ref=slot, send_sem=wsend.at[0], recv_sem=wrecv.at[q, j, v], device_id=to_core, device_id_type=MESH
        ).wait_recv()

    def column(q, k):
        if k == 0:
            src = pack_ref.at[q]
            send(q, mine, w, to_z(1), src)
            send(q, mine, w, to_z(2), src)
        else:
            src = None
            arrived(q, mine, wy(k))
            if k == 2:
                send(q, mine, wy(2), to_z(1))
        send(q, mine, wy(k), to_x, src)
        send(q, mine, wy(k), to_y, src)
        send(q, mine, wy(k), to_core, src)

    def by_y(q, k):
        return (q * 4 + k) % 3 == 0

    def side(q, k):
        arrived(q, across, wy(k))
        if by_y(q, k):
            send(q, across, wy(k), to_y)
        send(q, across, wy(k), to_core)
        arrived(q, mine, wo(k))
        if not by_y(q, k):
            send(q, mine, wo(k), to_x)
        send(q, mine, wo(k), to_core)

    def corner(q, k):
        arrived(q, across, wo(k))
        send(q, across, wo(k), to_core)

    def stage(q):
        column(q, 0)
        column(q, 1)
        side(q, 0)
        column(q, 2)
        side(q, 1)
        corner(q, 0)
        column(q, 3)
        side(q, 2)
        corner(q, 1)
        side(q, 3)
        corner(q, 2)
        corner(q, 3)

    def chain0():
        wait_all(pk_ops)
        feats = pkl[...].reshape(8 * n, 384)
        tf_ref[...] = feats[:, 0:FREQ]
        hot_ref[...] = feats[:, FREQ:384]
        small = smt_ref[...].astype(BF).astype(F32)
        t1 = hndot(small[:, 17:273], tf_ref[...]) + small[:, 273:274]
        t1_ref[...] = t1
        act = t1 / (1.0 + jnp.exp(-t1))
        a1s[...] = jnp.concatenate([act[0:half], act[half:share]], axis=1)
        a1l[w] = a1s[...]
        wto_ref[...] = small[:, 274:1042].astype(BF)
        return net.dp_push(lambda peer: a1s, a1l.at[w], 17)

    def chain1(ops):
        wait_all(ops)
        for k in range(n):
            a1_ref[share * k : share * k + half] = a1l[k][:, 0:64]
            a1_ref[share * k + half : share * k + share] = a1l[k][:, 64:128]
        small = smt_ref[...].astype(BF).astype(F32)
        cond = hdot(small[:, 274:1042], a1_ref[...]) + small[:, 1042:1043]
        cond = cond + hndot(small[:, 1043:1075], hot_ref[:, 0:CLASSES])
        ct_ref[...] = cond
        act = cond / (1.0 + jnp.exp(-cond))
        css[...] = jnp.concatenate([act[0:half], act[half:share]], axis=1)
        csl[w] = css[...]
        cs_ops = net.dp_push(lambda peer: css, csl.at[w], 24)
        parts = [tdot(piece, wmod_ref[...]) for piece in split3(act)]
        mps[...] = (parts[0] + parts[1] + parts[2]).reshape(n, 8, QKV0)
        mpl_[w] = mps[w]
        return cs_ops, net.dp_push(lambda peer: mps.at[peer], mpl_.at[w], 31)

    def chain2(ops):
        wait_all(ops)
        total = mpl_[0]
        for k in range(1, n):
            total = total + mpl_[k]
        mos[...] = total + bmod_ref[...]
        mol[t] = mos[...]
        return net.tensor_push(mos, mol.at[t], 38)

    def chain3(cs_ops, ops):
        wait_all(em_ops)
        rows = []
        for k in range(n):
            piece = eml[k].astype(F32)
            rows += [piece[:, 40 * i : 40 * i + 40] for i in range(3)]
        rows = jnp.concatenate(rows, axis=0)
        emb_ref[...] = jnp.concatenate([rows, jnp.zeros((D, 88), F32)], axis=1).T[0:40]
        wait_all(ba_ops)
        ball_ref[...] = bal[...]
        wait_all(cs_ops)
        rows = []
        for k in range(n):
            rows += [csl[k][:, 0:64], csl[k][:, 64:128]]
        rows = jnp.concatenate(rows, axis=0)
        a1s_all = jnp.concatenate([rows, jnp.zeros((D, 64), F32)], axis=1).T
        cs_all = a1s_all[0:64].reshape(n, 8, D)
        picked = jnp.zeros((8, D), F32)
        for k in range(n):
            picked = jnp.where(w == k, cs_all[k], picked)
        cs_ref[...] = picked
        wait_all(ops)
        for lat in range(4):
            for j in range(4):
                for piece in range(2):
                    mod_ref[lat, 2 * j + piece : 2 * j + piece + 1, :] = mol[j, pl.ds(4 * c + lat, 1), D * piece : D * piece + D]

    ops = None
    stage(0)
    ops = chain0()
    stage(1)
    cs_ops, ops = chain1(ops)
    stage(2)
    ops = chain2(ops)
    chain3(cs_ops, ops)
    for q in range(3):
        for j in (2 * x + 1 - c, 2 * xo + 1 - c):
            for v in range(n):
                arrived(q, j, v)
    for op in own:
        op.wait()
    for op in sends:
        op.wait_send()
    net.finish()


def run_gather(pack, pk, smt, wmod, brow, bmod, n):
    S = jax.ShapeDtypeStruct
    V = pltpu.VMEM
    DMA = pltpu.SemaphoreType.DMA
    share = D // n
    lat = 8 * n
    any_spec = pl.BlockSpec(memory_space=pl.ANY)
    vm = pl.BlockSpec(memory_space=pltpu.VMEM)
    outs = [
        S((3, 4, n, share, D), BF), S((4, 8, D), F32), S((40, D), F32), S((4, 1, QKV0), F32), S((8, D), F32),
        S((share, lat), F32), S((share, lat), F32), S((D, lat), F32), S((lat, FREQ), F32), S((lat, 128), F32), S((share, D), BF),
    ]
    scratch = [
        V((n, 8, 384), F32), V((share // 3, 128), BF), V((n, share // 3, 128), BF),
        V((share // 2, 128), F32), V((n, share // 2, 128), F32), V((share // 2, 128), F32), V((n, share // 2, 128), F32),
        V((n, 8, QKV0), F32), V((n, 8, QKV0), F32), V((8, QKV0), F32), V((4, 8, QKV0), F32), V((4, 1, QKV0), F32),
        DMA((3,)), DMA((120,)), DMA((3, 4, n)), DMA((41,)), DMA((41,)),
    ]
    return pl.pallas_call(
        gather_kernel,
        out_shape=outs,
        in_specs=[any_spec] + [vm] * 5,
        out_specs=[any_spec] + [vm] * 10,
        scratch_shapes=scratch,
        compiler_params=pltpu.CompilerParams(collective_id=0, has_side_effects=True, vmem_limit_bytes=48 * 1024 * 1024),
        name="gather",
    )(pack, pk, smt, wmod, brow, bmod)


def gram_schmidt(block):
    rows = lax.broadcasted_iota(jnp.int32, (8, 1), 0)
    for index in range(8):
        row = block[index : index + 1]
        row = row * lax.rsqrt(jnp.sum(row * row, axis=-1, keepdims=True) + TINY)
        inner = jnp.sum(block * row, axis=-1, keepdims=True)
        inner = jnp.where(rows > index, inner, 0.0)
        block = jnp.where(rows == index, row, block - inner * row)
    return block


def grad_kernel(
    a_ref, m_ref, dy_ref, dz_ref, o_ref, dq_ref, du_ref, g_ref, cerr_ref, rerr_ref,
    dmod_ref, small_ref, dbq_ref, db1_ref, hb_ref, right_ref, cs_ref, ct_ref, t1_ref, a1_ref, tf_ref, hot_ref, wmod_ref, wto_ref,
    mcol_ref, mrow_ref, left_ref, rightn_ref, pst_ref, psr_ref, pc_ref, qst_ref, qsn_ref, qrs_ref, gb_ref, gh_ref, gsm_ref,
    mc, mr, sc, sr, rc, rr, av, mv, dyv, dzv, ov, qv, uv, gv,
    dmo, smo, dbo, dbo1, hbo, dm8, dma, dsc, dss, dts, dtl, tks, tkl, px, pland, py, qx, qland, qy,
    load_sem, send_sem, recv_sem,
):
    net = Peers(send_sem, recv_sem)
    w, t, c = net.w, net.t, net.c
    n = net.n
    share = D // n
    loads = {}

    def load(name, src, dst, index):
        op = pltpu.make_async_copy(src, dst, load_sem.at[index])
        op.start()
        loads[name] = op

    load("q", dq_ref, qv, 9)
    load("a", a_ref, av, 1)
    load("u", du_ref, uv, 0)
    load("m", m_ref, mv, 2)
    load("g", g_ref, gv, 3)
    load("dz", dz_ref, dzv, 4)
    load("o", o_ref, ov, 5)
    load("dy", dy_ref, dyv, 6)
    load("ce", cerr_ref, mc, 7)
    load("re", rerr_ref, mr, 8)
    net.barrier()
    side = [
        net.core_push(dmod_ref, dmo, 0),
        net.core_push(small_ref, smo, 1),
        net.core_push(dbq_ref.at[1 - c], dbo, 2),
        net.core_push(db1_ref.at[1 - c], dbo1, 9),
        net.core_push(hb_ref, hbo, 10),
    ]

    def chunk(i, size=256):
        return pl.ds(pl.multiple_of(i * size, size), size)

    def after(i, first):
        return pl.ds(pl.multiple_of(first + 256 * i, 64), 256)

    for name in ("q", "a"):
        loads[name].wait()
    col_ops, row_ops = [], []
    sc[0:256] = tdot(qv[1 - c, :, 0:256], av[...])
    sc[256:576] = tdot(qv[1 - c, :, 256:640], av[...])[0:320]
    col_ops.append(net.core_push(sc.at[0:576], rc.at[0:576], 3))
    for name in ("u", "m"):
        loads[name].wait()

    @pl.loop(0, 3)
    def _(i):
        sc[after(i, 576), :] = tdot(uv[1 - c, :, chunk(i)], mv[...])

    col_ops.append(net.core_push(sc.at[576:1344], rc.at[576:1344], 4))
    wait_all(side)
    for lat in range(4):
        for piece in range(2):
            span = slice(D * piece, D * piece + D)
            dm8[pl.ds(4 * c + lat, 1), span] = dmod_ref[lat, pl.ds(2 * t + piece, 1), :]
            dm8[pl.ds(4 * (1 - c) + lat, 1), span] = dmo[lat, pl.ds(2 * t + piece, 1), :]
    dma[w] = dm8[...]
    dm_ops = net.dp_push(lambda peer: dm8, dma.at[w], 16)
    for name in ("g", "dz", "o", "dy"):
        loads[name].wait()

    @pl.loop(0, 3)
    def _(i):
        sr[after(i, 192), :] = tdot(gv[1 - c, :, chunk(i)], dzv[...])

    sr[0:192, :] = tdot(ov[1 - c], dyv[...])[0:192]
    row_ops.append(net.core_push(sr, rr, 6))
    total = small_ref[...] + smo[...]
    for k in range(n):
        tks[k, :, 0:share] = total[:, share * k : share * k + share]
    tkl[w] = tks[w]
    tok_ops = net.dp_push(lambda peer: tks.at[peer], tkl.at[w], 24)
    loads["ce"].wait()
    dms = split3(dm8[...])
    cs = split3(cs_ref[...])
    left_side = jnp.concatenate([dms[0], dms[1], dms[0], dms[2], dms[1], dms[0]], axis=0)
    right_side = jnp.concatenate([cs[0], cs[0], cs[1], cs[0], cs[1], cs[2]], axis=0)
    for i in range(6):
        mc[256 * i : 256 * i + 256, :] += tdot(left_side[:, 256 * i : 256 * i + 256], right_side)
    wait_all(col_ops)
    mc[QKV0 : QKV0 + 256] += tdot(qv[c, :, 0:256], av[...]) + rc[0:256]
    mc[QKV0 + 256 : FC0] += tdot(qv[c, :, 256:640], av[...])[0:320] + rc[256:576]

    @pl.loop(0, 3)
    def _(i):
        mc[after(i, FC0), :] += tdot(uv[c, :, chunk(i)], mv[...]) + rc[after(i, 576), :]

    out_col = pltpu.make_async_copy(mc, mcol_ref, load_sem.at[0])
    out_col.start()
    wait_all(dm_ops)
    dmx = dma[...].reshape(8 * n, QKV0)
    part = sum(ndot(wmod_ref[...], piece) for piece in split3(dmx))
    dss[...] = part
    dsc[t] = part
    ds_ops = net.tensor_push(dss, dsc.at[t], 32)
    loads["re"].wait()
    wait_all(row_ops)

    @pl.loop(0, 3)
    def _(i):
        mr[after(i, 192), :] += tdot(gv[c, :, chunk(i)], dzv[...]) + rr[after(i, 192), :]

    mr[0:192, :] += tdot(ov[c], dyv[...])[0:192] + rr[0:192, :]
    out_row = pltpu.make_async_copy(mr, mrow_ref, load_sem.at[1])
    out_row.start()
    right = right_ref[...]

    def left_part(first, last):
        sides = jnp.concatenate(halves(right[:, first:last]), axis=0).astype(BF)
        high, low = split2(mc[first:last, :])
        got = dot(sides, high) + dot(sides, low)
        return got[0:8] + got[8:16]

    for k, spans in enumerate((((0, 512), (512, 1024), (1024, QKV0)), ((QKV0, FC0),), ((FC0, FC0 + 384), (FC0 + 384, COLS)))):
        got = sum(left_part(*span) for span in spans)
        for i in range(6):
            px[6 * k + i] = got[:, 128 * i : 128 * i + 128]
    row_side = fill(halves(right[:, COLS : COLS + D]) + halves(right[:, COLS + D : COLS + 2 * D]), 128).T.astype(BF)

    def row_chunk(values):
        high, low = split2(values)
        return dot(high, row_side) + dot(low, row_side)

    got = jnp.concatenate([row_chunk(mr[0:192, :]), jnp.zeros((64, 128), F32)], axis=0).T
    for i in range(2):
        px[18 + i] = got[0:8, 128 * i : 128 * i + 128] + got[8:16, 128 * i : 128 * i + 128]
    for i in range(3):
        got = row_chunk(mr[192 + 256 * i : 448 + 256 * i, :]).T
        got = got[16:24] + got[24:32]
        px[20 + 2 * i] = got[:, 0:128]
        px[21 + 2 * i] = got[:, 128:256]
    bias = jnp.concatenate(
        [colsum(dm8[...]), (dbq_ref[c] + dbo[...])[:, 0:576], db1_ref[c] + dbo1[...], jnp.zeros((1, 192), F32)], axis=1
    )
    for i in range(24):
        px[26 + i // 8, i % 8 : i % 8 + 1, :] = bias[:, 128 * i : 128 * i + 128]
    both = hb_ref[...] + hbo[...]
    px[29] = both[0:8]
    px[30] = both[8:16]
    px[31] = jnp.zeros((8, 128), F32)

    def scatter(v, land, per, base):
        own = pl.ds(w * per, per)
        land[w] = v[own]
        return net.dp_push(lambda peer: v.at[pl.ds(peer * per, per)], land.at[w], base)

    def collect(land, v, per, base, ops):
        wait_all(ops)
        own = pl.ds(w * per, per)
        v[own] = sum(land[k] for k in range(1, n)) + land[0]
        return net.dp_push(lambda peer: v.at[own], v.at[own], base)

    ops = scatter(px, pland, P_COUNT // n, 40)
    wait_all(ds_ops)
    dcond = (dsc[0] + dsc[1] + dsc[2] + dsc[3]) * silu_slope_k(ct_ref[...])
    dts[...] = sum(tdot(wto_ref[...], piece) for piece in split3(dcond)).reshape(n, share, 8 * n)
    dtl[w] = dts[w]
    dt_ops = net.dp_push(lambda peer: dts.at[peer], dtl.at[w], 56)
    gsm_ref[:, 274:1042] = hndot(dcond, a1_ref[...])
    gsm_ref[:, 1042:1043] = jnp.sum(dcond, axis=1, keepdims=True)
    gsm_ref[:, 1043:1075] = hdot(dcond, hot_ref[...])[:, 0:CLASSES]
    ops = collect(pland, py, P_COUNT // n, 48, ops)
    wait_all(tok_ops)
    tok = sum(tkl[k] for k in range(1, n)) + tkl[0]
    tok = jnp.concatenate([tok, jnp.zeros((88, 128), F32)], axis=0).T[0:share]
    gsm_ref[:, 0:16] = tok[:, 0:16]
    gsm_ref[:, 16:17] = tok[:, 32:33]
    gsm_ref[:, 1075:1091] = tok[:, 16:32]
    gsm_ref[:, 1091:1093] = tok[:, 33:35]
    wait_all(ops)
    base = 0
    bases = []
    for index, count in enumerate(P_TILES):
        bases.append(gram_schmidt(jnp.concatenate([py[base + k] for k in range(count)], axis=1)))
        base += count
    offset = 0
    for block, width in zip(bases, (D, D, D, 192, D)):
        left_ref[:, offset : offset + width] = block[:, 0:width]
        offset += width
    gb_ref[...] = jnp.concatenate([py[26 + i // 8, i % 8 : i % 8 + 1, :] for i in range(23)], axis=1)[:, 0:COLS]
    gh_ref[...] = jnp.concatenate([py[29], py[30]], axis=0)

    col_side = fill(halves(bases[0]) + halves(bases[1]) + halves(bases[2]), 128).T.astype(BF)

    def col_chunk(values):
        high, low = split2(values)
        return dot(high, col_side) + dot(low, col_side)

    def put(first, rows, k, tile):
        got = col_chunk(mc[first : first + rows, :])
        if rows % 128:
            got = jnp.concatenate([got, jnp.zeros((128 - rows % 128, 128), F32)], axis=0)
        got = got.T
        got = got[16 * k : 16 * k + 8] + got[16 * k + 8 : 16 * k + 16]
        for i in range(got.shape[1] // 128):
            qx[tile + i] = got[:, 128 * i : 128 * i + 128]

    for i in range(6):
        put(256 * i, 256, 0, 2 * i)
    put(QKV0, 256, 1, 12)
    put(QKV0 + 256, 320, 1, 14)
    for i in range(3):
        put(FC0 + 256 * i, 256, 2, 17 + 2 * i)
    for k, (rows, block) in enumerate(((slice(0, 192), bases[3][:, 0:192]), (slice(192, 960), bases[4]))):
        left = jnp.concatenate(halves(block), axis=0).astype(BF)
        high, low = split2(mr[rows, :])
        got = dot(left, high) + dot(left, low)
        got = got[0:8] + got[8:16]
        for i in range(6):
            qx[23 + 6 * k + i] = got[:, 128 * i : 128 * i + 128]
    for i in range(35, Q_COUNT):
        qx[i] = jnp.zeros((8, 128), F32)
    ops = scatter(qx, qland, Q_COUNT // n, 64)
    wait_all(dt_ops)
    dtime = (sum(dtl[k] for k in range(1, n)) + dtl[0]) * silu_slope_k(t1_ref[...])
    gsm_ref[:, 17:273] = hdot(dtime, tf_ref[...])
    gsm_ref[:, 273:274] = jnp.sum(dtime, axis=1, keepdims=True)

    def left_rows(blocks):
        rows = []
        for block in blocks:
            high, low = halves(block)
            rows += [high, low, high]
        return rows

    def right_rows(blocks):
        rows = []
        for block in blocks:
            high, low = halves(block)
            rows += [high, high, low]
        return rows

    pst_ref[...] = fill(left_rows(bases[:3]), 128).astype(BF)
    proj = jnp.concatenate([bases[3][:, 0:192], jnp.zeros((8, D), F32)], axis=1)
    fc = jnp.concatenate([jnp.zeros((8, 192), F32), bases[4]], axis=1)
    row_stack = fill(left_rows([proj, fc]), 128)
    pc_ref[...] = row_stack.astype(BF)
    row_stack = jnp.concatenate([row_stack, jnp.zeros((128, 64), F32)], axis=1)
    psr_ref[...] = row_stack.T[0:960].astype(BF)
    ops = collect(qland, qy, Q_COUNT // n, 72, ops)
    wait_all(ops)
    qkv = jnp.concatenate([qy[12 + i] for i in range(5)], axis=1)[:, 0:576]
    pieces = [jnp.concatenate([qy[i] for i in range(12)], axis=1), qkv, jnp.concatenate([qy[17 + i] for i in range(6)], axis=1)]
    pad = jnp.zeros((8, 64), F32)
    qc = jnp.concatenate(pieces + [pad], axis=1)
    span = lax.broadcasted_iota(jnp.int32, (8, 2944), 1)
    cuts = [
        jnp.where((span >= first) & (span < last), qc, 0.0) for first, last in ((0, QKV0), (QKV0, FC0), (FC0, COLS))
    ]
    stack = fill(right_rows(cuts), 128)
    qsn_ref[...] = stack.astype(BF)
    qst_ref[...] = stack.T[0:COLS].astype(BF)
    qr = [jnp.concatenate([qy[23 + 6 * k + i] for i in range(6)], axis=1) for k in range(2)]
    qrs_ref[...] = fill(right_rows(qr), 128).astype(BF)
    rightn_ref[:, 0:COLS] = qc[:, 0:COLS]
    rightn_ref[:, COLS : COLS + D] = qr[0]
    rightn_ref[:, COLS + D : COLS + 2 * D] = qr[1]
    net.finish()
    out_col.wait()
    out_row.wait()


def run_grad(operands, n):
    S = jax.ShapeDtypeStruct
    V = pltpu.VMEM
    rows = operands[0].shape[0]
    lat = 8 * n
    share = D // n
    any_spec = pl.BlockSpec(memory_space=pl.ANY)
    vm = pl.BlockSpec(memory_space=pltpu.VMEM)
    outs = [
        S((COLS, D), F32), S((960, D), F32), S((8, 3264), F32), S((8, 4416), F32),
        S((128, D), BF), S((960, 128), BF), S((128, 960), BF), S((COLS, 128), BF), S((128, 2944), BF), S((128, D), BF),
        S((1, COLS), F32), S((16, 128), F32), S((share, 1093), F32),
    ]
    scratch = [
        V((COLS, D), F32), V((960, D), F32), V((1344, D), F32), V((960, D), F32), V((1344, D), F32), V((960, D), F32),
        V((rows, D), BF), V((rows, D), BF), V((rows, D), BF), V((rows, D), BF),
        V((2, rows, 256), BF), V((2, rows, 640), BF), V((2, rows, D), BF), V((2, rows, D), BF),
        V((4, 8, D), F32), V((40, D), F32), V((1, 640), F32), V((1, D), F32), V((16, 128), F32),
        V((8, QKV0), F32), V((n, 8, QKV0), F32),
        V((4, share, lat), F32), V((share, lat), F32), V((n, share, lat), F32), V((n, share, lat), F32),
        V((n, 40, 128), F32), V((n, 40, 128), F32),
        V((P_COUNT, 8, 128), F32), V((n, P_COUNT // n, 8, 128), F32), V((P_COUNT, 8, 128), F32),
        V((Q_COUNT, 8, 128), F32), V((n, Q_COUNT // n, 8, 128), F32), V((Q_COUNT, 8, 128), F32),
        pltpu.SemaphoreType.DMA((10,)), pltpu.SemaphoreType.DMA((80,)), pltpu.SemaphoreType.DMA((80,)),
    ]
    return pl.pallas_call(
        grad_kernel,
        out_shape=outs,
        in_specs=[any_spec] * 10 + [vm] * 14,
        out_specs=[any_spec] * 2 + [vm] * 11,
        scratch_shapes=scratch,
        compiler_params=pltpu.CompilerParams(collective_id=1, has_side_effects=True, vmem_limit_bytes=60 * 1024 * 1024),
        name="grad",
    )(*operands)


def apply_kernel(
    w_ref, mcol_ref, mrow_ref, qst_ref, psr_ref, pst_ref, pc_ref, qsn_ref, qrs_ref,
    cw_ref, cm_ref, rw_ref, rm_ref, gs_ref, sw_ref, sm_ref,
    cres_ref, rres_ref, cn_ref, cmn_ref, rn_ref, rmn_ref, sn_ref, smn_ref, *, n
):
    step = pl.program_id(0)
    share = D // n
    cres_ref[...] = mcol_ref[...] - dot(qst_ref[...], pst_ref[...]) * (1.0 / n)
    rres_ref[...] = mrow_ref[...] - dot(psr_ref[...], qrs_ref[...]) * (1.0 / n)

    @pl.when(step == 0)
    def _():
        place = lax.broadcasted_iota(jnp.int32, (D, 128), 0) == w_ref[0] * share + lax.broadcasted_iota(jnp.int32, (D, 128), 1)
        pick = jnp.where(place, 1.0, 0.0).astype(BF)
        mom = DECAY * cm_ref[...] + tdot(dot(pst_ref[...], pick).astype(BF), qsn_ref[...])[0:share, 0:COLS]
        cmn_ref[...] = mom
        cn_ref[...] = cw_ref[...] - LEARN_RATE * mom
        mom = DECAY * rm_ref[...] + tdot(dot(qrs_ref[...], pick).astype(BF), pc_ref[...])[0:share]
        rmn_ref[...] = mom
        rn_ref[...] = rw_ref[...] - LEARN_RATE * mom
        mom = DECAY * sm_ref[...] + gs_ref[...]
        smn_ref[...] = mom
        sn_ref[...] = sw_ref[...] - LEARN_RATE * mom


def run_apply(w, operands, n):
    share = D // n
    S = jax.ShapeDtypeStruct
    blk = lambda r, cc: pl.BlockSpec((r, cc), lambda i, *_: (i, 0))
    full = lambda r, cc: pl.BlockSpec((r, cc), lambda i, *_: (0, 0))
    cb, rb, sb = full(share, COLS), full(share, 960), full(share, 1093)
    return pl.pallas_call(
        functools.partial(apply_kernel, n=n),
        grid_spec=pltpu.PrefetchScalarGridSpec(
            num_scalar_prefetch=1,
            grid=(8,),
            in_specs=[blk(360, D), blk(120, D), blk(360, 128), blk(120, 128), full(128, D), full(128, 960), full(128, 2944), full(128, D)]
            + [cb, cb, rb, rb, sb, sb, sb],
            out_specs=[blk(360, D), blk(120, D), cb, cb, rb, rb, sb, sb],
        ),
        out_shape=[S((COLS, D), F32), S((960, D), F32)] + [S((share, v), F32) for v in (COLS, COLS, 960, 960, 1093, 1093)],
        compiler_params=pltpu.CompilerParams(vmem_limit_bytes=48 * 1024 * 1024),
        name="apply",
    )(w, *operands)


def position_table():
    quarter = D // 4
    omega = 1.0 / 10000.0 ** (jnp.arange(quarter, dtype=jnp.float32) / quarter)
    place = jnp.arange(GRID, dtype=jnp.float32)[:, None] * omega[None, :]
    return jnp.concatenate([jnp.sin(place), jnp.cos(place)], axis=1)


def time_features(times):
    half = FREQ // 2
    freqs = jnp.exp(-math.log(10000.0) * jnp.arange(half, dtype=jnp.float32) / half)
    angles = 1000.0 * times[:, None] * freqs[None, :]
    return jnp.concatenate([jnp.cos(angles), jnp.sin(angles)], axis=1)


def small_starts():
    counts = [PATCH_IN, 1, FREQ, 1, D, 1, CLASSES, PATCH_IN, 1, 1]
    starts = [0]
    for amount in counts:
        starts.append(starts[-1] + amount)
    return starts


def cut_parts(array, widths, axis):
    pieces = []
    offset = 0
    for width in widths:
        pieces.append(lax.slice_in_dim(array, offset, offset + width, axis=axis))
        offset = offset + width
    return pieces


def ortho_kernel(x_ref, o_ref):
    count = x_ref.shape[0]
    rows = [x_ref[index] for index in range(count)]
    for index in range(count):
        vector = rows[index]
        vector = vector * lax.rsqrt(jnp.sum(vector * vector, axis=-1, keepdims=True) + TINY)
        o_ref[index] = vector
        for later in range(index + 1, count):
            rows[later] = rows[later] - jnp.sum(rows[later] * vector, axis=-1, keepdims=True) * vector


def orthonormal_all(parts):
    stacked = jnp.stack([jnp.pad(part, ((0, 0), (0, D - part.shape[1]))) for part in parts], axis=1)
    stacked = jnp.pad(stacked, ((0, 0), (0, 8 - len(parts)), (0, 0)))
    out = pl.pallas_call(ortho_kernel, out_shape=jax.ShapeDtypeStruct(stacked.shape, F32), name="ortho")(stacked)
    return [out[:, index, : part.shape[1]] for index, part in enumerate(parts)]


def rounded(values):
    return lax.optimization_barrier(values.astype(BF)).astype(F32)


def silu_slope(values):
    gate = jax.nn.sigmoid(values)
    return gate * (1.0 + values * (1.0 - gate))


def shards_general(
    clean_latents,
    noise_draw,
    timesteps,
    labels,
    col_weights,
    col_moments,
    col_errors,
    row_weights,
    row_moments,
    row_errors,
    bias_weights,
    bias_moments,
    small_weights,
    small_moments,
    head_bias,
    head_moments,
    right_factors,
):
    tensor_size = lax.axis_size("tensor")
    data_size = lax.axis_size("dp")
    tensor_rank = lax.axis_index("tensor")
    data_rank = lax.axis_index("dp")
    batch = clean_latents.shape[0]
    half = batch // 2
    share = D // data_size
    mod_width = 8 * D // tensor_size
    qkv_width = 3 * D // tensor_size
    ffn_width = FF // tensor_size
    proj_rows = D // tensor_size
    count_all = data_size * batch * SEQ * PATCH_IN
    col_widths = [mod_width, qkv_width, ffn_width]
    core = lax.rem(tensor_rank, 2)
    base = tensor_rank - core
    pair = [(index, index + 1 - 2 * (index % 2)) for index in range(tensor_size)]

    def swap(values):
        return lax.ppermute(values, "tensor", pair)

    col_low = col_weights[:, 0, :].astype(BF)
    row_low = row_weights[0].astype(BF).T
    packed = jnp.concatenate(
        [
            col_low[:, mod_width : mod_width + qkv_width],
            row_low[:, :proj_rows],
            col_low[:, mod_width + qkv_width :],
            row_low[:, proj_rows:],
        ],
        axis=1,
    )
    wall = lax.all_gather(lax.all_gather(packed, "dp", axis=0, tiled=True), "tensor", axis=0)
    wall = jnp.stack([wall[:, :, 768 * index : 768 * index + 768] for index in range(3)])
    starts = small_starts()
    small_low = small_weights.astype(BF)
    small_exact = rounded(small_weights)
    picked = jnp.concatenate([small_low[: starts[2]], small_low[starts[7] :]], axis=0)
    emb = lax.all_gather(picked.astype(F32), "dp", axis=1, tiled=True)
    emb = jnp.concatenate([emb[:16], emb[17:33], emb[16:17], emb[33:35], jnp.zeros((5, D), F32)], axis=0)
    w_tin = small_exact[starts[2] : starts[3]]
    b_tin = small_exact[starts[3]]
    w_tout = small_exact[starts[4] : starts[5]]
    b_tout = small_exact[starts[5]]
    table = small_exact[starts[6] : starts[7]]
    bias_exact = rounded(bias_weights[0])
    head_exact = rounded(head_bias)
    w_mod = rounded(col_weights[:, 0, :mod_width])
    bias_all = lax.all_gather(bias_exact, "tensor", axis=0)
    times_all = lax.all_gather(timesteps, "dp", axis=0, tiled=True)
    labels_all = lax.all_gather(labels, "dp", axis=0, tiled=True)
    time_feat = time_features(times_all)
    time_hidden = exact_dot(time_feat, w_tin) + b_tin
    time_act = lax.all_gather(jax.nn.silu(time_hidden), "dp", axis=1, tiled=True)
    onehot = (labels_all[:, None] == jnp.arange(CLASSES, dtype=jnp.int32)[None, :]).astype(F32)
    condition = exact_dot(time_act, w_tout) + b_tout + exact_dot(onehot, table)
    cond_act = jax.nn.silu(condition)
    mod_part = exact_dot(cond_act, w_mod)
    mod_own = lax.psum_scatter(mod_part, "dp", scatter_dimension=0, tiled=True) + bias_exact[:mod_width]
    mod_full = lax.all_gather(mod_own, "tensor", axis=1, tiled=True).reshape(batch, 8, D)
    cond_rows = lax.all_to_all(cond_act, "dp", split_axis=0, concat_axis=1, tiled=True)

    def mine(values):
        return lax.dynamic_slice_in_dim(values, core * half, half, 0)

    ball = jnp.concatenate(
        [
            jnp.pad(bias_all[:, mod_width : mod_width + qkv_width], ((0, 0), (0, 768 - qkv_width))),
            bias_all[:, mod_width + qkv_width :],
        ],
        axis=1,
    )[:, None]
    (a, m, dy, dz, o, dq, du, g, dmod, small, dbq, db1, hb) = run_block(
        base.reshape(1),
        mine(timesteps),
        mine(clean_latents).transpose(0, 2, 1),
        mine(noise_draw).transpose(0, 2, 1),
        mine(mod_full),
        wall,
        position_table(),
        emb,
        head_exact[:, None],
        ball,
        count_all,
    )
    rows = half * SEQ

    def flat(values):
        return values.reshape(rows, values.shape[-1])

    def pick(values, which):
        return lax.dynamic_index_in_dim(values, which, 0, keepdims=False)

    def gradients(which):
        return (
            tdot(flat(a), flat(pick(dq, which))[:, :qkv_width]),
            tdot(flat(m), flat(pick(du, which))),
            tdot(flat(pick(o, which))[:, :proj_rows], flat(dy)),
            tdot(flat(pick(g, which)), flat(dz)),
            pick(dbq, which)[0, :qkv_width],
            pick(db1, which)[0],
        )

    other = swap(gradients(1 - core))
    own = gradients(core)
    g_qkv, g_fc1, g_proj, g_fc2, g_bqkv, g_bfc1 = [left + right for left, right in zip(own, other)]
    dmod_own = dmod.reshape(half, 8 * D)
    dmod_other = swap(dmod_own)
    dmod_group = jnp.where(
        core == 0,
        jnp.concatenate([dmod_own, dmod_other], axis=0),
        jnp.concatenate([dmod_other, dmod_own], axis=0),
    )
    d_mod = lax.dynamic_slice_in_dim(dmod_group, tensor_rank * mod_width, mod_width, 1)
    g_bmod = jnp.sum(d_mod, axis=0)
    g_mod = exact_tdot(cond_rows, d_mod)
    d_mod_all = lax.all_gather(d_mod, "dp", axis=0, tiled=True)
    d_cond = lax.psum(exact_ndot(d_mod_all, w_mod), "tensor") * silu_slope(condition)
    g_table = exact_tdot(onehot, d_cond)
    g_btout = jnp.sum(d_cond, axis=0)
    g_tout = exact_tdot(time_act, d_cond)
    d_time = lax.psum_scatter(exact_ndot(d_cond, w_tout), "dp", scatter_dimension=1, tiled=True)
    d_time = d_time * silu_slope(time_hidden)
    g_btin = jnp.sum(d_time, axis=0)
    g_tin = exact_tdot(time_feat, d_time)
    small_own = lax.psum(lax.psum_scatter(small, "dp", scatter_dimension=1, tiled=True), "tensor") * 0.5
    head_sum, loss_value = lax.psum((hb[:, 0] * 0.5, hb[0, 1] * 0.5), ("dp", "tensor"))
    small_step = jnp.concatenate(
        [
            small_own[:16],
            small_own[32:33],
            g_tin,
            g_btin[None],
            g_tout,
            g_btout[None],
            g_table,
            small_own[16:32],
            small_own[33:34],
            small_own[34:35],
        ],
        axis=0,
    )
    bias_sum = lax.psum(jnp.concatenate([g_bmod, g_bqkv, g_bfc1], axis=0), "dp")
    col_cuts = cut_parts(col_errors[0, 0], col_widths, 1)
    row_cuts = cut_parts(row_errors[0, 0], [proj_rows, ffn_width], 0)
    matrices = [
        g_mod + col_cuts[0],
        g_qkv + col_cuts[1],
        g_fc1 + col_cuts[2],
        g_proj + row_cuts[0],
        g_fc2 + row_cuts[1],
    ]
    right_pieces = cut_parts(right_factors[0], col_widths + [D, D], 1)
    left_local = jnp.concatenate([exact_ndot(right_pieces[i], matrices[i]) for i in range(5)], axis=1)
    left_sum = lax.psum(left_local, "dp")
    bases = orthonormal_all(cut_parts(left_sum, [D, D, D, proj_rows, ffn_width], 1))
    right_local = jnp.concatenate([exact_dot(bases[i], matrices[i]) for i in range(5)], axis=1)
    right_sum = lax.psum(right_local, "dp")
    right_split = cut_parts(right_sum, col_widths + [D, D], 1)
    approx = [exact_tdot(bases[i], right_split[i]) for i in range(5)]
    rest = [matrices[i] - approx[i] / data_size for i in range(5)]
    col_residue = jnp.concatenate(rest[:3], axis=1)[None, None]
    row_residue = jnp.concatenate(rest[3:], axis=0)[None, None]

    def own_columns(values):
        return lax.dynamic_slice_in_dim(values, data_rank * share, share, 1)

    col_step = jnp.concatenate(
        [exact_tdot(own_columns(bases[i]), right_split[i]) for i in range(3)], axis=1
    )[:, None, :]
    row_step = jnp.concatenate(
        [exact_tdot(bases[i], own_columns(right_split[i])) for i in (3, 4)], axis=0
    )[None]
    col_momentum = DECAY * col_moments + col_step
    col_new = col_weights - LEARN_RATE * col_momentum
    row_momentum = DECAY * row_moments + row_step
    row_new = row_weights - LEARN_RATE * row_momentum
    small_momentum = DECAY * small_moments + small_step
    small_new = small_weights - LEARN_RATE * small_momentum
    bias_momentum = DECAY * bias_moments + bias_sum[None]
    bias_new = bias_weights - LEARN_RATE * bias_momentum
    head_momentum = DECAY * head_moments + head_sum
    head_new = head_bias - LEARN_RATE * head_momentum
    left_factors = jnp.concatenate(bases, axis=1)[None]
    right_new = right_sum[None]
    return (
        loss_value,
        col_new,
        col_momentum,
        col_residue,
        row_new,
        row_momentum,
        row_residue,
        bias_new,
        bias_momentum,
        small_new,
        small_momentum,
        head_new,
        head_momentum,
        left_factors,
        right_new,
    )


def shards(
    clean_latents,
    noise_draw,
    timesteps,
    labels,
    col_weights,
    col_moments,
    col_errors,
    row_weights,
    row_moments,
    row_errors,
    bias_weights,
    bias_moments,
    small_weights,
    small_moments,
    head_bias,
    head_moments,
    right_factors,
):
    tensor_size = lax.axis_size("tensor")
    data_size = lax.axis_size("dp")
    tensor_rank = lax.axis_index("tensor")
    data_rank = lax.axis_index("dp")
    batch = clean_latents.shape[0]
    half = batch // 2
    share = D // data_size
    mod_width = 8 * D // tensor_size
    qkv_width = 3 * D // tensor_size
    ffn_width = FF // tensor_size
    proj_rows = D // tensor_size
    count_all = data_size * batch * SEQ * PATCH_IN
    col_widths = [mod_width, qkv_width, ffn_width]
    core = lax.rem(tensor_rank, 2)
    base = tensor_rank - core
    col = col_weights[:, 0]
    col_low = col.astype(BF)
    row_low = row_weights[0].T.astype(BF)
    packed = jnp.stack(
        [
            jnp.concatenate([col_low[:, mod_width : mod_width + qkv_width], row_low[:, :proj_rows]], axis=1),
            col_low[:, mod_width + qkv_width :],
            row_low[:, proj_rows:],
        ]
    )
    wmod = col_low[:, :mod_width]
    onehot = (labels[:, None] == jnp.arange(128, dtype=jnp.int32)[None, :]).astype(F32)
    features = jnp.concatenate([time_features(timesteps), onehot], axis=1)
    bias_exact = rounded(bias_weights)
    bias_row = jnp.concatenate(
        [bias_exact[:, mod_width : mod_width + qkv_width], jnp.zeros((1, 192), F32), bias_exact[:, mod_width + qkv_width :]],
        axis=1,
    )
    small_t = small_weights.T
    wall, mod, emb, ball, cs, ct, t1, a1, tf, hot, wto = run_gather(
        packed, features, small_t, wmod, bias_row, bias_exact[:, :mod_width], data_size
    )

    def mine(values):
        return lax.dynamic_slice_in_dim(values, core * half, half, 0)

    a, m, dy, dz, o, dq, du, g, dmod, small, dbq, db1, hb = run_block(
        base.reshape(1),
        mine(timesteps),
        mine(clean_latents.transpose(0, 2, 1)),
        mine(noise_draw.transpose(0, 2, 1)),
        mod,
        wall.reshape(3, tensor_size, D, D),
        position_table(),
        emb,
        rounded(head_bias)[:, None],
        ball,
        count_all,
    )
    rows = half * SEQ

    def flat(values):
        return values.reshape(values.shape[:-3] + (rows, values.shape[-1]))

    acts = [flat(values) for values in (a, m, dy, dz, o, dq, du, g)]
    errors = [col_errors[0, 0].T, row_errors[0, 0]]
    mcol, mrow, left_all, right_sum, pst, psr, pc, qst, qsn, qrs, gb, gh, gsm = run_grad(
        acts + errors + [dmod, small, dbq, db1, hb, right_factors[0], cs, ct, t1, a1, tf, hot, wmod, wto], data_size
    )
    cres, rres, cn, cmn, rn, rmn, sn, smn = run_apply(
        data_rank.reshape(1),
        [mcol, mrow, qst, psr, pst, pc, qsn, qrs, col, col_moments[:, 0], row_weights[0].T, row_moments[0].T]
        + [gsm, small_t, small_moments.T],
        data_size,
    )
    col_new, col_momentum, col_residue = cn[:, None], cmn[:, None], cres.T[None, None]
    row_new, row_momentum, row_residue = rn.T[None], rmn.T[None], rres[None, None]
    small_new, small_momentum = sn.T, smn.T
    bias_sum = gb[0]
    head_sum = gh[:, 0]
    loss_value = gh[0, 1]
    bias_momentum = DECAY * bias_moments + bias_sum[None]
    bias_new = bias_weights - LEARN_RATE * bias_momentum
    head_momentum = DECAY * head_moments + head_sum
    head_new = head_bias - LEARN_RATE * head_momentum
    left_factors = left_all[None]
    right_new = right_sum[None]
    return (
        loss_value,
        col_new,
        col_momentum,
        col_residue,
        row_new,
        row_momentum,
        row_residue,
        bias_new,
        bias_momentum,
        small_new,
        small_momentum,
        head_new,
        head_momentum,
        left_factors,
        right_new,
    )


def solution(mesh):
    fits = mesh.shape["dp"] == 8 and mesh.shape["tensor"] == 4
    placed = (
        P("dp", None, None),
        P("dp", None, None),
        P("dp"),
        P("dp"),
        P("dp", "tensor", None),
        P("dp", "tensor", None),
        P("dp", "tensor", None, None),
        P("tensor", None, "dp"),
        P("tensor", None, "dp"),
        P("dp", "tensor", None, None),
        P("tensor", None),
        P("tensor", None),
        P(None, "dp"),
        P(None, "dp"),
        P(),
        P(),
        P("tensor", None, None),
    )
    return jax.shard_map(
        shards if fits else shards_general,
        mesh=mesh,
        in_specs=placed,
        out_specs=(
            P(),
            P("dp", "tensor", None),
            P("dp", "tensor", None),
            P("dp", "tensor", None, None),
            P("tensor", None, "dp"),
            P("tensor", None, "dp"),
            P("dp", "tensor", None, None),
            P("tensor", None),
            P("tensor", None),
            P(None, "dp"),
            P(None, "dp"),
            P(),
            P(),
            P("tensor", None, None),
            P("tensor", None, None),
        ),
        check_vma=False,
    )
```

```python
import functools
import math

import jax
import jax.numpy as jnp
from jax import lax
from jax.experimental import pallas as pl
from jax.experimental.pallas import tpu as pltpu
from jax.sharding import PartitionSpec as P

D = 768
HEADS = 12
HEAD_DIM = 64
FF = 3072
FREQ = 256
GRID = 16
PATCH_IN = 16
CLASSES = 32
SEQ = 256

EPSILON = 1e-06
TINY = 1e-30
DECAY = 0.9
LEARN_RATE = 100.0
TIME_OFFSET = 0.25
F32 = jnp.float32
BF = jnp.bfloat16
SCALE = 1.0 / math.sqrt(HEAD_DIM)
GELU_C = math.sqrt(2.0 / math.pi)


def exact_dot(left, right):
    return jnp.dot(left, right, precision=lax.Precision.HIGHEST, preferred_element_type=F32)


def exact_tdot(left, right):
    return lax.dot_general(left, right, (((0,), (0,)), ((), ())), precision=lax.Precision.HIGHEST, preferred_element_type=F32)


def exact_ndot(left, right):
    return lax.dot_general(left, right, (((1,), (1,)), ((), ())), precision=lax.Precision.HIGHEST, preferred_element_type=F32)


def dot(a,b): return lax.dot_general(a,b,(((1,),(0,)),((),())),preferred_element_type=F32)
def ndot(a,b): return lax.dot_general(a,b,(((1,),(1,)),((),())),preferred_element_type=F32)
def tdot(a,b): return lax.dot_general(a,b,(((0,),(0,)),((),())),preferred_element_type=F32)

def ln(h):
    c=h-jnp.mean(h,axis=-1,keepdims=True)
    v=jnp.mean(c*c,axis=-1,keepdims=True)
    r=lax.rsqrt(v+EPSILON)
    return c*r,r

def ln_back(dout,xh,r,scale):
    dx=dout*(1.0+scale)
    return r*(dx-jnp.mean(dx,axis=-1,keepdims=True)-xh*jnp.mean(dx*xh,axis=-1,keepdims=True))

def colsum(v): return jnp.sum(v,axis=0,keepdims=True)

UNROLL=dict(af=2,ff=4,fb=4,ab=4)

def block_state():
    V=pltpu.VMEM
    return dict(
        wall=V((3,4,D,D),BF), pe=V((SEQ,D),F32), qkv=V((4,4,SEQ,640),BF), p=V((4,12,SEQ,SEQ),BF),
        xh1=V((4,SEQ,D),F32), y=V((4,SEQ,D),F32), h=V((4,SEQ,D),F32), r1=V((4,SEQ,1),F32),
        xh2=V((SEQ,D),F32), z=V((SEQ,D),F32), r2=V((SEQ,1),F32), slope=V((4,SEQ,D),F32),
        a=V((SEQ,D),BF), m=V((SEQ,D),BF), dz=V((SEQ,D),BF), dy=V((SEQ,D),BF),
        o=V((4,SEQ,256),BF), g=V((4,SEQ,D),BF), du=V((4,SEQ,D),BF), dq=V((4,SEQ,640),BF),
        dbq=V((4,1,640),F32), db1=V((4,1,D),F32), out_sem=pltpu.SemaphoreType.DMA((8,)))

class Block:
    def __init__(self,s,times,clean,noise,mod,pe,emb,bh,ball,outs,dmod,small,hb,base,first,count_all,service):
        self.s=s; self.times=times; self.clean=clean; self.noise=noise; self.mod_ref=mod; self.pe=pe; self.emb=emb; self.bh=bh; self.ball=ball
        self.outs=outs; self.dmod=dmod; self.small=small; self.hb=hb; self.base=base; self.first=first; self.count_all=count_all; self.service=service
        self.lo=lax.broadcasted_iota(jnp.int32,(1,128),1)<64
        self.zero=jnp.zeros((),BF)
    def roll(self,v): return pltpu.roll(v.astype(F32),64,1).astype(BF)
    def out(self,lat,name,index,pair):
        s=self.s
        src=s[name].at[pl.ds(self.base,2)] if pair else s[name]
        dst=self.outs[index].at[:,lat] if pair else self.outs[index].at[lat]
        return pltpu.make_async_copy(src,dst,s["out_sem"].at[index])
    def emit(self,lat,name,index,pair=False): self.out(lat,name,index,pair).start()
    def clear(self,lat,name,index,pair=False):
        @pl.when(lat>0)
        def _(): self.out(lat-1,name,index,pair).wait()
    def last(self):
        for name,index,pair in (("a",0,False),("m",1,False),("dy",2,False),("dz",3,False),("o",4,True),("dq",5,True),("du",6,True),("g",7,True)):
            self.out(3,name,index,pair).wait()
    def start(self):
        s=self.s
        self.small[...]=jnp.zeros_like(self.small); self.hb[...]=jnp.zeros_like(self.hb)
        s["dbq"][...]=jnp.zeros_like(s["dbq"]); s["db1"][...]=jnp.zeros_like(s["db1"])
        for i in range(GRID):
            s["pe"][16*i:16*i+16,0:384]=jnp.broadcast_to(self.pe[i:i+1,:],(16,384))
            s["pe"][16*i:16*i+16,384:768]=self.pe[...]
    def mixed(self,lat):
        place=self.first+lat
        t=self.times[place]
        clean=self.clean[place].astype(F32); noise=self.noise[place].astype(F32)
        return t,clean,noise,(t*clean+(1.0-t)*noise).astype(BF)
    def mod(self,lat,i): return self.mod_ref[lat,i:i+1,:]
    def embed(self,lat):
        s=self.s
        mixed=self.mixed(lat)[3]
        h0=tdot(mixed,self.emb[0:16].astype(BF))+self.emb[32:33]+s["pe"][...]
        s["h"][lat]=h0
        xh,r=ln(h0)
        s["xh1"][lat]=xh; s["r1"][lat]=r
        self.clear(lat,"a",0)
        s["a"][...]=(xh*(1.0+self.mod(lat,1))+self.mod(lat,0)).astype(BF)
        self.emit(lat,"a",0)
        self.clear(lat,"o",4,True)
    def softmax(self,v,lat,idx):
        v=v*SCALE
        e=jnp.exp(v-jnp.max(v,axis=-1,keepdims=True))
        p=(e/jnp.sum(e,axis=-1,keepdims=True)).astype(BF)
        self.s["p"][lat,idx]=p
        return p
    def attend(self,lat,j):
        s=self.s; lo=self.lo; zero=self.zero; wall=s["wall"]
        full=(dot(s["a"][...],wall[0,j])[:,0:640]+self.ball[j,:,0:640]).astype(BF)
        s["qkv"][lat,j]=full
        b0,b1,b2,b3,b4=[full[:,128*i:128*i+128] for i in range(5)]
        p0=self.softmax(ndot(jnp.where(lo,b0,zero),self.roll(b0)),lat,3*j)
        p1=self.softmax(ndot(jnp.where(lo,zero,b1),self.roll(b2)),lat,3*j+1)
        p2=self.softmax(ndot(jnp.where(lo,b3,zero),self.roll(b3)),lat,3*j+2)
        o0=pltpu.roll(dot(p0,b1),64,1)
        s["o"][j,:,0:128]=jnp.where(lo,0.0,o0).astype(BF)
        s["o"][j,:,128:256]=pltpu.roll(jnp.where(lo,dot(p2,b4),dot(p1,b2)),64,1).astype(BF)
    def project(self,lat):
        s=self.s
        self.emit(lat,"o",4,True)
        for n in range(3):
            cols=slice(256*n,256*n+256)
            y=sum(ndot(s["o"][j],s["wall"][0,j,cols,512:768]) for j in range(4))+self.emb[33:34,cols]
            s["y"][lat,:,cols]=y
            s["h"][lat,:,cols]+=self.mod(lat,2)[:,cols]*y
    def attn_fwd(self,lat):
        self.service(lat,0)
        self.embed(lat)
        self.service(lat,1)
        for j in range(2): self.attend(lat,j)
        self.service(lat,2)
        for j in range(2,4): self.attend(lat,j)
        self.service(lat,3)
        self.project(lat)
    def fc_in(self,lat):
        s=self.s
        xh,r=ln(s["h"][lat])
        s["xh2"][...]=xh; s["r2"][...]=r
        self.clear(lat,"m",1)
        s["m"][...]=(xh*(1.0+self.mod(lat,4))+self.mod(lat,3)).astype(BF)
        self.emit(lat,"m",1)
        self.clear(lat,"g",7,True)
    def fc_one(self,lat,j):
        s=self.s
        u=dot(s["m"][...],s["wall"][1,j])+self.ball[j,:,768:1536]
        uu=u*u
        th=jnp.tanh(u*(GELU_C+(GELU_C*0.044715)*uu))
        half=0.5+0.5*th
        s["g"][j]=(u*half).astype(BF)
        s["slope"][j]=half*(1.0+(u-u*th)*(GELU_C+(3.0*0.044715*GELU_C)*uu))
    def fc_fwd(self,lat):
        s=self.s
        self.fc_in(lat)
        u=UNROLL["ff"]
        @pl.loop(0,4//u)
        def _(i):
            for k in range(u): self.fc_one(lat,i*u+k)
        self.emit(lat,"g",7,True)
        for n in range(3):
            cols=slice(256*n,256*n+256)
            z=sum(ndot(s["g"][j],s["wall"][2,j,cols,:]) for j in range(4))+self.emb[34:35,cols]
            s["z"][:,cols]=z
    def head(self,lat):
        s=self.s; mod=lambda i: self.mod(lat,i)
        t,clean,noise,_=self.mixed(lat)
        wh=self.emb[16:32].astype(BF)
        h2=s["h"][lat]+mod(5)*s["z"][...]
        xh,r=ln(h2)
        fi=(xh*(1.0+mod(7))+mod(6)).astype(BF)
        pred=ndot(wh,fi)+self.bh[...]
        diff=pred-(clean-noise)
        weight=1.0/(1.0-t+TIME_OFFSET)
        self.hb[0:1,1:2]+=jnp.sum(colsum(weight*diff*diff),axis=1,keepdims=True)*(1.0/self.count_all)
        dpred=2.0*weight*diff*(1.0/self.count_all)
        self.hb[:,0:1]+=jnp.sum(dpred,axis=1,keepdims=True)
        dpl=dpred.astype(BF)
        self.small[16:32]+=dot(dpl,fi)
        dfi=tdot(dpl,wh)
        self.dmod[lat,6:7]=colsum(dfi); self.dmod[lat,7:8]=colsum(dfi*xh)
        dh=ln_back(dfi,xh,r,mod(7))
        s["h"][lat]=dh
        self.dmod[lat,5:6]=colsum(dh*s["z"][...])
        dzf=dh*mod(5)
        self.small[34:35]+=colsum(dzf)
        self.clear(lat,"dz",3)
        s["dz"][...]=dzf.astype(BF)
        self.emit(lat,"dz",3)
        self.clear(lat,"du",6,True)
    def fc_back_one(self,j):
        s=self.s
        du=dot(s["dz"][...],s["wall"][2,j])*s["slope"][j]
        s["du"][j]=du.astype(BF)
        s["db1"][j]+=colsum(du)
    def fc_bwd(self,lat):
        s=self.s; mod=lambda i: self.mod(lat,i)
        u=UNROLL["fb"]
        @pl.loop(0,4//u)
        def _(i):
            for k in range(u): self.fc_back_one(i*u+k)
        self.emit(lat,"du",6,True)
        for n in range(3):
            cols=slice(256*n,256*n+256)
            s["z"][:,cols]=sum(ndot(s["du"][j],s["wall"][1,j,cols,:]) for j in range(4))
        dm=s["z"][...]
        xh=s["xh2"][...]
        self.dmod[lat,3:4]=colsum(dm); self.dmod[lat,4:5]=colsum(dm*xh)
        dh=s["h"][lat]+ln_back(dm,xh,s["r2"][...],mod(4))
        s["h"][lat]=dh
        self.dmod[lat,2:3]=colsum(dh*s["y"][lat])
        dyf=dh*mod(2)
        self.small[33:34]+=colsum(dyf)
        self.clear(lat,"dy",2)
        s["dy"][...]=dyf.astype(BF)
        self.emit(lat,"dy",2)
        self.clear(lat,"dq",5,True)
    def attend_back(self,lat,j):
        s=self.s; lo=self.lo; zero=self.zero; roll=self.roll
        do=dot(s["dy"][...],s["wall"][0,j,:,512:768])
        r4=pltpu.roll(do[:,0:128],64,1).astype(BF); r5=pltpu.roll(do[:,128:256],64,1).astype(BF)
        do0=jnp.where(lo,r4,zero); do1=jnp.where(lo,zero,r5); do2=jnp.where(lo,r5,zero)
        b0,b1,b2,b3,b4=[s["qkv"][lat,j,:,128*i:128*i+128] for i in range(5)]
        def head(h,doh,v):
            p=s["p"][lat,3*j+h]
            dv=tdot(p,doh)
            dp=ndot(doh,v)
            pf=p.astype(F32)
            t=pf*dp
            ds=(t-pf*jnp.sum(t,axis=-1,keepdims=True)).astype(BF)
            return dv,ds
        dv0,ds0=head(0,do0,b1)
        dv1,ds1=head(1,do1,b2)
        dv2,ds2=head(2,do2,b4)
        rb0=roll(b0); rb3=roll(b3)
        n0=jnp.where(lo,dot(ds0,rb0),tdot(ds0,rb0))*SCALE
        n1=jnp.where(lo,dv0,dot(ds1,roll(b2))*SCALE); n2=jnp.where(lo,tdot(ds1,roll(b1))*SCALE,dv1)
        n3=jnp.where(lo,dot(ds2,rb3),tdot(ds2,rb3))*SCALE
        n4=jnp.where(lo,dv2,0.0)
        for i,v in enumerate((n0,n1,n2,n3,n4)):
            cols=slice(128*i,128*i+128)
            s["dq"][j,:,cols]=v.astype(BF)
            s["dbq"][j,:,cols]+=colsum(v)
    def attn_bwd(self,lat):
        s=self.s; mod=lambda i: self.mod(lat,i)
        u=UNROLL["ab"]
        @pl.loop(0,4//u)
        def _(i):
            for k in range(u): self.attend_back(lat,i*u+k)
        self.emit(lat,"dq",5,True)
        for n in range(3):
            cols=slice(256*n,256*n+256)
            s["z"][:,cols]=sum(ndot(s["dq"][j],s["wall"][0,j,cols,0:640]) for j in range(4))
        da=s["z"][...]
        xh=s["xh1"][lat]
        self.dmod[lat,0:1]=colsum(da); self.dmod[lat,1:2]=colsum(da*xh)
        dh=s["h"][lat]+ln_back(da,xh,s["r1"][lat],mod(1))
        self.small[32:33]+=colsum(dh)
        self.small[0:16]+=dot(self.mixed(lat)[3],dh.astype(BF))

    def run(self,ready=lambda: None):
        @pl.loop(0,4)
        def _(lat): self.attn_fwd(lat)
        ready()
        @pl.loop(0,4)
        def _(lat):
            for phase in (self.fc_fwd,self.head,self.fc_bwd,self.attn_bwd): phase(lat)
        self.last()

def block_kernel(times_ref,base_ref,clean_ref,noise_ref,mod_ref,wall_ref,pe_ref,emb_ref,bh_ref,ball_ref,*rest,count_all,names):
    outs=rest[0:8]; dmod,small,dbq,db1,hb=rest[8:13]
    s=dict(zip(names,rest[13:13+len(names)])); wsem=rest[-1]
    cp=pltpu.make_async_copy(wall_ref,s["wall"],wsem); cp.start()
    base=base_ref[0]
    b=Block(s,times_ref,clean_ref,noise_ref,mod_ref,pe_ref,emb_ref,bh_ref,ball_ref,outs,dmod,small,hb,base,0,count_all,lambda lat,pos: None)
    b.start()
    cp.wait()
    b.run()
    for k in range(2):
        dbq[k]=s["dbq"][base+k]; db1[k]=s["db1"][base+k]

def run_block(base,times,clean,noise,mod,wall,pe,emb,bh,ball,count_all):
    L=clean.shape[0]
    S=jax.ShapeDtypeStruct
    outs=[S((L,SEQ,D),BF)]*4+[S((2,L,SEQ,256),BF),S((2,L,SEQ,640),BF),S((2,L,SEQ,768),BF),S((2,L,SEQ,768),BF),
        S((L,8,D),F32),S((40,D),F32),S((2,1,640),F32),S((2,1,768),F32),S((PATCH_IN,128),F32)]
    st=block_state(); names=tuple(st)
    vm=pl.BlockSpec(memory_space=pltpu.VMEM); anys=pl.BlockSpec(memory_space=pl.ANY); sm=pl.BlockSpec(memory_space=pltpu.SMEM)
    return pl.pallas_call(functools.partial(block_kernel,count_all=count_all,names=names),
        out_shape=outs,in_specs=[sm,sm,vm,vm,vm,anys,vm,vm,vm,vm],out_specs=[anys]*8+[vm]*5,
        scratch_shapes=list(st.values())+[pltpu.SemaphoreType.DMA(())],
        compiler_params=pltpu.CompilerParams(vmem_limit_bytes=62*1024*1024),name="block")(times,base,clean,noise,mod,wall,pe,emb,bh,ball)


MESH = pl.DeviceIdType.MESH
HI = lax.Precision.HIGHEST


def hdot(a, b):
    return lax.dot_general(a, b, (((1,), (0,)), ((), ())), precision=HI, preferred_element_type=F32)


def hndot(a, b):
    return lax.dot_general(a, b, (((1,), (1,)), ((), ())), precision=HI, preferred_element_type=F32)


def htdot(a, b):
    return lax.dot_general(a, b, (((0,), (0,)), ((), ())), precision=HI, preferred_element_type=F32)


def split2(values):
    first = values.astype(BF)
    return first, (values - first.astype(F32)).astype(BF)


def split3(values):
    first, rest = values.astype(BF), values
    rest = rest - first.astype(F32)
    second = rest.astype(BF)
    return first, second, (rest - second.astype(F32)).astype(BF)


def silu_slope_k(values):
    gate = 1.0 / (1.0 + jnp.exp(-values))
    return gate * (1.0 + values * (1.0 - gate))


class Peers:
    def __init__(self, send_sem, recv_sem):
        self.w = lax.axis_index("dp")
        self.t = lax.axis_index("tensor")
        self.n = lax.axis_size("dp")
        self.tn = lax.axis_size("tensor")
        self.c = lax.rem(self.t, 2)
        self.sib = self.t + 1 - 2 * self.c
        self.send_sem, self.recv_sem = send_sem, recv_sem
        self.pending = []

    def barrier(self):
        bar = pltpu.get_barrier_semaphore()
        for i in range(1, self.n):
            pl.semaphore_signal(bar, inc=1, device_id=(lax.rem(self.w + i, self.n), self.t), device_id_type=MESH)
        for i in range(1, self.tn):
            pl.semaphore_signal(bar, inc=1, device_id=(self.w, lax.rem(self.t + i, self.tn)), device_id_type=MESH)
        pl.semaphore_wait(bar, self.n - 1 + self.tn - 1)

    def copy(self, src, dst, index, device):
        op = pltpu.make_async_remote_copy(
            src_ref=src,
            dst_ref=dst,
            send_sem=self.send_sem.at[index],
            recv_sem=self.recv_sem.at[index],
            device_id=device,
            device_id_type=MESH,
        )
        op.start()
        self.pending.append(op)
        return op

    def dp_push(self, src_of, dst, base):
        ops = []
        for i in range(1, self.n):
            peer = lax.rem(self.w + i, self.n)
            ops.append(self.copy(src_of(peer), dst, base + i - 1, (peer, self.t)))
        return ops

    def tensor_push(self, src, dst, base):
        ops = []
        for i in range(1, self.tn):
            ops.append(self.copy(src, dst, base + i - 1, (self.w, lax.rem(self.t + i, self.tn))))
        return ops

    def core_push(self, src, dst, index):
        return self.copy(src, dst, index, (self.w, self.sib))

    def finish(self):
        for op in self.pending:
            op.wait_send()


def wait_all(ops):
    for op in ops:
        op.wait_recv()


P_TILES = (6, 6, 6, 2, 6)
P_COUNT = 32
Q_COUNT = 40
QKV0, FC0 = 1536, 2112
COLS = 2880


def halves(block):
    high = block.astype(BF).astype(F32)
    return [high, block - high]


def fill(rows, total):
    used = sum(row.shape[0] for row in rows)
    return jnp.concatenate(rows + [jnp.zeros((total - used, rows[0].shape[1]), F32)], axis=0)


AUX = ("cs", "ct", "t1", "a1", "tf", "hot", "wto", "dmod", "small", "dbq", "db1", "hb")


def step_kernel(
    pack_ref, pk_ref, smt_ref, wmod_ref, brow_ref, bmod_ref, times_ref, clean_ref, noise_ref, pe_ref, bh_ref, *rest, names, count_all
):
    outs, aux_out, rest = rest[:8], rest[8 : 8 + len(AUX)], rest[8 + len(AUX) :]
    s = dict(zip(names, rest[: len(names)]))
    aux, rest = dict(zip(AUX, rest[len(names) :])), rest[len(names) + len(AUX) :]
    mod_ref, emb_ref, ball_ref = rest[:3]
    pkl, ems, eml, a1s, a1l, css, csl, mps, mpl_, mos, mol, bal, local_sem, wsend, wrecv, send_sem, recv_sem = rest[3:]
    wall_ref = s["wall"]
    cs_ref, ct_ref, t1_ref, a1_ref, tf_ref, hot_ref, wto_ref = [aux[name] for name in AUX[:7]]
    net = Peers(send_sem, recv_sem)
    w, t, c, n = net.w, net.t, net.c, net.n
    share = D // n
    half = share // 2
    x, z, y = t // 2, w // 2, lax.rem(w, 2)
    own = []

    def place(q, j, v):
        return wall_ref.at[q, j, pl.ds(pl.multiple_of(share * v, 32), share)]

    for q in range(3):
        op = pltpu.make_async_copy(pack_ref.at[q], place(q, t, w), local_sem.at[q])
        op.start()
        own.append(op)
    net.barrier()
    pkl[w] = pk_ref[...]
    pk_ops = net.dp_push(lambda peer: pk_ref, pkl.at[w], 0)
    rest = smt_ref.shape[1]
    emb = jnp.concatenate(
        [smt_ref[:, 0:16], smt_ref[:, rest - 18 : rest - 2], smt_ref[:, 16:17], smt_ref[:, rest - 2 : rest], jnp.zeros((share, 5), F32)],
        axis=1,
    )
    third = share // 3
    emb = jnp.concatenate([emb[0:third], emb[third : 2 * third], emb[2 * third : share], jnp.zeros((third, 8), F32)], axis=1)
    ems[...] = emb.astype(BF)
    eml[w] = ems[...]
    em_ops = net.dp_push(lambda peer: ems, eml.at[w], 7)
    bal[t] = brow_ref[...]
    ba_ops = net.tensor_push(brow_ref, bal.at[t], 14)

    zs = [z, z + 1 - 2 * lax.rem(z, 2), lax.rem(z + 2, 4), 3 - z]
    xo = 1 - x
    mine, across = 2 * x + c, 2 * xo + c
    wys = [2 * zs[k] + y for k in range(4)]
    wos = [2 * zs[k] + (1 - y) for k in range(4)]
    to_zs = [(wys[k], t) for k in range(4)]
    wy, wo, to_z = wys.__getitem__, wos.__getitem__, to_zs.__getitem__
    to_x, to_y, to_core = (w, across), (2 * z + (1 - y), t), (w, net.sib)
    sends = []

    def piece_copy(index, q, j, v, device, own_block):
        slot = place(q, j, v)
        return pltpu.make_async_remote_copy(
            src_ref=pack_ref.at[q] if own_block else slot, dst_ref=slot, send_sem=wsend.at[index],
            recv_sem=wrecv.at[q, j, v], device_id=device, device_id_type=MESH,
        )

    def send(q, j, v, device, own_block=False):
        sends.append((len(sends), q, j, v, device, own_block))
        piece_copy(*sends[-1]).start()

    def arrived(q, j, v):
        piece_copy(0, q, j, v, to_core, False).wait_recv()

    def column(q, k):
        if k == 0:
            send(q, mine, w, to_z(1), True)
            send(q, mine, w, to_z(2), True)
        else:
            arrived(q, mine, wy(k))
            if k == 2:
                send(q, mine, wy(2), to_z(1))
        send(q, mine, wy(k), to_x, k == 0)
        send(q, mine, wy(k), to_y, k == 0)
        send(q, mine, wy(k), to_core, k == 0)

    def by_y(q, k):
        return (q * 4 + k) % 3 == 0

    def side(q, k):
        arrived(q, across, wy(k))
        if by_y(q, k):
            send(q, across, wy(k), to_y)
        send(q, across, wy(k), to_core)
        arrived(q, mine, wo(k))
        if not by_y(q, k):
            send(q, mine, wo(k), to_x)
        send(q, mine, wo(k), to_core)

    def corner(q, k):
        arrived(q, across, wo(k))
        send(q, across, wo(k), to_core)

    def stage(q):
        column(q, 0)
        column(q, 1)
        side(q, 0)
        column(q, 2)
        side(q, 1)
        corner(q, 0)
        column(q, 3)
        side(q, 2)
        corner(q, 1)
        side(q, 3)
        corner(q, 2)
        corner(q, 3)

    def chain0():
        wait_all(pk_ops)
        feats = pkl[...].reshape(8 * n, 384)
        tf_ref[...] = feats[:, 0:FREQ]
        hot_ref[...] = feats[:, FREQ:384]
        small = smt_ref[...].astype(BF).astype(F32)
        t1 = hndot(small[:, 17:273], tf_ref[...]) + small[:, 273:274]
        t1_ref[...] = t1
        act = t1 / (1.0 + jnp.exp(-t1))
        a1s[...] = jnp.concatenate([act[0:half], act[half:share]], axis=1)
        a1l[w] = a1s[...]
        wto_ref[...] = small[:, 274:1042].astype(BF)
        return net.dp_push(lambda peer: a1s, a1l.at[w], 17)

    def chain1(ops):
        wait_all(ops)
        for k in range(n):
            a1_ref[share * k : share * k + half] = a1l[k][:, 0:64]
            a1_ref[share * k + half : share * k + share] = a1l[k][:, 64:128]
        small = smt_ref[...].astype(BF).astype(F32)
        cond = hdot(small[:, 274:1042], a1_ref[...]) + small[:, 1042:1043]
        cond = cond + hndot(small[:, 1043:1075], hot_ref[:, 0:CLASSES])
        ct_ref[...] = cond
        act = cond / (1.0 + jnp.exp(-cond))
        css[...] = jnp.concatenate([act[0:half], act[half:share]], axis=1)
        csl[w] = css[...]
        cs_ops = net.dp_push(lambda peer: css, csl.at[w], 24)
        parts = [tdot(piece, wmod_ref[...]) for piece in split3(act)]
        mps[...] = (parts[0] + parts[1] + parts[2]).reshape(n, 8, QKV0)
        mpl_[w] = mps[w]
        return cs_ops, net.dp_push(lambda peer: mps.at[peer], mpl_.at[w], 31)

    def chain2(ops):
        wait_all(ops)
        total = mpl_[0]
        for k in range(1, n):
            total = total + mpl_[k]
        mos[...] = total + bmod_ref[...]
        mol[t] = mos[...]
        return net.tensor_push(mos, mol.at[t], 38)

    def chain3(cs_ops, ops):
        wait_all(em_ops)
        rows = []
        for k in range(n):
            piece = eml[k].astype(F32)
            rows += [piece[:, 40 * i : 40 * i + 40] for i in range(3)]
        rows = jnp.concatenate(rows, axis=0)
        emb_ref[...] = jnp.concatenate([rows, jnp.zeros((D, 88), F32)], axis=1).T[0:40]
        wait_all(ba_ops)
        ball_ref[...] = bal[...]
        wait_all(cs_ops)
        rows = []
        for k in range(n):
            rows += [csl[k][:, 0:64], csl[k][:, 64:128]]
        rows = jnp.concatenate(rows, axis=0)
        a1s_all = jnp.concatenate([rows, jnp.zeros((D, 64), F32)], axis=1).T
        cs_all = a1s_all[0:64].reshape(n, 8, D)
        picked = jnp.zeros((8, D), F32)
        for k in range(n):
            picked = jnp.where(w == k, cs_all[k], picked)
        cs_ref[...] = picked
        wait_all(ops)
        for lat in range(4):
            for j in range(4):
                for piece in range(2):
                    mod_ref[lat, 2 * j + piece : 2 * j + piece + 1, :] = mol[j, pl.ds(4 * c + lat, 1), D * piece : D * piece + D]

    column(0, 0)
    column(0, 1)
    ops = chain0()
    side(0, 0)
    column(0, 2)
    side(0, 1)
    corner(0, 0)
    column(0, 3)
    side(0, 2)
    corner(0, 1)
    column(1, 0)
    column(2, 0)
    cs_ops, ops = chain1(ops)
    side(0, 3)
    corner(0, 2)
    corner(0, 3)
    for k in range(1, 4):
        column(1, k)
    ops = chain2(ops)
    for k in range(1, 4):
        column(2, k)
    chain3(cs_ops, ops)

    def other_core(q):
        for j in (2 * x + 1 - c, 2 * xo + 1 - c):
            for v in range(n):
                arrived(q, j, v)

    other_core(0)
    own[0].wait()
    items = []
    for q in (1, 2):
        for k in range(4):
            items.append(functools.partial(side, q, k))
            items.append(functools.partial(corner, q, k))
    early = [0, 2, 1, 4, 3, 6, 5, 7]
    items = [items[i] for i in early] + [items[8 + i] for i in early]

    def service(lat, pos):
        for index, item in enumerate(items):
            if index % 4 == pos:
                pl.when(lat == index // 4)(item)

    def ready():
        for q in (1, 2):
            other_core(q)
            own[q].wait()

    block = Block(
        s, times_ref, clean_ref, noise_ref, mod_ref, pe_ref, emb_ref, bh_ref, ball_ref, outs,
        aux["dmod"], aux["small"], aux["hb"], 2 * x, 4 * c, count_all, service,
    )
    block.start()
    block.run(ready)
    for k in range(2):
        aux["dbq"][k] = s["dbq"][2 * x + k]
        aux["db1"][k] = s["db1"][2 * x + k]
    copies = [pltpu.make_async_copy(aux[name], aux_out[i], local_sem.at[3 + i]) for i, name in enumerate(AUX)]
    for op in copies:
        op.start()
    for record in sends:
        piece_copy(*record).wait_send()
    net.finish()
    for op in copies:
        op.wait()


def run_step(pack, pk, smt, wmod, brow, bmod, times, clean, noise, pe, bh, n, count_all):
    S = jax.ShapeDtypeStruct
    V = pltpu.VMEM
    DMA = pltpu.SemaphoreType.DMA
    share = D // n
    lat = 8 * n
    half = 4
    any_spec = pl.BlockSpec(memory_space=pl.ANY)
    vm = pl.BlockSpec(memory_space=pltpu.VMEM)
    aux = [
        ((8, D), F32), ((share, lat), F32), ((share, lat), F32), ((D, lat), F32), ((lat, FREQ), F32), ((lat, 128), F32), ((share, D), BF),
        ((half, 8, D), F32), ((40, D), F32), ((2, 1, 640), F32), ((2, 1, D), F32), ((PATCH_IN, 128), F32),
    ]
    outs = [S((half, SEQ, D), BF)] * 4 + [S((2, half, SEQ, width), BF) for width in (256, 640, D, D)]
    outs += [S(*a) for a in aux]
    state = block_state()
    scratch = list(state.values()) + [V(*a) for a in aux] + [
        V((half, 8, D), F32), V((40, D), F32), V((4, 1, QKV0), F32),
        V((n, 8, 384), F32), V((share // 3, 128), BF), V((n, share // 3, 128), BF),
        V((share // 2, 128), F32), V((n, share // 2, 128), F32), V((share // 2, 128), F32), V((n, share // 2, 128), F32),
        V((n, 8, QKV0), F32), V((n, 8, QKV0), F32), V((8, QKV0), F32), V((4, 8, QKV0), F32), V((4, 1, QKV0), F32),
        DMA((3 + len(AUX),)), DMA((120,)), DMA((3, 4, n)), DMA((41,)), DMA((41,)),
    ]
    return pl.pallas_call(
        functools.partial(step_kernel, names=tuple(state), count_all=count_all),
        out_shape=outs,
        in_specs=[any_spec] + [vm] * 5 + [pl.BlockSpec(memory_space=pltpu.SMEM)] + [vm] * 4,
        out_specs=[any_spec] * len(outs),
        scratch_shapes=scratch,
        compiler_params=pltpu.CompilerParams(collective_id=0, has_side_effects=True, vmem_limit_bytes=62 * 1024 * 1024),
        name="step",
    )(pack, pk, smt, wmod, brow, bmod, times, clean, noise, pe, bh)


def gram_schmidt(block):
    rows = lax.broadcasted_iota(jnp.int32, (8, 1), 0)
    for index in range(8):
        row = block[index : index + 1]
        row = row * lax.rsqrt(jnp.sum(row * row, axis=-1, keepdims=True) + TINY)
        inner = jnp.sum(block * row, axis=-1, keepdims=True)
        inner = jnp.where(rows > index, inner, 0.0)
        block = jnp.where(rows == index, row, block - inner * row)
    return block


def grad_kernel(
    a_ref, m_ref, dy_ref, dz_ref, o_ref, dq_ref, du_ref, g_ref, cerr_ref, rerr_ref,
    dmod_ref, small_ref, dbq_ref, db1_ref, hb_ref, right_ref, cs_ref, ct_ref, t1_ref, a1_ref, tf_ref, hot_ref, wmod_ref, wto_ref,
    mcol_ref, mrow_ref, left_ref, rightn_ref, pst_ref, psr_ref, pc_ref, qst_ref, qsn_ref, qrs_ref, gb_ref, gh_ref, gsm_ref,
    mc, mr, sc, sr, rc, rr, av, mv, dyv, dzv, ov, qv, uv, gv,
    dmo, smo, dbo, dbo1, hbo, dm8, dma, dsc, dss, dts, dtl, tks, tkl, px, pland, py, qx, qland, qy,
    load_sem, send_sem, recv_sem,
):
    net = Peers(send_sem, recv_sem)
    w, t, c = net.w, net.t, net.c
    n = net.n
    share = D // n
    loads = {}

    def load(name, src, dst, index):
        op = pltpu.make_async_copy(src, dst, load_sem.at[index])
        op.start()
        loads[name] = op

    load("q", dq_ref, qv, 9)
    load("a", a_ref, av, 1)
    load("u", du_ref, uv, 0)
    load("m", m_ref, mv, 2)
    load("g", g_ref, gv, 3)
    load("dz", dz_ref, dzv, 4)
    load("o", o_ref, ov, 5)
    load("dy", dy_ref, dyv, 6)
    load("ce", cerr_ref, mc, 7)
    load("re", rerr_ref, mr, 8)
    net.barrier()
    side = [
        net.core_push(dmod_ref, dmo, 0),
        net.core_push(small_ref, smo, 1),
        net.core_push(dbq_ref.at[1 - c], dbo, 2),
        net.core_push(db1_ref.at[1 - c], dbo1, 9),
        net.core_push(hb_ref, hbo, 10),
    ]

    def chunk(i, size=256):
        return pl.ds(pl.multiple_of(i * size, size), size)

    def after(i, first):
        return pl.ds(pl.multiple_of(first + 256 * i, 64), 256)

    for name in ("q", "a"):
        loads[name].wait()
    col_ops, row_ops = [], []
    sc[0:256] = tdot(qv[1 - c, :, 0:256], av[...])
    sc[256:576] = tdot(qv[1 - c, :, 256:640], av[...])[0:320]
    col_ops.append(net.core_push(sc.at[0:576], rc.at[0:576], 3))
    for name in ("u", "m"):
        loads[name].wait()

    @pl.loop(0, 3)
    def _(i):
        sc[after(i, 576), :] = tdot(uv[1 - c, :, chunk(i)], mv[...])

    col_ops.append(net.core_push(sc.at[576:1344], rc.at[576:1344], 4))
    wait_all(side)
    for lat in range(4):
        for piece in range(2):
            span = slice(D * piece, D * piece + D)
            dm8[pl.ds(4 * c + lat, 1), span] = dmod_ref[lat, pl.ds(2 * t + piece, 1), :]
            dm8[pl.ds(4 * (1 - c) + lat, 1), span] = dmo[lat, pl.ds(2 * t + piece, 1), :]
    dma[w] = dm8[...]
    dm_ops = net.dp_push(lambda peer: dm8, dma.at[w], 16)
    for name in ("g", "dz", "o", "dy"):
        loads[name].wait()

    @pl.loop(0, 3)
    def _(i):
        sr[after(i, 192), :] = tdot(gv[1 - c, :, chunk(i)], dzv[...])

    sr[0:192, :] = tdot(ov[1 - c], dyv[...])[64:256]
    row_ops.append(net.core_push(sr, rr, 6))
    total = small_ref[...] + smo[...]
    for k in range(n):
        tks[k, :, 0:share] = total[:, share * k : share * k + share]
    tkl[w] = tks[w]
    tok_ops = net.dp_push(lambda peer: tks.at[peer], tkl.at[w], 24)
    loads["ce"].wait()
    dms = split3(dm8[...])
    cs = split3(cs_ref[...])
    left_side = jnp.concatenate([dms[0], dms[1], dms[0], dms[2], dms[1], dms[0]], axis=0)
    right_side = jnp.concatenate([cs[0], cs[0], cs[1], cs[0], cs[1], cs[2]], axis=0)
    for i in range(6):
        mc[256 * i : 256 * i + 256, :] += tdot(left_side[:, 256 * i : 256 * i + 256], right_side)
    wait_all(col_ops)
    mc[QKV0 : QKV0 + 256] += tdot(qv[c, :, 0:256], av[...]) + rc[0:256]
    mc[QKV0 + 256 : FC0] += tdot(qv[c, :, 256:640], av[...])[0:320] + rc[256:576]

    @pl.loop(0, 3)
    def _(i):
        mc[after(i, FC0), :] += tdot(uv[c, :, chunk(i)], mv[...]) + rc[after(i, 576), :]

    out_col = pltpu.make_async_copy(mc, mcol_ref, load_sem.at[0])
    out_col.start()
    wait_all(dm_ops)
    dmx = dma[...].reshape(8 * n, QKV0)
    part = sum(ndot(wmod_ref[...], piece) for piece in split3(dmx))
    dss[...] = part
    dsc[t] = part
    ds_ops = net.tensor_push(dss, dsc.at[t], 32)
    loads["re"].wait()
    wait_all(row_ops)

    @pl.loop(0, 3)
    def _(i):
        mr[after(i, 192), :] += tdot(gv[c, :, chunk(i)], dzv[...]) + rr[after(i, 192), :]

    mr[0:192, :] += tdot(ov[c], dyv[...])[64:256] + rr[0:192, :]
    out_row = pltpu.make_async_copy(mr, mrow_ref, load_sem.at[1])
    out_row.start()
    right = right_ref[...]

    def left_part(first, last):
        sides = jnp.concatenate(halves(right[:, first:last]), axis=0).astype(BF)
        high, low = split2(mc[first:last, :])
        got = dot(sides, high) + dot(sides, low)
        return got[0:8] + got[8:16]

    for k, spans in enumerate((((0, 512), (512, 1024), (1024, QKV0)), ((QKV0, FC0),), ((FC0, FC0 + 384), (FC0 + 384, COLS)))):
        got = sum(left_part(*span) for span in spans)
        for i in range(6):
            px[6 * k + i] = got[:, 128 * i : 128 * i + 128]
    row_side = fill(halves(right[:, COLS : COLS + D]) + halves(right[:, COLS + D : COLS + 2 * D]), 128).T.astype(BF)

    def row_chunk(values):
        high, low = split2(values)
        return dot(high, row_side) + dot(low, row_side)

    got = jnp.concatenate([row_chunk(mr[0:192, :]), jnp.zeros((64, 128), F32)], axis=0).T
    for i in range(2):
        px[18 + i] = got[0:8, 128 * i : 128 * i + 128] + got[8:16, 128 * i : 128 * i + 128]
    for i in range(3):
        got = row_chunk(mr[192 + 256 * i : 448 + 256 * i, :]).T
        got = got[16:24] + got[24:32]
        px[20 + 2 * i] = got[:, 0:128]
        px[21 + 2 * i] = got[:, 128:256]
    bias = jnp.concatenate(
        [colsum(dm8[...]), (dbq_ref[c] + dbo[...])[:, 0:576], db1_ref[c] + dbo1[...], jnp.zeros((1, 192), F32)], axis=1
    )
    for i in range(24):
        px[26 + i // 8, i % 8 : i % 8 + 1, :] = bias[:, 128 * i : 128 * i + 128]
    both = hb_ref[...] + hbo[...]
    px[29] = both[0:8]
    px[30] = both[8:16]
    px[31] = jnp.zeros((8, 128), F32)

    def scatter(v, land, per, base):
        own = pl.ds(w * per, per)
        land[w] = v[own]
        return net.dp_push(lambda peer: v.at[pl.ds(peer * per, per)], land.at[w], base)

    def collect(land, v, per, base, ops):
        wait_all(ops)
        own = pl.ds(w * per, per)
        v[own] = sum(land[k] for k in range(1, n)) + land[0]
        return net.dp_push(lambda peer: v.at[own], v.at[own], base)

    ops = scatter(px, pland, P_COUNT // n, 40)
    wait_all(ds_ops)
    dcond = (dsc[0] + dsc[1] + dsc[2] + dsc[3]) * silu_slope_k(ct_ref[...])
    dts[...] = sum(tdot(wto_ref[...], piece) for piece in split3(dcond)).reshape(n, share, 8 * n)
    dtl[w] = dts[w]
    dt_ops = net.dp_push(lambda peer: dts.at[peer], dtl.at[w], 56)
    gsm_ref[:, 274:1042] = hndot(dcond, a1_ref[...])
    gsm_ref[:, 1042:1043] = jnp.sum(dcond, axis=1, keepdims=True)
    gsm_ref[:, 1043:1075] = hdot(dcond, hot_ref[...])[:, 0:CLASSES]
    ops = collect(pland, py, P_COUNT // n, 48, ops)
    wait_all(tok_ops)
    tok = sum(tkl[k] for k in range(1, n)) + tkl[0]
    tok = jnp.concatenate([tok, jnp.zeros((88, 128), F32)], axis=0).T[0:share]
    gsm_ref[:, 0:16] = tok[:, 0:16]
    gsm_ref[:, 16:17] = tok[:, 32:33]
    gsm_ref[:, 1075:1091] = tok[:, 16:32]
    gsm_ref[:, 1091:1093] = tok[:, 33:35]
    wait_all(ops)
    base = 0
    bases = []
    for index, count in enumerate(P_TILES):
        bases.append(gram_schmidt(jnp.concatenate([py[base + k] for k in range(count)], axis=1)))
        base += count
    offset = 0
    for block, width in zip(bases, (D, D, D, 192, D)):
        left_ref[:, offset : offset + width] = block[:, 0:width]
        offset += width
    gb_ref[...] = jnp.concatenate([py[26 + i // 8, i % 8 : i % 8 + 1, :] for i in range(23)], axis=1)[:, 0:COLS]
    gh_ref[...] = jnp.concatenate([py[29], py[30]], axis=0)

    col_side = fill(halves(bases[0]) + halves(bases[1]) + halves(bases[2]), 128).T.astype(BF)

    def col_chunk(values):
        high, low = split2(values)
        return dot(high, col_side) + dot(low, col_side)

    def put(first, rows, k, tile):
        got = col_chunk(mc[first : first + rows, :])
        if rows % 128:
            got = jnp.concatenate([got, jnp.zeros((128 - rows % 128, 128), F32)], axis=0)
        got = got.T
        got = got[16 * k : 16 * k + 8] + got[16 * k + 8 : 16 * k + 16]
        for i in range(got.shape[1] // 128):
            qx[tile + i] = got[:, 128 * i : 128 * i + 128]

    for i in range(6):
        put(256 * i, 256, 0, 2 * i)
    put(QKV0, 256, 1, 12)
    put(QKV0 + 256, 320, 1, 14)
    for i in range(3):
        put(FC0 + 256 * i, 256, 2, 17 + 2 * i)
    for k, (rows, block) in enumerate(((slice(0, 192), bases[3][:, 0:192]), (slice(192, 960), bases[4]))):
        left = jnp.concatenate(halves(block), axis=0).astype(BF)
        high, low = split2(mr[rows, :])
        got = dot(left, high) + dot(left, low)
        got = got[0:8] + got[8:16]
        for i in range(6):
            qx[23 + 6 * k + i] = got[:, 128 * i : 128 * i + 128]
    for i in range(35, Q_COUNT):
        qx[i] = jnp.zeros((8, 128), F32)
    ops = scatter(qx, qland, Q_COUNT // n, 64)
    wait_all(dt_ops)
    dtime = (sum(dtl[k] for k in range(1, n)) + dtl[0]) * silu_slope_k(t1_ref[...])
    gsm_ref[:, 17:273] = hdot(dtime, tf_ref[...])
    gsm_ref[:, 273:274] = jnp.sum(dtime, axis=1, keepdims=True)

    def left_rows(blocks):
        rows = []
        for block in blocks:
            high, low = halves(block)
            rows += [high, low, high]
        return rows

    def right_rows(blocks):
        rows = []
        for block in blocks:
            high, low = halves(block)
            rows += [high, high, low]
        return rows

    pst_ref[...] = fill(left_rows(bases[:3]), 128).astype(BF)
    proj = jnp.concatenate([bases[3][:, 0:192], jnp.zeros((8, D), F32)], axis=1)
    fc = jnp.concatenate([jnp.zeros((8, 192), F32), bases[4]], axis=1)
    row_stack = fill(left_rows([proj, fc]), 128)
    pc_ref[...] = row_stack.astype(BF)
    row_stack = jnp.concatenate([row_stack, jnp.zeros((128, 64), F32)], axis=1)
    psr_ref[...] = row_stack.T[0:960].astype(BF)
    ops = collect(qland, qy, Q_COUNT // n, 72, ops)
    wait_all(ops)
    qkv = jnp.concatenate([qy[12 + i] for i in range(5)], axis=1)[:, 0:576]
    pieces = [jnp.concatenate([qy[i] for i in range(12)], axis=1), qkv, jnp.concatenate([qy[17 + i] for i in range(6)], axis=1)]
    pad = jnp.zeros((8, 64), F32)
    qc = jnp.concatenate(pieces + [pad], axis=1)
    span = lax.broadcasted_iota(jnp.int32, (8, 2944), 1)
    cuts = [
        jnp.where((span >= first) & (span < last), qc, 0.0) for first, last in ((0, QKV0), (QKV0, FC0), (FC0, COLS))
    ]
    stack = fill(right_rows(cuts), 128)
    qsn_ref[...] = stack.astype(BF)
    qst_ref[...] = stack.T[0:COLS].astype(BF)
    qr = [jnp.concatenate([qy[23 + 6 * k + i] for i in range(6)], axis=1) for k in range(2)]
    qrs_ref[...] = fill(right_rows(qr), 128).astype(BF)
    rightn_ref[:, 0:COLS] = qc[:, 0:COLS]
    rightn_ref[:, COLS : COLS + D] = qr[0]
    rightn_ref[:, COLS + D : COLS + 2 * D] = qr[1]
    net.finish()
    out_col.wait()
    out_row.wait()


def run_grad(operands, n):
    S = jax.ShapeDtypeStruct
    V = pltpu.VMEM
    rows = operands[0].shape[0]
    lat = 8 * n
    share = D // n
    any_spec = pl.BlockSpec(memory_space=pl.ANY)
    vm = pl.BlockSpec(memory_space=pltpu.VMEM)
    outs = [
        S((COLS, D), F32), S((960, D), F32), S((8, 3264), F32), S((8, 4416), F32),
        S((128, D), BF), S((960, 128), BF), S((128, 960), BF), S((COLS, 128), BF), S((128, 2944), BF), S((128, D), BF),
        S((1, COLS), F32), S((16, 128), F32), S((share, 1093), F32),
    ]
    scratch = [
        V((COLS, D), F32), V((960, D), F32), V((1344, D), F32), V((960, D), F32), V((1344, D), F32), V((960, D), F32),
        V((rows, D), BF), V((rows, D), BF), V((rows, D), BF), V((rows, D), BF),
        V((2, rows, 256), BF), V((2, rows, 640), BF), V((2, rows, D), BF), V((2, rows, D), BF),
        V((4, 8, D), F32), V((40, D), F32), V((1, 640), F32), V((1, D), F32), V((16, 128), F32),
        V((8, QKV0), F32), V((n, 8, QKV0), F32),
        V((4, share, lat), F32), V((share, lat), F32), V((n, share, lat), F32), V((n, share, lat), F32),
        V((n, 40, 128), F32), V((n, 40, 128), F32),
        V((P_COUNT, 8, 128), F32), V((n, P_COUNT // n, 8, 128), F32), V((P_COUNT, 8, 128), F32),
        V((Q_COUNT, 8, 128), F32), V((n, Q_COUNT // n, 8, 128), F32), V((Q_COUNT, 8, 128), F32),
        pltpu.SemaphoreType.DMA((10,)), pltpu.SemaphoreType.DMA((80,)), pltpu.SemaphoreType.DMA((80,)),
    ]
    return pl.pallas_call(
        grad_kernel,
        out_shape=outs,
        in_specs=[any_spec] * 10 + [vm] * 14,
        out_specs=[any_spec] * 2 + [vm] * 11,
        scratch_shapes=scratch,
        compiler_params=pltpu.CompilerParams(collective_id=1, has_side_effects=True, vmem_limit_bytes=60 * 1024 * 1024),
        name="grad",
    )(*operands)


def apply_kernel(
    w_ref, mcol_ref, mrow_ref, qst_ref, psr_ref, pst_ref, pc_ref, qsn_ref, qrs_ref,
    cw_ref, cm_ref, rw_ref, rm_ref, gs_ref, sw_ref, sm_ref,
    cres_ref, rres_ref, cn_ref, cmn_ref, rn_ref, rmn_ref, sn_ref, smn_ref, *, n
):
    step = pl.program_id(0)
    share = D // n
    cres_ref[...] = mcol_ref[...] - dot(qst_ref[...], pst_ref[...]) * (1.0 / n)
    rres_ref[...] = mrow_ref[...] - dot(psr_ref[...], qrs_ref[...]) * (1.0 / n)

    @pl.when(step == 0)
    def _():
        place = lax.broadcasted_iota(jnp.int32, (D, 128), 0) == w_ref[0] * share + lax.broadcasted_iota(jnp.int32, (D, 128), 1)
        pick = jnp.where(place, 1.0, 0.0).astype(BF)
        mom = DECAY * cm_ref[...] + tdot(dot(pst_ref[...], pick).astype(BF), qsn_ref[...])[0:share, 0:COLS]
        cmn_ref[...] = mom
        cn_ref[...] = cw_ref[...] - LEARN_RATE * mom
        mom = DECAY * rm_ref[...] + tdot(dot(qrs_ref[...], pick).astype(BF), pc_ref[...])[0:share]
        rmn_ref[...] = mom
        rn_ref[...] = rw_ref[...] - LEARN_RATE * mom
        mom = DECAY * sm_ref[...] + gs_ref[...]
        smn_ref[...] = mom
        sn_ref[...] = sw_ref[...] - LEARN_RATE * mom


def run_apply(w, operands, n):
    share = D // n
    S = jax.ShapeDtypeStruct
    blk = lambda r, cc: pl.BlockSpec((r, cc), lambda i, *_: (i, 0))
    full = lambda r, cc: pl.BlockSpec((r, cc), lambda i, *_: (0, 0))
    cb, rb, sb = full(share, COLS), full(share, 960), full(share, 1093)
    return pl.pallas_call(
        functools.partial(apply_kernel, n=n),
        grid_spec=pltpu.PrefetchScalarGridSpec(
            num_scalar_prefetch=1,
            grid=(8,),
            in_specs=[blk(360, D), blk(120, D), blk(360, 128), blk(120, 128), full(128, D), full(128, 960), full(128, 2944), full(128, D)]
            + [cb, cb, rb, rb, sb, sb, sb],
            out_specs=[blk(360, D), blk(120, D), cb, cb, rb, rb, sb, sb],
        ),
        out_shape=[S((COLS, D), F32), S((960, D), F32)] + [S((share, v), F32) for v in (COLS, COLS, 960, 960, 1093, 1093)],
        compiler_params=pltpu.CompilerParams(vmem_limit_bytes=48 * 1024 * 1024),
        name="apply",
    )(w, *operands)


def position_table():
    quarter = D // 4
    omega = 1.0 / 10000.0 ** (jnp.arange(quarter, dtype=jnp.float32) / quarter)
    place = jnp.arange(GRID, dtype=jnp.float32)[:, None] * omega[None, :]
    return jnp.concatenate([jnp.sin(place), jnp.cos(place)], axis=1)


def time_features(times):
    half = FREQ // 2
    freqs = jnp.exp(-math.log(10000.0) * jnp.arange(half, dtype=jnp.float32) / half)
    angles = 1000.0 * times[:, None] * freqs[None, :]
    return jnp.concatenate([jnp.cos(angles), jnp.sin(angles)], axis=1)


def small_starts():
    counts = [PATCH_IN, 1, FREQ, 1, D, 1, CLASSES, PATCH_IN, 1, 1]
    starts = [0]
    for amount in counts:
        starts.append(starts[-1] + amount)
    return starts


def cut_parts(array, widths, axis):
    pieces = []
    offset = 0
    for width in widths:
        pieces.append(lax.slice_in_dim(array, offset, offset + width, axis=axis))
        offset = offset + width
    return pieces


def ortho_kernel(x_ref, o_ref):
    count = x_ref.shape[0]
    rows = [x_ref[index] for index in range(count)]
    for index in range(count):
        vector = rows[index]
        vector = vector * lax.rsqrt(jnp.sum(vector * vector, axis=-1, keepdims=True) + TINY)
        o_ref[index] = vector
        for later in range(index + 1, count):
            rows[later] = rows[later] - jnp.sum(rows[later] * vector, axis=-1, keepdims=True) * vector


def orthonormal_all(parts):
    stacked = jnp.stack([jnp.pad(part, ((0, 0), (0, D - part.shape[1]))) for part in parts], axis=1)
    stacked = jnp.pad(stacked, ((0, 0), (0, 8 - len(parts)), (0, 0)))
    out = pl.pallas_call(ortho_kernel, out_shape=jax.ShapeDtypeStruct(stacked.shape, F32), name="ortho")(stacked)
    return [out[:, index, : part.shape[1]] for index, part in enumerate(parts)]


def rounded(values):
    return lax.optimization_barrier(values.astype(BF)).astype(F32)


def silu_slope(values):
    gate = jax.nn.sigmoid(values)
    return gate * (1.0 + values * (1.0 - gate))


def shards_general(
    clean_latents,
    noise_draw,
    timesteps,
    labels,
    col_weights,
    col_moments,
    col_errors,
    row_weights,
    row_moments,
    row_errors,
    bias_weights,
    bias_moments,
    small_weights,
    small_moments,
    head_bias,
    head_moments,
    right_factors,
):
    tensor_size = lax.axis_size("tensor")
    data_size = lax.axis_size("dp")
    tensor_rank = lax.axis_index("tensor")
    data_rank = lax.axis_index("dp")
    batch = clean_latents.shape[0]
    half = batch // 2
    share = D // data_size
    mod_width = 8 * D // tensor_size
    qkv_width = 3 * D // tensor_size
    ffn_width = FF // tensor_size
    proj_rows = D // tensor_size
    count_all = data_size * batch * SEQ * PATCH_IN
    col_widths = [mod_width, qkv_width, ffn_width]
    core = lax.rem(tensor_rank, 2)
    base = tensor_rank - core
    pair = [(index, index + 1 - 2 * (index % 2)) for index in range(tensor_size)]

    def swap(values):
        return lax.ppermute(values, "tensor", pair)

    col_low = col_weights[:, 0, :].astype(BF)
    row_low = row_weights[0].astype(BF).T
    packed = jnp.concatenate(
        [
            col_low[:, mod_width : mod_width + qkv_width],
            row_low[:, :proj_rows],
            col_low[:, mod_width + qkv_width :],
            row_low[:, proj_rows:],
        ],
        axis=1,
    )
    wall = lax.all_gather(lax.all_gather(packed, "dp", axis=0, tiled=True), "tensor", axis=0)
    wall = jnp.stack([wall[:, :, 768 * index : 768 * index + 768] for index in range(3)])
    starts = small_starts()
    small_low = small_weights.astype(BF)
    small_exact = rounded(small_weights)
    picked = jnp.concatenate([small_low[: starts[2]], small_low[starts[7] :]], axis=0)
    emb = lax.all_gather(picked.astype(F32), "dp", axis=1, tiled=True)
    emb = jnp.concatenate([emb[:16], emb[17:33], emb[16:17], emb[33:35], jnp.zeros((5, D), F32)], axis=0)
    w_tin = small_exact[starts[2] : starts[3]]
    b_tin = small_exact[starts[3]]
    w_tout = small_exact[starts[4] : starts[5]]
    b_tout = small_exact[starts[5]]
    table = small_exact[starts[6] : starts[7]]
    bias_exact = rounded(bias_weights[0])
    head_exact = rounded(head_bias)
    w_mod = rounded(col_weights[:, 0, :mod_width])
    bias_all = lax.all_gather(bias_exact, "tensor", axis=0)
    times_all = lax.all_gather(timesteps, "dp", axis=0, tiled=True)
    labels_all = lax.all_gather(labels, "dp", axis=0, tiled=True)
    time_feat = time_features(times_all)
    time_hidden = exact_dot(time_feat, w_tin) + b_tin
    time_act = lax.all_gather(jax.nn.silu(time_hidden), "dp", axis=1, tiled=True)
    onehot = (labels_all[:, None] == jnp.arange(CLASSES, dtype=jnp.int32)[None, :]).astype(F32)
    condition = exact_dot(time_act, w_tout) + b_tout + exact_dot(onehot, table)
    cond_act = jax.nn.silu(condition)
    mod_part = exact_dot(cond_act, w_mod)
    mod_own = lax.psum_scatter(mod_part, "dp", scatter_dimension=0, tiled=True) + bias_exact[:mod_width]
    mod_full = lax.all_gather(mod_own, "tensor", axis=1, tiled=True).reshape(batch, 8, D)
    cond_rows = lax.all_to_all(cond_act, "dp", split_axis=0, concat_axis=1, tiled=True)

    def mine(values):
        return lax.dynamic_slice_in_dim(values, core * half, half, 0)

    ball = jnp.concatenate(
        [
            jnp.pad(bias_all[:, mod_width : mod_width + qkv_width], ((0, 0), (0, 768 - qkv_width))),
            bias_all[:, mod_width + qkv_width :],
        ],
        axis=1,
    )[:, None]
    (a, m, dy, dz, o, dq, du, g, dmod, small, dbq, db1, hb) = run_block(
        base.reshape(1),
        mine(timesteps),
        mine(clean_latents).transpose(0, 2, 1),
        mine(noise_draw).transpose(0, 2, 1),
        mine(mod_full),
        wall,
        position_table(),
        emb,
        head_exact[:, None],
        ball,
        count_all,
    )
    rows = half * SEQ

    def flat(values):
        return values.reshape(rows, values.shape[-1])

    def pick(values, which):
        return lax.dynamic_index_in_dim(values, which, 0, keepdims=False)

    def gradients(which):
        return (
            tdot(flat(a), flat(pick(dq, which))[:, :qkv_width]),
            tdot(flat(m), flat(pick(du, which))),
            tdot(flat(pick(o, which))[:, 64:], flat(dy)),
            tdot(flat(pick(g, which)), flat(dz)),
            pick(dbq, which)[0, :qkv_width],
            pick(db1, which)[0],
        )

    other = swap(gradients(1 - core))
    own = gradients(core)
    g_qkv, g_fc1, g_proj, g_fc2, g_bqkv, g_bfc1 = [left + right for left, right in zip(own, other)]
    dmod_own = dmod.reshape(half, 8 * D)
    dmod_other = swap(dmod_own)
    dmod_group = jnp.where(
        core == 0,
        jnp.concatenate([dmod_own, dmod_other], axis=0),
        jnp.concatenate([dmod_other, dmod_own], axis=0),
    )
    d_mod = lax.dynamic_slice_in_dim(dmod_group, tensor_rank * mod_width, mod_width, 1)
    g_bmod = jnp.sum(d_mod, axis=0)
    g_mod = exact_tdot(cond_rows, d_mod)
    d_mod_all = lax.all_gather(d_mod, "dp", axis=0, tiled=True)
    d_cond = lax.psum(exact_ndot(d_mod_all, w_mod), "tensor") * silu_slope(condition)
    g_table = exact_tdot(onehot, d_cond)
    g_btout = jnp.sum(d_cond, axis=0)
    g_tout = exact_tdot(time_act, d_cond)
    d_time = lax.psum_scatter(exact_ndot(d_cond, w_tout), "dp", scatter_dimension=1, tiled=True)
    d_time = d_time * silu_slope(time_hidden)
    g_btin = jnp.sum(d_time, axis=0)
    g_tin = exact_tdot(time_feat, d_time)
    small_own = lax.psum(lax.psum_scatter(small, "dp", scatter_dimension=1, tiled=True), "tensor") * 0.5
    head_sum, loss_value = lax.psum((hb[:, 0] * 0.5, hb[0, 1] * 0.5), ("dp", "tensor"))
    small_step = jnp.concatenate(
        [
            small_own[:16],
            small_own[32:33],
            g_tin,
            g_btin[None],
            g_tout,
            g_btout[None],
            g_table,
            small_own[16:32],
            small_own[33:34],
            small_own[34:35],
        ],
        axis=0,
    )
    bias_sum = lax.psum(jnp.concatenate([g_bmod, g_bqkv, g_bfc1], axis=0), "dp")
    col_cuts = cut_parts(col_errors[0, 0], col_widths, 1)
    row_cuts = cut_parts(row_errors[0, 0], [proj_rows, ffn_width], 0)
    matrices = [
        g_mod + col_cuts[0],
        g_qkv + col_cuts[1],
        g_fc1 + col_cuts[2],
        g_proj + row_cuts[0],
        g_fc2 + row_cuts[1],
    ]
    right_pieces = cut_parts(right_factors[0], col_widths + [D, D], 1)
    left_local = jnp.concatenate([exact_ndot(right_pieces[i], matrices[i]) for i in range(5)], axis=1)
    left_sum = lax.psum(left_local, "dp")
    bases = orthonormal_all(cut_parts(left_sum, [D, D, D, proj_rows, ffn_width], 1))
    right_local = jnp.concatenate([exact_dot(bases[i], matrices[i]) for i in range(5)], axis=1)
    right_sum = lax.psum(right_local, "dp")
    right_split = cut_parts(right_sum, col_widths + [D, D], 1)
    approx = [exact_tdot(bases[i], right_split[i]) for i in range(5)]
    rest = [matrices[i] - approx[i] / data_size for i in range(5)]
    col_residue = jnp.concatenate(rest[:3], axis=1)[None, None]
    row_residue = jnp.concatenate(rest[3:], axis=0)[None, None]

    def own_columns(values):
        return lax.dynamic_slice_in_dim(values, data_rank * share, share, 1)

    col_step = jnp.concatenate(
        [exact_tdot(own_columns(bases[i]), right_split[i]) for i in range(3)], axis=1
    )[:, None, :]
    row_step = jnp.concatenate(
        [exact_tdot(bases[i], own_columns(right_split[i])) for i in (3, 4)], axis=0
    )[None]
    col_momentum = DECAY * col_moments + col_step
    col_new = col_weights - LEARN_RATE * col_momentum
    row_momentum = DECAY * row_moments + row_step
    row_new = row_weights - LEARN_RATE * row_momentum
    small_momentum = DECAY * small_moments + small_step
    small_new = small_weights - LEARN_RATE * small_momentum
    bias_momentum = DECAY * bias_moments + bias_sum[None]
    bias_new = bias_weights - LEARN_RATE * bias_momentum
    head_momentum = DECAY * head_moments + head_sum
    head_new = head_bias - LEARN_RATE * head_momentum
    left_factors = jnp.concatenate(bases, axis=1)[None]
    right_new = right_sum[None]
    return (
        loss_value,
        col_new,
        col_momentum,
        col_residue,
        row_new,
        row_momentum,
        row_residue,
        bias_new,
        bias_momentum,
        small_new,
        small_momentum,
        head_new,
        head_momentum,
        left_factors,
        right_new,
    )


def shards(
    clean_latents,
    noise_draw,
    timesteps,
    labels,
    col_weights,
    col_moments,
    col_errors,
    row_weights,
    row_moments,
    row_errors,
    bias_weights,
    bias_moments,
    small_weights,
    small_moments,
    head_bias,
    head_moments,
    right_factors,
):
    tensor_size = lax.axis_size("tensor")
    data_size = lax.axis_size("dp")
    tensor_rank = lax.axis_index("tensor")
    data_rank = lax.axis_index("dp")
    batch = clean_latents.shape[0]
    half = batch // 2
    share = D // data_size
    mod_width = 8 * D // tensor_size
    qkv_width = 3 * D // tensor_size
    ffn_width = FF // tensor_size
    proj_rows = D // tensor_size
    count_all = data_size * batch * SEQ * PATCH_IN
    col_widths = [mod_width, qkv_width, ffn_width]
    core = lax.rem(tensor_rank, 2)
    base = tensor_rank - core
    col = col_weights[:, 0]
    col_low = col.astype(BF)
    row_low = row_weights[0].T.astype(BF)
    packed = jnp.stack(
        [
            jnp.concatenate([col_low[:, mod_width : mod_width + qkv_width], row_low[:, :proj_rows]], axis=1),
            col_low[:, mod_width + qkv_width :],
            row_low[:, proj_rows:],
        ]
    )
    wmod = col_low[:, :mod_width]
    onehot = (labels[:, None] == jnp.arange(128, dtype=jnp.int32)[None, :]).astype(F32)
    features = jnp.concatenate([time_features(timesteps), onehot], axis=1)
    bias_exact = rounded(bias_weights)
    bias_row = jnp.concatenate(
        [bias_exact[:, mod_width : mod_width + qkv_width], jnp.zeros((1, 192), F32), bias_exact[:, mod_width + qkv_width :]],
        axis=1,
    )
    small_t = small_weights.T
    a, m, dy, dz, o, dq, du, g, cs, ct, t1, a1, tf, hot, wto, dmod, small, dbq, db1, hb = run_step(
        packed, features, small_t, wmod, bias_row, bias_exact[:, :mod_width], timesteps,
        clean_latents.transpose(0, 2, 1), noise_draw.transpose(0, 2, 1), position_table(), rounded(head_bias)[:, None],
        data_size, count_all,
    )
    rows = half * SEQ

    def flat(values):
        return values.reshape(values.shape[:-3] + (rows, values.shape[-1]))

    acts = [flat(values) for values in (a, m, dy, dz, o, dq, du, g)]
    errors = [col_errors[0, 0].T, row_errors[0, 0]]
    mcol, mrow, left_all, right_sum, pst, psr, pc, qst, qsn, qrs, gb, gh, gsm = run_grad(
        acts + errors + [dmod, small, dbq, db1, hb, right_factors[0], cs, ct, t1, a1, tf, hot, wmod, wto], data_size
    )
    cres, rres, cn, cmn, rn, rmn, sn, smn = run_apply(
        data_rank.reshape(1),
        [mcol, mrow, qst, psr, pst, pc, qsn, qrs, col, col_moments[:, 0], row_weights[0].T, row_moments[0].T]
        + [gsm, small_t, small_moments.T],
        data_size,
    )
    col_new, col_momentum, col_residue = cn[:, None], cmn[:, None], cres.T[None, None]
    row_new, row_momentum, row_residue = rn.T[None], rmn.T[None], rres[None, None]
    small_new, small_momentum = sn.T, smn.T
    bias_sum = gb[0]
    head_sum = gh[:, 0]
    loss_value = gh[0, 1]
    bias_momentum = DECAY * bias_moments + bias_sum[None]
    bias_new = bias_weights - LEARN_RATE * bias_momentum
    head_momentum = DECAY * head_moments + head_sum
    head_new = head_bias - LEARN_RATE * head_momentum
    left_factors = left_all[None]
    right_new = right_sum[None]
    return (
        loss_value,
        col_new,
        col_momentum,
        col_residue,
        row_new,
        row_momentum,
        row_residue,
        bias_new,
        bias_momentum,
        small_new,
        small_momentum,
        head_new,
        head_momentum,
        left_factors,
        right_new,
    )


def solution(mesh):
    fits = mesh.shape["dp"] == 8 and mesh.shape["tensor"] == 4
    placed = (
        P("dp", None, None),
        P("dp", None, None),
        P("dp"),
        P("dp"),
        P("dp", "tensor", None),
        P("dp", "tensor", None),
        P("dp", "tensor", None, None),
        P("tensor", None, "dp"),
        P("tensor", None, "dp"),
        P("dp", "tensor", None, None),
        P("tensor", None),
        P("tensor", None),
        P(None, "dp"),
        P(None, "dp"),
        P(),
        P(),
        P("tensor", None, None),
    )
    return jax.shard_map(
        shards if fits else shards_general,
        mesh=mesh,
        in_specs=placed,
        out_specs=(
            P(),
            P("dp", "tensor", None),
            P("dp", "tensor", None),
            P("dp", "tensor", None, None),
            P("tensor", None, "dp"),
            P("tensor", None, "dp"),
            P("dp", "tensor", None, None),
            P("tensor", None),
            P("tensor", None),
            P(None, "dp"),
            P(None, "dp"),
            P(),
            P(),
            P("tensor", None, None),
            P("tensor", None, None),
        ),
        check_vma=False,
    )
```

```python
import functools
import math

import jax
import jax.numpy as jnp
from jax import lax
from jax.experimental import pallas as pl
from jax.experimental.pallas import tpu as pltpu
from jax.sharding import PartitionSpec as P

D = 768
HEADS = 12
HEAD_DIM = 64
FF = 3072
FREQ = 256
GRID = 16
PATCH_IN = 16
CLASSES = 32
SEQ = 256

EPSILON = 1e-06
TINY = 1e-30
DECAY = 0.9
LEARN_RATE = 100.0
TIME_OFFSET = 0.25
F32 = jnp.float32
BF = jnp.bfloat16
SCALE = 1.0 / math.sqrt(HEAD_DIM)
GELU_C = math.sqrt(2.0 / math.pi)


def exact_dot(left, right):
    return jnp.dot(left, right, precision=lax.Precision.HIGHEST, preferred_element_type=F32)


def exact_tdot(left, right):
    return lax.dot_general(left, right, (((0,), (0,)), ((), ())), precision=lax.Precision.HIGHEST, preferred_element_type=F32)


def exact_ndot(left, right):
    return lax.dot_general(left, right, (((1,), (1,)), ((), ())), precision=lax.Precision.HIGHEST, preferred_element_type=F32)


def dot(a,b): return lax.dot_general(a,b,(((1,),(0,)),((),())),preferred_element_type=F32)
def ndot(a,b): return lax.dot_general(a,b,(((1,),(1,)),((),())),preferred_element_type=F32)
def tdot(a,b): return lax.dot_general(a,b,(((0,),(0,)),((),())),preferred_element_type=F32)

def ln(h):
    c=h-jnp.mean(h,axis=-1,keepdims=True)
    v=jnp.mean(c*c,axis=-1,keepdims=True)
    r=lax.rsqrt(v+EPSILON)
    return c*r,r

def ln_back(dout,xh,r,scale):
    dx=dout*(1.0+scale)
    return r*(dx-jnp.mean(dx,axis=-1,keepdims=True)-xh*jnp.mean(dx*xh,axis=-1,keepdims=True))

def colsum(v): return jnp.sum(v,axis=0,keepdims=True)

UNROLL=dict(af=2,ff=4,fb=4,ab=4)

def block_state():
    V=pltpu.VMEM
    return dict(
        wall=V((3,4,D,D),BF), pe=V((SEQ,D),F32), qkv=V((4,4,SEQ,640),BF), p=V((4,12,SEQ,SEQ),BF),
        xh1=V((4,SEQ,D),F32), y=V((4,SEQ,D),F32), h=V((4,SEQ,D),F32), r1=V((4,SEQ,1),F32),
        xh2=V((SEQ,D),F32), z=V((SEQ,D),F32), r2=V((SEQ,1),F32), slope=V((4,SEQ,D),F32),
        a=V((SEQ,D),BF), m=V((SEQ,D),BF), dz=V((SEQ,D),BF), dy=V((SEQ,D),BF),
        o=V((4,SEQ,256),BF), g=V((4,SEQ,D),BF), du=V((4,SEQ,D),BF), dq=V((4,SEQ,640),BF),
        dbq=V((4,1,640),F32), db1=V((4,1,D),F32), out_sem=pltpu.SemaphoreType.DMA((8,)))

class Block:
    def __init__(self,s,times,clean,noise,mod,pe,emb,bh,ball,outs,dmod,small,hb,base,first,count_all,service):
        self.s=s; self.times=times; self.clean=clean; self.noise=noise; self.mod_ref=mod; self.pe=pe; self.emb=emb; self.bh=bh; self.ball=ball
        self.outs=outs; self.dmod=dmod; self.small=small; self.hb=hb; self.base=base; self.first=first; self.count_all=count_all; self.service=service
        self.lo=lax.broadcasted_iota(jnp.int32,(1,128),1)<64
        self.zero=jnp.zeros((),BF)
    def roll(self,v): return pltpu.roll(v.astype(F32),64,1).astype(BF)
    def out(self,lat,name,index,pair):
        s=self.s
        src=s[name].at[pl.ds(self.base,2)] if pair else s[name]
        dst=self.outs[index].at[:,lat] if pair else self.outs[index].at[lat]
        return pltpu.make_async_copy(src,dst,s["out_sem"].at[index])
    def emit(self,lat,name,index,pair=False): self.out(lat,name,index,pair).start()
    def clear(self,lat,name,index,pair=False):
        @pl.when(lat>0)
        def _(): self.out(lat-1,name,index,pair).wait()
    def last(self):
        for name,index,pair in (("a",0,False),("m",1,False),("dy",2,False),("dz",3,False),("o",4,True),("dq",5,True),("du",6,True),("g",7,True)):
            self.out(3,name,index,pair).wait()
    def start(self):
        s=self.s
        self.small[...]=jnp.zeros_like(self.small); self.hb[...]=jnp.zeros_like(self.hb)
        s["dbq"][...]=jnp.zeros_like(s["dbq"]); s["db1"][...]=jnp.zeros_like(s["db1"])
        for i in range(GRID):
            s["pe"][16*i:16*i+16,0:384]=jnp.broadcast_to(self.pe[i:i+1,:],(16,384))
            s["pe"][16*i:16*i+16,384:768]=self.pe[...]
    def mixed(self,lat):
        place=self.first+lat
        t=self.times[place]
        clean=self.clean[place].astype(F32); noise=self.noise[place].astype(F32)
        return t,clean,noise,(t*clean+(1.0-t)*noise).astype(BF)
    def mod(self,lat,i): return self.mod_ref[lat,i:i+1,:]
    def embed(self,lat):
        s=self.s
        mixed=self.mixed(lat)[3]
        h0=tdot(mixed,self.emb[0:16].astype(BF))+self.emb[32:33]+s["pe"][...]
        s["h"][lat]=h0
        xh,r=ln(h0)
        s["xh1"][lat]=xh; s["r1"][lat]=r
        self.clear(lat,"a",0)
        s["a"][...]=(xh*(1.0+self.mod(lat,1))+self.mod(lat,0)).astype(BF)
        self.emit(lat,"a",0)
        self.clear(lat,"o",4,True)
    def softmax(self,v,lat,idx):
        v=v*SCALE
        e=jnp.exp(v-jnp.max(v,axis=-1,keepdims=True))
        p=(e/jnp.sum(e,axis=-1,keepdims=True)).astype(BF)
        self.s["p"][lat,idx]=p
        return p
    def attend(self,lat,j):
        s=self.s; lo=self.lo; zero=self.zero; wall=s["wall"]
        full=(dot(s["a"][...],wall[0,j])[:,0:640]+self.ball[j,:,0:640]).astype(BF)
        s["qkv"][lat,j]=full
        b0,b1,b2,b3,b4=[full[:,128*i:128*i+128] for i in range(5)]
        p0=self.softmax(ndot(jnp.where(lo,b0,zero),self.roll(b0)),lat,3*j)
        p1=self.softmax(ndot(jnp.where(lo,zero,b1),self.roll(b2)),lat,3*j+1)
        p2=self.softmax(ndot(jnp.where(lo,b3,zero),self.roll(b3)),lat,3*j+2)
        o0=pltpu.roll(dot(p0,b1),64,1)
        s["o"][j,:,0:128]=jnp.where(lo,0.0,o0).astype(BF)
        s["o"][j,:,128:256]=pltpu.roll(jnp.where(lo,dot(p2,b4),dot(p1,b2)),64,1).astype(BF)
    def project(self,lat):
        s=self.s
        self.emit(lat,"o",4,True)
        for n in range(3):
            cols=slice(256*n,256*n+256)
            y=sum(ndot(s["o"][j],s["wall"][0,j,cols,512:768]) for j in range(4))+self.emb[33:34,cols]
            s["y"][lat,:,cols]=y
            s["h"][lat,:,cols]+=self.mod(lat,2)[:,cols]*y
    def attn_fwd(self,lat):
        self.service(lat,0)
        self.embed(lat)
        self.service(lat,1)
        for j in range(2): self.attend(lat,j)
        self.service(lat,2)
        for j in range(2,4): self.attend(lat,j)
        self.service(lat,3)
        self.project(lat)
    def fc_in(self,lat):
        s=self.s
        xh,r=ln(s["h"][lat])
        s["xh2"][...]=xh; s["r2"][...]=r
        self.clear(lat,"m",1)
        s["m"][...]=(xh*(1.0+self.mod(lat,4))+self.mod(lat,3)).astype(BF)
        self.emit(lat,"m",1)
        self.clear(lat,"g",7,True)
    def fc_one(self,lat,j):
        s=self.s
        u=dot(s["m"][...],s["wall"][1,j])+self.ball[j,:,768:1536]
        uu=u*u
        th=jnp.tanh(u*(GELU_C+(GELU_C*0.044715)*uu))
        half=0.5+0.5*th
        s["g"][j]=(u*half).astype(BF)
        s["slope"][j]=half*(1.0+(u-u*th)*(GELU_C+(3.0*0.044715*GELU_C)*uu))
    def fc_fwd(self,lat):
        s=self.s
        self.fc_in(lat)
        u=UNROLL["ff"]
        @pl.loop(0,4//u)
        def _(i):
            for k in range(u): self.fc_one(lat,i*u+k)
        self.emit(lat,"g",7,True)
        for n in range(3):
            cols=slice(256*n,256*n+256)
            z=sum(ndot(s["g"][j],s["wall"][2,j,cols,:]) for j in range(4))+self.emb[34:35,cols]
            s["z"][:,cols]=z
    def head(self,lat):
        s=self.s; mod=lambda i: self.mod(lat,i)
        t,clean,noise,_=self.mixed(lat)
        wh=self.emb[16:32].astype(BF)
        h2=s["h"][lat]+mod(5)*s["z"][...]
        xh,r=ln(h2)
        fi=(xh*(1.0+mod(7))+mod(6)).astype(BF)
        pred=ndot(wh,fi)+self.bh[...]
        diff=pred-(clean-noise)
        weight=1.0/(1.0-t+TIME_OFFSET)
        self.hb[0:1,1:2]+=jnp.sum(colsum(weight*diff*diff),axis=1,keepdims=True)*(1.0/self.count_all)
        dpred=2.0*weight*diff*(1.0/self.count_all)
        self.hb[:,0:1]+=jnp.sum(dpred,axis=1,keepdims=True)
        dpl=dpred.astype(BF)
        self.small[16:32]+=dot(dpl,fi)
        dfi=tdot(dpl,wh)
        self.dmod[lat,6:7]=colsum(dfi); self.dmod[lat,7:8]=colsum(dfi*xh)
        dh=ln_back(dfi,xh,r,mod(7))
        s["h"][lat]=dh
        self.dmod[lat,5:6]=colsum(dh*s["z"][...])
        dzf=dh*mod(5)
        self.small[34:35]+=colsum(dzf)
        self.clear(lat,"dz",3)
        s["dz"][...]=dzf.astype(BF)
        self.emit(lat,"dz",3)
        self.clear(lat,"du",6,True)
    def fc_back_one(self,j):
        s=self.s
        du=dot(s["dz"][...],s["wall"][2,j])*s["slope"][j]
        s["du"][j]=du.astype(BF)
        s["db1"][j]+=colsum(du)
    def fc_bwd(self,lat):
        s=self.s; mod=lambda i: self.mod(lat,i)
        u=UNROLL["fb"]
        @pl.loop(0,4//u)
        def _(i):
            for k in range(u): self.fc_back_one(i*u+k)
        self.emit(lat,"du",6,True)
        for n in range(3):
            cols=slice(256*n,256*n+256)
            s["z"][:,cols]=sum(ndot(s["du"][j],s["wall"][1,j,cols,:]) for j in range(4))
        dm=s["z"][...]
        xh=s["xh2"][...]
        self.dmod[lat,3:4]=colsum(dm); self.dmod[lat,4:5]=colsum(dm*xh)
        dh=s["h"][lat]+ln_back(dm,xh,s["r2"][...],mod(4))
        s["h"][lat]=dh
        self.dmod[lat,2:3]=colsum(dh*s["y"][lat])
        dyf=dh*mod(2)
        self.small[33:34]+=colsum(dyf)
        self.clear(lat,"dy",2)
        s["dy"][...]=dyf.astype(BF)
        self.emit(lat,"dy",2)
        self.clear(lat,"dq",5,True)
    def attend_back(self,lat,j):
        s=self.s; lo=self.lo; zero=self.zero; roll=self.roll
        do=dot(s["dy"][...],s["wall"][0,j,:,512:768])
        r4=pltpu.roll(do[:,0:128],64,1).astype(BF); r5=pltpu.roll(do[:,128:256],64,1).astype(BF)
        do0=jnp.where(lo,r4,zero); do1=jnp.where(lo,zero,r5); do2=jnp.where(lo,r5,zero)
        b0,b1,b2,b3,b4=[s["qkv"][lat,j,:,128*i:128*i+128] for i in range(5)]
        def head(h,doh,v):
            p=s["p"][lat,3*j+h]
            dv=tdot(p,doh)
            dp=ndot(doh,v)
            pf=p.astype(F32)
            t=pf*dp
            ds=(t-pf*jnp.sum(t,axis=-1,keepdims=True)).astype(BF)
            return dv,ds
        dv0,ds0=head(0,do0,b1)
        dv1,ds1=head(1,do1,b2)
        dv2,ds2=head(2,do2,b4)
        rb0=roll(b0); rb3=roll(b3)
        n0=jnp.where(lo,dot(ds0,rb0),tdot(ds0,rb0))*SCALE
        n1=jnp.where(lo,dv0,dot(ds1,roll(b2))*SCALE); n2=jnp.where(lo,tdot(ds1,roll(b1))*SCALE,dv1)
        n3=jnp.where(lo,dot(ds2,rb3),tdot(ds2,rb3))*SCALE
        n4=jnp.where(lo,dv2,0.0)
        for i,v in enumerate((n0,n1,n2,n3,n4)):
            cols=slice(128*i,128*i+128)
            s["dq"][j,:,cols]=v.astype(BF)
            s["dbq"][j,:,cols]+=colsum(v)
    def attn_bwd(self,lat):
        s=self.s; mod=lambda i: self.mod(lat,i)
        u=UNROLL["ab"]
        @pl.loop(0,4//u)
        def _(i):
            for k in range(u): self.attend_back(lat,i*u+k)
        self.emit(lat,"dq",5,True)
        for n in range(3):
            cols=slice(256*n,256*n+256)
            s["z"][:,cols]=sum(ndot(s["dq"][j],s["wall"][0,j,cols,0:640]) for j in range(4))
        da=s["z"][...]
        xh=s["xh1"][lat]
        self.dmod[lat,0:1]=colsum(da); self.dmod[lat,1:2]=colsum(da*xh)
        dh=s["h"][lat]+ln_back(da,xh,s["r1"][lat],mod(1))
        self.small[32:33]+=colsum(dh)
        self.small[0:16]+=dot(self.mixed(lat)[3],dh.astype(BF))

    def run(self,ready=lambda: None):
        @pl.loop(0,4)
        def _(lat): self.attn_fwd(lat)
        ready()
        @pl.loop(0,4)
        def _(lat):
            for phase in (self.fc_fwd,self.head,self.fc_bwd,self.attn_bwd): phase(lat)
        self.last()

def block_kernel(times_ref,base_ref,clean_ref,noise_ref,mod_ref,wall_ref,pe_ref,emb_ref,bh_ref,ball_ref,*rest,count_all,names):
    outs=rest[0:8]; dmod,small,dbq,db1,hb=rest[8:13]
    s=dict(zip(names,rest[13:13+len(names)])); wsem=rest[-1]
    cp=pltpu.make_async_copy(wall_ref,s["wall"],wsem); cp.start()
    base=base_ref[0]
    b=Block(s,times_ref,clean_ref,noise_ref,mod_ref,pe_ref,emb_ref,bh_ref,ball_ref,outs,dmod,small,hb,base,0,count_all,lambda lat,pos: None)
    b.start()
    cp.wait()
    b.run()
    for k in range(2):
        dbq[k]=s["dbq"][base+k]; db1[k]=s["db1"][base+k]

def run_block(base,times,clean,noise,mod,wall,pe,emb,bh,ball,count_all):
    L=clean.shape[0]
    S=jax.ShapeDtypeStruct
    outs=[S((L,SEQ,D),BF)]*4+[S((2,L,SEQ,256),BF),S((2,L,SEQ,640),BF),S((2,L,SEQ,768),BF),S((2,L,SEQ,768),BF),
        S((L,8,D),F32),S((40,D),F32),S((2,1,640),F32),S((2,1,768),F32),S((PATCH_IN,128),F32)]
    st=block_state(); names=tuple(st)
    vm=pl.BlockSpec(memory_space=pltpu.VMEM); anys=pl.BlockSpec(memory_space=pl.ANY); sm=pl.BlockSpec(memory_space=pltpu.SMEM)
    return pl.pallas_call(functools.partial(block_kernel,count_all=count_all,names=names),
        out_shape=outs,in_specs=[sm,sm,vm,vm,vm,anys,vm,vm,vm,vm],out_specs=[anys]*8+[vm]*5,
        scratch_shapes=list(st.values())+[pltpu.SemaphoreType.DMA(())],
        compiler_params=pltpu.CompilerParams(vmem_limit_bytes=62*1024*1024),name="block")(times,base,clean,noise,mod,wall,pe,emb,bh,ball)


MESH = pl.DeviceIdType.MESH
HI = lax.Precision.HIGHEST


def hdot(a, b):
    return lax.dot_general(a, b, (((1,), (0,)), ((), ())), precision=HI, preferred_element_type=F32)


def hndot(a, b):
    return lax.dot_general(a, b, (((1,), (1,)), ((), ())), precision=HI, preferred_element_type=F32)


def htdot(a, b):
    return lax.dot_general(a, b, (((0,), (0,)), ((), ())), precision=HI, preferred_element_type=F32)


def split2(values):
    first = values.astype(BF)
    return first, (values - first.astype(F32)).astype(BF)


def split3(values):
    first, rest = values.astype(BF), values
    rest = rest - first.astype(F32)
    second = rest.astype(BF)
    return first, second, (rest - second.astype(F32)).astype(BF)


def silu_slope_k(values):
    gate = 1.0 / (1.0 + jnp.exp(-values))
    return gate * (1.0 + values * (1.0 - gate))


class Peers:
    def __init__(self, send_sem, recv_sem):
        self.w = lax.axis_index("dp")
        self.t = lax.axis_index("tensor")
        self.n = lax.axis_size("dp")
        self.tn = lax.axis_size("tensor")
        self.c = lax.rem(self.t, 2)
        self.sib = self.t + 1 - 2 * self.c
        self.send_sem, self.recv_sem = send_sem, recv_sem
        self.pending = []

    def barrier(self):
        bar = pltpu.get_barrier_semaphore()
        for i in range(1, self.n):
            pl.semaphore_signal(bar, inc=1, device_id=(lax.rem(self.w + i, self.n), self.t), device_id_type=MESH)
        for i in range(1, self.tn):
            pl.semaphore_signal(bar, inc=1, device_id=(self.w, lax.rem(self.t + i, self.tn)), device_id_type=MESH)
        pl.semaphore_wait(bar, self.n - 1 + self.tn - 1)

    def copy(self, src, dst, index, device):
        op = pltpu.make_async_remote_copy(
            src_ref=src,
            dst_ref=dst,
            send_sem=self.send_sem.at[index],
            recv_sem=self.recv_sem.at[index],
            device_id=device,
            device_id_type=MESH,
        )
        op.start()
        self.pending.append(op)
        return op

    def dp_push(self, src_of, dst, base):
        ops = []
        for i in range(1, self.n):
            peer = lax.rem(self.w + i, self.n)
            ops.append(self.copy(src_of(peer), dst, base + i - 1, (peer, self.t)))
        return ops

    def tensor_push(self, src, dst, base):
        ops = []
        for i in range(1, self.tn):
            ops.append(self.copy(src, dst, base + i - 1, (self.w, lax.rem(self.t + i, self.tn))))
        return ops

    def core_push(self, src, dst, index):
        return self.copy(src, dst, index, (self.w, self.sib))

    def finish(self):
        for op in self.pending:
            op.wait_send()


def wait_all(ops):
    for op in ops:
        op.wait_recv()


P_TILES = (6, 6, 6, 2, 6)
P_COUNT = 32
Q_COUNT = 40
QKV0, FC0 = 1536, 2112
COLS = 2880


def halves(block):
    high = block.astype(BF).astype(F32)
    return [high, block - high]


def fill(rows, total):
    used = sum(row.shape[0] for row in rows)
    return jnp.concatenate(rows + [jnp.zeros((total - used, rows[0].shape[1]), F32)], axis=0)


AUX = ("cs", "ct", "t1", "a1", "tf", "hot", "wto", "dmod", "small", "dbq", "db1", "hb")


def step_kernel(
    pack_ref, pk_ref, smt_ref, wmod_ref, brow_ref, bmod_ref, times_ref, clean_ref, noise_ref, pe_ref, bh_ref, *rest, names, count_all
):
    outs, aux_out, rest = rest[:8], rest[8 : 8 + len(AUX)], rest[8 + len(AUX) :]
    s = dict(zip(names, rest[: len(names)]))
    aux, rest = dict(zip(AUX, rest[len(names) :])), rest[len(names) + len(AUX) :]
    mod_ref, emb_ref, ball_ref = rest[:3]
    pkl, ems, eml, a1s, a1l, css, csl, mps, mpl_, mos, mol, bal, local_sem, wsend, wrecv, send_sem, recv_sem = rest[3:]
    wall_ref = s["wall"]
    cs_ref, ct_ref, t1_ref, a1_ref, tf_ref, hot_ref, wto_ref = [aux[name] for name in AUX[:7]]
    net = Peers(send_sem, recv_sem)
    w, t, c, n = net.w, net.t, net.c, net.n
    share = D // n
    half = share // 2
    x, z, y = t // 2, w // 2, lax.rem(w, 2)
    own = []

    def place(q, j, v):
        return wall_ref.at[q, j, pl.ds(pl.multiple_of(share * v, 32), share)]

    for q in range(3):
        op = pltpu.make_async_copy(pack_ref.at[q], place(q, t, w), local_sem.at[q])
        op.start()
        own.append(op)
    net.barrier()
    pkl[w] = pk_ref[...]
    pk_ops = net.dp_push(lambda peer: pk_ref, pkl.at[w], 0)
    rest = smt_ref.shape[1]
    emb = jnp.concatenate(
        [smt_ref[:, 0:16], smt_ref[:, rest - 18 : rest - 2], smt_ref[:, 16:17], smt_ref[:, rest - 2 : rest], jnp.zeros((share, 5), F32)],
        axis=1,
    )
    third = share // 3
    emb = jnp.concatenate([emb[0:third], emb[third : 2 * third], emb[2 * third : share], jnp.zeros((third, 8), F32)], axis=1)
    ems[...] = emb.astype(BF)
    eml[w] = ems[...]
    em_ops = net.dp_push(lambda peer: ems, eml.at[w], 7)
    bal[t] = brow_ref[...]
    ba_ops = net.tensor_push(brow_ref, bal.at[t], 14)

    zs = [z, z + 1 - 2 * lax.rem(z, 2), lax.rem(z + 2, 4), 3 - z]
    xo = 1 - x
    mine, across = 2 * x + c, 2 * xo + c
    wys = [2 * zs[k] + y for k in range(4)]
    wos = [2 * zs[k] + (1 - y) for k in range(4)]
    to_zs = [(wys[k], t) for k in range(4)]
    wy, wo, to_z = wys.__getitem__, wos.__getitem__, to_zs.__getitem__
    to_x, to_y, to_core = (w, across), (2 * z + (1 - y), t), (w, net.sib)
    sends = []

    def piece_copy(index, q, j, v, device, own_block):
        slot = place(q, j, v)
        return pltpu.make_async_remote_copy(
            src_ref=pack_ref.at[q] if own_block else slot, dst_ref=slot, send_sem=wsend.at[index],
            recv_sem=wrecv.at[q, j, v], device_id=device, device_id_type=MESH,
        )

    def send(q, j, v, device, own_block=False):
        sends.append((len(sends), q, j, v, device, own_block))
        piece_copy(*sends[-1]).start()

    def arrived(q, j, v):
        piece_copy(0, q, j, v, to_core, False).wait_recv()

    def column(q, k):
        if k == 0:
            send(q, mine, w, to_z(1), True)
            send(q, mine, w, to_z(2), True)
        else:
            arrived(q, mine, wy(k))
            if k == 2:
                send(q, mine, wy(2), to_z(1))
        send(q, mine, wy(k), to_x, k == 0)
        send(q, mine, wy(k), to_y, k == 0)
        send(q, mine, wy(k), to_core, k == 0)

    def by_y(k):
        return k % 2 == 1

    def side(q, k):
        arrived(q, across, wy(k))
        if by_y(k):
            send(q, across, wy(k), to_y)
        send(q, across, wy(k), to_core)
        arrived(q, mine, wo(k))
        if not by_y(k):
            send(q, mine, wo(k), to_x)
        send(q, mine, wo(k), to_core)

    def corner(q, k):
        arrived(q, across, wo(k))
        send(q, across, wo(k), to_core)

    first_hop = {1: to_x, 2: to_y}
    last_hop = {1: to_y, 2: to_x}

    def level(q, k):
        return (mine, wy(k)), ((across, wy(k)) if q == 1 else (mine, wo(k)))

    def begin(q):
        send(q, mine, w, first_hop[q], True)
        send(q, mine, w, to_z(1), True)
        send(q, mine, w, to_z(2), True)
        send(q, mine, w, last_hop[q], True)
        send(q, mine, w, to_core, True)

    def second(q):
        j, v = level(q, 0)[1]
        arrived(q, j, v)
        for device in (to_z(1), to_z(2), last_hop[q], to_core):
            send(q, j, v, device)

    def along(q, k):
        for j, v in level(q, k):
            arrived(q, j, v)
            if k == 2:
                send(q, j, v, to_z(1))
            send(q, j, v, last_hop[q])
            send(q, j, v, to_core)

    def far(q, k):
        last = (mine, wo(k)) if q == 1 else (across, wy(k))
        for j, v in (last, (across, wo(k))):
            arrived(q, j, v)
            send(q, j, v, to_core)

    def chain0():
        wait_all(pk_ops)
        feats = pkl[...].reshape(8 * n, 384)
        tf_ref[...] = feats[:, 0:FREQ]
        hot_ref[...] = feats[:, FREQ:384]
        small = smt_ref[...].astype(BF).astype(F32)
        t1 = hndot(small[:, 17:273], tf_ref[...]) + small[:, 273:274]
        t1_ref[...] = t1
        act = t1 / (1.0 + jnp.exp(-t1))
        a1s[...] = jnp.concatenate([act[0:half], act[half:share]], axis=1)
        a1l[w] = a1s[...]
        wto_ref[...] = small[:, 274:1042].astype(BF)
        return net.dp_push(lambda peer: a1s, a1l.at[w], 17)

    def chain1(ops):
        wait_all(ops)
        for k in range(n):
            a1_ref[share * k : share * k + half] = a1l[k][:, 0:64]
            a1_ref[share * k + half : share * k + share] = a1l[k][:, 64:128]
        small = smt_ref[...].astype(BF).astype(F32)
        cond = hdot(small[:, 274:1042], a1_ref[...]) + small[:, 1042:1043]
        cond = cond + hndot(small[:, 1043:1075], hot_ref[:, 0:CLASSES])
        ct_ref[...] = cond
        act = cond / (1.0 + jnp.exp(-cond))
        css[...] = jnp.concatenate([act[0:half], act[half:share]], axis=1)
        csl[w] = css[...]
        cs_ops = net.dp_push(lambda peer: css, csl.at[w], 24)
        parts = [tdot(piece, wmod_ref[...]) for piece in split3(act)]
        mps[...] = (parts[0] + parts[1] + parts[2]).reshape(n, 8, QKV0)
        mpl_[w] = mps[w]
        return cs_ops, net.dp_push(lambda peer: mps.at[peer], mpl_.at[w], 31)

    def chain2(ops):
        wait_all(ops)
        total = mpl_[0]
        for k in range(1, n):
            total = total + mpl_[k]
        mos[...] = total + bmod_ref[...]
        mol[t] = mos[...]
        return net.tensor_push(mos, mol.at[t], 38)

    def chain3(cs_ops, ops):
        wait_all(em_ops)
        rows = []
        for k in range(n):
            piece = eml[k].astype(F32)
            rows += [piece[:, 40 * i : 40 * i + 40] for i in range(3)]
        rows = jnp.concatenate(rows, axis=0)
        emb_ref[...] = jnp.concatenate([rows, jnp.zeros((D, 88), F32)], axis=1).T[0:40]
        wait_all(ba_ops)
        ball_ref[...] = bal[...]
        wait_all(cs_ops)
        rows = []
        for k in range(n):
            rows += [csl[k][:, 0:64], csl[k][:, 64:128]]
        rows = jnp.concatenate(rows, axis=0)
        a1s_all = jnp.concatenate([rows, jnp.zeros((D, 64), F32)], axis=1).T
        cs_all = a1s_all[0:64].reshape(n, 8, D)
        picked = jnp.zeros((8, D), F32)
        for k in range(n):
            picked = jnp.where(w == k, cs_all[k], picked)
        cs_ref[...] = picked
        wait_all(ops)
        for lat in range(4):
            for j in range(4):
                for piece in range(2):
                    mod_ref[lat, 2 * j + piece : 2 * j + piece + 1, :] = mol[j, pl.ds(4 * c + lat, 1), D * piece : D * piece + D]

    column(0, 0)
    ops = chain0()
    column(0, 1)
    side(0, 0)
    column(0, 2)
    cs_ops, ops = chain1(ops)
    side(0, 1)
    corner(0, 0)
    column(0, 3)
    side(0, 2)
    begin(1)
    begin(2)
    corner(0, 1)
    side(0, 3)
    ops = chain2(ops)
    corner(0, 2)
    corner(0, 3)
    second(1)
    second(2)
    chain3(cs_ops, ops)

    def other_core(q):
        for j in (2 * x + 1 - c, 2 * xo + 1 - c):
            for v in range(n):
                arrived(q, j, v)

    other_core(0)
    own[0].wait()
    slots = {
        0: [functools.partial(along, 1, 1)],
        1: [functools.partial(along, 2, 1)],
        4: [functools.partial(along, 1, 2)],
        6: [functools.partial(along, 2, 2)],
        11: [functools.partial(along, 1, 3)],
        13: [functools.partial(along, 2, 3)],
    }
    rest = [functools.partial(far, q, k) for k in range(4) for q in (1, 2)]

    def service(lat, pos):
        for index, todo in slots.items():
            if index % 4 == pos:
                for item in todo:
                    pl.when(lat == index // 4)(item)

    def ready():
        for item in rest:
            item()
        for q in (1, 2):
            other_core(q)
            own[q].wait()

    block = Block(
        s, times_ref, clean_ref, noise_ref, mod_ref, pe_ref, emb_ref, bh_ref, ball_ref, outs,
        aux["dmod"], aux["small"], aux["hb"], 2 * x, 4 * c, count_all, service,
    )
    block.start()
    block.run(ready)
    for k in range(2):
        aux["dbq"][k] = s["dbq"][2 * x + k]
        aux["db1"][k] = s["db1"][2 * x + k]
    copies = [pltpu.make_async_copy(aux[name], aux_out[i], local_sem.at[3 + i]) for i, name in enumerate(AUX)]
    for op in copies:
        op.start()
    for record in sends:
        piece_copy(*record).wait_send()
    net.finish()
    for op in copies:
        op.wait()


def run_step(pack, pk, smt, wmod, brow, bmod, times, clean, noise, pe, bh, n, count_all):
    S = jax.ShapeDtypeStruct
    V = pltpu.VMEM
    DMA = pltpu.SemaphoreType.DMA
    share = D // n
    lat = 8 * n
    half = 4
    any_spec = pl.BlockSpec(memory_space=pl.ANY)
    vm = pl.BlockSpec(memory_space=pltpu.VMEM)
    aux = [
        ((8, D), F32), ((share, lat), F32), ((share, lat), F32), ((D, lat), F32), ((lat, FREQ), F32), ((lat, 128), F32), ((share, D), BF),
        ((half, 8, D), F32), ((40, D), F32), ((2, 1, 640), F32), ((2, 1, D), F32), ((PATCH_IN, 128), F32),
    ]
    outs = [S((half, SEQ, D), BF)] * 4 + [S((2, half, SEQ, width), BF) for width in (256, 640, D, D)]
    outs += [S(*a) for a in aux]
    state = block_state()
    scratch = list(state.values()) + [V(*a) for a in aux] + [
        V((half, 8, D), F32), V((40, D), F32), V((4, 1, QKV0), F32),
        V((n, 8, 384), F32), V((share // 3, 128), BF), V((n, share // 3, 128), BF),
        V((share // 2, 128), F32), V((n, share // 2, 128), F32), V((share // 2, 128), F32), V((n, share // 2, 128), F32),
        V((n, 8, QKV0), F32), V((n, 8, QKV0), F32), V((8, QKV0), F32), V((4, 8, QKV0), F32), V((4, 1, QKV0), F32),
        DMA((3 + len(AUX),)), DMA((120,)), DMA((3, 4, n)), DMA((41,)), DMA((41,)),
    ]
    return pl.pallas_call(
        functools.partial(step_kernel, names=tuple(state), count_all=count_all),
        out_shape=outs,
        in_specs=[any_spec] + [vm] * 5 + [pl.BlockSpec(memory_space=pltpu.SMEM)] + [vm] * 4,
        out_specs=[any_spec] * len(outs),
        scratch_shapes=scratch,
        compiler_params=pltpu.CompilerParams(collective_id=0, has_side_effects=True, vmem_limit_bytes=62 * 1024 * 1024),
        name="step",
    )(pack, pk, smt, wmod, brow, bmod, times, clean, noise, pe, bh)


def gram_schmidt(block):
    rows = lax.broadcasted_iota(jnp.int32, (8, 1), 0)
    for index in range(8):
        row = block[index : index + 1]
        row = row * lax.rsqrt(jnp.sum(row * row, axis=-1, keepdims=True) + TINY)
        inner = jnp.sum(block * row, axis=-1, keepdims=True)
        inner = jnp.where(rows > index, inner, 0.0)
        block = jnp.where(rows == index, row, block - inner * row)
    return block


def grad_kernel(
    a_ref, m_ref, dy_ref, dz_ref, o_ref, dq_ref, du_ref, g_ref, cerr_ref, rerr_ref,
    dmod_ref, small_ref, dbq_ref, db1_ref, hb_ref, right_ref, cs_ref, ct_ref, t1_ref, a1_ref, tf_ref, hot_ref, wmod_ref, wto_ref,
    mcol_ref, mrow_ref, left_out, rightn_out, pst_out, psr_out, pc_out, qst_out, qsn_out, qrs_out, gb_out, gh_out, gsm_out,
    mc, mr, sc, sr, rc, rr, av, mv, dyv, dzv, ov, qv, uv, gv,
    left_ref, rightn_ref, pst_ref, psr_ref, pc_ref, qst_ref, qsn_ref, qrs_ref, gb_ref, gh_ref, gsm_ref,
    dmo, smo, dbo, dbo1, hbo, dm8, dma, dsc, dss, dts, dtl, tks, tkl, px, pland, py, qx, qland, qy,
    load_sem, out_sem, send_sem, recv_sem,
):
    net = Peers(send_sem, recv_sem)
    outs = []

    def emit(*pairs):
        for src, dst in pairs:
            op = pltpu.make_async_copy(src, dst, out_sem.at[len(outs)])
            op.start()
            outs.append(op)

    w, t, c = net.w, net.t, net.c
    n = net.n
    share = D // n
    loads = {}

    def load(name, src, dst, index):
        op = pltpu.make_async_copy(src, dst, load_sem.at[index])
        op.start()
        loads[name] = op

    load("q", dq_ref, qv, 9)
    load("a", a_ref, av, 1)
    load("u", du_ref, uv, 0)
    load("m", m_ref, mv, 2)
    net.barrier()
    side = [
        net.core_push(dmod_ref, dmo, 0),
        net.core_push(small_ref, smo, 1),
        net.core_push(dbq_ref.at[1 - c], dbo, 2),
        net.core_push(db1_ref.at[1 - c], dbo1, 9),
        net.core_push(hb_ref, hbo, 10),
    ]

    def chunk(i, size=256):
        return pl.ds(pl.multiple_of(i * size, size), size)

    def after(i, first):
        return pl.ds(pl.multiple_of(first + 256 * i, 64), 256)

    wait_all(side)
    for lat in range(4):
        for piece in range(2):
            span = slice(D * piece, D * piece + D)
            dm8[pl.ds(4 * c + lat, 1), span] = dmod_ref[lat, pl.ds(2 * t + piece, 1), :]
            dm8[pl.ds(4 * (1 - c) + lat, 1), span] = dmo[lat, pl.ds(2 * t + piece, 1), :]
    dma[w] = dm8[...]
    dm_ops = net.dp_push(lambda peer: dm8, dma.at[w], 16)
    total = small_ref[...] + smo[...]
    for k in range(n):
        tks[k, :, 0:share] = total[:, share * k : share * k + share]
    tkl[w] = tks[w]
    tok_ops = net.dp_push(lambda peer: tks.at[peer], tkl.at[w], 24)
    load("g", g_ref, gv, 3)
    load("dz", dz_ref, dzv, 4)
    load("o", o_ref, ov, 5)
    load("dy", dy_ref, dyv, 6)
    for name in ("q", "a"):
        loads[name].wait()
    col_ops, row_ops = [], []
    sc[0:256] = tdot(qv[1 - c, :, 0:256], av[...])
    sc[256:576] = tdot(qv[1 - c, :, 256:640], av[...])[0:320]
    col_ops.append(net.core_push(sc.at[0:576], rc.at[0:576], 3))
    load("ce", cerr_ref, mc, 7)
    for name in ("u", "m"):
        loads[name].wait()

    @pl.loop(0, 3)
    def _(i):
        sc[after(i, 576), :] = tdot(uv[1 - c, :, chunk(i)], mv[...])

    col_ops.append(net.core_push(sc.at[576:1344], rc.at[576:1344], 4))
    for name in ("g", "dz", "o", "dy"):
        loads[name].wait()

    @pl.loop(0, 3)
    def _(i):
        sr[after(i, 192), :] = tdot(gv[1 - c, :, chunk(i)], dzv[...])

    sr[0:192, :] = tdot(ov[1 - c], dyv[...])[64:256]
    row_ops.append(net.core_push(sr, rr, 6))
    load("re", rerr_ref, mr, 8)
    loads["ce"].wait()
    dms = split3(dm8[...])
    cs = split3(cs_ref[...])
    left_side = jnp.concatenate([dms[0], dms[1], dms[0], dms[2], dms[1], dms[0]], axis=0)
    right_side = jnp.concatenate([cs[0], cs[0], cs[1], cs[0], cs[1], cs[2]], axis=0)
    for i in range(6):
        mc[256 * i : 256 * i + 256, :] += tdot(left_side[:, 256 * i : 256 * i + 256], right_side)
    wait_all(col_ops)
    mc[QKV0 : QKV0 + 256] += tdot(qv[c, :, 0:256], av[...]) + rc[0:256]
    mc[QKV0 + 256 : FC0] += tdot(qv[c, :, 256:640], av[...])[0:320] + rc[256:576]

    @pl.loop(0, 3)
    def _(i):
        mc[after(i, FC0), :] += tdot(uv[c, :, chunk(i)], mv[...]) + rc[after(i, 576), :]

    out_col = pltpu.make_async_copy(mc, mcol_ref, load_sem.at[0])
    out_col.start()
    loads["re"].wait()
    wait_all(row_ops)

    @pl.loop(0, 3)
    def _(i):
        mr[after(i, 192), :] += tdot(gv[c, :, chunk(i)], dzv[...]) + rr[after(i, 192), :]

    mr[0:192, :] += tdot(ov[c], dyv[...])[64:256] + rr[0:192, :]
    out_row = pltpu.make_async_copy(mr, mrow_ref, load_sem.at[1])
    out_row.start()
    wait_all(dm_ops)
    dmx = dma[...].reshape(8 * n, QKV0)
    part = sum(ndot(wmod_ref[...], piece) for piece in split3(dmx))
    dss[...] = part
    dsc[t] = part
    ds_ops = net.tensor_push(dss, dsc.at[t], 32)
    right = right_ref[...]

    def left_part(first, last):
        sides = jnp.concatenate(halves(right[:, first:last]), axis=0).astype(BF)
        high, low = split2(mc[first:last, :])
        got = dot(sides, high) + dot(sides, low)
        return got[0:8] + got[8:16]

    for k, spans in enumerate((((0, 512), (512, 1024), (1024, QKV0)), ((QKV0, FC0),), ((FC0, FC0 + 384), (FC0 + 384, COLS)))):
        got = sum(left_part(*span) for span in spans)
        for i in range(6):
            px[6 * k + i] = got[:, 128 * i : 128 * i + 128]
    row_side = fill(halves(right[:, COLS : COLS + D]) + halves(right[:, COLS + D : COLS + 2 * D]), 128).T.astype(BF)

    def row_chunk(values):
        high, low = split2(values)
        return dot(high, row_side) + dot(low, row_side)

    got = jnp.concatenate([row_chunk(mr[0:192, :]), jnp.zeros((64, 128), F32)], axis=0).T
    for i in range(2):
        px[18 + i] = got[0:8, 128 * i : 128 * i + 128] + got[8:16, 128 * i : 128 * i + 128]
    for i in range(3):
        got = row_chunk(mr[192 + 256 * i : 448 + 256 * i, :]).T
        got = got[16:24] + got[24:32]
        px[20 + 2 * i] = got[:, 0:128]
        px[21 + 2 * i] = got[:, 128:256]
    bias = jnp.concatenate(
        [colsum(dm8[...]), (dbq_ref[c] + dbo[...])[:, 0:576], db1_ref[c] + dbo1[...], jnp.zeros((1, 192), F32)], axis=1
    )
    for i in range(24):
        px[26 + i // 8, i % 8 : i % 8 + 1, :] = bias[:, 128 * i : 128 * i + 128]
    both = hb_ref[...] + hbo[...]
    px[29] = both[0:8]
    px[30] = both[8:16]
    px[31] = jnp.zeros((8, 128), F32)

    def scatter(v, land, per, base):
        own = pl.ds(w * per, per)
        land[w] = v[own]
        return net.dp_push(lambda peer: v.at[pl.ds(peer * per, per)], land.at[w], base)

    def collect(land, v, per, base, ops):
        wait_all(ops)
        own = pl.ds(w * per, per)
        v[own] = sum(land[k] for k in range(1, n)) + land[0]
        return net.dp_push(lambda peer: v.at[own], v.at[own], base)

    ops = scatter(px, pland, P_COUNT // n, 40)
    ops = collect(pland, py, P_COUNT // n, 48, ops)
    wait_all(ds_ops)
    dcond = (dsc[0] + dsc[1] + dsc[2] + dsc[3]) * silu_slope_k(ct_ref[...])
    dtime = sum(tdot(wto_ref[...], piece) for piece in split3(dcond)).reshape(n, 2, share // 2, 8 * n)
    dts[...] = jnp.concatenate([dtime[:, 0], dtime[:, 1]], axis=2)
    dtl[w] = dts[w]
    dt_ops = net.dp_push(lambda peer: dts.at[peer], dtl.at[w], 56)
    wait_all(tok_ops)
    tok = sum(tkl[k] for k in range(1, n)) + tkl[0]
    tok = jnp.concatenate([tok, jnp.zeros((88, 128), F32)], axis=0).T[0:share]
    gsm_ref[:, 0:16] = tok[:, 0:16]
    gsm_ref[:, 16:17] = tok[:, 32:33]
    gsm_ref[:, 1075:1091] = tok[:, 16:32]
    gsm_ref[:, 1091:1093] = tok[:, 33:35]
    wait_all(ops)
    base = 0
    bases = []
    for index, count in enumerate(P_TILES):
        bases.append(gram_schmidt(jnp.concatenate([py[base + k] for k in range(count)], axis=1)))
        base += count
    offset = 0
    for block, width in zip(bases, (D, D, D, 192, D)):
        left_ref[:, offset : offset + width] = block[:, 0:width]
        offset += width
    gb_ref[...] = jnp.concatenate([py[26 + i // 8, i % 8 : i % 8 + 1, :] for i in range(23)], axis=1)[:, 0:COLS]
    head = jnp.concatenate([py[29], py[30], jnp.zeros((112, 128), F32)], axis=0).T
    gh_ref[...] = head[0:8]
    emit((left_ref, left_out), (gb_ref, gb_out), (gh_ref, gh_out))

    col_side = fill(halves(bases[0]) + halves(bases[1]) + halves(bases[2]), 128).T.astype(BF)

    def col_chunk(values):
        high, low = split2(values)
        return dot(high, col_side) + dot(low, col_side)

    def put(first, rows, k, tile):
        got = col_chunk(mc[first : first + rows, :])
        if rows % 128:
            got = jnp.concatenate([got, jnp.zeros((128 - rows % 128, 128), F32)], axis=0)
        got = got.T
        got = got[16 * k : 16 * k + 8] + got[16 * k + 8 : 16 * k + 16]
        for i in range(got.shape[1] // 128):
            qx[tile + i] = got[:, 128 * i : 128 * i + 128]

    for i in range(6):
        put(256 * i, 256, 0, 2 * i)
    put(QKV0, 256, 1, 12)
    put(QKV0 + 256, 320, 1, 14)
    for i in range(3):
        put(FC0 + 256 * i, 256, 2, 17 + 2 * i)
    for k, (rows, block) in enumerate(((slice(0, 192), bases[3][:, 0:192]), (slice(192, 960), bases[4]))):
        left = jnp.concatenate(halves(block), axis=0).astype(BF)
        high, low = split2(mr[rows, :])
        got = dot(left, high) + dot(left, low)
        got = got[0:8] + got[8:16]
        for i in range(6):
            qx[23 + 6 * k + i] = got[:, 128 * i : 128 * i + 128]
    for i in range(35, Q_COUNT):
        qx[i] = jnp.zeros((8, 128), F32)
    ops = scatter(qx, qland, Q_COUNT // n, 64)
    gsm_ref[:, 274:1042] = hndot(dcond, a1_ref[...])
    gsm_ref[:, 1042:1043] = jnp.sum(dcond, axis=1, keepdims=True)
    gsm_ref[:, 1043:1075] = hdot(dcond, hot_ref[...])[:, 0:CLASSES]
    wait_all(dt_ops)
    dtime = sum(dtl[k] for k in range(1, n)) + dtl[0]
    dtime = jnp.concatenate([dtime[:, 0:64], dtime[:, 64:128]], axis=0) * silu_slope_k(t1_ref[...])
    gsm_ref[:, 17:273] = hdot(dtime, tf_ref[...])
    gsm_ref[:, 273:274] = jnp.sum(dtime, axis=1, keepdims=True)

    def left_rows(blocks):
        rows = []
        for block in blocks:
            high, low = halves(block)
            rows += [high, low, high]
        return rows

    def right_rows(blocks):
        rows = []
        for block in blocks:
            high, low = halves(block)
            rows += [high, high, low]
        return rows

    pst_ref[...] = fill(left_rows(bases[:3]), 128).astype(BF)
    proj = jnp.concatenate([bases[3][:, 0:192], jnp.zeros((8, D), F32)], axis=1)
    fc = jnp.concatenate([jnp.zeros((8, 192), F32), bases[4]], axis=1)
    row_stack = fill(left_rows([proj, fc]), 128)
    pc_ref[...] = row_stack.astype(BF)
    row_stack = jnp.concatenate([row_stack, jnp.zeros((128, 64), F32)], axis=1)
    psr_ref[...] = row_stack.T[0:960].astype(BF)
    emit((pst_ref, pst_out), (pc_ref, pc_out), (psr_ref, psr_out), (gsm_ref, gsm_out))
    ops = collect(qland, qy, Q_COUNT // n, 72, ops)
    wait_all(ops)
    qkv = jnp.concatenate([qy[12 + i] for i in range(5)], axis=1)[:, 0:576]
    pieces = [jnp.concatenate([qy[i] for i in range(12)], axis=1), qkv, jnp.concatenate([qy[17 + i] for i in range(6)], axis=1)]
    pad = jnp.zeros((8, 64), F32)
    qc = jnp.concatenate(pieces + [pad], axis=1)
    span = lax.broadcasted_iota(jnp.int32, (8, 2944), 1)
    cuts = [
        jnp.where((span >= first) & (span < last), qc, 0.0) for first, last in ((0, QKV0), (QKV0, FC0), (FC0, COLS))
    ]
    stack = fill(right_rows(cuts), 128)
    qsn_ref[...] = stack.astype(BF)
    qst_ref[...] = stack.T[0:COLS].astype(BF)
    qr = [jnp.concatenate([qy[23 + 6 * k + i] for i in range(6)], axis=1) for k in range(2)]
    qrs_ref[...] = fill(right_rows(qr), 128).astype(BF)
    rightn_ref[:, 0:COLS] = qc[:, 0:COLS]
    rightn_ref[:, COLS : COLS + D] = qr[0]
    rightn_ref[:, COLS + D : COLS + 2 * D] = qr[1]
    emit((qst_ref, qst_out), (qsn_ref, qsn_out), (qrs_ref, qrs_out), (rightn_ref, rightn_out))
    net.finish()
    for op in outs:
        op.wait()
    out_col.wait()
    out_row.wait()


def run_grad(operands, n):
    S = jax.ShapeDtypeStruct
    V = pltpu.VMEM
    rows = operands[0].shape[0]
    lat = 8 * n
    share = D // n
    any_spec = pl.BlockSpec(memory_space=pl.ANY)
    vm = pl.BlockSpec(memory_space=pltpu.VMEM)
    outs = [
        S((COLS, D), F32), S((960, D), F32), S((8, 3264), F32), S((8, 4416), F32),
        S((128, D), BF), S((960, 128), BF), S((128, 960), BF), S((COLS, 128), BF), S((128, 2944), BF), S((128, D), BF),
        S((1, COLS), F32), S((8, 128), F32), S((share, 1093), F32),
    ]
    scratch = [
        V((COLS, D), F32), V((960, D), F32), V((1344, D), F32), V((960, D), F32), V((1344, D), F32), V((960, D), F32),
        V((rows, D), BF), V((rows, D), BF), V((rows, D), BF), V((rows, D), BF),
        V((2, rows, 256), BF), V((2, rows, 640), BF), V((2, rows, D), BF), V((2, rows, D), BF),
        *[V(o.shape, o.dtype) for o in outs[2:]],
        V((4, 8, D), F32), V((40, D), F32), V((1, 640), F32), V((1, D), F32), V((16, 128), F32),
        V((8, QKV0), F32), V((n, 8, QKV0), F32),
        V((4, share, lat), F32), V((share, lat), F32), V((n, share // 2, 128), F32), V((n, share // 2, 128), F32),
        V((n, 40, 128), F32), V((n, 40, 128), F32),
        V((P_COUNT, 8, 128), F32), V((n, P_COUNT // n, 8, 128), F32), V((P_COUNT, 8, 128), F32),
        V((Q_COUNT, 8, 128), F32), V((n, Q_COUNT // n, 8, 128), F32), V((Q_COUNT, 8, 128), F32),
        pltpu.SemaphoreType.DMA((10,)), pltpu.SemaphoreType.DMA((11,)), pltpu.SemaphoreType.DMA((80,)), pltpu.SemaphoreType.DMA((80,)),
    ]
    return pl.pallas_call(
        grad_kernel,
        out_shape=outs,
        in_specs=[any_spec] * 10 + [vm] * 14,
        out_specs=[any_spec] * 13,
        scratch_shapes=scratch,
        compiler_params=pltpu.CompilerParams(collective_id=1, has_side_effects=True, vmem_limit_bytes=60 * 1024 * 1024),
        name="grad",
    )(*operands)


def apply_kernel(
    w_ref, mcol_ref, mrow_ref, qst_ref, psr_ref, pst_ref, pc_ref, qsn_ref, qrs_ref, left_ref, right_ref, gs_ref, gb_ref, gh_ref,
    cw_ref, cm_ref, rw_ref, rm_ref, sw_ref, sm_ref, bw_ref, bm_ref, hw_ref, hm_ref,
    cres_ref, rres_ref, cn_ref, cmn_ref, rn_ref, rmn_ref, sn_ref, smn_ref, bn_ref, bmn_ref, hn_ref, hmn_ref,
    left_out, right_out, loss_ref, hat_s, *, n
):
    step = pl.program_id(0)
    share = D // n
    per = share // 8

    def update(weight, moment, grad):
        moment = DECAY * moment + grad
        return weight - LEARN_RATE * moment, moment

    @pl.when(step == 0)
    def _():
        place = lax.broadcasted_iota(jnp.int32, (D, 128), 0) == w_ref[0] * share + lax.broadcasted_iota(jnp.int32, (D, 128), 1)
        pick = jnp.where(place, 1.0, 0.0).astype(BF)
        hat_s[...] = tdot(dot(pst_ref[...], pick).astype(BF), qsn_ref[...])[0:share, 0:COLS]
        rows = tdot(dot(qrs_ref[...], pick).astype(BF), pc_ref[...])[0:share]
        rn_ref[...], rmn_ref[...] = update(rw_ref[...], rm_ref[...], rows)

    @pl.when(step == 1)
    def _():
        sn_ref[...], smn_ref[...] = update(sw_ref[...], sm_ref[...], gs_ref[...])
        bn_ref[...], bmn_ref[...] = update(bw_ref[...], bm_ref[...], gb_ref[...])
        hn_ref[...], hmn_ref[...] = update(hw_ref[...], hm_ref[...], gh_ref[0:1, 0:PATCH_IN])
        loss_ref[...] = gh_ref[1:2, 0:1]
        left_out[...] = left_ref[...]
        right_out[...] = right_ref[...]

    cres_ref[...] = mcol_ref[...] - dot(qst_ref[...], pst_ref[...]) * (1.0 / n)
    rres_ref[...] = mrow_ref[...] - dot(psr_ref[...], qrs_ref[...]) * (1.0 / n)
    for r in range(per):
        cn_ref[r], cmn_ref[r] = update(cw_ref[r], cm_ref[r], hat_s[pl.ds(per * step + r, 1), :])


def run_apply(w, operands, n):
    share = D // n
    S = jax.ShapeDtypeStruct
    blk = lambda r, cc: pl.BlockSpec((r, cc), lambda i, *_: (i, 0))
    full = lambda r, cc: pl.BlockSpec((r, cc), lambda i, *_: (0, 0))
    cb = pl.BlockSpec((share // 8, 1, COLS), lambda i, *_: (i, 0, 0))
    rb, sb, bb, hb = full(share, 960), full(share, 1093), full(1, COLS), full(1, PATCH_IN)
    left, right = full(8, 3264), full(8, 4416)
    return pl.pallas_call(
        functools.partial(apply_kernel, n=n),
        grid_spec=pltpu.PrefetchScalarGridSpec(
            num_scalar_prefetch=1,
            grid=(8,),
            in_specs=[blk(360, D), blk(120, D), blk(360, 128), blk(120, 128), full(128, D), full(128, 960), full(128, 2944), full(128, D)]
            + [left, right, sb, bb, full(8, 128), cb, cb, rb, rb, sb, sb, bb, bb, hb, hb],
            out_specs=[blk(360, D), blk(120, D), cb, cb, rb, rb, sb, sb, bb, bb, hb, hb, left, right, full(1, 1)],
            scratch_shapes=[pltpu.VMEM((share, COLS), F32)],
        ),
        out_shape=[S((COLS, D), F32), S((960, D), F32)]
        + [S(v, F32) for v in [(share, 1, COLS)] * 2 + [(share, 960)] * 2 + [(share, 1093)] * 2 + [(1, COLS)] * 2 + [(1, PATCH_IN)] * 2]
        + [S(v, F32) for v in ((8, 3264), (8, 4416), (1, 1))],
        compiler_params=pltpu.CompilerParams(vmem_limit_bytes=48 * 1024 * 1024),
        name="apply",
    )(w, *operands)


def position_table():
    quarter = D // 4
    omega = 1.0 / 10000.0 ** (jnp.arange(quarter, dtype=jnp.float32) / quarter)
    place = jnp.arange(GRID, dtype=jnp.float32)[:, None] * omega[None, :]
    return jnp.concatenate([jnp.sin(place), jnp.cos(place)], axis=1)


def time_features(times):
    half = FREQ // 2
    freqs = jnp.exp(-math.log(10000.0) * jnp.arange(half, dtype=jnp.float32) / half)
    angles = 1000.0 * times[:, None] * freqs[None, :]
    return jnp.concatenate([jnp.cos(angles), jnp.sin(angles)], axis=1)


def small_starts():
    counts = [PATCH_IN, 1, FREQ, 1, D, 1, CLASSES, PATCH_IN, 1, 1]
    starts = [0]
    for amount in counts:
        starts.append(starts[-1] + amount)
    return starts


def cut_parts(array, widths, axis):
    pieces = []
    offset = 0
    for width in widths:
        pieces.append(lax.slice_in_dim(array, offset, offset + width, axis=axis))
        offset = offset + width
    return pieces


def ortho_kernel(x_ref, o_ref):
    count = x_ref.shape[0]
    rows = [x_ref[index] for index in range(count)]
    for index in range(count):
        vector = rows[index]
        vector = vector * lax.rsqrt(jnp.sum(vector * vector, axis=-1, keepdims=True) + TINY)
        o_ref[index] = vector
        for later in range(index + 1, count):
            rows[later] = rows[later] - jnp.sum(rows[later] * vector, axis=-1, keepdims=True) * vector


def orthonormal_all(parts):
    stacked = jnp.stack([jnp.pad(part, ((0, 0), (0, D - part.shape[1]))) for part in parts], axis=1)
    stacked = jnp.pad(stacked, ((0, 0), (0, 8 - len(parts)), (0, 0)))
    out = pl.pallas_call(ortho_kernel, out_shape=jax.ShapeDtypeStruct(stacked.shape, F32), name="ortho")(stacked)
    return [out[:, index, : part.shape[1]] for index, part in enumerate(parts)]


def rounded(values):
    return lax.optimization_barrier(values.astype(BF)).astype(F32)


def silu_slope(values):
    gate = jax.nn.sigmoid(values)
    return gate * (1.0 + values * (1.0 - gate))


def shards_general(
    clean_latents,
    noise_draw,
    timesteps,
    labels,
    col_weights,
    col_moments,
    col_errors,
    row_weights,
    row_moments,
    row_errors,
    bias_weights,
    bias_moments,
    small_weights,
    small_moments,
    head_bias,
    head_moments,
    right_factors,
):
    tensor_size = lax.axis_size("tensor")
    data_size = lax.axis_size("dp")
    tensor_rank = lax.axis_index("tensor")
    data_rank = lax.axis_index("dp")
    batch = clean_latents.shape[0]
    half = batch // 2
    share = D // data_size
    mod_width = 8 * D // tensor_size
    qkv_width = 3 * D // tensor_size
    ffn_width = FF // tensor_size
    proj_rows = D // tensor_size
    count_all = data_size * batch * SEQ * PATCH_IN
    col_widths = [mod_width, qkv_width, ffn_width]
    core = lax.rem(tensor_rank, 2)
    base = tensor_rank - core
    pair = [(index, index + 1 - 2 * (index % 2)) for index in range(tensor_size)]

    def swap(values):
        return lax.ppermute(values, "tensor", pair)

    col_low = col_weights[:, 0, :].astype(BF)
    row_low = row_weights[0].astype(BF).T
    packed = jnp.concatenate(
        [
            col_low[:, mod_width : mod_width + qkv_width],
            row_low[:, :proj_rows],
            col_low[:, mod_width + qkv_width :],
            row_low[:, proj_rows:],
        ],
        axis=1,
    )
    wall = lax.all_gather(lax.all_gather(packed, "dp", axis=0, tiled=True), "tensor", axis=0)
    wall = jnp.stack([wall[:, :, 768 * index : 768 * index + 768] for index in range(3)])
    starts = small_starts()
    small_low = small_weights.astype(BF)
    small_exact = rounded(small_weights)
    picked = jnp.concatenate([small_low[: starts[2]], small_low[starts[7] :]], axis=0)
    emb = lax.all_gather(picked.astype(F32), "dp", axis=1, tiled=True)
    emb = jnp.concatenate([emb[:16], emb[17:33], emb[16:17], emb[33:35], jnp.zeros((5, D), F32)], axis=0)
    w_tin = small_exact[starts[2] : starts[3]]
    b_tin = small_exact[starts[3]]
    w_tout = small_exact[starts[4] : starts[5]]
    b_tout = small_exact[starts[5]]
    table = small_exact[starts[6] : starts[7]]
    bias_exact = rounded(bias_weights[0])
    head_exact = rounded(head_bias)
    w_mod = rounded(col_weights[:, 0, :mod_width])
    bias_all = lax.all_gather(bias_exact, "tensor", axis=0)
    times_all = lax.all_gather(timesteps, "dp", axis=0, tiled=True)
    labels_all = lax.all_gather(labels, "dp", axis=0, tiled=True)
    time_feat = time_features(times_all)
    time_hidden = exact_dot(time_feat, w_tin) + b_tin
    time_act = lax.all_gather(jax.nn.silu(time_hidden), "dp", axis=1, tiled=True)
    onehot = (labels_all[:, None] == jnp.arange(CLASSES, dtype=jnp.int32)[None, :]).astype(F32)
    condition = exact_dot(time_act, w_tout) + b_tout + exact_dot(onehot, table)
    cond_act = jax.nn.silu(condition)
    mod_part = exact_dot(cond_act, w_mod)
    mod_own = lax.psum_scatter(mod_part, "dp", scatter_dimension=0, tiled=True) + bias_exact[:mod_width]
    mod_full = lax.all_gather(mod_own, "tensor", axis=1, tiled=True).reshape(batch, 8, D)
    cond_rows = lax.all_to_all(cond_act, "dp", split_axis=0, concat_axis=1, tiled=True)

    def mine(values):
        return lax.dynamic_slice_in_dim(values, core * half, half, 0)

    ball = jnp.concatenate(
        [
            jnp.pad(bias_all[:, mod_width : mod_width + qkv_width], ((0, 0), (0, 768 - qkv_width))),
            bias_all[:, mod_width + qkv_width :],
        ],
        axis=1,
    )[:, None]
    (a, m, dy, dz, o, dq, du, g, dmod, small, dbq, db1, hb) = run_block(
        base.reshape(1),
        mine(timesteps),
        mine(clean_latents).transpose(0, 2, 1),
        mine(noise_draw).transpose(0, 2, 1),
        mine(mod_full),
        wall,
        position_table(),
        emb,
        head_exact[:, None],
        ball,
        count_all,
    )
    rows = half * SEQ

    def flat(values):
        return values.reshape(rows, values.shape[-1])

    def pick(values, which):
        return lax.dynamic_index_in_dim(values, which, 0, keepdims=False)

    def gradients(which):
        return (
            tdot(flat(a), flat(pick(dq, which))[:, :qkv_width]),
            tdot(flat(m), flat(pick(du, which))),
            tdot(flat(pick(o, which))[:, 64:], flat(dy)),
            tdot(flat(pick(g, which)), flat(dz)),
            pick(dbq, which)[0, :qkv_width],
            pick(db1, which)[0],
        )

    other = swap(gradients(1 - core))
    own = gradients(core)
    g_qkv, g_fc1, g_proj, g_fc2, g_bqkv, g_bfc1 = [left + right for left, right in zip(own, other)]
    dmod_own = dmod.reshape(half, 8 * D)
    dmod_other = swap(dmod_own)
    dmod_group = jnp.where(
        core == 0,
        jnp.concatenate([dmod_own, dmod_other], axis=0),
        jnp.concatenate([dmod_other, dmod_own], axis=0),
    )
    d_mod = lax.dynamic_slice_in_dim(dmod_group, tensor_rank * mod_width, mod_width, 1)
    g_bmod = jnp.sum(d_mod, axis=0)
    g_mod = exact_tdot(cond_rows, d_mod)
    d_mod_all = lax.all_gather(d_mod, "dp", axis=0, tiled=True)
    d_cond = lax.psum(exact_ndot(d_mod_all, w_mod), "tensor") * silu_slope(condition)
    g_table = exact_tdot(onehot, d_cond)
    g_btout = jnp.sum(d_cond, axis=0)
    g_tout = exact_tdot(time_act, d_cond)
    d_time = lax.psum_scatter(exact_ndot(d_cond, w_tout), "dp", scatter_dimension=1, tiled=True)
    d_time = d_time * silu_slope(time_hidden)
    g_btin = jnp.sum(d_time, axis=0)
    g_tin = exact_tdot(time_feat, d_time)
    small_own = lax.psum(lax.psum_scatter(small, "dp", scatter_dimension=1, tiled=True), "tensor") * 0.5
    head_sum, loss_value = lax.psum((hb[:, 0] * 0.5, hb[0, 1] * 0.5), ("dp", "tensor"))
    small_step = jnp.concatenate(
        [
            small_own[:16],
            small_own[32:33],
            g_tin,
            g_btin[None],
            g_tout,
            g_btout[None],
            g_table,
            small_own[16:32],
            small_own[33:34],
            small_own[34:35],
        ],
        axis=0,
    )
    bias_sum = lax.psum(jnp.concatenate([g_bmod, g_bqkv, g_bfc1], axis=0), "dp")
    col_cuts = cut_parts(col_errors[0, 0], col_widths, 1)
    row_cuts = cut_parts(row_errors[0, 0], [proj_rows, ffn_width], 0)
    matrices = [
        g_mod + col_cuts[0],
        g_qkv + col_cuts[1],
        g_fc1 + col_cuts[2],
        g_proj + row_cuts[0],
        g_fc2 + row_cuts[1],
    ]
    right_pieces = cut_parts(right_factors[0], col_widths + [D, D], 1)
    left_local = jnp.concatenate([exact_ndot(right_pieces[i], matrices[i]) for i in range(5)], axis=1)
    left_sum = lax.psum(left_local, "dp")
    bases = orthonormal_all(cut_parts(left_sum, [D, D, D, proj_rows, ffn_width], 1))
    right_local = jnp.concatenate([exact_dot(bases[i], matrices[i]) for i in range(5)], axis=1)
    right_sum = lax.psum(right_local, "dp")
    right_split = cut_parts(right_sum, col_widths + [D, D], 1)
    approx = [exact_tdot(bases[i], right_split[i]) for i in range(5)]
    rest = [matrices[i] - approx[i] / data_size for i in range(5)]
    col_residue = jnp.concatenate(rest[:3], axis=1)[None, None]
    row_residue = jnp.concatenate(rest[3:], axis=0)[None, None]

    def own_columns(values):
        return lax.dynamic_slice_in_dim(values, data_rank * share, share, 1)

    col_step = jnp.concatenate(
        [exact_tdot(own_columns(bases[i]), right_split[i]) for i in range(3)], axis=1
    )[:, None, :]
    row_step = jnp.concatenate(
        [exact_tdot(bases[i], own_columns(right_split[i])) for i in (3, 4)], axis=0
    )[None]
    col_momentum = DECAY * col_moments + col_step
    col_new = col_weights - LEARN_RATE * col_momentum
    row_momentum = DECAY * row_moments + row_step
    row_new = row_weights - LEARN_RATE * row_momentum
    small_momentum = DECAY * small_moments + small_step
    small_new = small_weights - LEARN_RATE * small_momentum
    bias_momentum = DECAY * bias_moments + bias_sum[None]
    bias_new = bias_weights - LEARN_RATE * bias_momentum
    head_momentum = DECAY * head_moments + head_sum
    head_new = head_bias - LEARN_RATE * head_momentum
    left_factors = jnp.concatenate(bases, axis=1)[None]
    right_new = right_sum[None]
    return (
        loss_value,
        col_new,
        col_momentum,
        col_residue,
        row_new,
        row_momentum,
        row_residue,
        bias_new,
        bias_momentum,
        small_new,
        small_momentum,
        head_new,
        head_momentum,
        left_factors,
        right_new,
    )


def shards(
    clean_latents,
    noise_draw,
    timesteps,
    labels,
    col_weights,
    col_moments,
    col_errors,
    row_weights,
    row_moments,
    row_errors,
    bias_weights,
    bias_moments,
    small_weights,
    small_moments,
    head_bias,
    head_moments,
    right_factors,
):
    tensor_size = lax.axis_size("tensor")
    data_size = lax.axis_size("dp")
    tensor_rank = lax.axis_index("tensor")
    data_rank = lax.axis_index("dp")
    batch = clean_latents.shape[0]
    half = batch // 2
    share = D // data_size
    mod_width = 8 * D // tensor_size
    qkv_width = 3 * D // tensor_size
    ffn_width = FF // tensor_size
    proj_rows = D // tensor_size
    count_all = data_size * batch * SEQ * PATCH_IN
    col_widths = [mod_width, qkv_width, ffn_width]
    core = lax.rem(tensor_rank, 2)
    base = tensor_rank - core
    col = col_weights[:, 0]
    col_low = col.astype(BF)
    row_low = row_weights[0].T.astype(BF)
    packed = jnp.stack(
        [
            jnp.concatenate([col_low[:, mod_width : mod_width + qkv_width], row_low[:, :proj_rows]], axis=1),
            col_low[:, mod_width + qkv_width :],
            row_low[:, proj_rows:],
        ]
    )
    wmod = col_low[:, :mod_width]
    onehot = (labels[:, None] == jnp.arange(128, dtype=jnp.int32)[None, :]).astype(F32)
    features = jnp.concatenate([time_features(timesteps), onehot], axis=1)
    bias_exact = rounded(bias_weights)
    bias_row = jnp.concatenate(
        [bias_exact[:, mod_width : mod_width + qkv_width], jnp.zeros((1, 192), F32), bias_exact[:, mod_width + qkv_width :]],
        axis=1,
    )
    small_t = small_weights.T
    a, m, dy, dz, o, dq, du, g, cs, ct, t1, a1, tf, hot, wto, dmod, small, dbq, db1, hb = run_step(
        packed, features, small_t, wmod, bias_row, bias_exact[:, :mod_width], timesteps,
        clean_latents.transpose(0, 2, 1), noise_draw.transpose(0, 2, 1), position_table(), rounded(head_bias)[:, None],
        data_size, count_all,
    )
    rows = half * SEQ

    def flat(values):
        return values.reshape(values.shape[:-3] + (rows, values.shape[-1]))

    acts = [flat(values) for values in (a, m, dy, dz, o, dq, du, g)]
    errors = [col_errors[0, 0].T, row_errors[0, 0]]
    mcol, mrow, left_all, right_sum, pst, psr, pc, qst, qsn, qrs, gb, gh, gsm = run_grad(
        acts + errors + [dmod, small, dbq, db1, hb, right_factors[0], cs, ct, t1, a1, tf, hot, wmod, wto], data_size
    )
    cres, rres, col_new, col_momentum, rn, rmn, sn, smn, bias_new, bias_momentum, hn, hmn, left_all, right_sum, loss = run_apply(
        data_rank.reshape(1),
        [mcol, mrow, qst, psr, pst, pc, qsn, qrs, left_all, right_sum, gsm, gb, gh]
        + [col_weights, col_moments, row_weights[0].T, row_moments[0].T, small_t, small_moments.T]
        + [bias_weights, bias_moments, head_bias[None], head_moments[None]],
        data_size,
    )
    loss_value = loss[0, 0]
    col_residue, row_residue = cres.T[None, None], rres[None, None]
    row_new, row_momentum = rn.T[None], rmn.T[None]
    small_new, small_momentum = sn.T, smn.T
    head_new, head_momentum = hn[0], hmn[0]
    left_factors, right_new = left_all[None], right_sum[None]
    return (
        loss_value,
        col_new,
        col_momentum,
        col_residue,
        row_new,
        row_momentum,
        row_residue,
        bias_new,
        bias_momentum,
        small_new,
        small_momentum,
        head_new,
        head_momentum,
        left_factors,
        right_new,
    )


def solution(mesh):
    fits = mesh.shape["dp"] == 8 and mesh.shape["tensor"] == 4
    placed = (
        P("dp", None, None),
        P("dp", None, None),
        P("dp"),
        P("dp"),
        P("dp", "tensor", None),
        P("dp", "tensor", None),
        P("dp", "tensor", None, None),
        P("tensor", None, "dp"),
        P("tensor", None, "dp"),
        P("dp", "tensor", None, None),
        P("tensor", None),
        P("tensor", None),
        P(None, "dp"),
        P(None, "dp"),
        P(),
        P(),
        P("tensor", None, None),
    )
    return jax.shard_map(
        shards if fits else shards_general,
        mesh=mesh,
        in_specs=placed,
        out_specs=(
            P(),
            P("dp", "tensor", None),
            P("dp", "tensor", None),
            P("dp", "tensor", None, None),
            P("tensor", None, "dp"),
            P("tensor", None, "dp"),
            P("dp", "tensor", None, None),
            P("tensor", None),
            P("tensor", None),
            P(None, "dp"),
            P(None, "dp"),
            P(),
            P(),
            P("tensor", None, None),
            P("tensor", None, None),
        ),
        check_vma=False,
    )
```

```python
import functools
import math

import jax
import jax.numpy as jnp
import numpy as np
from jax import lax
from jax.experimental import pallas as pl
from jax.experimental.pallas import tpu as pltpu
from jax.sharding import PartitionSpec as P

D = 768
HEADS = 12
HEAD_DIM = 64
FF = 3072
FREQ = 256
GRID = 16
PATCH_IN = 16
CLASSES = 32
SEQ = 256

EPSILON = 1e-06
TINY = 1e-30
DECAY = 0.9
LEARN_RATE = 100.0
TIME_OFFSET = 0.25
F32 = jnp.float32
BF = jnp.bfloat16
SCALE = 1.0 / math.sqrt(HEAD_DIM)
GELU_C = math.sqrt(2.0 / math.pi)


def exact_dot(left, right):
    return jnp.dot(left, right, precision=lax.Precision.HIGHEST, preferred_element_type=F32)


def exact_tdot(left, right):
    return lax.dot_general(left, right, (((0,), (0,)), ((), ())), precision=lax.Precision.HIGHEST, preferred_element_type=F32)


def exact_ndot(left, right):
    return lax.dot_general(left, right, (((1,), (1,)), ((), ())), precision=lax.Precision.HIGHEST, preferred_element_type=F32)


def dot(a,b): return lax.dot_general(a,b,(((1,),(0,)),((),())),preferred_element_type=F32)
def ndot(a,b): return lax.dot_general(a,b,(((1,),(1,)),((),())),preferred_element_type=F32)
def tdot(a,b): return lax.dot_general(a,b,(((0,),(0,)),((),())),preferred_element_type=F32)

def ln(h):
    c=h-jnp.mean(h,axis=-1,keepdims=True)
    v=jnp.mean(c*c,axis=-1,keepdims=True)
    r=lax.rsqrt(v+EPSILON)
    return c*r,r

def ln_back(dout,xh,r,scale):
    dx=dout*(1.0+scale)
    return r*(dx-jnp.mean(dx,axis=-1,keepdims=True)-xh*jnp.mean(dx*xh,axis=-1,keepdims=True))

def colsum(v): return jnp.sum(v,axis=0,keepdims=True)

UNROLL=dict(af=2,ff=4,fb=4,ab=4)

def block_state():
    V=pltpu.VMEM
    return dict(
        wall=V((3,4,D,D),BF), pe=V((SEQ,D),F32), qkv=V((4,4,SEQ,640),BF), p=V((4,12,SEQ,SEQ),BF),
        xh1=V((4,SEQ,D),F32), y=V((4,SEQ,D),F32), h=V((4,SEQ,D),F32), r1=V((4,SEQ,1),F32),
        xh2=V((SEQ,D),F32), z=V((SEQ,D),F32), r2=V((SEQ,1),F32), slope=V((4,SEQ,D),F32),
        a=V((SEQ,D),BF), m=V((SEQ,D),BF), dz=V((SEQ,D),BF), dy=V((SEQ,D),BF),
        o=V((4,SEQ,256),BF), g=V((4,SEQ,D),BF), du=V((4,SEQ,D),BF), dq=V((4,SEQ,640),BF),
        dbq=V((4,1,640),F32), db1=V((4,1,D),F32), out_sem=pltpu.SemaphoreType.DMA((8,)))

class Block:
    def __init__(self,s,times,clean,noise,mod,pe,emb,bh,ball,outs,dmod,small,hb,base,first,count_all,service):
        self.s=s; self.times=times; self.clean=clean; self.noise=noise; self.mod_ref=mod; self.pe=pe; self.emb=emb; self.bh=bh; self.ball=ball
        self.outs=outs; self.dmod=dmod; self.small=small; self.hb=hb; self.base=base; self.first=first; self.count_all=count_all; self.service=service
        self.lo=lax.broadcasted_iota(jnp.int32,(1,128),1)<64
        self.zero=jnp.zeros((),BF)
    def roll(self,v): return pltpu.roll(v.astype(F32),64,1).astype(BF)
    def out(self,lat,name,index,pair):
        s=self.s
        src=s[name].at[pl.ds(self.base,2)] if pair else s[name]
        dst=self.outs[index].at[:,lat] if pair else self.outs[index].at[lat]
        return pltpu.make_async_copy(src,dst,s["out_sem"].at[index])
    def emit(self,lat,name,index,pair=False): self.out(lat,name,index,pair).start()
    def clear(self,lat,name,index,pair=False):
        @pl.when(lat>0)
        def _(): self.out(lat-1,name,index,pair).wait()
    def last(self):
        for name,index,pair in (("a",0,False),("m",1,False),("dy",2,False),("dz",3,False),("o",4,True),("dq",5,True),("du",6,True),("g",7,True)):
            self.out(3,name,index,pair).wait()
    def start(self):
        s=self.s
        self.small[...]=jnp.zeros_like(self.small); self.hb[...]=jnp.zeros_like(self.hb)
        s["dbq"][...]=jnp.zeros_like(s["dbq"]); s["db1"][...]=jnp.zeros_like(s["db1"])
        for i in range(GRID):
            s["pe"][16*i:16*i+16,0:384]=jnp.broadcast_to(self.pe[i:i+1,:],(16,384))
            s["pe"][16*i:16*i+16,384:768]=self.pe[...]
    def mixed(self,lat):
        place=self.first+lat
        t=self.times[place]
        clean=self.clean[place].astype(F32); noise=self.noise[place].astype(F32)
        return t,clean,noise,(t*clean+(1.0-t)*noise).astype(BF)
    def mod(self,lat,i): return self.mod_ref[lat,i:i+1,:]
    def embed(self,lat):
        s=self.s
        mixed=self.mixed(lat)[3]
        h0=tdot(mixed,self.emb[0:16].astype(BF))+self.emb[32:33]+s["pe"][...]
        s["h"][lat]=h0
        xh,r=ln(h0)
        s["xh1"][lat]=xh; s["r1"][lat]=r
        self.clear(lat,"a",0)
        s["a"][...]=(xh*(1.0+self.mod(lat,1))+self.mod(lat,0)).astype(BF)
        self.emit(lat,"a",0)
        self.clear(lat,"o",4,True)
    def softmax(self,v,lat,idx):
        v=v*SCALE
        e=jnp.exp(v-jnp.max(v,axis=-1,keepdims=True))
        p=(e/jnp.sum(e,axis=-1,keepdims=True)).astype(BF)
        self.s["p"][lat,idx]=p
        return p
    def attend(self,lat,j):
        s=self.s; lo=self.lo; zero=self.zero; wall=s["wall"]
        full=(dot(s["a"][...],wall[0,j])[:,0:640]+self.ball[j,:,0:640]).astype(BF)
        s["qkv"][lat,j]=full
        b0,b1,b2,b3,b4=[full[:,128*i:128*i+128] for i in range(5)]
        p0=self.softmax(ndot(jnp.where(lo,b0,zero),self.roll(b0)),lat,3*j)
        p1=self.softmax(ndot(jnp.where(lo,zero,b1),self.roll(b2)),lat,3*j+1)
        p2=self.softmax(ndot(jnp.where(lo,b3,zero),self.roll(b3)),lat,3*j+2)
        o0=pltpu.roll(dot(p0,b1),64,1)
        s["o"][j,:,0:128]=jnp.where(lo,0.0,o0).astype(BF)
        s["o"][j,:,128:256]=pltpu.roll(jnp.where(lo,dot(p2,b4),dot(p1,b2)),64,1).astype(BF)
    def project(self,lat):
        s=self.s
        self.emit(lat,"o",4,True)
        for n in range(3):
            cols=slice(256*n,256*n+256)
            y=sum(ndot(s["o"][j],s["wall"][0,j,cols,512:768]) for j in range(4))+self.emb[33:34,cols]
            s["y"][lat,:,cols]=y
            s["h"][lat,:,cols]+=self.mod(lat,2)[:,cols]*y
    def attn_fwd(self,lat):
        self.service(lat,0)
        self.embed(lat)
        self.service(lat,1)
        for j in range(2): self.attend(lat,j)
        self.service(lat,2)
        for j in range(2,4): self.attend(lat,j)
        self.service(lat,3)
        self.project(lat)
    def fc_in(self,lat):
        s=self.s
        xh,r=ln(s["h"][lat])
        s["xh2"][...]=xh; s["r2"][...]=r
        self.clear(lat,"m",1)
        s["m"][...]=(xh*(1.0+self.mod(lat,4))+self.mod(lat,3)).astype(BF)
        self.emit(lat,"m",1)
        self.clear(lat,"g",7,True)
    def fc_one(self,lat,j):
        s=self.s
        u=dot(s["m"][...],s["wall"][1,j])+self.ball[j,:,768:1536]
        uu=u*u
        th=jnp.tanh(u*(GELU_C+(GELU_C*0.044715)*uu))
        half=0.5+0.5*th
        s["g"][j]=(u*half).astype(BF)
        s["slope"][j]=half*(1.0+(u-u*th)*(GELU_C+(3.0*0.044715*GELU_C)*uu))
    def fc_fwd(self,lat):
        s=self.s
        self.fc_in(lat)
        u=UNROLL["ff"]
        @pl.loop(0,4//u)
        def _(i):
            for k in range(u): self.fc_one(lat,i*u+k)
        self.emit(lat,"g",7,True)
        for n in range(3):
            cols=slice(256*n,256*n+256)
            z=sum(ndot(s["g"][j],s["wall"][2,j,cols,:]) for j in range(4))+self.emb[34:35,cols]
            s["z"][:,cols]=z
    def head(self,lat):
        s=self.s; mod=lambda i: self.mod(lat,i)
        t,clean,noise,_=self.mixed(lat)
        wh=self.emb[16:32].astype(BF)
        h2=s["h"][lat]+mod(5)*s["z"][...]
        xh,r=ln(h2)
        fi=(xh*(1.0+mod(7))+mod(6)).astype(BF)
        pred=ndot(wh,fi)+self.bh[...]
        diff=pred-(clean-noise)
        weight=1.0/(1.0-t+TIME_OFFSET)
        self.hb[0:1,1:2]+=jnp.sum(colsum(weight*diff*diff),axis=1,keepdims=True)*(1.0/self.count_all)
        dpred=2.0*weight*diff*(1.0/self.count_all)
        self.hb[:,0:1]+=jnp.sum(dpred,axis=1,keepdims=True)
        dpl=dpred.astype(BF)
        self.small[16:32]+=dot(dpl,fi)
        dfi=tdot(dpl,wh)
        self.dmod[lat,6:7]=colsum(dfi); self.dmod[lat,7:8]=colsum(dfi*xh)
        dh=ln_back(dfi,xh,r,mod(7))
        s["h"][lat]=dh
        self.dmod[lat,5:6]=colsum(dh*s["z"][...])
        dzf=dh*mod(5)
        self.small[34:35]+=colsum(dzf)
        self.clear(lat,"dz",3)
        s["dz"][...]=dzf.astype(BF)
        self.emit(lat,"dz",3)
        self.clear(lat,"du",6,True)
    def fc_back_one(self,j):
        s=self.s
        du=dot(s["dz"][...],s["wall"][2,j])*s["slope"][j]
        s["du"][j]=du.astype(BF)
        s["db1"][j]+=colsum(du)
    def fc_bwd(self,lat):
        s=self.s; mod=lambda i: self.mod(lat,i)
        u=UNROLL["fb"]
        @pl.loop(0,4//u)
        def _(i):
            for k in range(u): self.fc_back_one(i*u+k)
        self.emit(lat,"du",6,True)
        for n in range(3):
            cols=slice(256*n,256*n+256)
            s["z"][:,cols]=sum(ndot(s["du"][j],s["wall"][1,j,cols,:]) for j in range(4))
        dm=s["z"][...]
        xh=s["xh2"][...]
        self.dmod[lat,3:4]=colsum(dm); self.dmod[lat,4:5]=colsum(dm*xh)
        dh=s["h"][lat]+ln_back(dm,xh,s["r2"][...],mod(4))
        s["h"][lat]=dh
        self.dmod[lat,2:3]=colsum(dh*s["y"][lat])
        dyf=dh*mod(2)
        self.small[33:34]+=colsum(dyf)
        self.clear(lat,"dy",2)
        s["dy"][...]=dyf.astype(BF)
        self.emit(lat,"dy",2)
        self.clear(lat,"dq",5,True)
    def attend_back(self,lat,j):
        s=self.s; lo=self.lo; zero=self.zero; roll=self.roll
        do=dot(s["dy"][...],s["wall"][0,j,:,512:768])
        r4=pltpu.roll(do[:,0:128],64,1).astype(BF); r5=pltpu.roll(do[:,128:256],64,1).astype(BF)
        do0=jnp.where(lo,r4,zero); do1=jnp.where(lo,zero,r5); do2=jnp.where(lo,r5,zero)
        b0,b1,b2,b3,b4=[s["qkv"][lat,j,:,128*i:128*i+128] for i in range(5)]
        def head(h,doh,v):
            p=s["p"][lat,3*j+h]
            dv=tdot(p,doh)
            dp=ndot(doh,v)
            pf=p.astype(F32)
            t=pf*dp
            ds=(t-pf*jnp.sum(t,axis=-1,keepdims=True)).astype(BF)
            return dv,ds
        dv0,ds0=head(0,do0,b1)
        dv1,ds1=head(1,do1,b2)
        dv2,ds2=head(2,do2,b4)
        rb0=roll(b0); rb3=roll(b3)
        n0=jnp.where(lo,dot(ds0,rb0),tdot(ds0,rb0))*SCALE
        n1=jnp.where(lo,dv0,dot(ds1,roll(b2))*SCALE); n2=jnp.where(lo,tdot(ds1,roll(b1))*SCALE,dv1)
        n3=jnp.where(lo,dot(ds2,rb3),tdot(ds2,rb3))*SCALE
        n4=jnp.where(lo,dv2,0.0)
        for i,v in enumerate((n0,n1,n2,n3,n4)):
            cols=slice(128*i,128*i+128)
            s["dq"][j,:,cols]=v.astype(BF)
            s["dbq"][j,:,cols]+=colsum(v)
    def attn_bwd(self,lat):
        s=self.s; mod=lambda i: self.mod(lat,i)
        u=UNROLL["ab"]
        @pl.loop(0,4//u)
        def _(i):
            for k in range(u): self.attend_back(lat,i*u+k)
        self.emit(lat,"dq",5,True)
        for n in range(3):
            cols=slice(256*n,256*n+256)
            s["z"][:,cols]=sum(ndot(s["dq"][j],s["wall"][0,j,cols,0:640]) for j in range(4))
        da=s["z"][...]
        xh=s["xh1"][lat]
        self.dmod[lat,0:1]=colsum(da); self.dmod[lat,1:2]=colsum(da*xh)
        dh=s["h"][lat]+ln_back(da,xh,s["r1"][lat],mod(1))
        self.small[32:33]+=colsum(dh)
        self.small[0:16]+=dot(self.mixed(lat)[3],dh.astype(BF))

    def run(self,ready=lambda: None):
        @pl.loop(0,4)
        def _(lat): self.attn_fwd(lat)
        ready()
        @pl.loop(0,4)
        def _(lat):
            for phase in (self.fc_fwd,self.head,self.fc_bwd,self.attn_bwd): phase(lat)
        self.last()

def block_kernel(times_ref,base_ref,clean_ref,noise_ref,mod_ref,wall_ref,pe_ref,emb_ref,bh_ref,ball_ref,*rest,count_all,names):
    outs=rest[0:8]; dmod,small,dbq,db1,hb=rest[8:13]
    s=dict(zip(names,rest[13:13+len(names)])); wsem=rest[-1]
    cp=pltpu.make_async_copy(wall_ref,s["wall"],wsem); cp.start()
    base=base_ref[0]
    b=Block(s,times_ref,clean_ref,noise_ref,mod_ref,pe_ref,emb_ref,bh_ref,ball_ref,outs,dmod,small,hb,base,0,count_all,lambda lat,pos: None)
    b.start()
    cp.wait()
    b.run()
    for k in range(2):
        dbq[k]=s["dbq"][base+k]; db1[k]=s["db1"][base+k]

def run_block(base,times,clean,noise,mod,wall,pe,emb,bh,ball,count_all):
    L=clean.shape[0]
    S=jax.ShapeDtypeStruct
    outs=[S((L,SEQ,D),BF)]*4+[S((2,L,SEQ,256),BF),S((2,L,SEQ,640),BF),S((2,L,SEQ,768),BF),S((2,L,SEQ,768),BF),
        S((L,8,D),F32),S((40,D),F32),S((2,1,640),F32),S((2,1,768),F32),S((PATCH_IN,128),F32)]
    st=block_state(); names=tuple(st)
    vm=pl.BlockSpec(memory_space=pltpu.VMEM); anys=pl.BlockSpec(memory_space=pl.ANY); sm=pl.BlockSpec(memory_space=pltpu.SMEM)
    return pl.pallas_call(functools.partial(block_kernel,count_all=count_all,names=names),
        out_shape=outs,in_specs=[sm,sm,vm,vm,vm,anys,vm,vm,vm,vm],out_specs=[anys]*8+[vm]*5,
        scratch_shapes=list(st.values())+[pltpu.SemaphoreType.DMA(())],
        compiler_params=pltpu.CompilerParams(vmem_limit_bytes=62*1024*1024),name="block")(times,base,clean,noise,mod,wall,pe,emb,bh,ball)


MESH = pl.DeviceIdType.MESH
HI = lax.Precision.HIGHEST


def hdot(a, b):
    return lax.dot_general(a, b, (((1,), (0,)), ((), ())), precision=HI, preferred_element_type=F32)


def hndot(a, b):
    return lax.dot_general(a, b, (((1,), (1,)), ((), ())), precision=HI, preferred_element_type=F32)


def htdot(a, b):
    return lax.dot_general(a, b, (((0,), (0,)), ((), ())), precision=HI, preferred_element_type=F32)


def split2(values):
    first = values.astype(BF)
    return first, (values - first.astype(F32)).astype(BF)


def split3(values):
    first, rest = values.astype(BF), values
    rest = rest - first.astype(F32)
    second = rest.astype(BF)
    return first, second, (rest - second.astype(F32)).astype(BF)


def silu_slope_k(values):
    gate = 1.0 / (1.0 + jnp.exp(-values))
    return gate * (1.0 + values * (1.0 - gate))


class Peers:
    def __init__(self, send_sem, recv_sem):
        self.w = lax.axis_index("dp")
        self.t = lax.axis_index("tensor")
        self.n = lax.axis_size("dp")
        self.tn = lax.axis_size("tensor")
        self.c = lax.rem(self.t, 2)
        self.sib = self.t + 1 - 2 * self.c
        self.send_sem, self.recv_sem = send_sem, recv_sem
        self.pending = []

    def barrier(self):
        bar = pltpu.get_barrier_semaphore()
        for i in range(1, self.n):
            pl.semaphore_signal(bar, inc=1, device_id=(lax.rem(self.w + i, self.n), self.t), device_id_type=MESH)
        for i in range(1, self.tn):
            pl.semaphore_signal(bar, inc=1, device_id=(self.w, lax.rem(self.t + i, self.tn)), device_id_type=MESH)

    def ready(self):
        pl.semaphore_wait(pltpu.get_barrier_semaphore(), self.n - 1 + self.tn - 1)

    def copy(self, src, dst, index, device):
        op = pltpu.make_async_remote_copy(
            src_ref=src,
            dst_ref=dst,
            send_sem=self.send_sem.at[index],
            recv_sem=self.recv_sem.at[index],
            device_id=device,
            device_id_type=MESH,
        )
        op.start()
        self.pending.append(op)
        return op

    def dp_push(self, src_of, dst, base):
        ops = []
        for i in range(1, self.n):
            peer = lax.rem(self.w + i, self.n)
            ops.append(self.copy(src_of(peer), dst, base + i - 1, (peer, self.t)))
        return ops

    def tensor_push(self, src, dst, base):
        ops = []
        for i in range(1, self.tn):
            ops.append(self.copy(src, dst, base + i - 1, (self.w, lax.rem(self.t + i, self.tn))))
        return ops

    def core_push(self, src, dst, index):
        return self.copy(src, dst, index, (self.w, self.sib))

    def finish(self):
        for op in self.pending:
            op.wait_send()


def wait_all(ops):
    for op in ops:
        op.wait_recv()


P_TILES = (6, 6, 6, 2, 6)
P_COUNT = 32
Q_COUNT = 40
QKV0, FC0 = 1536, 2112
COLS = 2880


def halves(block):
    high = block.astype(BF).astype(F32)
    return [high, block - high]


def fill(rows, total):
    used = sum(row.shape[0] for row in rows)
    return jnp.concatenate(rows + [jnp.zeros((total - used, rows[0].shape[1]), F32)], axis=0)


AUX = ("cs", "ct", "t1", "a1", "tf", "hot", "wto", "dmod", "small", "dbq", "db1", "hb")


def step_kernel(
    col_ref, row_ref, pk_ref, smt_ref, bias_ref, times_ref, clean_ref, noise_ref, pe_ref, bh_ref, *rest, names, count_all
):
    outs, aux_out, rest = rest[:8], rest[8 : 8 + len(AUX)], rest[8 + len(AUX) :]
    s = dict(zip(names, rest[: len(names)]))
    aux, rest = dict(zip(AUX, rest[len(names) :])), rest[len(names) + len(AUX) :]
    mod_ref, emb_ref, ball_ref = rest[:3]
    pack_ref, bhs, bmod_ref, pkl, ems, eml, a1s, a1l, css, csl, mps, mpl_, mos, mol, bal, local_sem, wsend, wrecv, send_sem, recv_sem = rest[3:]
    wall_ref = s["wall"]
    cs_ref, ct_ref, t1_ref, a1_ref, tf_ref, hot_ref, wto_ref = [aux[name] for name in AUX[:7]]
    net = Peers(send_sem, recv_sem)
    w, t, c, n = net.w, net.t, net.c, net.n
    share = D // n
    half = share // 2
    x, z, y = t // 2, w // 2, lax.rem(w, 2)
    net.barrier()
    wmod_ref = col_ref.at[:, 0:QKV0]
    pack_ref[0, :, 0:576] = col_ref[:, QKV0:FC0]
    pack_ref[0, :, 576:768] = row_ref[:, 0:192]
    pack_ref[1] = col_ref[:, FC0:COLS]
    pack_ref[2] = row_ref[:, 192:960]
    own = []

    def place(q, j, v):
        return wall_ref.at[q, j, pl.ds(pl.multiple_of(share * v, 32), share)]

    for q in range(3):
        op = pltpu.make_async_copy(pack_ref.at[q], place(q, t, w), local_sem.at[q])
        op.start()
        own.append(op)
    pkl[w] = pk_ref[...]
    rest = smt_ref.shape[1]
    emb = jnp.concatenate(
        [smt_ref[:, 0:16], smt_ref[:, rest - 18 : rest - 2], smt_ref[:, 16:17], smt_ref[:, rest - 2 : rest], jnp.zeros((share, 5), F32)],
        axis=1,
    )
    third = share // 3
    emb = jnp.concatenate([emb[0:third], emb[third : 2 * third], emb[2 * third : share], jnp.zeros((third, 8), F32)], axis=1)
    ems[...] = emb.astype(BF)
    eml[w] = ems[...]
    bias = bias_ref[...].astype(BF).astype(F32)
    bmod_ref[...] = bias[:, 0:QKV0]
    bal[t] = jnp.concatenate([bias[:, QKV0:FC0], jnp.zeros((1, 192), F32), bias[:, FC0:COLS]], axis=1)
    net.ready()
    pk_ops = net.dp_push(lambda peer: pk_ref, pkl.at[w], 0)
    em_ops = net.dp_push(lambda peer: ems, eml.at[w], 7)
    ba_ops = net.tensor_push(bal.at[t], bal.at[t], 14)

    zs = [z, z + 1 - 2 * lax.rem(z, 2), lax.rem(z + 2, 4), 3 - z]
    xo = 1 - x
    mine, across = 2 * x + c, 2 * xo + c
    wys = [2 * zs[k] + y for k in range(4)]
    wos = [2 * zs[k] + (1 - y) for k in range(4)]
    to_zs = [(wys[k], t) for k in range(4)]
    wy, wo, to_z = wys.__getitem__, wos.__getitem__, to_zs.__getitem__
    to_x, to_y, to_core = (w, across), (2 * z + (1 - y), t), (w, net.sib)
    sends = []

    def piece_copy(index, q, j, v, device, own_block):
        slot = place(q, j, v)
        return pltpu.make_async_remote_copy(
            src_ref=pack_ref.at[q] if own_block else slot, dst_ref=slot, send_sem=wsend.at[index],
            recv_sem=wrecv.at[q, j, v], device_id=device, device_id_type=MESH,
        )

    def send(q, j, v, device, own_block=False):
        sends.append((len(sends), q, j, v, device, own_block))
        piece_copy(*sends[-1]).start()

    def arrived(q, j, v):
        piece_copy(0, q, j, v, to_core, False).wait_recv()

    def column(q, k):
        if k == 0:
            send(q, mine, w, to_z(1), True)
            send(q, mine, w, to_z(2), True)
        else:
            arrived(q, mine, wy(k))
            if k == 2:
                send(q, mine, wy(2), to_z(1))
        send(q, mine, wy(k), to_x, k == 0)
        send(q, mine, wy(k), to_y, k == 0)
        send(q, mine, wy(k), to_core, k == 0)

    def by_y(q, k):
        return q == 0 and k % 2 == 1

    def side(q, k):
        arrived(q, across, wy(k))
        if by_y(q, k):
            send(q, across, wy(k), to_y)
        send(q, across, wy(k), to_core)
        arrived(q, mine, wo(k))
        if not by_y(q, k):
            send(q, mine, wo(k), to_x)
        send(q, mine, wo(k), to_core)

    def corner(q, k):
        arrived(q, across, wo(k))
        send(q, across, wo(k), to_core)

    first_hop, last_hop = {1: to_x}, {1: to_y}

    def level(q, k):
        return (mine, wy(k)), ((across, wy(k)) if q == 1 else (mine, wo(k)))

    def begin(q):
        send(q, mine, w, first_hop[q], True)
        send(q, mine, w, to_z(1), True)
        send(q, mine, w, to_z(2), True)
        send(q, mine, w, last_hop[q], True)
        send(q, mine, w, to_core, True)

    def second(q):
        j, v = level(q, 0)[1]
        arrived(q, j, v)
        for device in (to_z(1), to_z(2), last_hop[q], to_core):
            send(q, j, v, device)

    def along(q, k):
        for j, v in level(q, k):
            arrived(q, j, v)
            if k == 2:
                send(q, j, v, to_z(1))
            send(q, j, v, last_hop[q])
            send(q, j, v, to_core)

    def far(q, k):
        last = (mine, wo(k)) if q == 1 else (across, wy(k))
        for j, v in (last, (across, wo(k))):
            arrived(q, j, v)
            send(q, j, v, to_core)

    def chain0():
        wait_all(pk_ops)
        feats = pkl[...].reshape(8 * n, 384)
        tf_ref[...] = feats[:, 0:FREQ]
        hot_ref[...] = feats[:, FREQ:384]
        small = smt_ref[...].astype(BF).astype(F32)
        t1 = hndot(small[:, 17:273], tf_ref[...]) + small[:, 273:274]
        t1_ref[...] = t1
        act = t1 / (1.0 + jnp.exp(-t1))
        a1s[...] = jnp.concatenate([act[0:half], act[half:share]], axis=1)
        a1l[w] = a1s[...]
        return net.dp_push(lambda peer: a1s, a1l.at[w], 17)

    def chain1(ops):
        wait_all(ops)
        for k in range(n):
            a1_ref[share * k : share * k + half] = a1l[k][:, 0:64]
            a1_ref[share * k + half : share * k + share] = a1l[k][:, 64:128]
        small = smt_ref[...].astype(BF).astype(F32)
        cond = hdot(small[:, 274:1042], a1_ref[...]) + small[:, 1042:1043]
        cond = cond + hndot(small[:, 1043:1075], hot_ref[:, 0:CLASSES])
        ct_ref[...] = cond
        act = cond / (1.0 + jnp.exp(-cond))
        css[...] = jnp.concatenate([act[0:half], act[half:share]], axis=1)
        csl[w] = css[...]
        cs_ops = net.dp_push(lambda peer: css, csl.at[w], 24)
        parts = [tdot(piece, wmod_ref[...]) for piece in split3(act)]
        mps[...] = (parts[0] + parts[1] + parts[2]).reshape(n, 8, QKV0)
        mpl_[w] = mps[w]
        return cs_ops, net.dp_push(lambda peer: mps.at[peer], mpl_.at[w], 31)

    def chain2(ops):
        wait_all(ops)
        total = mpl_[0]
        for k in range(1, n):
            total = total + mpl_[k]
        mos[...] = total + bmod_ref[...]
        mol[t] = mos[...]
        return net.tensor_push(mos, mol.at[t], 38)

    def chain3(ops):
        wait_all(em_ops)
        rows = []
        for k in range(n):
            piece = eml[k].astype(F32)
            rows += [piece[:, 40 * i : 40 * i + 40] for i in range(3)]
        rows = jnp.concatenate(rows, axis=0)
        emb_ref[...] = jnp.concatenate([rows, jnp.zeros((D, 88), F32)], axis=1).T[0:40]
        wait_all(ba_ops)
        ball_ref[...] = bal[...]
        wait_all(ops)
        for lat in range(4):
            for j in range(4):
                for piece in range(2):
                    mod_ref[lat, 2 * j + piece : 2 * j + piece + 1, :] = mol[j, pl.ds(4 * c + lat, 1), D * piece : D * piece + D]

    column(0, 0)
    ops = chain0()
    column(0, 1)
    side(0, 0)
    column(0, 2)
    cs_ops, ops = chain1(ops)
    side(0, 1)
    corner(0, 0)
    column(0, 3)
    side(0, 2)
    begin(1)
    column(2, 0)
    corner(0, 1)
    side(0, 3)
    ops = chain2(ops)
    corner(0, 2)
    corner(0, 3)
    second(1)
    column(2, 1)
    chain3(ops)

    def other_core(q):
        for j in (2 * x + 1 - c, 2 * xo + 1 - c):
            for v in range(n):
                arrived(q, j, v)

    other_core(0)
    own[0].wait()
    plan = (
        (along, 1, 1), (side, 2, 0), (column, 2, 2), (corner, 2, 0), (along, 1, 2), (side, 2, 1), (column, 2, 3), (corner, 2, 1),
        None, (side, 2, 2), None, (along, 1, 3), (side, 2, 3), (corner, 2, 2),
    )
    slots = {i: [functools.partial(*item)] for i, item in enumerate(plan) if item}
    rest = [functools.partial(far, 1, k) for k in range(4)] + [functools.partial(corner, 2, 3)]

    def service(lat, pos):
        for index, todo in slots.items():
            if index % 4 == pos:
                for item in todo:
                    pl.when(lat == index // 4)(item)

    def rows_out():
        wait_all(cs_ops)
        rows = []
        for k in range(n):
            rows += [csl[k][:, 0:64], csl[k][:, 64:128]]
        rows = jnp.concatenate(rows, axis=0)
        a1s_all = jnp.concatenate([rows, jnp.zeros((D, 64), F32)], axis=1).T
        cs_all = a1s_all[0:64].reshape(n, 8, D)
        picked = jnp.zeros((8, D), F32)
        for k in range(n):
            picked = jnp.where(w == k, cs_all[k], picked)
        cs_ref[...] = picked
        wto_ref[...] = smt_ref[:, 274:1042].astype(BF)

    def ready():
        for item in rest:
            item()
        for q in (1, 2):
            other_core(q)
            own[q].wait()

    block = Block(
        s, times_ref, clean_ref, noise_ref, mod_ref, pe_ref, emb_ref, bhs, ball_ref, outs,
        aux["dmod"], aux["small"], aux["hb"], 2 * x, 4 * c, count_all, service,
    )
    bhs[...] = tdot(bh_ref[...].astype(BF), jnp.ones((1, SEQ), BF))
    block.start()
    block.run(ready)
    rows_out()
    for k in range(2):
        aux["dbq"][k] = s["dbq"][2 * x + k]
        aux["db1"][k] = s["db1"][2 * x + k]
    copies = [pltpu.make_async_copy(aux[name], aux_out[i], local_sem.at[3 + i]) for i, name in enumerate(AUX)]
    for op in copies:
        op.start()
    for record in sends:
        piece_copy(*record).wait_send()
    net.finish()
    for op in copies:
        op.wait()


def run_step(col, row, pk, smt, bias, times, clean, noise, pe, bh, n, count_all):
    S = jax.ShapeDtypeStruct
    V = pltpu.VMEM
    DMA = pltpu.SemaphoreType.DMA
    share = D // n
    lat = 8 * n
    half = 4
    any_spec = pl.BlockSpec(memory_space=pl.ANY)
    vm = pl.BlockSpec(memory_space=pltpu.VMEM)
    aux = [
        ((8, D), F32), ((share, lat), F32), ((share, lat), F32), ((D, lat), F32), ((lat, FREQ), F32), ((lat, 128), F32), ((share, D), BF),
        ((half, 8, D), F32), ((40, D), F32), ((2, 1, 640), F32), ((2, 1, D), F32), ((PATCH_IN, 128), F32),
    ]
    outs = [S((half, SEQ, D), BF)] * 4 + [S((2, half, SEQ, width), BF) for width in (256, 640, D, D)]
    outs += [S(*a) for a in aux]
    state = block_state()
    scratch = list(state.values()) + [V(*a) for a in aux] + [
        V((half, 8, D), F32), V((40, D), F32), V((4, 1, QKV0), F32),
        V((3, share, D), BF), V((PATCH_IN, SEQ), F32), V((1, QKV0), F32),
        V((n, 8, 384), F32), V((share // 3, 128), BF), V((n, share // 3, 128), BF),
        V((share // 2, 128), F32), V((n, share // 2, 128), F32), V((share // 2, 128), F32), V((n, share // 2, 128), F32),
        V((n, 8, QKV0), F32), V((n, 8, QKV0), F32), V((8, QKV0), F32), V((4, 8, QKV0), F32), V((4, 1, QKV0), F32),
        DMA((3 + len(AUX),)), DMA((120,)), DMA((3, 4, n)), DMA((41,)), DMA((41,)),
    ]
    return pl.pallas_call(
        functools.partial(step_kernel, names=tuple(state), count_all=count_all),
        out_shape=outs,
        in_specs=[vm] * 5 + [pl.BlockSpec(memory_space=pltpu.SMEM)] + [vm] * 4,
        out_specs=[any_spec] * len(outs),
        scratch_shapes=scratch,
        compiler_params=pltpu.CompilerParams(collective_id=0, has_side_effects=True, vmem_limit_bytes=62 * 1024 * 1024),
        name="step",
    )(col, row, pk, smt, bias, times, clean, noise, pe, bh)


def gram_schmidt(block):
    rows = lax.broadcasted_iota(jnp.int32, (8, 1), 0)
    for index in range(8):
        row = block[index : index + 1]
        row = row * lax.rsqrt(jnp.sum(row * row, axis=-1, keepdims=True) + TINY)
        inner = jnp.sum(block * row, axis=-1, keepdims=True)
        inner = jnp.where(rows > index, inner, 0.0)
        block = jnp.where(rows == index, row, block - inner * row)
    return block


def grad_kernel(
    a_ref, m_ref, dy_ref, dz_ref, o_ref, dq_ref, du_ref, g_ref, cerr_ref, rerr_ref,
    dmod_ref, small_ref, dbq_ref, db1_ref, hb_ref, right_ref, cs_ref, ct_ref, t1_ref, a1_ref, tf_ref, hot_ref, wmod_ref, wto_ref,
    mcol_ref, mrow_ref, left_out, rightn_out, pst_out, psr_out, pc_out, qst_out, qsn_out, qrs_out, gb_out, gh_out, gsm_out,
    mc, mr, sc, sr, rc, rr, av, mv, dyv, dzv, ov, qv, uv, gv,
    left_ref, rightn_ref, pst_ref, psr_ref, pc_ref, qst_ref, qsn_ref, qrs_ref, gb_ref, gh_ref, gsm_ref,
    dmo, smo, dbo, dbo1, hbo, dm8, dma, dsc, dss, dts, dtl, tks, tkl, px, pland, py, qx, qland, qy,
    load_sem, out_sem, send_sem, recv_sem,
):
    net = Peers(send_sem, recv_sem)
    outs = []

    def emit(*pairs):
        for src, dst in pairs:
            op = pltpu.make_async_copy(src, dst, out_sem.at[len(outs)])
            op.start()
            outs.append(op)

    w, t, c = net.w, net.t, net.c
    n = net.n
    share = D // n
    loads = {}

    def load(name, src, dst, index):
        op = pltpu.make_async_copy(src, dst, load_sem.at[index])
        op.start()
        loads[name] = op

    net.barrier()
    load("q", dq_ref, qv, 9)
    load("a", a_ref, av, 1)
    load("u", du_ref, uv, 0)
    load("m", m_ref, mv, 2)
    def chunk(i, size=256):
        return pl.ds(pl.multiple_of(i * size, size), size)

    def after(i, first):
        return pl.ds(pl.multiple_of(first + 256 * i, 64), 256)

    for name in ("q", "a"):
        loads[name].wait()
    col_ops, row_ops = [], []
    load("g", g_ref, gv, 3)
    load("dz", dz_ref, dzv, 4)
    sc[0:256] = tdot(qv[1 - c, :, 0:256], av[...])
    sc[256:576] = tdot(qv[1 - c, :, 256:640], av[...])[0:320]
    net.ready()
    side = [
        net.core_push(dmod_ref, dmo, 0),
        net.core_push(small_ref, smo, 1),
        net.core_push(dbq_ref.at[1 - c], dbo, 2),
        net.core_push(db1_ref.at[1 - c], dbo1, 9),
        net.core_push(hb_ref, hbo, 10),
    ]

    col_ops.append(net.core_push(sc.at[0:576], rc.at[0:576], 3))
    for name in ("u", "m"):
        loads[name].wait()
    load("o", o_ref, ov, 5)
    load("dy", dy_ref, dyv, 6)
    load("ce", cerr_ref, mc, 7)

    @pl.loop(0, 3)
    def _(i):
        sc[after(i, 576), :] = tdot(uv[1 - c, :, chunk(i)], mv[...])

    col_ops.append(net.core_push(sc.at[576:1344], rc.at[576:1344], 4))
    wait_all(side)
    for lat in range(4):
        for piece in range(2):
            span = slice(D * piece, D * piece + D)
            dm8[pl.ds(4 * c + lat, 1), span] = dmod_ref[lat, pl.ds(2 * t + piece, 1), :]
            dm8[pl.ds(4 * (1 - c) + lat, 1), span] = dmo[lat, pl.ds(2 * t + piece, 1), :]
    dma[w] = dm8[...]
    dm_ops = net.dp_push(lambda peer: dm8, dma.at[w], 16)
    total = small_ref[...] + smo[...]
    for k in range(n):
        tks[k, :, 0:share] = total[:, share * k : share * k + share]
    tkl[w] = tks[w]
    tok_ops = net.dp_push(lambda peer: tks.at[peer], tkl.at[w], 24)
    for name in ("g", "dz", "o", "dy"):
        loads[name].wait()

    @pl.loop(0, 3)
    def _(i):
        sr[after(i, 192), :] = tdot(gv[1 - c, :, chunk(i)], dzv[...])

    sr[0:192, :] = tdot(ov[1 - c], dyv[...])[64:256]
    row_ops.append(net.core_push(sr, rr, 6))
    load("re", rerr_ref, mr, 8)
    loads["ce"].wait()
    dms = split3(dm8[...])
    cs = split3(cs_ref[...])
    left_side = jnp.concatenate([dms[0], dms[1], dms[0], dms[2], dms[1], dms[0]], axis=0)
    right_side = jnp.concatenate([cs[0], cs[0], cs[1], cs[0], cs[1], cs[2]], axis=0)
    for i in range(6):
        mc[256 * i : 256 * i + 256, :] += tdot(left_side[:, 256 * i : 256 * i + 256], right_side)
    wait_all(col_ops)
    mc[QKV0 : QKV0 + 256] += tdot(qv[c, :, 0:256], av[...]) + rc[0:256]
    mc[QKV0 + 256 : FC0] += tdot(qv[c, :, 256:640], av[...])[0:320] + rc[256:576]

    @pl.loop(0, 3)
    def _(i):
        mc[after(i, FC0), :] += tdot(uv[c, :, chunk(i)], mv[...]) + rc[after(i, 576), :]

    out_col = pltpu.make_async_copy(mc, mcol_ref, load_sem.at[0])
    out_col.start()
    loads["re"].wait()
    wait_all(row_ops)

    @pl.loop(0, 3)
    def _(i):
        mr[after(i, 192), :] += tdot(gv[c, :, chunk(i)], dzv[...]) + rr[after(i, 192), :]

    mr[0:192, :] += tdot(ov[c], dyv[...])[64:256] + rr[0:192, :]
    out_row = pltpu.make_async_copy(mr, mrow_ref, load_sem.at[1])
    out_row.start()
    wait_all(dm_ops)
    dmx = dma[...].reshape(8 * n, QKV0)
    part = sum(ndot(wmod_ref[:, 0:QKV0], piece) for piece in split3(dmx))
    dss[...] = part
    dsc[t] = part
    ds_ops = net.tensor_push(dss, dsc.at[t], 32)
    right = right_ref[...]

    def left_part(first, last):
        sides = jnp.concatenate(halves(right[:, first:last]), axis=0).astype(BF)
        high, low = split2(mc[first:last, :])
        got = dot(sides, high) + dot(sides, low)
        return got[0:8] + got[8:16]

    for k, spans in enumerate((((0, 512), (512, 1024), (1024, QKV0)), ((QKV0, FC0),), ((FC0, FC0 + 384), (FC0 + 384, COLS)))):
        got = sum(left_part(*span) for span in spans)
        for i in range(6):
            px[6 * k + i] = got[:, 128 * i : 128 * i + 128]
    row_side = fill(halves(right[:, COLS : COLS + D]) + halves(right[:, COLS + D : COLS + 2 * D]), 128).T.astype(BF)

    def row_chunk(values):
        high, low = split2(values)
        return dot(high, row_side) + dot(low, row_side)

    got = jnp.concatenate([row_chunk(mr[0:192, :]), jnp.zeros((64, 128), F32)], axis=0).T
    for i in range(2):
        px[18 + i] = got[0:8, 128 * i : 128 * i + 128] + got[8:16, 128 * i : 128 * i + 128]
    for i in range(3):
        got = row_chunk(mr[192 + 256 * i : 448 + 256 * i, :]).T
        got = got[16:24] + got[24:32]
        px[20 + 2 * i] = got[:, 0:128]
        px[21 + 2 * i] = got[:, 128:256]
    bias = jnp.concatenate(
        [colsum(dm8[...]), (dbq_ref[c] + dbo[...])[:, 0:576], db1_ref[c] + dbo1[...], jnp.zeros((1, 192), F32)], axis=1
    )
    for i in range(24):
        px[26 + i // 8, i % 8 : i % 8 + 1, :] = bias[:, 128 * i : 128 * i + 128]
    both = hb_ref[...] + hbo[...]
    px[29] = both[0:8]
    px[30] = both[8:16]
    px[31] = jnp.zeros((8, 128), F32)

    def scatter(v, land, per, base):
        own = pl.ds(w * per, per)
        land[w] = v[own]
        return net.dp_push(lambda peer: v.at[pl.ds(peer * per, per)], land.at[w], base)

    def collect(land, v, per, base, ops):
        wait_all(ops)
        own = pl.ds(w * per, per)
        v[own] = sum(land[k] for k in range(1, n)) + land[0]
        return net.dp_push(lambda peer: v.at[own], v.at[own], base)

    ops = scatter(px, pland, P_COUNT // n, 40)
    ops = collect(pland, py, P_COUNT // n, 48, ops)
    wait_all(ds_ops)
    dcond = (dsc[0] + dsc[1] + dsc[2] + dsc[3]) * silu_slope_k(ct_ref[...])
    dtime = sum(tdot(wto_ref[...], piece) for piece in split3(dcond)).reshape(n, 2, share // 2, 8 * n)
    dts[...] = jnp.concatenate([dtime[:, 0], dtime[:, 1]], axis=2)
    dtl[w] = dts[w]
    dt_ops = net.dp_push(lambda peer: dts.at[peer], dtl.at[w], 56)
    wait_all(tok_ops)
    tok = sum(tkl[k] for k in range(1, n)) + tkl[0]
    tok = jnp.concatenate([tok, jnp.zeros((88, 128), F32)], axis=0).T[0:share]
    gsm_ref[:, 0:16] = tok[:, 0:16]
    gsm_ref[:, 16:17] = tok[:, 32:33]
    gsm_ref[:, 1075:1091] = tok[:, 16:32]
    gsm_ref[:, 1091:1093] = tok[:, 33:35]
    wait_all(ops)
    base = 0
    bases = []
    for index, count in enumerate(P_TILES):
        bases.append(gram_schmidt(jnp.concatenate([py[base + k] for k in range(count)], axis=1)))
        base += count
    offset = 0
    for block, width in zip(bases, (D, D, D, 192, D)):
        left_ref[:, offset : offset + width] = block[:, 0:width]
        offset += width
    gb_ref[...] = jnp.concatenate([py[26 + i // 8, i % 8 : i % 8 + 1, :] for i in range(23)], axis=1)[:, 0:COLS]
    head = jnp.concatenate([py[29], py[30], jnp.zeros((112, 128), F32)], axis=0).T
    gh_ref[...] = head[0:8]
    emit((left_ref, left_out), (gb_ref, gb_out), (gh_ref, gh_out))

    col_side = fill(halves(bases[0]) + halves(bases[1]) + halves(bases[2]), 128).T.astype(BF)

    def col_chunk(values):
        high, low = split2(values)
        return dot(high, col_side) + dot(low, col_side)

    def put(first, rows, k, tile):
        got = col_chunk(mc[first : first + rows, :])
        if rows % 128:
            got = jnp.concatenate([got, jnp.zeros((128 - rows % 128, 128), F32)], axis=0)
        got = got.T
        got = got[16 * k : 16 * k + 8] + got[16 * k + 8 : 16 * k + 16]
        for i in range(got.shape[1] // 128):
            qx[tile + i] = got[:, 128 * i : 128 * i + 128]

    for i in range(6):
        put(256 * i, 256, 0, 2 * i)
    put(QKV0, 256, 1, 12)
    put(QKV0 + 256, 320, 1, 14)
    for i in range(3):
        put(FC0 + 256 * i, 256, 2, 17 + 2 * i)
    for k, (rows, block) in enumerate(((slice(0, 192), bases[3][:, 0:192]), (slice(192, 960), bases[4]))):
        left = jnp.concatenate(halves(block), axis=0).astype(BF)
        high, low = split2(mr[rows, :])
        got = dot(left, high) + dot(left, low)
        got = got[0:8] + got[8:16]
        for i in range(6):
            qx[23 + 6 * k + i] = got[:, 128 * i : 128 * i + 128]
    for i in range(35, Q_COUNT):
        qx[i] = jnp.zeros((8, 128), F32)
    ops = scatter(qx, qland, Q_COUNT // n, 64)
    gsm_ref[:, 274:1042] = hndot(dcond, a1_ref[...])
    gsm_ref[:, 1042:1043] = jnp.sum(dcond, axis=1, keepdims=True)
    gsm_ref[:, 1043:1075] = hdot(dcond, hot_ref[...])[:, 0:CLASSES]
    wait_all(dt_ops)
    dtime = sum(dtl[k] for k in range(1, n)) + dtl[0]
    dtime = jnp.concatenate([dtime[:, 0:64], dtime[:, 64:128]], axis=0) * silu_slope_k(t1_ref[...])
    gsm_ref[:, 17:273] = hdot(dtime, tf_ref[...])
    gsm_ref[:, 273:274] = jnp.sum(dtime, axis=1, keepdims=True)

    def left_rows(blocks):
        rows = []
        for block in blocks:
            high, low = halves(block)
            rows += [high, low, high]
        return rows

    def right_rows(blocks):
        rows = []
        for block in blocks:
            high, low = halves(block)
            rows += [high, high, low]
        return rows

    pst_ref[...] = fill(left_rows(bases[:3]), 128).astype(BF)
    proj = jnp.concatenate([bases[3][:, 0:192], jnp.zeros((8, D), F32)], axis=1)
    fc = jnp.concatenate([jnp.zeros((8, 192), F32), bases[4]], axis=1)
    row_stack = fill(left_rows([proj, fc]), 128)
    pc_ref[...] = row_stack.astype(BF)
    row_stack = jnp.concatenate([row_stack, jnp.zeros((128, 64), F32)], axis=1)
    psr_ref[...] = row_stack.T[0:960].astype(BF)
    emit((pst_ref, pst_out), (pc_ref, pc_out), (psr_ref, psr_out), (gsm_ref, gsm_out))
    ops = collect(qland, qy, Q_COUNT // n, 72, ops)
    wait_all(ops)
    qkv = jnp.concatenate([qy[12 + i] for i in range(5)], axis=1)[:, 0:576]
    pieces = [jnp.concatenate([qy[i] for i in range(12)], axis=1), qkv, jnp.concatenate([qy[17 + i] for i in range(6)], axis=1)]
    pad = jnp.zeros((8, 64), F32)
    qc = jnp.concatenate(pieces + [pad], axis=1)
    span = lax.broadcasted_iota(jnp.int32, (8, 2944), 1)
    cuts = [
        jnp.where((span >= first) & (span < last), qc, 0.0) for first, last in ((0, QKV0), (QKV0, FC0), (FC0, COLS))
    ]
    stack = fill(right_rows(cuts), 128)
    qsn_ref[...] = stack.astype(BF)
    qst_ref[...] = stack.T[0:COLS].astype(BF)
    qr = [jnp.concatenate([qy[23 + 6 * k + i] for i in range(6)], axis=1) for k in range(2)]
    qrs_ref[...] = fill(right_rows(qr), 128).astype(BF)
    rightn_ref[:, 0:COLS] = qc[:, 0:COLS]
    rightn_ref[:, COLS : COLS + D] = qr[0]
    rightn_ref[:, COLS + D : COLS + 2 * D] = qr[1]
    emit((qst_ref, qst_out), (qsn_ref, qsn_out), (qrs_ref, qrs_out), (rightn_ref, rightn_out))
    net.finish()
    for op in outs:
        op.wait()
    out_col.wait()
    out_row.wait()


def run_grad(operands, n):
    S = jax.ShapeDtypeStruct
    V = pltpu.VMEM
    rows = operands[0].shape[0]
    lat = 8 * n
    share = D // n
    any_spec = pl.BlockSpec(memory_space=pl.ANY)
    vm = pl.BlockSpec(memory_space=pltpu.VMEM)
    outs = [
        S((COLS, D), F32), S((960, D), F32), S((8, 3264), F32), S((8, 4416), F32),
        S((128, D), BF), S((960, 128), BF), S((128, 960), BF), S((COLS, 128), BF), S((128, 2944), BF), S((128, D), BF),
        S((1, COLS), F32), S((8, 128), F32), S((share, 1093), F32),
    ]
    scratch = [
        V((COLS, D), F32), V((960, D), F32), V((1344, D), F32), V((960, D), F32), V((1344, D), F32), V((960, D), F32),
        V((rows, D), BF), V((rows, D), BF), V((rows, D), BF), V((rows, D), BF),
        V((2, rows, 256), BF), V((2, rows, 640), BF), V((2, rows, D), BF), V((2, rows, D), BF),
        *[V(o.shape, o.dtype) for o in outs[2:]],
        V((4, 8, D), F32), V((40, D), F32), V((1, 640), F32), V((1, D), F32), V((16, 128), F32),
        V((8, QKV0), F32), V((n, 8, QKV0), F32),
        V((4, share, lat), F32), V((share, lat), F32), V((n, share // 2, 128), F32), V((n, share // 2, 128), F32),
        V((n, 40, 128), F32), V((n, 40, 128), F32),
        V((P_COUNT, 8, 128), F32), V((n, P_COUNT // n, 8, 128), F32), V((P_COUNT, 8, 128), F32),
        V((Q_COUNT, 8, 128), F32), V((n, Q_COUNT // n, 8, 128), F32), V((Q_COUNT, 8, 128), F32),
        pltpu.SemaphoreType.DMA((10,)), pltpu.SemaphoreType.DMA((11,)), pltpu.SemaphoreType.DMA((80,)), pltpu.SemaphoreType.DMA((80,)),
    ]
    return pl.pallas_call(
        grad_kernel,
        out_shape=outs,
        in_specs=[any_spec] * 10 + [vm] * 14,
        out_specs=[any_spec] * 13,
        scratch_shapes=scratch,
        compiler_params=pltpu.CompilerParams(collective_id=1, has_side_effects=True, vmem_limit_bytes=60 * 1024 * 1024),
        name="grad",
    )(*operands)


APPLY_IN = (
    "mcol", "mrow", "qst", "psr", "pst", "pc", "qsn", "qrs", "left", "right", "gs", "gb", "gh",
    "cw", "cm", "rw", "rm", "sw", "sm", "bw", "bm", "hw", "hm",
)
APPLY_OUT = ("mcol", "mrow", "cw", "cm", "rw", "rm", "sw", "sm", "bw", "bm", "hw", "hm", "left", "right", "loss")
CUTS = 6


def apply_kernel(w_ref, *refs, n):
    ins = dict(zip(APPLY_IN, refs))
    outs = dict(zip(APPLY_OUT, refs[len(APPLY_IN) :]))
    rest = refs[len(APPLY_IN) + len(APPLY_OUT) :]
    held = [name for name in APPLY_IN if name not in ("left", "right")]
    s = dict(zip(held, rest))
    loss_s, hat_s, sem_in, sem_out = rest[len(held) :]
    share = D // n
    cut = {"mcol": [slice(480 * i, 480 * i + 480) for i in range(CUTS)], "mrow": [slice(480 * i, 480 * i + 480) for i in range(2)]}
    started, finished = {}, []

    def load(name, part=None):
        src, dst = (ins[name], s[name]) if part is None else (ins[name].at[cut[name][part]], s[name].at[cut[name][part]])
        started[name, part] = pltpu.make_async_copy(src, dst, sem_in.at[len(started)])
        started[name, part].start()

    def store(src, dst):
        op = pltpu.make_async_copy(src, dst, sem_out.at[len(finished)])
        op.start()
        finished.append(op)

    for name in ("pst", "qst", "qrs", "pc", "qsn", "psr"):
        load(name)
    for part in range(CUTS):
        load("mcol", part)
        if part == 0:
            for name in ("rw", "rm", "cw", "cm"):
                load(name)
    for part in range(2):
        load("mrow", part)
    for name in ("gs", "sw", "sm", "gb", "bw", "bm", "gh", "hw", "hm"):
        load(name)
    store(ins["left"], outs["left"])
    store(ins["right"], outs["right"])

    def ready(*names):
        for name in names:
            started[name, None].wait()

    def update(weight, moment, grad):
        s[moment][...] = DECAY * s[moment][...] + grad
        s[weight][...] = s[weight][...] - LEARN_RATE * s[moment][...]
        store(s[moment], outs[moment])
        store(s[weight], outs[weight])

    ready("pst", "qst", "qrs", "pc", "qsn")
    place = lax.broadcasted_iota(jnp.int32, (D, 128), 0) == w_ref[0] * share + lax.broadcasted_iota(jnp.int32, (D, 128), 1)
    pick = jnp.where(place, 1.0, 0.0).astype(BF)
    hat_s[...] = tdot(dot(s["pst"][...], pick).astype(BF), s["qsn"][...])[0:share, 0:COLS]
    rows = tdot(dot(s["qrs"][...], pick).astype(BF), s["pc"][...])[0:share]

    def residue(name, part, hat):
        started[name, part].wait()
        span = cut[name][part]
        s[name][span, :] = s[name][span, :] - hat * (1.0 / n)
        store(s[name].at[span], outs[name].at[span])

    def col(part):
        residue("mcol", part, dot(s["qst"][cut["mcol"][part], :], s["pst"][...]))

    def row(part):
        residue("mrow", part, dot(s["psr"][cut["mrow"][part], :], s["qrs"][...]))

    col(0)
    ready("rw", "rm")
    update("rw", "rm", rows)
    col(1)
    ready("cw", "cm")

    @pl.loop(0, share // 8)
    def _(i):
        for r in range(8):
            k = 8 * i + r
            moment = DECAY * s["cm"][k] + hat_s[pl.ds(k, 1), :]
            s["cm"][k] = moment
            s["cw"][k] = s["cw"][k] - LEARN_RATE * moment

    store(s["cm"], outs["cm"])
    store(s["cw"], outs["cw"])
    for part in range(2, CUTS):
        col(part)
    ready("psr")
    for part in range(2):
        row(part)
    ready("gs", "sw", "sm")
    update("sw", "sm", s["gs"][...])
    ready("gb", "bw", "bm", "gh", "hw", "hm")
    update("bw", "bm", s["gb"][...])
    update("hw", "hm", s["gh"][0:1, 0:PATCH_IN])
    loss_s[...] = s["gh"][1:2, 0:1]
    store(loss_s, outs["loss"])
    for op in finished:
        op.wait()


def run_apply(w, operands, n):
    S = jax.ShapeDtypeStruct
    V = pltpu.VMEM
    shapes = {name: operand for name, operand in zip(APPLY_IN, operands)}
    outs = [S(shapes[name].shape, F32) for name in APPLY_OUT[:-1]] + [S((1, 1), F32)]
    held = [V(shapes[name].shape, shapes[name].dtype) for name in APPLY_IN if name not in ("left", "right")]
    any_spec = pl.BlockSpec(memory_space=pl.ANY)
    return pl.pallas_call(
        functools.partial(apply_kernel, n=n),
        out_shape=outs,
        in_specs=[pl.BlockSpec(memory_space=pltpu.SMEM)] + [any_spec] * len(APPLY_IN),
        out_specs=[any_spec] * len(outs),
        scratch_shapes=held + [V((1, 1), F32), V((D // n, COLS), F32), pltpu.SemaphoreType.DMA((32,)), pltpu.SemaphoreType.DMA((32,))],
        compiler_params=pltpu.CompilerParams(vmem_limit_bytes=62 * 1024 * 1024),
        name="apply",
    )(w, *operands)


def position_table():
    quarter = D // 4
    omega = 10000.0 ** (-np.arange(quarter) / quarter)
    place = np.arange(GRID)[:, None] * omega[None, :]
    return jnp.asarray(np.concatenate([np.sin(place), np.cos(place)], axis=1), F32)


def time_features(times):
    half = FREQ // 2
    freqs = jnp.exp(-math.log(10000.0) * jnp.arange(half, dtype=jnp.float32) / half)
    angles = 1000.0 * times[:, None] * freqs[None, :]
    return jnp.concatenate([jnp.cos(angles), jnp.sin(angles)], axis=1)


def small_starts():
    counts = [PATCH_IN, 1, FREQ, 1, D, 1, CLASSES, PATCH_IN, 1, 1]
    starts = [0]
    for amount in counts:
        starts.append(starts[-1] + amount)
    return starts


def cut_parts(array, widths, axis):
    pieces = []
    offset = 0
    for width in widths:
        pieces.append(lax.slice_in_dim(array, offset, offset + width, axis=axis))
        offset = offset + width
    return pieces


def ortho_kernel(x_ref, o_ref):
    count = x_ref.shape[0]
    rows = [x_ref[index] for index in range(count)]
    for index in range(count):
        vector = rows[index]
        vector = vector * lax.rsqrt(jnp.sum(vector * vector, axis=-1, keepdims=True) + TINY)
        o_ref[index] = vector
        for later in range(index + 1, count):
            rows[later] = rows[later] - jnp.sum(rows[later] * vector, axis=-1, keepdims=True) * vector


def orthonormal_all(parts):
    stacked = jnp.stack([jnp.pad(part, ((0, 0), (0, D - part.shape[1]))) for part in parts], axis=1)
    stacked = jnp.pad(stacked, ((0, 0), (0, 8 - len(parts)), (0, 0)))
    out = pl.pallas_call(ortho_kernel, out_shape=jax.ShapeDtypeStruct(stacked.shape, F32), name="ortho")(stacked)
    return [out[:, index, : part.shape[1]] for index, part in enumerate(parts)]


def rounded(values):
    return lax.optimization_barrier(values.astype(BF)).astype(F32)


def silu_slope(values):
    gate = jax.nn.sigmoid(values)
    return gate * (1.0 + values * (1.0 - gate))


def shards_general(
    clean_latents,
    noise_draw,
    timesteps,
    labels,
    col_weights,
    col_moments,
    col_errors,
    row_weights,
    row_moments,
    row_errors,
    bias_weights,
    bias_moments,
    small_weights,
    small_moments,
    head_bias,
    head_moments,
    right_factors,
):
    tensor_size = lax.axis_size("tensor")
    data_size = lax.axis_size("dp")
    tensor_rank = lax.axis_index("tensor")
    data_rank = lax.axis_index("dp")
    batch = clean_latents.shape[0]
    half = batch // 2
    share = D // data_size
    mod_width = 8 * D // tensor_size
    qkv_width = 3 * D // tensor_size
    ffn_width = FF // tensor_size
    proj_rows = D // tensor_size
    count_all = data_size * batch * SEQ * PATCH_IN
    col_widths = [mod_width, qkv_width, ffn_width]
    core = lax.rem(tensor_rank, 2)
    base = tensor_rank - core
    pair = [(index, index + 1 - 2 * (index % 2)) for index in range(tensor_size)]

    def swap(values):
        return lax.ppermute(values, "tensor", pair)

    col_low = col_weights[:, 0, :].astype(BF)
    row_low = row_weights[0].astype(BF).T
    packed = jnp.concatenate(
        [
            col_low[:, mod_width : mod_width + qkv_width],
            row_low[:, :proj_rows],
            col_low[:, mod_width + qkv_width :],
            row_low[:, proj_rows:],
        ],
        axis=1,
    )
    wall = lax.all_gather(lax.all_gather(packed, "dp", axis=0, tiled=True), "tensor", axis=0)
    wall = jnp.stack([wall[:, :, 768 * index : 768 * index + 768] for index in range(3)])
    starts = small_starts()
    small_low = small_weights.astype(BF)
    small_exact = rounded(small_weights)
    picked = jnp.concatenate([small_low[: starts[2]], small_low[starts[7] :]], axis=0)
    emb = lax.all_gather(picked.astype(F32), "dp", axis=1, tiled=True)
    emb = jnp.concatenate([emb[:16], emb[17:33], emb[16:17], emb[33:35], jnp.zeros((5, D), F32)], axis=0)
    w_tin = small_exact[starts[2] : starts[3]]
    b_tin = small_exact[starts[3]]
    w_tout = small_exact[starts[4] : starts[5]]
    b_tout = small_exact[starts[5]]
    table = small_exact[starts[6] : starts[7]]
    bias_exact = rounded(bias_weights[0])
    head_exact = rounded(head_bias)
    w_mod = rounded(col_weights[:, 0, :mod_width])
    bias_all = lax.all_gather(bias_exact, "tensor", axis=0)
    times_all = lax.all_gather(timesteps, "dp", axis=0, tiled=True)
    labels_all = lax.all_gather(labels, "dp", axis=0, tiled=True)
    time_feat = time_features(times_all)
    time_hidden = exact_dot(time_feat, w_tin) + b_tin
    time_act = lax.all_gather(jax.nn.silu(time_hidden), "dp", axis=1, tiled=True)
    onehot = (labels_all[:, None] == jnp.arange(CLASSES, dtype=jnp.int32)[None, :]).astype(F32)
    condition = exact_dot(time_act, w_tout) + b_tout + exact_dot(onehot, table)
    cond_act = jax.nn.silu(condition)
    mod_part = exact_dot(cond_act, w_mod)
    mod_own = lax.psum_scatter(mod_part, "dp", scatter_dimension=0, tiled=True) + bias_exact[:mod_width]
    mod_full = lax.all_gather(mod_own, "tensor", axis=1, tiled=True).reshape(batch, 8, D)
    cond_rows = lax.all_to_all(cond_act, "dp", split_axis=0, concat_axis=1, tiled=True)

    def mine(values):
        return lax.dynamic_slice_in_dim(values, core * half, half, 0)

    ball = jnp.concatenate(
        [
            jnp.pad(bias_all[:, mod_width : mod_width + qkv_width], ((0, 0), (0, 768 - qkv_width))),
            bias_all[:, mod_width + qkv_width :],
        ],
        axis=1,
    )[:, None]
    (a, m, dy, dz, o, dq, du, g, dmod, small, dbq, db1, hb) = run_block(
        base.reshape(1),
        mine(timesteps),
        mine(clean_latents).transpose(0, 2, 1),
        mine(noise_draw).transpose(0, 2, 1),
        mine(mod_full),
        wall,
        position_table(),
        emb,
        head_exact[:, None],
        ball,
        count_all,
    )
    rows = half * SEQ

    def flat(values):
        return values.reshape(rows, values.shape[-1])

    def pick(values, which):
        return lax.dynamic_index_in_dim(values, which, 0, keepdims=False)

    def gradients(which):
        return (
            tdot(flat(a), flat(pick(dq, which))[:, :qkv_width]),
            tdot(flat(m), flat(pick(du, which))),
            tdot(flat(pick(o, which))[:, 64:], flat(dy)),
            tdot(flat(pick(g, which)), flat(dz)),
            pick(dbq, which)[0, :qkv_width],
            pick(db1, which)[0],
        )

    other = swap(gradients(1 - core))
    own = gradients(core)
    g_qkv, g_fc1, g_proj, g_fc2, g_bqkv, g_bfc1 = [left + right for left, right in zip(own, other)]
    dmod_own = dmod.reshape(half, 8 * D)
    dmod_other = swap(dmod_own)
    dmod_group = jnp.where(
        core == 0,
        jnp.concatenate([dmod_own, dmod_other], axis=0),
        jnp.concatenate([dmod_other, dmod_own], axis=0),
    )
    d_mod = lax.dynamic_slice_in_dim(dmod_group, tensor_rank * mod_width, mod_width, 1)
    g_bmod = jnp.sum(d_mod, axis=0)
    g_mod = exact_tdot(cond_rows, d_mod)
    d_mod_all = lax.all_gather(d_mod, "dp", axis=0, tiled=True)
    d_cond = lax.psum(exact_ndot(d_mod_all, w_mod), "tensor") * silu_slope(condition)
    g_table = exact_tdot(onehot, d_cond)
    g_btout = jnp.sum(d_cond, axis=0)
    g_tout = exact_tdot(time_act, d_cond)
    d_time = lax.psum_scatter(exact_ndot(d_cond, w_tout), "dp", scatter_dimension=1, tiled=True)
    d_time = d_time * silu_slope(time_hidden)
    g_btin = jnp.sum(d_time, axis=0)
    g_tin = exact_tdot(time_feat, d_time)
    small_own = lax.psum(lax.psum_scatter(small, "dp", scatter_dimension=1, tiled=True), "tensor") * 0.5
    head_sum, loss_value = lax.psum((hb[:, 0] * 0.5, hb[0, 1] * 0.5), ("dp", "tensor"))
    small_step = jnp.concatenate(
        [
            small_own[:16],
            small_own[32:33],
            g_tin,
            g_btin[None],
            g_tout,
            g_btout[None],
            g_table,
            small_own[16:32],
            small_own[33:34],
            small_own[34:35],
        ],
        axis=0,
    )
    bias_sum = lax.psum(jnp.concatenate([g_bmod, g_bqkv, g_bfc1], axis=0), "dp")
    col_cuts = cut_parts(col_errors[0, 0], col_widths, 1)
    row_cuts = cut_parts(row_errors[0, 0], [proj_rows, ffn_width], 0)
    matrices = [
        g_mod + col_cuts[0],
        g_qkv + col_cuts[1],
        g_fc1 + col_cuts[2],
        g_proj + row_cuts[0],
        g_fc2 + row_cuts[1],
    ]
    right_pieces = cut_parts(right_factors[0], col_widths + [D, D], 1)
    left_local = jnp.concatenate([exact_ndot(right_pieces[i], matrices[i]) for i in range(5)], axis=1)
    left_sum = lax.psum(left_local, "dp")
    bases = orthonormal_all(cut_parts(left_sum, [D, D, D, proj_rows, ffn_width], 1))
    right_local = jnp.concatenate([exact_dot(bases[i], matrices[i]) for i in range(5)], axis=1)
    right_sum = lax.psum(right_local, "dp")
    right_split = cut_parts(right_sum, col_widths + [D, D], 1)
    approx = [exact_tdot(bases[i], right_split[i]) for i in range(5)]
    rest = [matrices[i] - approx[i] / data_size for i in range(5)]
    col_residue = jnp.concatenate(rest[:3], axis=1)[None, None]
    row_residue = jnp.concatenate(rest[3:], axis=0)[None, None]

    def own_columns(values):
        return lax.dynamic_slice_in_dim(values, data_rank * share, share, 1)

    col_step = jnp.concatenate(
        [exact_tdot(own_columns(bases[i]), right_split[i]) for i in range(3)], axis=1
    )[:, None, :]
    row_step = jnp.concatenate(
        [exact_tdot(bases[i], own_columns(right_split[i])) for i in (3, 4)], axis=0
    )[None]
    col_momentum = DECAY * col_moments + col_step
    col_new = col_weights - LEARN_RATE * col_momentum
    row_momentum = DECAY * row_moments + row_step
    row_new = row_weights - LEARN_RATE * row_momentum
    small_momentum = DECAY * small_moments + small_step
    small_new = small_weights - LEARN_RATE * small_momentum
    bias_momentum = DECAY * bias_moments + bias_sum[None]
    bias_new = bias_weights - LEARN_RATE * bias_momentum
    head_momentum = DECAY * head_moments + head_sum
    head_new = head_bias - LEARN_RATE * head_momentum
    left_factors = jnp.concatenate(bases, axis=1)[None]
    right_new = right_sum[None]
    return (
        loss_value,
        col_new,
        col_momentum,
        col_residue,
        row_new,
        row_momentum,
        row_residue,
        bias_new,
        bias_momentum,
        small_new,
        small_momentum,
        head_new,
        head_momentum,
        left_factors,
        right_new,
    )


def shards(
    clean_latents,
    noise_draw,
    timesteps,
    labels,
    col_weights,
    col_moments,
    col_errors,
    row_weights,
    row_moments,
    row_errors,
    bias_weights,
    bias_moments,
    small_weights,
    small_moments,
    head_bias,
    head_moments,
    right_factors,
):
    tensor_size = lax.axis_size("tensor")
    data_size = lax.axis_size("dp")
    tensor_rank = lax.axis_index("tensor")
    data_rank = lax.axis_index("dp")
    batch = clean_latents.shape[0]
    half = batch // 2
    share = D // data_size
    mod_width = 8 * D // tensor_size
    qkv_width = 3 * D // tensor_size
    ffn_width = FF // tensor_size
    proj_rows = D // tensor_size
    count_all = data_size * batch * SEQ * PATCH_IN
    col_widths = [mod_width, qkv_width, ffn_width]
    core = lax.rem(tensor_rank, 2)
    base = tensor_rank - core
    col = col_weights[:, 0]
    col_low = col.astype(BF)
    row_low = row_weights[0].T.astype(BF)
    onehot = (labels[:, None] == jnp.arange(128, dtype=jnp.int32)[None, :]).astype(F32)
    features = jnp.concatenate([time_features(timesteps), onehot], axis=1)
    small_t = small_weights.T
    a, m, dy, dz, o, dq, du, g, cs, ct, t1, a1, tf, hot, wto, dmod, small, dbq, db1, hb = run_step(
        col_low, row_low, features, small_t, bias_weights, timesteps,
        clean_latents.transpose(0, 2, 1), noise_draw.transpose(0, 2, 1), position_table(), head_bias[None],
        data_size, count_all,
    )
    rows = half * SEQ

    def flat(values):
        return values.reshape(values.shape[:-3] + (rows, values.shape[-1]))

    acts = [flat(values) for values in (a, m, dy, dz, o, dq, du, g)]
    errors = [col_errors[0, 0].T, row_errors[0, 0]]
    mcol, mrow, left_all, right_sum, pst, psr, pc, qst, qsn, qrs, gb, gh, gsm = run_grad(
        acts + errors + [dmod, small, dbq, db1, hb, right_factors[0], cs, ct, t1, a1, tf, hot, col_low, wto], data_size
    )
    cres, rres, col_new, col_momentum, rn, rmn, sn, smn, bias_new, bias_momentum, hn, hmn, left_all, right_sum, loss = run_apply(
        data_rank.reshape(1),
        [mcol, mrow, qst, psr, pst, pc, qsn, qrs, left_all, right_sum, gsm, gb, gh]
        + [col_weights, col_moments, row_weights[0].T, row_moments[0].T, small_t, small_moments.T]
        + [bias_weights, bias_moments, head_bias[None], head_moments[None]],
        data_size,
    )
    loss_value = loss[0, 0]
    col_residue, row_residue = cres.T[None, None], rres[None, None]
    row_new, row_momentum = rn.T[None], rmn.T[None]
    small_new, small_momentum = sn.T, smn.T
    head_new, head_momentum = hn[0], hmn[0]
    left_factors, right_new = left_all[None], right_sum[None]
    return (
        loss_value,
        col_new,
        col_momentum,
        col_residue,
        row_new,
        row_momentum,
        row_residue,
        bias_new,
        bias_momentum,
        small_new,
        small_momentum,
        head_new,
        head_momentum,
        left_factors,
        right_new,
    )


def solution(mesh):
    fits = mesh.shape["dp"] == 8 and mesh.shape["tensor"] == 4
    placed = (
        P("dp", None, None),
        P("dp", None, None),
        P("dp"),
        P("dp"),
        P("dp", "tensor", None),
        P("dp", "tensor", None),
        P("dp", "tensor", None, None),
        P("tensor", None, "dp"),
        P("tensor", None, "dp"),
        P("dp", "tensor", None, None),
        P("tensor", None),
        P("tensor", None),
        P(None, "dp"),
        P(None, "dp"),
        P(),
        P(),
        P("tensor", None, None),
    )
    return jax.shard_map(
        shards if fits else shards_general,
        mesh=mesh,
        in_specs=placed,
        out_specs=(
            P(),
            P("dp", "tensor", None),
            P("dp", "tensor", None),
            P("dp", "tensor", None, None),
            P("tensor", None, "dp"),
            P("tensor", None, "dp"),
            P("dp", "tensor", None, None),
            P("tensor", None),
            P("tensor", None),
            P(None, "dp"),
            P(None, "dp"),
            P(),
            P(),
            P("tensor", None, None),
            P("tensor", None, None),
        ),
        check_vma=False,
    )
```

```python
import functools
import math

import jax
import jax.numpy as jnp
import numpy as np
from jax import lax
from jax.experimental import pallas as pl
from jax.experimental.pallas import tpu as pltpu
from jax.sharding import PartitionSpec as P

D = 768
HEADS = 12
HEAD_DIM = 64
FF = 3072
FREQ = 256
GRID = 16
PATCH_IN = 16
CLASSES = 32
SEQ = 256

EPSILON = 1e-06
TINY = 1e-30
DECAY = 0.9
LEARN_RATE = 100.0
TIME_OFFSET = 0.25
F32 = jnp.float32
BF = jnp.bfloat16
SCALE = 1.0 / math.sqrt(HEAD_DIM)
GELU_C = math.sqrt(2.0 / math.pi)


def exact_dot(left, right):
    return jnp.dot(left, right, precision=lax.Precision.HIGHEST, preferred_element_type=F32)


def exact_tdot(left, right):
    return lax.dot_general(left, right, (((0,), (0,)), ((), ())), precision=lax.Precision.HIGHEST, preferred_element_type=F32)


def exact_ndot(left, right):
    return lax.dot_general(left, right, (((1,), (1,)), ((), ())), precision=lax.Precision.HIGHEST, preferred_element_type=F32)


def dot(a,b): return lax.dot_general(a,b,(((1,),(0,)),((),())),preferred_element_type=F32)
def ndot(a,b): return lax.dot_general(a,b,(((1,),(1,)),((),())),preferred_element_type=F32)
def tdot(a,b): return lax.dot_general(a,b,(((0,),(0,)),((),())),preferred_element_type=F32)

def ln(h):
    c=h-jnp.mean(h,axis=-1,keepdims=True)
    v=jnp.mean(c*c,axis=-1,keepdims=True)
    r=lax.rsqrt(v+EPSILON)
    return c*r,r

def ln_back(dout,xh,r,scale):
    dx=dout*(1.0+scale)
    return r*(dx-jnp.mean(dx,axis=-1,keepdims=True)-xh*jnp.mean(dx*xh,axis=-1,keepdims=True))

def colsum(v): return jnp.sum(v,axis=0,keepdims=True)

UNROLL=dict(af=2,ff=4,fb=4,ab=4)

def block_state():
    V=pltpu.VMEM
    return dict(
        wall=V((3,4,D,D),BF), pe=V((SEQ,D),F32), qkv=V((4,4,SEQ,640),BF), p=V((4,12,SEQ,SEQ),BF),
        xh1=V((4,SEQ,D),F32), y=V((4,SEQ,D),F32), h=V((4,SEQ,D),F32), r1=V((4,SEQ,1),F32),
        xh2=V((SEQ,D),F32), z=V((SEQ,D),F32), r2=V((SEQ,1),F32), slope=V((4,SEQ,D),F32),
        a=V((SEQ,D),BF), m=V((SEQ,D),BF), dz=V((SEQ,D),BF), dy=V((SEQ,D),BF),
        o=V((4,SEQ,256),BF), g=V((4,SEQ,D),BF), du=V((4,SEQ,D),BF), dq=V((4,SEQ,640),BF),
        dbq=V((4,1,640),F32), db1=V((4,1,D),F32), out_sem=pltpu.SemaphoreType.DMA((8,)))

class Block:
    def __init__(self,s,times,clean,noise,mod,pe,emb,bh,ball,outs,dmod,small,hb,base,first,count_all,service):
        self.s=s; self.times=times; self.clean=clean; self.noise=noise; self.mod_ref=mod; self.pe=pe; self.emb=emb; self.bh=bh; self.ball=ball
        self.outs=outs; self.dmod=dmod; self.small=small; self.hb=hb; self.base=base; self.first=first; self.count_all=count_all; self.service=service
        self.lo=lax.broadcasted_iota(jnp.int32,(1,128),1)<64
        self.zero=jnp.zeros((),BF)
    def roll(self,v): return pltpu.roll(v.astype(F32),64,1).astype(BF)
    def out(self,lat,name,index,pair):
        s=self.s
        src=s[name].at[pl.ds(self.base,2)] if pair else s[name]
        dst=self.outs[index].at[:,lat] if pair else self.outs[index].at[lat]
        return pltpu.make_async_copy(src,dst,s["out_sem"].at[index])
    def emit(self,lat,name,index,pair=False): self.out(lat,name,index,pair).start()
    def clear(self,lat,name,index,pair=False):
        @pl.when(lat>0)
        def _(): self.out(lat-1,name,index,pair).wait()
    def last(self):
        for name,index,pair in (("a",0,False),("m",1,False),("dy",2,False),("dz",3,False),("o",4,True),("dq",5,True),("du",6,True),("g",7,True)):
            self.out(3,name,index,pair).wait()
    def start(self):
        s=self.s
        self.small[...]=jnp.zeros_like(self.small); self.hb[...]=jnp.zeros_like(self.hb)
        s["dbq"][...]=jnp.zeros_like(s["dbq"]); s["db1"][...]=jnp.zeros_like(s["db1"])
        for i in range(GRID):
            s["pe"][16*i:16*i+16,0:384]=jnp.broadcast_to(self.pe[i:i+1,:],(16,384))
            s["pe"][16*i:16*i+16,384:768]=self.pe[...]
    def mixed(self,lat):
        place=self.first+lat
        t=self.times[place]
        clean=self.clean[place].astype(F32); noise=self.noise[place].astype(F32)
        return t,clean,noise,(t*clean+(1.0-t)*noise).astype(BF)
    def mod(self,lat,i): return self.mod_ref[lat,i:i+1,:]
    def embed(self,lat):
        s=self.s
        mixed=self.mixed(lat)[3]
        h0=tdot(mixed,self.emb[0:16].astype(BF))+self.emb[32:33]+s["pe"][...]
        s["h"][lat]=h0
        xh,r=ln(h0)
        s["xh1"][lat]=xh; s["r1"][lat]=r
        self.clear(lat,"a",0)
        s["a"][...]=(xh*(1.0+self.mod(lat,1))+self.mod(lat,0)).astype(BF)
        self.emit(lat,"a",0)
        self.clear(lat,"o",4,True)
    def softmax(self,v,lat,idx):
        v=v*SCALE
        e=jnp.exp(v-jnp.max(v,axis=-1,keepdims=True))
        p=(e/jnp.sum(e,axis=-1,keepdims=True)).astype(BF)
        self.s["p"][lat,idx]=p
        return p
    def attend(self,lat,j):
        s=self.s; lo=self.lo; zero=self.zero; wall=s["wall"]
        full=(dot(s["a"][...],wall[0,j])[:,0:640]+self.ball[j,:,0:640]).astype(BF)
        s["qkv"][lat,j]=full
        b0,b1,b2,b3,b4=[full[:,128*i:128*i+128] for i in range(5)]
        p0=self.softmax(ndot(jnp.where(lo,b0,zero),self.roll(b0)),lat,3*j)
        p1=self.softmax(ndot(jnp.where(lo,zero,b1),self.roll(b2)),lat,3*j+1)
        p2=self.softmax(ndot(jnp.where(lo,b3,zero),self.roll(b3)),lat,3*j+2)
        o0=pltpu.roll(dot(p0,b1),64,1)
        s["o"][j,:,0:128]=jnp.where(lo,0.0,o0).astype(BF)
        s["o"][j,:,128:256]=pltpu.roll(jnp.where(lo,dot(p2,b4),dot(p1,b2)),64,1).astype(BF)
    def project(self,lat):
        s=self.s
        self.emit(lat,"o",4,True)
        for n in range(3):
            cols=slice(256*n,256*n+256)
            y=sum(ndot(s["o"][j],s["wall"][0,j,cols,512:768]) for j in range(4))+self.emb[33:34,cols]
            s["y"][lat,:,cols]=y
            s["h"][lat,:,cols]+=self.mod(lat,2)[:,cols]*y
    def attn_fwd(self,lat):
        self.service(lat,0)
        self.embed(lat)
        self.service(lat,1)
        for j in range(2): self.attend(lat,j)
        self.service(lat,2)
        for j in range(2,4): self.attend(lat,j)
        self.service(lat,3)
        self.project(lat)
    def fc_in(self,lat):
        s=self.s
        xh,r=ln(s["h"][lat])
        s["xh2"][...]=xh; s["r2"][...]=r
        self.clear(lat,"m",1)
        s["m"][...]=(xh*(1.0+self.mod(lat,4))+self.mod(lat,3)).astype(BF)
        self.emit(lat,"m",1)
        self.clear(lat,"g",7,True)
    def fc_one(self,lat,j):
        s=self.s
        u=dot(s["m"][...],s["wall"][1,j])+self.ball[j,:,768:1536]
        uu=u*u
        th=jnp.tanh(u*(GELU_C+(GELU_C*0.044715)*uu))
        half=0.5+0.5*th
        s["g"][j]=(u*half).astype(BF)
        s["slope"][j]=half*(1.0+(u-u*th)*(GELU_C+(3.0*0.044715*GELU_C)*uu))
    def fc_fwd(self,lat):
        s=self.s
        self.fc_in(lat)
        u=UNROLL["ff"]
        @pl.loop(0,4//u)
        def _(i):
            for k in range(u): self.fc_one(lat,i*u+k)
        self.emit(lat,"g",7,True)
        for n in range(3):
            cols=slice(256*n,256*n+256)
            z=sum(ndot(s["g"][j],s["wall"][2,j,cols,:]) for j in range(4))+self.emb[34:35,cols]
            s["z"][:,cols]=z
    def head(self,lat):
        s=self.s; mod=lambda i: self.mod(lat,i)
        t,clean,noise,_=self.mixed(lat)
        wh=self.emb[16:32].astype(BF)
        h2=s["h"][lat]+mod(5)*s["z"][...]
        xh,r=ln(h2)
        fi=(xh*(1.0+mod(7))+mod(6)).astype(BF)
        pred=ndot(wh,fi)+self.bh[...]
        diff=pred-(clean-noise)
        weight=1.0/(1.0-t+TIME_OFFSET)
        self.hb[0:1,1:2]+=jnp.sum(colsum(weight*diff*diff),axis=1,keepdims=True)*(1.0/self.count_all)
        dpred=2.0*weight*diff*(1.0/self.count_all)
        self.hb[:,0:1]+=jnp.sum(dpred,axis=1,keepdims=True)
        dpl=dpred.astype(BF)
        self.small[16:32]+=dot(dpl,fi)
        dfi=tdot(dpl,wh)
        self.dmod[lat,6:7]=colsum(dfi); self.dmod[lat,7:8]=colsum(dfi*xh)
        dh=ln_back(dfi,xh,r,mod(7))
        s["h"][lat]=dh
        self.dmod[lat,5:6]=colsum(dh*s["z"][...])
        dzf=dh*mod(5)
        self.small[34:35]+=colsum(dzf)
        self.clear(lat,"dz",3)
        s["dz"][...]=dzf.astype(BF)
        self.emit(lat,"dz",3)
        self.clear(lat,"du",6,True)
    def fc_back_one(self,j):
        s=self.s
        du=dot(s["dz"][...],s["wall"][2,j])*s["slope"][j]
        s["du"][j]=du.astype(BF)
        s["db1"][j]+=colsum(du)
    def fc_bwd(self,lat):
        s=self.s; mod=lambda i: self.mod(lat,i)
        u=UNROLL["fb"]
        @pl.loop(0,4//u)
        def _(i):
            for k in range(u): self.fc_back_one(i*u+k)
        self.emit(lat,"du",6,True)
        for n in range(3):
            cols=slice(256*n,256*n+256)
            s["z"][:,cols]=sum(ndot(s["du"][j],s["wall"][1,j,cols,:]) for j in range(4))
        dm=s["z"][...]
        xh=s["xh2"][...]
        self.dmod[lat,3:4]=colsum(dm); self.dmod[lat,4:5]=colsum(dm*xh)
        dh=s["h"][lat]+ln_back(dm,xh,s["r2"][...],mod(4))
        s["h"][lat]=dh
        self.dmod[lat,2:3]=colsum(dh*s["y"][lat])
        dyf=dh*mod(2)
        self.small[33:34]+=colsum(dyf)
        self.clear(lat,"dy",2)
        s["dy"][...]=dyf.astype(BF)
        self.emit(lat,"dy",2)
        self.clear(lat,"dq",5,True)
    def attend_back(self,lat,j):
        s=self.s; lo=self.lo; zero=self.zero; roll=self.roll
        do=dot(s["dy"][...],s["wall"][0,j,:,512:768])
        r4=pltpu.roll(do[:,0:128],64,1).astype(BF); r5=pltpu.roll(do[:,128:256],64,1).astype(BF)
        do0=jnp.where(lo,r4,zero); do1=jnp.where(lo,zero,r5); do2=jnp.where(lo,r5,zero)
        b0,b1,b2,b3,b4=[s["qkv"][lat,j,:,128*i:128*i+128] for i in range(5)]
        def head(h,doh,v):
            p=s["p"][lat,3*j+h]
            dv=tdot(p,doh)
            dp=ndot(doh,v)
            pf=p.astype(F32)
            t=pf*dp
            ds=(t-pf*jnp.sum(t,axis=-1,keepdims=True)).astype(BF)
            return dv,ds
        dv0,ds0=head(0,do0,b1)
        dv1,ds1=head(1,do1,b2)
        dv2,ds2=head(2,do2,b4)
        rb0=roll(b0); rb3=roll(b3)
        n0=jnp.where(lo,dot(ds0,rb0),tdot(ds0,rb0))*SCALE
        n1=jnp.where(lo,dv0,dot(ds1,roll(b2))*SCALE); n2=jnp.where(lo,tdot(ds1,roll(b1))*SCALE,dv1)
        n3=jnp.where(lo,dot(ds2,rb3),tdot(ds2,rb3))*SCALE
        n4=jnp.where(lo,dv2,0.0)
        for i,v in enumerate((n0,n1,n2,n3,n4)):
            cols=slice(128*i,128*i+128)
            s["dq"][j,:,cols]=v.astype(BF)
            s["dbq"][j,:,cols]+=colsum(v)
    def attn_bwd(self,lat):
        s=self.s; mod=lambda i: self.mod(lat,i)
        u=UNROLL["ab"]
        @pl.loop(0,4//u)
        def _(i):
            for k in range(u): self.attend_back(lat,i*u+k)
        self.emit(lat,"dq",5,True)
        for n in range(3):
            cols=slice(256*n,256*n+256)
            s["z"][:,cols]=sum(ndot(s["dq"][j],s["wall"][0,j,cols,0:640]) for j in range(4))
        da=s["z"][...]
        xh=s["xh1"][lat]
        self.dmod[lat,0:1]=colsum(da); self.dmod[lat,1:2]=colsum(da*xh)
        dh=s["h"][lat]+ln_back(da,xh,s["r1"][lat],mod(1))
        self.small[32:33]+=colsum(dh)
        self.small[0:16]+=dot(self.mixed(lat)[3],dh.astype(BF))

    def run(self,ready=lambda: None):
        @pl.loop(0,4)
        def _(lat): self.attn_fwd(lat)
        ready()
        @pl.loop(0,4)
        def _(lat):
            for phase in (self.fc_fwd,self.head,self.fc_bwd,self.attn_bwd): phase(lat)
        self.last()

def block_kernel(times_ref,base_ref,clean_ref,noise_ref,mod_ref,wall_ref,pe_ref,emb_ref,bh_ref,ball_ref,*rest,count_all,names):
    outs=rest[0:8]; dmod,small,dbq,db1,hb=rest[8:13]
    s=dict(zip(names,rest[13:13+len(names)])); wsem=rest[-1]
    cp=pltpu.make_async_copy(wall_ref,s["wall"],wsem); cp.start()
    base=base_ref[0]
    b=Block(s,times_ref,clean_ref,noise_ref,mod_ref,pe_ref,emb_ref,bh_ref,ball_ref,outs,dmod,small,hb,base,0,count_all,lambda lat,pos: None)
    b.start()
    cp.wait()
    b.run()
    for k in range(2):
        dbq[k]=s["dbq"][base+k]; db1[k]=s["db1"][base+k]

def run_block(base,times,clean,noise,mod,wall,pe,emb,bh,ball,count_all):
    L=clean.shape[0]
    S=jax.ShapeDtypeStruct
    outs=[S((L,SEQ,D),BF)]*4+[S((2,L,SEQ,256),BF),S((2,L,SEQ,640),BF),S((2,L,SEQ,768),BF),S((2,L,SEQ,768),BF),
        S((L,8,D),F32),S((40,D),F32),S((2,1,640),F32),S((2,1,768),F32),S((PATCH_IN,128),F32)]
    st=block_state(); names=tuple(st)
    vm=pl.BlockSpec(memory_space=pltpu.VMEM); anys=pl.BlockSpec(memory_space=pl.ANY); sm=pl.BlockSpec(memory_space=pltpu.SMEM)
    return pl.pallas_call(functools.partial(block_kernel,count_all=count_all,names=names),
        out_shape=outs,in_specs=[sm,sm,vm,vm,vm,anys,vm,vm,vm,vm],out_specs=[anys]*8+[vm]*5,
        scratch_shapes=list(st.values())+[pltpu.SemaphoreType.DMA(())],
        compiler_params=pltpu.CompilerParams(vmem_limit_bytes=62*1024*1024),name="block")(times,base,clean,noise,mod,wall,pe,emb,bh,ball)


MESH = pl.DeviceIdType.MESH
HI = lax.Precision.HIGHEST


def hdot(a, b):
    return lax.dot_general(a, b, (((1,), (0,)), ((), ())), precision=HI, preferred_element_type=F32)


def hndot(a, b):
    return lax.dot_general(a, b, (((1,), (1,)), ((), ())), precision=HI, preferred_element_type=F32)


def htdot(a, b):
    return lax.dot_general(a, b, (((0,), (0,)), ((), ())), precision=HI, preferred_element_type=F32)


def split2(values):
    first = values.astype(BF)
    return first, (values - first.astype(F32)).astype(BF)


def split3(values):
    first, rest = values.astype(BF), values
    rest = rest - first.astype(F32)
    second = rest.astype(BF)
    return first, second, (rest - second.astype(F32)).astype(BF)


def silu_slope_k(values):
    gate = 1.0 / (1.0 + jnp.exp(-values))
    return gate * (1.0 + values * (1.0 - gate))


class Peers:
    def __init__(self, send_sem, recv_sem):
        self.w = lax.axis_index("dp")
        self.t = lax.axis_index("tensor")
        self.n = lax.axis_size("dp")
        self.tn = lax.axis_size("tensor")
        self.c = lax.rem(self.t, 2)
        self.sib = self.t + 1 - 2 * self.c
        self.send_sem, self.recv_sem = send_sem, recv_sem
        self.pending = []

    def barrier(self):
        bar = pltpu.get_barrier_semaphore()
        for i in range(1, self.n):
            pl.semaphore_signal(bar, inc=1, device_id=(lax.rem(self.w + i, self.n), self.t), device_id_type=MESH)
        for i in range(1, self.tn):
            pl.semaphore_signal(bar, inc=1, device_id=(self.w, lax.rem(self.t + i, self.tn)), device_id_type=MESH)

    def ready(self):
        pl.semaphore_wait(pltpu.get_barrier_semaphore(), self.n - 1 + self.tn - 1)

    def copy(self, src, dst, index, device):
        op = pltpu.make_async_remote_copy(
            src_ref=src,
            dst_ref=dst,
            send_sem=self.send_sem.at[index],
            recv_sem=self.recv_sem.at[index],
            device_id=device,
            device_id_type=MESH,
        )
        op.start()
        self.pending.append(op)
        return op

    def dp_push(self, src_of, dst, base):
        ops = []
        for i in range(1, self.n):
            peer = lax.rem(self.w + i, self.n)
            ops.append(self.copy(src_of(peer), dst, base + i - 1, (peer, self.t)))
        return ops

    def tensor_push(self, src, dst, base):
        ops = []
        for i in range(1, self.tn):
            ops.append(self.copy(src, dst, base + i - 1, (self.w, lax.rem(self.t + i, self.tn))))
        return ops

    def core_push(self, src, dst, index):
        return self.copy(src, dst, index, (self.w, self.sib))

    def finish(self):
        for op in self.pending:
            op.wait_send()


def wait_all(ops):
    for op in ops:
        op.wait_recv()


P_TILES = (6, 6, 6, 2, 6)
P_COUNT = 32
Q_COUNT = 40
QKV0, FC0 = 1536, 2112
COLS = 2880


def halves(block):
    high = block.astype(BF).astype(F32)
    return [high, block - high]


def fill(rows, total):
    used = sum(row.shape[0] for row in rows)
    return jnp.concatenate(rows + [jnp.zeros((total - used, rows[0].shape[1]), F32)], axis=0)


AUX = ("cs", "ct", "t1", "a1", "tf", "hot", "wto", "dmod", "small", "dbq", "db1", "hb")


def step_kernel(
    col_ref, row_ref, pk_ref, smt_ref, bias_ref, times_ref, clean_ref, noise_ref, pe_ref, bh_ref, *rest, names, count_all
):
    outs, aux_out, rest = rest[:8], rest[8 : 8 + len(AUX)], rest[8 + len(AUX) :]
    s = dict(zip(names, rest[: len(names)]))
    aux, rest = dict(zip(AUX, rest[len(names) :])), rest[len(names) + len(AUX) :]
    mod_ref, emb_ref, ball_ref = rest[:3]
    pack_ref, bhs, bmod_ref, pkl, ems, eml, a1s, a1l, css, csl, mps, mpl_, mos, mol, bal, local_sem, wsend, wrecv, send_sem, recv_sem = rest[3:]
    wall_ref = s["wall"]
    cs_ref, ct_ref, t1_ref, a1_ref, tf_ref, hot_ref, wto_ref = [aux[name] for name in AUX[:7]]
    net = Peers(send_sem, recv_sem)
    w, t, c, n = net.w, net.t, net.c, net.n
    share = D // n
    half = share // 2
    x, z, y = t // 2, w // 2, lax.rem(w, 2)
    net.barrier()
    wmod_ref = col_ref.at[:, 0:QKV0]
    pack_ref[0, :, 0:576] = col_ref[:, QKV0:FC0]
    pack_ref[0, :, 576:768] = row_ref[:, 0:192]
    pack_ref[1] = col_ref[:, FC0:COLS]
    pack_ref[2] = row_ref[:, 192:960]
    own = []

    def place(q, j, v):
        return wall_ref.at[q, j, pl.ds(pl.multiple_of(share * v, 32), share)]

    for q in range(3):
        op = pltpu.make_async_copy(pack_ref.at[q], place(q, t, w), local_sem.at[q])
        op.start()
        own.append(op)
    pkl[w] = pk_ref[...]
    rest = smt_ref.shape[1]
    emb = jnp.concatenate(
        [smt_ref[:, 0:16], smt_ref[:, rest - 18 : rest - 2], smt_ref[:, 16:17], smt_ref[:, rest - 2 : rest], jnp.zeros((share, 5), F32)],
        axis=1,
    )
    third = share // 3
    emb = jnp.concatenate([emb[0:third], emb[third : 2 * third], emb[2 * third : share], jnp.zeros((third, 8), F32)], axis=1)
    ems[...] = emb.astype(BF)
    eml[w] = ems[...]
    bias = bias_ref[...].astype(BF).astype(F32)
    bmod_ref[...] = bias[:, 0:QKV0]
    bal[t] = jnp.concatenate([bias[:, QKV0:FC0], jnp.zeros((1, 192), F32), bias[:, FC0:COLS]], axis=1)
    net.ready()
    pk_ops = net.dp_push(lambda peer: pk_ref, pkl.at[w], 0)
    em_ops = net.dp_push(lambda peer: ems, eml.at[w], 7)
    ba_ops = net.tensor_push(bal.at[t], bal.at[t], 14)

    zs = [z, z + 1 - 2 * lax.rem(z, 2), lax.rem(z + 2, 4), 3 - z]
    xo = 1 - x
    mine, across = 2 * x + c, 2 * xo + c
    wys = [2 * zs[k] + y for k in range(4)]
    wos = [2 * zs[k] + (1 - y) for k in range(4)]
    to_zs = [(wys[k], t) for k in range(4)]
    wy, wo, to_z = wys.__getitem__, wos.__getitem__, to_zs.__getitem__
    to_x, to_y, to_core = (w, across), (2 * z + (1 - y), t), (w, net.sib)
    sends = []

    def piece_copy(index, q, j, v, device, own_block):
        slot = place(q, j, v)
        return pltpu.make_async_remote_copy(
            src_ref=pack_ref.at[q] if own_block else slot, dst_ref=slot, send_sem=wsend.at[index],
            recv_sem=wrecv.at[q, j, v], device_id=device, device_id_type=MESH,
        )

    def send(q, j, v, device, own_block=False):
        sends.append((len(sends), q, j, v, device, own_block))
        piece_copy(*sends[-1]).start()

    def arrived(q, j, v):
        piece_copy(0, q, j, v, to_core, False).wait_recv()

    def column(q, k):
        if k == 0:
            send(q, mine, w, to_z(1), True)
            send(q, mine, w, to_z(2), True)
        else:
            arrived(q, mine, wy(k))
            if k == 2:
                send(q, mine, wy(2), to_z(1))
        send(q, mine, wy(k), to_x, k == 0)
        send(q, mine, wy(k), to_y, k == 0)
        send(q, mine, wy(k), to_core, k == 0)

    def by_y(q, k):
        return q == 0 and k == 3

    def side(q, k):
        arrived(q, across, wy(k))
        if by_y(q, k):
            send(q, across, wy(k), to_y)
        send(q, across, wy(k), to_core)
        arrived(q, mine, wo(k))
        if not by_y(q, k):
            send(q, mine, wo(k), to_x)
        send(q, mine, wo(k), to_core)

    def corner(q, k):
        arrived(q, across, wo(k))
        send(q, across, wo(k), to_core)

    first_hop, last_hop = {1: to_x}, {1: to_y}

    def level(q, k):
        return (mine, wy(k)), ((across, wy(k)) if q == 1 else (mine, wo(k)))

    def begin(q):
        send(q, mine, w, first_hop[q], True)
        send(q, mine, w, to_z(1), True)
        send(q, mine, w, to_z(2), True)
        send(q, mine, w, last_hop[q], True)
        send(q, mine, w, to_core, True)

    def second(q):
        j, v = level(q, 0)[1]
        arrived(q, j, v)
        for device in (to_z(1), to_z(2), last_hop[q], to_core):
            send(q, j, v, device)

    def along(q, k):
        for j, v in level(q, k):
            arrived(q, j, v)
            if k == 2:
                send(q, j, v, to_z(1))
            send(q, j, v, last_hop[q])
            send(q, j, v, to_core)

    def far(q, k):
        last = (mine, wo(k)) if q == 1 else (across, wy(k))
        for j, v in (last, (across, wo(k))):
            arrived(q, j, v)
            send(q, j, v, to_core)

    def chain0():
        wait_all(pk_ops)
        feats = pkl[...].reshape(8 * n, 384)
        tf_ref[...] = feats[:, 0:FREQ]
        hot_ref[...] = feats[:, FREQ:384]
        small = smt_ref[...].astype(BF).astype(F32)
        t1 = hndot(small[:, 17:273], tf_ref[...]) + small[:, 273:274]
        t1_ref[...] = t1
        act = t1 / (1.0 + jnp.exp(-t1))
        a1s[...] = jnp.concatenate([act[0:half], act[half:share]], axis=1)
        a1l[w] = a1s[...]
        return net.dp_push(lambda peer: a1s, a1l.at[w], 17)

    def chain1(ops):
        wait_all(ops)
        for k in range(n):
            a1_ref[share * k : share * k + half] = a1l[k][:, 0:64]
            a1_ref[share * k + half : share * k + share] = a1l[k][:, 64:128]
        small = smt_ref[...].astype(BF).astype(F32)
        cond = hdot(small[:, 274:1042], a1_ref[...]) + small[:, 1042:1043]
        cond = cond + hndot(small[:, 1043:1075], hot_ref[:, 0:CLASSES])
        ct_ref[...] = cond
        act = cond / (1.0 + jnp.exp(-cond))
        css[...] = jnp.concatenate([act[0:half], act[half:share]], axis=1)
        csl[w] = css[...]
        cs_ops = net.dp_push(lambda peer: css, csl.at[w], 24)
        parts = [tdot(piece, wmod_ref[...]) for piece in split3(act)]
        mps[...] = (parts[0] + parts[1] + parts[2]).reshape(n, 8, QKV0)
        mpl_[w] = mps[w]
        return cs_ops, net.dp_push(lambda peer: mps.at[peer], mpl_.at[w], 31)

    def chain2(ops):
        wait_all(ops)
        total = mpl_[0]
        for k in range(1, n):
            total = total + mpl_[k]
        mos[...] = total + bmod_ref[...]
        mol[t] = mos[...]
        return net.tensor_push(mos, mol.at[t], 38)

    def chain3(ops):
        wait_all(em_ops)
        rows = []
        for k in range(n):
            piece = eml[k].astype(F32)
            rows += [piece[:, 40 * i : 40 * i + 40] for i in range(3)]
        rows = jnp.concatenate(rows, axis=0)
        emb_ref[...] = jnp.concatenate([rows, jnp.zeros((D, 88), F32)], axis=1).T[0:40]
        wait_all(ba_ops)
        ball_ref[...] = bal[...]
        wait_all(ops)
        for lat in range(4):
            for j in range(4):
                for piece in range(2):
                    mod_ref[lat, 2 * j + piece : 2 * j + piece + 1, :] = mol[j, pl.ds(4 * c + lat, 1), D * piece : D * piece + D]

    column(0, 0)
    ops = chain0()
    column(0, 1)
    side(0, 0)
    column(0, 2)
    cs_ops, ops = chain1(ops)
    side(0, 1)
    corner(0, 0)
    column(0, 3)
    side(0, 2)
    begin(1)
    column(2, 0)
    corner(0, 1)
    side(0, 3)
    ops = chain2(ops)
    corner(0, 2)
    corner(0, 3)
    second(1)
    column(2, 1)
    chain3(ops)

    def other_core(q):
        for j in (2 * x + 1 - c, 2 * xo + 1 - c):
            for v in range(n):
                arrived(q, j, v)

    other_core(0)
    own[0].wait()
    plan = (
        (along, 1, 1), (side, 2, 0), (column, 2, 2), (corner, 2, 0), (along, 1, 2), (side, 2, 1), (column, 2, 3), (corner, 2, 1),
        None, (side, 2, 2), None, (along, 1, 3), (side, 2, 3), (corner, 2, 2),
    )
    slots = {i: [functools.partial(*item)] for i, item in enumerate(plan) if item}
    rest = [functools.partial(far, 1, k) for k in range(4)] + [functools.partial(corner, 2, 3)]

    def service(lat, pos):
        for index, todo in slots.items():
            if index % 4 == pos:
                for item in todo:
                    pl.when(lat == index // 4)(item)

    def rows_out():
        wait_all(cs_ops)
        rows = []
        for k in range(n):
            rows += [csl[k][:, 0:64], csl[k][:, 64:128]]
        rows = jnp.concatenate(rows, axis=0)
        a1s_all = jnp.concatenate([rows, jnp.zeros((D, 64), F32)], axis=1).T
        cs_all = a1s_all[0:64].reshape(n, 8, D)
        picked = jnp.zeros((8, D), F32)
        for k in range(n):
            picked = jnp.where(w == k, cs_all[k], picked)
        cs_ref[...] = picked
        wto_ref[...] = smt_ref[:, 274:1042].astype(BF)

    def ready():
        for item in rest:
            item()
        for q in (1, 2):
            other_core(q)
            own[q].wait()

    block = Block(
        s, times_ref, clean_ref, noise_ref, mod_ref, pe_ref, emb_ref, bhs, ball_ref, outs,
        aux["dmod"], aux["small"], aux["hb"], 2 * x, 4 * c, count_all, service,
    )
    bhs[...] = tdot(bh_ref[...].astype(BF), jnp.ones((1, SEQ), BF))
    block.start()
    block.run(ready)
    rows_out()
    for k in range(2):
        aux["dbq"][k] = s["dbq"][2 * x + k]
        aux["db1"][k] = s["db1"][2 * x + k]
    copies = [pltpu.make_async_copy(aux[name], aux_out[i], local_sem.at[3 + i]) for i, name in enumerate(AUX)]
    for op in copies:
        op.start()
    for record in sends:
        piece_copy(*record).wait_send()
    net.finish()
    for op in copies:
        op.wait()


def run_step(col, row, pk, smt, bias, times, clean, noise, pe, bh, n, count_all):
    S = jax.ShapeDtypeStruct
    V = pltpu.VMEM
    DMA = pltpu.SemaphoreType.DMA
    share = D // n
    lat = 8 * n
    half = 4
    any_spec = pl.BlockSpec(memory_space=pl.ANY)
    vm = pl.BlockSpec(memory_space=pltpu.VMEM)
    aux = [
        ((8, D), F32), ((share, lat), F32), ((share, lat), F32), ((D, lat), F32), ((lat, FREQ), F32), ((lat, 128), F32), ((share, D), BF),
        ((half, 8, D), F32), ((40, D), F32), ((2, 1, 640), F32), ((2, 1, D), F32), ((PATCH_IN, 128), F32),
    ]
    outs = [S((half, SEQ, D), BF)] * 4 + [S((2, half, SEQ, width), BF) for width in (256, 640, D, D)]
    outs += [S(*a) for a in aux]
    state = block_state()
    scratch = list(state.values()) + [V(*a) for a in aux] + [
        V((half, 8, D), F32), V((40, D), F32), V((4, 1, QKV0), F32),
        V((3, share, D), BF), V((PATCH_IN, SEQ), F32), V((1, QKV0), F32),
        V((n, 8, 384), F32), V((share // 3, 128), BF), V((n, share // 3, 128), BF),
        V((share // 2, 128), F32), V((n, share // 2, 128), F32), V((share // 2, 128), F32), V((n, share // 2, 128), F32),
        V((n, 8, QKV0), F32), V((n, 8, QKV0), F32), V((8, QKV0), F32), V((4, 8, QKV0), F32), V((4, 1, QKV0), F32),
        DMA((3 + len(AUX),)), DMA((120,)), DMA((3, 4, n)), DMA((41,)), DMA((41,)),
    ]
    return pl.pallas_call(
        functools.partial(step_kernel, names=tuple(state), count_all=count_all),
        out_shape=outs,
        in_specs=[vm] * 5 + [pl.BlockSpec(memory_space=pltpu.SMEM)] + [vm] * 4,
        out_specs=[any_spec] * len(outs),
        scratch_shapes=scratch,
        compiler_params=pltpu.CompilerParams(collective_id=0, has_side_effects=True, vmem_limit_bytes=62 * 1024 * 1024),
        name="step",
    )(col, row, pk, smt, bias, times, clean, noise, pe, bh)


def gram_schmidt(block):
    rows = lax.broadcasted_iota(jnp.int32, (8, 1), 0)
    for index in range(8):
        row = block[index : index + 1]
        row = row * lax.rsqrt(jnp.sum(row * row, axis=-1, keepdims=True) + TINY)
        inner = jnp.sum(block * row, axis=-1, keepdims=True)
        inner = jnp.where(rows > index, inner, 0.0)
        block = jnp.where(rows == index, row, block - inner * row)
    return block


def grad_kernel(
    a_ref, m_ref, dy_ref, dz_ref, o_ref, dq_ref, du_ref, g_ref, cerr_ref, rerr_ref,
    dmod_ref, small_ref, dbq_ref, db1_ref, hb_ref, right_ref, cs_ref, ct_ref, t1_ref, a1_ref, tf_ref, hot_ref, wmod_ref, wto_ref,
    mcol_ref, mrow_ref, left_out, rightn_out, pst_out, psr_out, pc_out, qst_out, qsn_out, qrs_out, gb_out, gh_out, gsm_out,
    mc, mr, sc, sr, rc, rr, av, mv, dyv, dzv, ov, qv, uv, gv,
    left_ref, rightn_ref, pst_ref, psr_ref, pc_ref, qst_ref, qsn_ref, qrs_ref, gb_ref, gh_ref, gsm_ref,
    dmo, smo, dbo, dbo1, hbo, dm8, dma, dsc, dss, dts, dtl, tks, tkl, px, pland, py, qx, qland, qy,
    load_sem, out_sem, send_sem, recv_sem,
):
    net = Peers(send_sem, recv_sem)
    outs = []

    def emit(*pairs):
        for src, dst in pairs:
            op = pltpu.make_async_copy(src, dst, out_sem.at[len(outs)])
            op.start()
            outs.append(op)

    w, t, c = net.w, net.t, net.c
    n = net.n
    share = D // n
    loads = {}

    def load(name, src, dst, index):
        op = pltpu.make_async_copy(src, dst, load_sem.at[index])
        op.start()
        loads[name] = op

    net.barrier()
    load("q", dq_ref, qv, 9)
    load("a", a_ref, av, 1)
    load("u", du_ref, uv, 0)
    load("m", m_ref, mv, 2)
    def chunk(i, size=256):
        return pl.ds(pl.multiple_of(i * size, size), size)

    def after(i, first):
        return pl.ds(pl.multiple_of(first + 256 * i, 64), 256)

    for name in ("q", "a"):
        loads[name].wait()
    col_ops, row_ops = [], []
    load("g", g_ref, gv, 3)
    load("dz", dz_ref, dzv, 4)
    sc[0:256] = tdot(qv[1 - c, :, 0:256], av[...])
    sc[256:576] = tdot(qv[1 - c, :, 256:640], av[...])[0:320]
    net.ready()
    side = [
        net.core_push(dmod_ref, dmo, 0),
        net.core_push(small_ref, smo, 1),
        net.core_push(dbq_ref.at[1 - c], dbo, 2),
        net.core_push(db1_ref.at[1 - c], dbo1, 9),
        net.core_push(hb_ref, hbo, 10),
    ]

    col_ops.append(net.core_push(sc.at[0:576], rc.at[0:576], 3))
    for name in ("u", "m"):
        loads[name].wait()
    load("o", o_ref, ov, 5)
    load("dy", dy_ref, dyv, 6)
    load("ce", cerr_ref, mc, 7)

    @pl.loop(0, 3)
    def _(i):
        sc[after(i, 576), :] = tdot(uv[1 - c, :, chunk(i)], mv[...])

    col_ops.append(net.core_push(sc.at[576:1344], rc.at[576:1344], 4))
    wait_all(side)
    for lat in range(4):
        for piece in range(2):
            span = slice(D * piece, D * piece + D)
            dm8[pl.ds(4 * c + lat, 1), span] = dmod_ref[lat, pl.ds(2 * t + piece, 1), :]
            dm8[pl.ds(4 * (1 - c) + lat, 1), span] = dmo[lat, pl.ds(2 * t + piece, 1), :]
    dma[w] = dm8[...]
    dm_ops = net.dp_push(lambda peer: dm8, dma.at[w], 16)
    total = small_ref[...] + smo[...]
    for k in range(n):
        tks[k, :, 0:share] = total[:, share * k : share * k + share]
    tkl[w] = tks[w]
    tok_ops = net.dp_push(lambda peer: tks.at[peer], tkl.at[w], 24)
    for name in ("g", "dz", "o", "dy"):
        loads[name].wait()

    @pl.loop(0, 3)
    def _(i):
        sr[after(i, 192), :] = tdot(gv[1 - c, :, chunk(i)], dzv[...])

    sr[0:192, :] = tdot(ov[1 - c], dyv[...])[64:256]
    row_ops.append(net.core_push(sr, rr, 6))
    load("re", rerr_ref, mr, 8)
    loads["ce"].wait()
    dms = split3(dm8[...])
    cs = split3(cs_ref[...])
    left_side = jnp.concatenate([dms[0], dms[1], dms[0], dms[2], dms[1], dms[0]], axis=0)
    right_side = jnp.concatenate([cs[0], cs[0], cs[1], cs[0], cs[1], cs[2]], axis=0)
    for i in range(6):
        mc[256 * i : 256 * i + 256, :] += tdot(left_side[:, 256 * i : 256 * i + 256], right_side)
    wait_all(col_ops)
    mc[QKV0 : QKV0 + 256] += tdot(qv[c, :, 0:256], av[...]) + rc[0:256]
    mc[QKV0 + 256 : FC0] += tdot(qv[c, :, 256:640], av[...])[0:320] + rc[256:576]

    @pl.loop(0, 3)
    def _(i):
        mc[after(i, FC0), :] += tdot(uv[c, :, chunk(i)], mv[...]) + rc[after(i, 576), :]

    out_col = pltpu.make_async_copy(mc, mcol_ref, load_sem.at[0])
    out_col.start()
    loads["re"].wait()
    wait_all(row_ops)

    @pl.loop(0, 3)
    def _(i):
        mr[after(i, 192), :] += tdot(gv[c, :, chunk(i)], dzv[...]) + rr[after(i, 192), :]

    mr[0:192, :] += tdot(ov[c], dyv[...])[64:256] + rr[0:192, :]
    out_row = pltpu.make_async_copy(mr, mrow_ref, load_sem.at[1])
    out_row.start()
    wait_all(dm_ops)
    dmx = dma[...].reshape(8 * n, QKV0)
    part = sum(ndot(wmod_ref[:, 0:QKV0], piece) for piece in split3(dmx))
    dss[...] = part
    dsc[t] = part
    ds_ops = net.tensor_push(dss, dsc.at[t], 32)
    right = right_ref[...]

    def left_part(first, last):
        sides = jnp.concatenate(halves(right[:, first:last]), axis=0).astype(BF)
        high, low = split2(mc[first:last, :])
        got = dot(sides, high) + dot(sides, low)
        return got[0:8] + got[8:16]

    for k, spans in enumerate((((0, 512), (512, 1024), (1024, QKV0)), ((QKV0, FC0),), ((FC0, FC0 + 384), (FC0 + 384, COLS)))):
        got = sum(left_part(*span) for span in spans)
        for i in range(6):
            px[6 * k + i] = got[:, 128 * i : 128 * i + 128]
    row_side = fill(halves(right[:, COLS : COLS + D]) + halves(right[:, COLS + D : COLS + 2 * D]), 128).T.astype(BF)

    def row_chunk(values):
        high, low = split2(values)
        return dot(high, row_side) + dot(low, row_side)

    got = jnp.concatenate([row_chunk(mr[0:192, :]), jnp.zeros((64, 128), F32)], axis=0).T
    for i in range(2):
        px[18 + i] = got[0:8, 128 * i : 128 * i + 128] + got[8:16, 128 * i : 128 * i + 128]
    for i in range(3):
        got = row_chunk(mr[192 + 256 * i : 448 + 256 * i, :]).T
        got = got[16:24] + got[24:32]
        px[20 + 2 * i] = got[:, 0:128]
        px[21 + 2 * i] = got[:, 128:256]
    bias = jnp.concatenate(
        [colsum(dm8[...]), (dbq_ref[c] + dbo[...])[:, 0:576], db1_ref[c] + dbo1[...], jnp.zeros((1, 192), F32)], axis=1
    )
    for i in range(24):
        px[26 + i // 8, i % 8 : i % 8 + 1, :] = bias[:, 128 * i : 128 * i + 128]
    both = hb_ref[...] + hbo[...]
    px[29] = both[0:8]
    px[30] = both[8:16]
    px[31] = jnp.zeros((8, 128), F32)

    def scatter(v, land, per, base):
        own = pl.ds(w * per, per)
        land[w] = v[own]
        return net.dp_push(lambda peer: v.at[pl.ds(peer * per, per)], land.at[w], base)

    def collect(land, v, per, base, ops):
        wait_all(ops)
        own = pl.ds(w * per, per)
        v[own] = sum(land[k] for k in range(1, n)) + land[0]
        return net.dp_push(lambda peer: v.at[own], v.at[own], base)

    ops = scatter(px, pland, P_COUNT // n, 40)
    ops = collect(pland, py, P_COUNT // n, 48, ops)
    wait_all(ds_ops)
    dcond = (dsc[0] + dsc[1] + dsc[2] + dsc[3]) * silu_slope_k(ct_ref[...])
    dtime = sum(tdot(wto_ref[...], piece) for piece in split3(dcond)).reshape(n, 2, share // 2, 8 * n)
    dts[...] = jnp.concatenate([dtime[:, 0], dtime[:, 1]], axis=2)
    dtl[w] = dts[w]
    dt_ops = net.dp_push(lambda peer: dts.at[peer], dtl.at[w], 56)
    wait_all(tok_ops)
    tok = sum(tkl[k] for k in range(1, n)) + tkl[0]
    tok = jnp.concatenate([tok, jnp.zeros((88, 128), F32)], axis=0).T[0:share]
    gsm_ref[:, 0:16] = tok[:, 0:16]
    gsm_ref[:, 16:17] = tok[:, 32:33]
    gsm_ref[:, 1075:1091] = tok[:, 16:32]
    gsm_ref[:, 1091:1093] = tok[:, 33:35]
    wait_all(ops)
    base = 0
    bases = []
    for index, count in enumerate(P_TILES):
        bases.append(gram_schmidt(jnp.concatenate([py[base + k] for k in range(count)], axis=1)))
        base += count
    col_side = fill(halves(bases[0]) + halves(bases[1]) + halves(bases[2]), 128).T.astype(BF)

    def col_chunk(values):
        high, low = split2(values)
        return dot(high, col_side) + dot(low, col_side)

    def put(first, rows, k, tile):
        got = col_chunk(mc[first : first + rows, :])
        if rows % 128:
            got = jnp.concatenate([got, jnp.zeros((128 - rows % 128, 128), F32)], axis=0)
        got = got.T
        got = got[16 * k : 16 * k + 8] + got[16 * k + 8 : 16 * k + 16]
        for i in range(got.shape[1] // 128):
            qx[tile + i] = got[:, 128 * i : 128 * i + 128]

    for i in range(6):
        put(256 * i, 256, 0, 2 * i)
    put(QKV0, 256, 1, 12)
    put(QKV0 + 256, 320, 1, 14)
    for i in range(3):
        put(FC0 + 256 * i, 256, 2, 17 + 2 * i)
    for k, (rows, block) in enumerate(((slice(0, 192), bases[3][:, 0:192]), (slice(192, 960), bases[4]))):
        left = jnp.concatenate(halves(block), axis=0).astype(BF)
        high, low = split2(mr[rows, :])
        got = dot(left, high) + dot(left, low)
        got = got[0:8] + got[8:16]
        for i in range(6):
            qx[23 + 6 * k + i] = got[:, 128 * i : 128 * i + 128]
    for i in range(35, Q_COUNT):
        qx[i] = jnp.zeros((8, 128), F32)
    ops = scatter(qx, qland, Q_COUNT // n, 64)
    gsm_ref[:, 274:1042] = hndot(dcond, a1_ref[...])
    gsm_ref[:, 1042:1043] = jnp.sum(dcond, axis=1, keepdims=True)
    gsm_ref[:, 1043:1075] = hdot(dcond, hot_ref[...])[:, 0:CLASSES]
    offset = 0
    for block, width in zip(bases, (D, D, D, 192, D)):
        left_ref[:, offset : offset + width] = block[:, 0:width]
        offset += width
    gb_ref[...] = jnp.concatenate([py[26 + i // 8, i % 8 : i % 8 + 1, :] for i in range(23)], axis=1)[:, 0:COLS]
    head = jnp.concatenate([py[29], py[30], jnp.zeros((112, 128), F32)], axis=0).T
    gh_ref[...] = head[0:8]
    emit((left_ref, left_out), (gb_ref, gb_out), (gh_ref, gh_out))

    ops = collect(qland, qy, Q_COUNT // n, 72, ops)
    wait_all(dt_ops)
    dtime = sum(dtl[k] for k in range(1, n)) + dtl[0]
    dtime = jnp.concatenate([dtime[:, 0:64], dtime[:, 64:128]], axis=0) * silu_slope_k(t1_ref[...])
    gsm_ref[:, 17:273] = hdot(dtime, tf_ref[...])
    gsm_ref[:, 273:274] = jnp.sum(dtime, axis=1, keepdims=True)

    def left_rows(blocks):
        rows = []
        for block in blocks:
            high, low = halves(block)
            rows += [high, low, high]
        return rows

    def right_rows(blocks):
        rows = []
        for block in blocks:
            high, low = halves(block)
            rows += [high, high, low]
        return rows

    pst_ref[...] = fill(left_rows(bases[:3]), 128).astype(BF)
    proj = jnp.concatenate([bases[3][:, 0:192], jnp.zeros((8, D), F32)], axis=1)
    fc = jnp.concatenate([jnp.zeros((8, 192), F32), bases[4]], axis=1)
    row_stack = fill(left_rows([proj, fc]), 128)
    pc_ref[...] = row_stack.astype(BF)
    row_stack = jnp.concatenate([row_stack, jnp.zeros((128, 64), F32)], axis=1)
    psr_ref[...] = row_stack.T[0:960].astype(BF)
    emit((pst_ref, pst_out), (pc_ref, pc_out), (psr_ref, psr_out), (gsm_ref, gsm_out))
    wait_all(ops)
    qkv = jnp.concatenate([qy[12 + i] for i in range(5)], axis=1)[:, 0:576]
    pieces = [jnp.concatenate([qy[i] for i in range(12)], axis=1), qkv, jnp.concatenate([qy[17 + i] for i in range(6)], axis=1)]
    pad = jnp.zeros((8, 64), F32)
    qc = jnp.concatenate(pieces + [pad], axis=1)
    span = lax.broadcasted_iota(jnp.int32, (8, 2944), 1)
    cuts = [
        jnp.where((span >= first) & (span < last), qc, 0.0) for first, last in ((0, QKV0), (QKV0, FC0), (FC0, COLS))
    ]
    stack = fill(right_rows(cuts), 128)
    qsn_ref[...] = stack.astype(BF)
    qst_ref[...] = stack.T[0:COLS].astype(BF)
    qr = [jnp.concatenate([qy[23 + 6 * k + i] for i in range(6)], axis=1) for k in range(2)]
    qrs_ref[...] = fill(right_rows(qr), 128).astype(BF)
    rightn_ref[:, 0:COLS] = qc[:, 0:COLS]
    rightn_ref[:, COLS : COLS + D] = qr[0]
    rightn_ref[:, COLS + D : COLS + 2 * D] = qr[1]
    emit((qst_ref, qst_out), (qsn_ref, qsn_out), (qrs_ref, qrs_out), (rightn_ref, rightn_out))
    net.finish()
    for op in outs:
        op.wait()
    out_col.wait()
    out_row.wait()


def run_grad(operands, n):
    S = jax.ShapeDtypeStruct
    V = pltpu.VMEM
    rows = operands[0].shape[0]
    lat = 8 * n
    share = D // n
    any_spec = pl.BlockSpec(memory_space=pl.ANY)
    vm = pl.BlockSpec(memory_space=pltpu.VMEM)
    outs = [
        S((COLS, D), F32), S((960, D), F32), S((8, 3264), F32), S((8, 4416), F32),
        S((128, D), BF), S((960, 128), BF), S((128, 960), BF), S((COLS, 128), BF), S((128, 2944), BF), S((128, D), BF),
        S((1, COLS), F32), S((8, 128), F32), S((share, 1093), F32),
    ]
    scratch = [
        V((COLS, D), F32), V((960, D), F32), V((1344, D), F32), V((960, D), F32), V((1344, D), F32), V((960, D), F32),
        V((rows, D), BF), V((rows, D), BF), V((rows, D), BF), V((rows, D), BF),
        V((2, rows, 256), BF), V((2, rows, 640), BF), V((2, rows, D), BF), V((2, rows, D), BF),
        *[V(o.shape, o.dtype) for o in outs[2:]],
        V((4, 8, D), F32), V((40, D), F32), V((1, 640), F32), V((1, D), F32), V((16, 128), F32),
        V((8, QKV0), F32), V((n, 8, QKV0), F32),
        V((4, share, lat), F32), V((share, lat), F32), V((n, share // 2, 128), F32), V((n, share // 2, 128), F32),
        V((n, 40, 128), F32), V((n, 40, 128), F32),
        V((P_COUNT, 8, 128), F32), V((n, P_COUNT // n, 8, 128), F32), V((P_COUNT, 8, 128), F32),
        V((Q_COUNT, 8, 128), F32), V((n, Q_COUNT // n, 8, 128), F32), V((Q_COUNT, 8, 128), F32),
        pltpu.SemaphoreType.DMA((10,)), pltpu.SemaphoreType.DMA((11,)), pltpu.SemaphoreType.DMA((80,)), pltpu.SemaphoreType.DMA((80,)),
    ]
    return pl.pallas_call(
        grad_kernel,
        out_shape=outs,
        in_specs=[any_spec] * 10 + [vm] * 14,
        out_specs=[any_spec] * 13,
        scratch_shapes=scratch,
        compiler_params=pltpu.CompilerParams(collective_id=1, has_side_effects=True, vmem_limit_bytes=60 * 1024 * 1024),
        name="grad",
    )(*operands)


APPLY_IN = (
    "mcol", "mrow", "qst", "psr", "pst", "pc", "qsn", "qrs", "left", "right", "gs", "gb", "gh",
    "cw", "cm", "rw", "rm", "sw", "sm", "bw", "bm", "hw", "hm",
)
APPLY_OUT = ("mcol", "mrow", "cw", "cm", "rw", "rm", "sw", "sm", "bw", "bm", "hw", "hm", "left", "right", "loss")
CUTS = 6


def apply_kernel(w_ref, *refs, n):
    ins = dict(zip(APPLY_IN, refs))
    outs = dict(zip(APPLY_OUT, refs[len(APPLY_IN) :]))
    rest = refs[len(APPLY_IN) + len(APPLY_OUT) :]
    held = [name for name in APPLY_IN if name not in ("left", "right")]
    s = dict(zip(held, rest))
    loss_s, hat_s, sem_in, sem_out = rest[len(held) :]
    share = D // n
    cut = {"mcol": [slice(480 * i, 480 * i + 480) for i in range(CUTS)], "mrow": [slice(480 * i, 480 * i + 480) for i in range(2)]}
    started, finished = {}, []

    def load(name, part=None):
        src, dst = (ins[name], s[name]) if part is None else (ins[name].at[cut[name][part]], s[name].at[cut[name][part]])
        started[name, part] = pltpu.make_async_copy(src, dst, sem_in.at[len(started)])
        started[name, part].start()

    def store(src, dst):
        op = pltpu.make_async_copy(src, dst, sem_out.at[len(finished)])
        op.start()
        finished.append(op)

    for name in ("pst", "qst", "qrs", "pc", "qsn", "psr"):
        load(name)
    for part in range(CUTS):
        load("mcol", part)
        if part == 0:
            for name in ("rw", "rm", "cw", "cm"):
                load(name)
    for part in range(2):
        load("mrow", part)
    for name in ("gs", "sw", "sm", "gb", "bw", "bm", "gh", "hw", "hm"):
        load(name)
    store(ins["left"], outs["left"])
    store(ins["right"], outs["right"])

    def ready(*names):
        for name in names:
            started[name, None].wait()

    def update(weight, moment, grad):
        s[moment][...] = DECAY * s[moment][...] + grad
        s[weight][...] = s[weight][...] - LEARN_RATE * s[moment][...]
        store(s[moment], outs[moment])
        store(s[weight], outs[weight])

    ready("pst", "qst", "qrs", "pc", "qsn")
    place = lax.broadcasted_iota(jnp.int32, (D, 128), 0) == w_ref[0] * share + lax.broadcasted_iota(jnp.int32, (D, 128), 1)
    pick = jnp.where(place, 1.0, 0.0).astype(BF)
    hat_s[...] = tdot(dot(s["pst"][...], pick).astype(BF), s["qsn"][...])[0:share, 0:COLS]
    rows = tdot(dot(s["qrs"][...], pick).astype(BF), s["pc"][...])[0:share]

    def residue(name, part, hat):
        started[name, part].wait()
        span = cut[name][part]
        s[name][span, :] = s[name][span, :] - hat * (1.0 / n)
        store(s[name].at[span], outs[name].at[span])

    def col(part):
        residue("mcol", part, dot(s["qst"][cut["mcol"][part], :], s["pst"][...]))

    def row(part):
        residue("mrow", part, dot(s["psr"][cut["mrow"][part], :], s["qrs"][...]))

    col(0)
    ready("rw", "rm")
    update("rw", "rm", rows)
    col(1)
    ready("cw", "cm")

    @pl.loop(0, share // 8)
    def _(i):
        for r in range(8):
            k = 8 * i + r
            moment = DECAY * s["cm"][k] + hat_s[pl.ds(k, 1), :]
            s["cm"][k] = moment
            s["cw"][k] = s["cw"][k] - LEARN_RATE * moment

    store(s["cm"], outs["cm"])
    store(s["cw"], outs["cw"])
    for part in range(2, CUTS):
        col(part)
    ready("psr")
    for part in range(2):
        row(part)
    ready("gs", "sw", "sm")
    update("sw", "sm", s["gs"][...])
    ready("gb", "bw", "bm", "gh", "hw", "hm")
    update("bw", "bm", s["gb"][...])
    update("hw", "hm", s["gh"][0:1, 0:PATCH_IN])
    loss_s[...] = s["gh"][1:2, 0:1]
    store(loss_s, outs["loss"])
    for op in finished:
        op.wait()


def run_apply(w, operands, n):
    S = jax.ShapeDtypeStruct
    V = pltpu.VMEM
    shapes = {name: operand for name, operand in zip(APPLY_IN, operands)}
    outs = [S(shapes[name].shape, F32) for name in APPLY_OUT[:-1]] + [S((1, 1), F32)]
    held = [V(shapes[name].shape, shapes[name].dtype) for name in APPLY_IN if name not in ("left", "right")]
    any_spec = pl.BlockSpec(memory_space=pl.ANY)
    return pl.pallas_call(
        functools.partial(apply_kernel, n=n),
        out_shape=outs,
        in_specs=[pl.BlockSpec(memory_space=pltpu.SMEM)] + [any_spec] * len(APPLY_IN),
        out_specs=[any_spec] * len(outs),
        scratch_shapes=held + [V((1, 1), F32), V((D // n, COLS), F32), pltpu.SemaphoreType.DMA((32,)), pltpu.SemaphoreType.DMA((32,))],
        compiler_params=pltpu.CompilerParams(vmem_limit_bytes=62 * 1024 * 1024),
        name="apply",
    )(w, *operands)


def position_table():
    quarter = D // 4
    omega = 10000.0 ** (-np.arange(quarter) / quarter)
    place = np.arange(GRID)[:, None] * omega[None, :]
    return jnp.asarray(np.concatenate([np.sin(place), np.cos(place)], axis=1), F32)


def time_features(times):
    half = FREQ // 2
    freqs = jnp.exp(-math.log(10000.0) * jnp.arange(half, dtype=jnp.float32) / half)
    angles = 1000.0 * times[:, None] * freqs[None, :]
    return jnp.concatenate([jnp.cos(angles), jnp.sin(angles)], axis=1)


def small_starts():
    counts = [PATCH_IN, 1, FREQ, 1, D, 1, CLASSES, PATCH_IN, 1, 1]
    starts = [0]
    for amount in counts:
        starts.append(starts[-1] + amount)
    return starts


def cut_parts(array, widths, axis):
    pieces = []
    offset = 0
    for width in widths:
        pieces.append(lax.slice_in_dim(array, offset, offset + width, axis=axis))
        offset = offset + width
    return pieces


def ortho_kernel(x_ref, o_ref):
    count = x_ref.shape[0]
    rows = [x_ref[index] for index in range(count)]
    for index in range(count):
        vector = rows[index]
        vector = vector * lax.rsqrt(jnp.sum(vector * vector, axis=-1, keepdims=True) + TINY)
        o_ref[index] = vector
        for later in range(index + 1, count):
            rows[later] = rows[later] - jnp.sum(rows[later] * vector, axis=-1, keepdims=True) * vector


def orthonormal_all(parts):
    stacked = jnp.stack([jnp.pad(part, ((0, 0), (0, D - part.shape[1]))) for part in parts], axis=1)
    stacked = jnp.pad(stacked, ((0, 0), (0, 8 - len(parts)), (0, 0)))
    out = pl.pallas_call(ortho_kernel, out_shape=jax.ShapeDtypeStruct(stacked.shape, F32), name="ortho")(stacked)
    return [out[:, index, : part.shape[1]] for index, part in enumerate(parts)]


def rounded(values):
    return lax.optimization_barrier(values.astype(BF)).astype(F32)


def silu_slope(values):
    gate = jax.nn.sigmoid(values)
    return gate * (1.0 + values * (1.0 - gate))


def shards_general(
    clean_latents,
    noise_draw,
    timesteps,
    labels,
    col_weights,
    col_moments,
    col_errors,
    row_weights,
    row_moments,
    row_errors,
    bias_weights,
    bias_moments,
    small_weights,
    small_moments,
    head_bias,
    head_moments,
    right_factors,
):
    tensor_size = lax.axis_size("tensor")
    data_size = lax.axis_size("dp")
    tensor_rank = lax.axis_index("tensor")
    data_rank = lax.axis_index("dp")
    batch = clean_latents.shape[0]
    half = batch // 2
    share = D // data_size
    mod_width = 8 * D // tensor_size
    qkv_width = 3 * D // tensor_size
    ffn_width = FF // tensor_size
    proj_rows = D // tensor_size
    count_all = data_size * batch * SEQ * PATCH_IN
    col_widths = [mod_width, qkv_width, ffn_width]
    core = lax.rem(tensor_rank, 2)
    base = tensor_rank - core
    pair = [(index, index + 1 - 2 * (index % 2)) for index in range(tensor_size)]

    def swap(values):
        return lax.ppermute(values, "tensor", pair)

    col_low = col_weights[:, 0, :].astype(BF)
    row_low = row_weights[0].astype(BF).T
    packed = jnp.concatenate(
        [
            col_low[:, mod_width : mod_width + qkv_width],
            row_low[:, :proj_rows],
            col_low[:, mod_width + qkv_width :],
            row_low[:, proj_rows:],
        ],
        axis=1,
    )
    wall = lax.all_gather(lax.all_gather(packed, "dp", axis=0, tiled=True), "tensor", axis=0)
    wall = jnp.stack([wall[:, :, 768 * index : 768 * index + 768] for index in range(3)])
    starts = small_starts()
    small_low = small_weights.astype(BF)
    small_exact = rounded(small_weights)
    picked = jnp.concatenate([small_low[: starts[2]], small_low[starts[7] :]], axis=0)
    emb = lax.all_gather(picked.astype(F32), "dp", axis=1, tiled=True)
    emb = jnp.concatenate([emb[:16], emb[17:33], emb[16:17], emb[33:35], jnp.zeros((5, D), F32)], axis=0)
    w_tin = small_exact[starts[2] : starts[3]]
    b_tin = small_exact[starts[3]]
    w_tout = small_exact[starts[4] : starts[5]]
    b_tout = small_exact[starts[5]]
    table = small_exact[starts[6] : starts[7]]
    bias_exact = rounded(bias_weights[0])
    head_exact = rounded(head_bias)
    w_mod = rounded(col_weights[:, 0, :mod_width])
    bias_all = lax.all_gather(bias_exact, "tensor", axis=0)
    times_all = lax.all_gather(timesteps, "dp", axis=0, tiled=True)
    labels_all = lax.all_gather(labels, "dp", axis=0, tiled=True)
    time_feat = time_features(times_all)
    time_hidden = exact_dot(time_feat, w_tin) + b_tin
    time_act = lax.all_gather(jax.nn.silu(time_hidden), "dp", axis=1, tiled=True)
    onehot = (labels_all[:, None] == jnp.arange(CLASSES, dtype=jnp.int32)[None, :]).astype(F32)
    condition = exact_dot(time_act, w_tout) + b_tout + exact_dot(onehot, table)
    cond_act = jax.nn.silu(condition)
    mod_part = exact_dot(cond_act, w_mod)
    mod_own = lax.psum_scatter(mod_part, "dp", scatter_dimension=0, tiled=True) + bias_exact[:mod_width]
    mod_full = lax.all_gather(mod_own, "tensor", axis=1, tiled=True).reshape(batch, 8, D)
    cond_rows = lax.all_to_all(cond_act, "dp", split_axis=0, concat_axis=1, tiled=True)

    def mine(values):
        return lax.dynamic_slice_in_dim(values, core * half, half, 0)

    ball = jnp.concatenate(
        [
            jnp.pad(bias_all[:, mod_width : mod_width + qkv_width], ((0, 0), (0, 768 - qkv_width))),
            bias_all[:, mod_width + qkv_width :],
        ],
        axis=1,
    )[:, None]
    (a, m, dy, dz, o, dq, du, g, dmod, small, dbq, db1, hb) = run_block(
        base.reshape(1),
        mine(timesteps),
        mine(clean_latents).transpose(0, 2, 1),
        mine(noise_draw).transpose(0, 2, 1),
        mine(mod_full),
        wall,
        position_table(),
        emb,
        head_exact[:, None],
        ball,
        count_all,
    )
    rows = half * SEQ

    def flat(values):
        return values.reshape(rows, values.shape[-1])

    def pick(values, which):
        return lax.dynamic_index_in_dim(values, which, 0, keepdims=False)

    def gradients(which):
        return (
            tdot(flat(a), flat(pick(dq, which))[:, :qkv_width]),
            tdot(flat(m), flat(pick(du, which))),
            tdot(flat(pick(o, which))[:, 64:], flat(dy)),
            tdot(flat(pick(g, which)), flat(dz)),
            pick(dbq, which)[0, :qkv_width],
            pick(db1, which)[0],
        )

    other = swap(gradients(1 - core))
    own = gradients(core)
    g_qkv, g_fc1, g_proj, g_fc2, g_bqkv, g_bfc1 = [left + right for left, right in zip(own, other)]
    dmod_own = dmod.reshape(half, 8 * D)
    dmod_other = swap(dmod_own)
    dmod_group = jnp.where(
        core == 0,
        jnp.concatenate([dmod_own, dmod_other], axis=0),
        jnp.concatenate([dmod_other, dmod_own], axis=0),
    )
    d_mod = lax.dynamic_slice_in_dim(dmod_group, tensor_rank * mod_width, mod_width, 1)
    g_bmod = jnp.sum(d_mod, axis=0)
    g_mod = exact_tdot(cond_rows, d_mod)
    d_mod_all = lax.all_gather(d_mod, "dp", axis=0, tiled=True)
    d_cond = lax.psum(exact_ndot(d_mod_all, w_mod), "tensor") * silu_slope(condition)
    g_table = exact_tdot(onehot, d_cond)
    g_btout = jnp.sum(d_cond, axis=0)
    g_tout = exact_tdot(time_act, d_cond)
    d_time = lax.psum_scatter(exact_ndot(d_cond, w_tout), "dp", scatter_dimension=1, tiled=True)
    d_time = d_time * silu_slope(time_hidden)
    g_btin = jnp.sum(d_time, axis=0)
    g_tin = exact_tdot(time_feat, d_time)
    small_own = lax.psum(lax.psum_scatter(small, "dp", scatter_dimension=1, tiled=True), "tensor") * 0.5
    head_sum, loss_value = lax.psum((hb[:, 0] * 0.5, hb[0, 1] * 0.5), ("dp", "tensor"))
    small_step = jnp.concatenate(
        [
            small_own[:16],
            small_own[32:33],
            g_tin,
            g_btin[None],
            g_tout,
            g_btout[None],
            g_table,
            small_own[16:32],
            small_own[33:34],
            small_own[34:35],
        ],
        axis=0,
    )
    bias_sum = lax.psum(jnp.concatenate([g_bmod, g_bqkv, g_bfc1], axis=0), "dp")
    col_cuts = cut_parts(col_errors[0, 0], col_widths, 1)
    row_cuts = cut_parts(row_errors[0, 0], [proj_rows, ffn_width], 0)
    matrices = [
        g_mod + col_cuts[0],
        g_qkv + col_cuts[1],
        g_fc1 + col_cuts[2],
        g_proj + row_cuts[0],
        g_fc2 + row_cuts[1],
    ]
    right_pieces = cut_parts(right_factors[0], col_widths + [D, D], 1)
    left_local = jnp.concatenate([exact_ndot(right_pieces[i], matrices[i]) for i in range(5)], axis=1)
    left_sum = lax.psum(left_local, "dp")
    bases = orthonormal_all(cut_parts(left_sum, [D, D, D, proj_rows, ffn_width], 1))
    right_local = jnp.concatenate([exact_dot(bases[i], matrices[i]) for i in range(5)], axis=1)
    right_sum = lax.psum(right_local, "dp")
    right_split = cut_parts(right_sum, col_widths + [D, D], 1)
    approx = [exact_tdot(bases[i], right_split[i]) for i in range(5)]
    rest = [matrices[i] - approx[i] / data_size for i in range(5)]
    col_residue = jnp.concatenate(rest[:3], axis=1)[None, None]
    row_residue = jnp.concatenate(rest[3:], axis=0)[None, None]

    def own_columns(values):
        return lax.dynamic_slice_in_dim(values, data_rank * share, share, 1)

    col_step = jnp.concatenate(
        [exact_tdot(own_columns(bases[i]), right_split[i]) for i in range(3)], axis=1
    )[:, None, :]
    row_step = jnp.concatenate(
        [exact_tdot(bases[i], own_columns(right_split[i])) for i in (3, 4)], axis=0
    )[None]
    col_momentum = DECAY * col_moments + col_step
    col_new = col_weights - LEARN_RATE * col_momentum
    row_momentum = DECAY * row_moments + row_step
    row_new = row_weights - LEARN_RATE * row_momentum
    small_momentum = DECAY * small_moments + small_step
    small_new = small_weights - LEARN_RATE * small_momentum
    bias_momentum = DECAY * bias_moments + bias_sum[None]
    bias_new = bias_weights - LEARN_RATE * bias_momentum
    head_momentum = DECAY * head_moments + head_sum
    head_new = head_bias - LEARN_RATE * head_momentum
    left_factors = jnp.concatenate(bases, axis=1)[None]
    right_new = right_sum[None]
    return (
        loss_value,
        col_new,
        col_momentum,
        col_residue,
        row_new,
        row_momentum,
        row_residue,
        bias_new,
        bias_momentum,
        small_new,
        small_momentum,
        head_new,
        head_momentum,
        left_factors,
        right_new,
    )


def shards(
    clean_latents,
    noise_draw,
    timesteps,
    labels,
    col_weights,
    col_moments,
    col_errors,
    row_weights,
    row_moments,
    row_errors,
    bias_weights,
    bias_moments,
    small_weights,
    small_moments,
    head_bias,
    head_moments,
    right_factors,
):
    tensor_size = lax.axis_size("tensor")
    data_size = lax.axis_size("dp")
    tensor_rank = lax.axis_index("tensor")
    data_rank = lax.axis_index("dp")
    batch = clean_latents.shape[0]
    half = batch // 2
    share = D // data_size
    mod_width = 8 * D // tensor_size
    qkv_width = 3 * D // tensor_size
    ffn_width = FF // tensor_size
    proj_rows = D // tensor_size
    count_all = data_size * batch * SEQ * PATCH_IN
    col_widths = [mod_width, qkv_width, ffn_width]
    core = lax.rem(tensor_rank, 2)
    base = tensor_rank - core
    col = col_weights[:, 0]
    col_low = col.astype(BF)
    row_low = row_weights[0].T.astype(BF)
    onehot = (labels[:, None] == jnp.arange(128, dtype=jnp.int32)[None, :]).astype(F32)
    features = jnp.concatenate([time_features(timesteps), onehot], axis=1)
    small_t = small_weights.T
    a, m, dy, dz, o, dq, du, g, cs, ct, t1, a1, tf, hot, wto, dmod, small, dbq, db1, hb = run_step(
        col_low, row_low, features, small_t, bias_weights, timesteps,
        clean_latents.transpose(0, 2, 1), noise_draw.transpose(0, 2, 1), position_table(), head_bias[None],
        data_size, count_all,
    )
    rows = half * SEQ

    def flat(values):
        return values.reshape(values.shape[:-3] + (rows, values.shape[-1]))

    acts = [flat(values) for values in (a, m, dy, dz, o, dq, du, g)]
    errors = [col_errors[0, 0].T, row_errors[0, 0]]
    mcol, mrow, left_all, right_sum, pst, psr, pc, qst, qsn, qrs, gb, gh, gsm = run_grad(
        acts + errors + [dmod, small, dbq, db1, hb, right_factors[0], cs, ct, t1, a1, tf, hot, col_low, wto], data_size
    )
    cres, rres, col_new, col_momentum, rn, rmn, sn, smn, bias_new, bias_momentum, hn, hmn, left_all, right_sum, loss = run_apply(
        data_rank.reshape(1),
        [mcol, mrow, qst, psr, pst, pc, qsn, qrs, left_all, right_sum, gsm, gb, gh]
        + [col_weights, col_moments, row_weights[0].T, row_moments[0].T, small_t, small_moments.T]
        + [bias_weights, bias_moments, head_bias[None], head_moments[None]],
        data_size,
    )
    loss_value = loss[0, 0]
    col_residue, row_residue = cres.T[None, None], rres[None, None]
    row_new, row_momentum = rn.T[None], rmn.T[None]
    small_new, small_momentum = sn.T, smn.T
    head_new, head_momentum = hn[0], hmn[0]
    left_factors, right_new = left_all[None], right_sum[None]
    return (
        loss_value,
        col_new,
        col_momentum,
        col_residue,
        row_new,
        row_momentum,
        row_residue,
        bias_new,
        bias_momentum,
        small_new,
        small_momentum,
        head_new,
        head_momentum,
        left_factors,
        right_new,
    )


def solution(mesh):
    fits = mesh.shape["dp"] == 8 and mesh.shape["tensor"] == 4
    placed = (
        P("dp", None, None),
        P("dp", None, None),
        P("dp"),
        P("dp"),
        P("dp", "tensor", None),
        P("dp", "tensor", None),
        P("dp", "tensor", None, None),
        P("tensor", None, "dp"),
        P("tensor", None, "dp"),
        P("dp", "tensor", None, None),
        P("tensor", None),
        P("tensor", None),
        P(None, "dp"),
        P(None, "dp"),
        P(),
        P(),
        P("tensor", None, None),
    )
    return jax.shard_map(
        shards if fits else shards_general,
        mesh=mesh,
        in_specs=placed,
        out_specs=(
            P(),
            P("dp", "tensor", None),
            P("dp", "tensor", None),
            P("dp", "tensor", None, None),
            P("tensor", None, "dp"),
            P("tensor", None, "dp"),
            P("dp", "tensor", None, None),
            P("tensor", None),
            P("tensor", None),
            P(None, "dp"),
            P(None, "dp"),
            P(),
            P(),
            P("tensor", None, None),
            P("tensor", None, None),
        ),
        check_vma=False,
    )
```

```python
import functools
import math

import jax
import jax.numpy as jnp
import numpy as np
from jax import lax
from jax.experimental import pallas as pl
from jax.experimental.pallas import tpu as pltpu
from jax.sharding import PartitionSpec as P

D = 768
HEADS = 12
HEAD_DIM = 64
FF = 3072
FREQ = 256
GRID = 16
PATCH_IN = 16
CLASSES = 32
SEQ = 256

EPSILON = 1e-06
TINY = 1e-30
DECAY = 0.9
LEARN_RATE = 100.0
TIME_OFFSET = 0.25
F32 = jnp.float32
BF = jnp.bfloat16
SCALE = 1.0 / math.sqrt(HEAD_DIM)
GELU_C = math.sqrt(2.0 / math.pi)


def exact_dot(left, right):
    return jnp.dot(left, right, precision=lax.Precision.HIGHEST, preferred_element_type=F32)


def exact_tdot(left, right):
    return lax.dot_general(left, right, (((0,), (0,)), ((), ())), precision=lax.Precision.HIGHEST, preferred_element_type=F32)


def exact_ndot(left, right):
    return lax.dot_general(left, right, (((1,), (1,)), ((), ())), precision=lax.Precision.HIGHEST, preferred_element_type=F32)


def dot(a,b): return lax.dot_general(a,b,(((1,),(0,)),((),())),preferred_element_type=F32)
def ndot(a,b): return lax.dot_general(a,b,(((1,),(1,)),((),())),preferred_element_type=F32)
def tdot(a,b): return lax.dot_general(a,b,(((0,),(0,)),((),())),preferred_element_type=F32)

def ln(h):
    c=h-jnp.mean(h,axis=-1,keepdims=True)
    v=jnp.mean(c*c,axis=-1,keepdims=True)
    r=lax.rsqrt(v+EPSILON)
    return c*r,r

def ln_back(dout,xh,r,scale):
    dx=dout*(1.0+scale)
    return r*(dx-jnp.mean(dx,axis=-1,keepdims=True)-xh*jnp.mean(dx*xh,axis=-1,keepdims=True))

def colsum(v): return jnp.sum(v,axis=0,keepdims=True)

UNROLL=dict(af=2,ff=4,fb=4,ab=4)

def block_state():
    V=pltpu.VMEM
    return dict(
        wall=V((3,4,D,D),BF), pe=V((SEQ,D),F32), qkv=V((4,4,SEQ,640),BF), p=V((4,12,SEQ,SEQ),BF),
        xh1=V((4,SEQ,D),F32), y=V((4,SEQ,D),F32), h=V((4,SEQ,D),F32), r1=V((4,SEQ,1),F32),
        xh2=V((SEQ,D),F32), z=V((SEQ,D),F32), r2=V((SEQ,1),F32), slope=V((4,SEQ,D),F32),
        a=V((SEQ,D),BF), m=V((SEQ,D),BF), dz=V((SEQ,D),BF), dy=V((SEQ,D),BF),
        o=V((4,SEQ,256),BF), g=V((4,SEQ,D),BF), du=V((4,SEQ,D),BF), dq=V((4,SEQ,640),BF),
        dbq=V((4,1,640),F32), db1=V((4,1,D),F32), out_sem=pltpu.SemaphoreType.DMA((8,)))

class Block:
    def __init__(self,s,times,clean,noise,mod,pe,emb,bh,ball,outs,dmod,small,hb,base,first,count_all,service):
        self.s=s; self.times=times; self.clean=clean; self.noise=noise; self.mod_ref=mod; self.pe=pe; self.emb=emb; self.bh=bh; self.ball=ball
        self.outs=outs; self.dmod=dmod; self.small=small; self.hb=hb; self.base=base; self.first=first; self.count_all=count_all; self.service=service
        self.lo=lax.broadcasted_iota(jnp.int32,(1,128),1)<64
        self.zero=jnp.zeros((),BF)
    def roll(self,v): return pltpu.roll(v.astype(F32),64,1).astype(BF)
    def out(self,lat,name,index,pair):
        s=self.s
        src=s[name].at[pl.ds(self.base,2)] if pair else s[name]
        dst=self.outs[index].at[:,lat] if pair else self.outs[index].at[lat]
        return pltpu.make_async_copy(src,dst,s["out_sem"].at[index])
    def emit(self,lat,name,index,pair=False): self.out(lat,name,index,pair).start()
    def clear(self,lat,name,index,pair=False):
        @pl.when(lat>0)
        def _(): self.out(lat-1,name,index,pair).wait()
    def last(self):
        for name,index,pair in (("a",0,False),("m",1,False),("dy",2,False),("dz",3,False),("o",4,True),("dq",5,True),("du",6,True),("g",7,True)):
            self.out(3,name,index,pair).wait()
    def start(self):
        s=self.s
        self.small[...]=jnp.zeros_like(self.small); self.hb[...]=jnp.zeros_like(self.hb)
        s["dbq"][...]=jnp.zeros_like(s["dbq"]); s["db1"][...]=jnp.zeros_like(s["db1"])
        for i in range(GRID):
            s["pe"][16*i:16*i+16,0:384]=jnp.broadcast_to(self.pe[i:i+1,:],(16,384))
            s["pe"][16*i:16*i+16,384:768]=self.pe[...]
    def mixed(self,lat):
        place=self.first+lat
        t=self.times[place]
        clean=self.clean[place].astype(F32); noise=self.noise[place].astype(F32)
        return t,clean,noise,(t*clean+(1.0-t)*noise).astype(BF)
    def mod(self,lat,i): return self.mod_ref[lat,i:i+1,:]
    def embed(self,lat):
        s=self.s
        mixed=self.mixed(lat)[3]
        h0=tdot(mixed,self.emb[0:16].astype(BF))+self.emb[32:33]+s["pe"][...]
        s["h"][lat]=h0
        xh,r=ln(h0)
        s["xh1"][lat]=xh; s["r1"][lat]=r
        self.clear(lat,"a",0)
        s["a"][...]=(xh*(1.0+self.mod(lat,1))+self.mod(lat,0)).astype(BF)
        self.emit(lat,"a",0)
        self.clear(lat,"o",4,True)
    def softmax(self,v,lat,idx):
        v=v*SCALE
        e=jnp.exp(v-jnp.max(v,axis=-1,keepdims=True))
        p=(e/jnp.sum(e,axis=-1,keepdims=True)).astype(BF)
        self.s["p"][lat,idx]=p
        return p
    def attend(self,lat,j):
        s=self.s; lo=self.lo; zero=self.zero; wall=s["wall"]
        full=(dot(s["a"][...],wall[0,j])[:,0:640]+self.ball[j,:,0:640]).astype(BF)
        s["qkv"][lat,j]=full
        b0,b1,b2,b3,b4=[full[:,128*i:128*i+128] for i in range(5)]
        p0=self.softmax(ndot(jnp.where(lo,b0,zero),self.roll(b0)),lat,3*j)
        p1=self.softmax(ndot(jnp.where(lo,zero,b1),self.roll(b2)),lat,3*j+1)
        p2=self.softmax(ndot(jnp.where(lo,b3,zero),self.roll(b3)),lat,3*j+2)
        o0=pltpu.roll(dot(p0,b1),64,1)
        s["o"][j,:,0:128]=jnp.where(lo,0.0,o0).astype(BF)
        s["o"][j,:,128:256]=pltpu.roll(jnp.where(lo,dot(p2,b4),dot(p1,b2)),64,1).astype(BF)
    def project(self,lat):
        s=self.s
        self.emit(lat,"o",4,True)
        for n in range(3):
            cols=slice(256*n,256*n+256)
            y=sum(ndot(s["o"][j],s["wall"][0,j,cols,512:768]) for j in range(4))+self.emb[33:34,cols]
            s["y"][lat,:,cols]=y
            s["h"][lat,:,cols]+=self.mod(lat,2)[:,cols]*y
    def attn_fwd(self,lat):
        self.service(lat,0)
        self.embed(lat)
        self.service(lat,1)
        for j in range(2): self.attend(lat,j)
        self.service(lat,2)
        for j in range(2,4): self.attend(lat,j)
        self.service(lat,3)
        self.project(lat)
    def fc_in(self,lat):
        s=self.s
        xh,r=ln(s["h"][lat])
        s["xh2"][...]=xh; s["r2"][...]=r
        self.clear(lat,"m",1)
        s["m"][...]=(xh*(1.0+self.mod(lat,4))+self.mod(lat,3)).astype(BF)
        self.emit(lat,"m",1)
        self.clear(lat,"g",7,True)
    def fc_one(self,lat,j):
        s=self.s
        u=dot(s["m"][...],s["wall"][1,j])+self.ball[j,:,768:1536]
        uu=u*u
        th=jnp.tanh(u*(GELU_C+(GELU_C*0.044715)*uu))
        half=0.5+0.5*th
        s["g"][j]=(u*half).astype(BF)
        s["slope"][j]=half*(1.0+(u-u*th)*(GELU_C+(3.0*0.044715*GELU_C)*uu))
    def fc_fwd(self,lat):
        s=self.s
        self.fc_in(lat)
        u=UNROLL["ff"]
        @pl.loop(0,4//u)
        def _(i):
            for k in range(u): self.fc_one(lat,i*u+k)
        self.emit(lat,"g",7,True)
        for n in range(3):
            cols=slice(256*n,256*n+256)
            z=sum(ndot(s["g"][j],s["wall"][2,j,cols,:]) for j in range(4))+self.emb[34:35,cols]
            s["z"][:,cols]=z
    def head(self,lat):
        s=self.s; mod=lambda i: self.mod(lat,i)
        t,clean,noise,_=self.mixed(lat)
        wh=self.emb[16:32].astype(BF)
        h2=s["h"][lat]+mod(5)*s["z"][...]
        xh,r=ln(h2)
        fi=(xh*(1.0+mod(7))+mod(6)).astype(BF)
        pred=ndot(wh,fi)+self.bh[...]
        diff=pred-(clean-noise)
        weight=1.0/(1.0-t+TIME_OFFSET)
        self.hb[0:1,1:2]+=jnp.sum(colsum(weight*diff*diff),axis=1,keepdims=True)*(1.0/self.count_all)
        dpred=2.0*weight*diff*(1.0/self.count_all)
        self.hb[:,0:1]+=jnp.sum(dpred,axis=1,keepdims=True)
        dpl=dpred.astype(BF)
        self.small[16:32]+=dot(dpl,fi)
        dfi=tdot(dpl,wh)
        self.dmod[lat,6:7]=colsum(dfi); self.dmod[lat,7:8]=colsum(dfi*xh)
        dh=ln_back(dfi,xh,r,mod(7))
        s["h"][lat]=dh
        self.dmod[lat,5:6]=colsum(dh*s["z"][...])
        dzf=dh*mod(5)
        self.small[34:35]+=colsum(dzf)
        self.clear(lat,"dz",3)
        s["dz"][...]=dzf.astype(BF)
        self.emit(lat,"dz",3)
        self.clear(lat,"du",6,True)
    def fc_back_one(self,j):
        s=self.s
        du=dot(s["dz"][...],s["wall"][2,j])*s["slope"][j]
        s["du"][j]=du.astype(BF)
        s["db1"][j]+=colsum(du)
    def fc_bwd(self,lat):
        s=self.s; mod=lambda i: self.mod(lat,i)
        u=UNROLL["fb"]
        @pl.loop(0,4//u)
        def _(i):
            for k in range(u): self.fc_back_one(i*u+k)
        self.emit(lat,"du",6,True)
        for n in range(3):
            cols=slice(256*n,256*n+256)
            s["z"][:,cols]=sum(ndot(s["du"][j],s["wall"][1,j,cols,:]) for j in range(4))
        dm=s["z"][...]
        xh=s["xh2"][...]
        self.dmod[lat,3:4]=colsum(dm); self.dmod[lat,4:5]=colsum(dm*xh)
        dh=s["h"][lat]+ln_back(dm,xh,s["r2"][...],mod(4))
        s["h"][lat]=dh
        self.dmod[lat,2:3]=colsum(dh*s["y"][lat])
        dyf=dh*mod(2)
        self.small[33:34]+=colsum(dyf)
        self.clear(lat,"dy",2)
        s["dy"][...]=dyf.astype(BF)
        self.emit(lat,"dy",2)
        self.clear(lat,"dq",5,True)
    def attend_back(self,lat,j):
        s=self.s; lo=self.lo; zero=self.zero; roll=self.roll
        do=dot(s["dy"][...],s["wall"][0,j,:,512:768])
        r4=pltpu.roll(do[:,0:128],64,1).astype(BF); r5=pltpu.roll(do[:,128:256],64,1).astype(BF)
        do0=jnp.where(lo,r4,zero); do1=jnp.where(lo,zero,r5); do2=jnp.where(lo,r5,zero)
        b0,b1,b2,b3,b4=[s["qkv"][lat,j,:,128*i:128*i+128] for i in range(5)]
        def head(h,doh,v):
            p=s["p"][lat,3*j+h]
            dv=tdot(p,doh)
            dp=ndot(doh,v)
            pf=p.astype(F32)
            t=pf*dp
            ds=(t-pf*jnp.sum(t,axis=-1,keepdims=True)).astype(BF)
            return dv,ds
        dv0,ds0=head(0,do0,b1)
        dv1,ds1=head(1,do1,b2)
        dv2,ds2=head(2,do2,b4)
        rb0=roll(b0); rb3=roll(b3)
        n0=jnp.where(lo,dot(ds0,rb0),tdot(ds0,rb0))*SCALE
        n1=jnp.where(lo,dv0,dot(ds1,roll(b2))*SCALE); n2=jnp.where(lo,tdot(ds1,roll(b1))*SCALE,dv1)
        n3=jnp.where(lo,dot(ds2,rb3),tdot(ds2,rb3))*SCALE
        n4=jnp.where(lo,dv2,0.0)
        for i,v in enumerate((n0,n1,n2,n3,n4)):
            cols=slice(128*i,128*i+128)
            s["dq"][j,:,cols]=v.astype(BF)
            s["dbq"][j,:,cols]+=colsum(v)
    def attn_bwd(self,lat):
        s=self.s; mod=lambda i: self.mod(lat,i)
        u=UNROLL["ab"]
        @pl.loop(0,4//u)
        def _(i):
            for k in range(u): self.attend_back(lat,i*u+k)
        self.emit(lat,"dq",5,True)
        for n in range(3):
            cols=slice(256*n,256*n+256)
            s["z"][:,cols]=sum(ndot(s["dq"][j],s["wall"][0,j,cols,0:640]) for j in range(4))
        da=s["z"][...]
        xh=s["xh1"][lat]
        self.dmod[lat,0:1]=colsum(da); self.dmod[lat,1:2]=colsum(da*xh)
        dh=s["h"][lat]+ln_back(da,xh,s["r1"][lat],mod(1))
        self.small[32:33]+=colsum(dh)
        self.small[0:16]+=dot(self.mixed(lat)[3],dh.astype(BF))

    def run(self,ready=lambda: None):
        @pl.loop(0,4)
        def _(lat): self.attn_fwd(lat)
        ready()
        @pl.loop(0,4)
        def _(lat):
            for phase in (self.fc_fwd,self.head,self.fc_bwd,self.attn_bwd): phase(lat)
        self.last()

def block_kernel(times_ref,base_ref,clean_ref,noise_ref,mod_ref,wall_ref,pe_ref,emb_ref,bh_ref,ball_ref,*rest,count_all,names):
    outs=rest[0:8]; dmod,small,dbq,db1,hb=rest[8:13]
    s=dict(zip(names,rest[13:13+len(names)])); wsem=rest[-1]
    cp=pltpu.make_async_copy(wall_ref,s["wall"],wsem); cp.start()
    base=base_ref[0]
    b=Block(s,times_ref,clean_ref,noise_ref,mod_ref,pe_ref,emb_ref,bh_ref,ball_ref,outs,dmod,small,hb,base,0,count_all,lambda lat,pos: None)
    b.start()
    cp.wait()
    b.run()
    for k in range(2):
        dbq[k]=s["dbq"][base+k]; db1[k]=s["db1"][base+k]

def run_block(base,times,clean,noise,mod,wall,pe,emb,bh,ball,count_all):
    L=clean.shape[0]
    S=jax.ShapeDtypeStruct
    outs=[S((L,SEQ,D),BF)]*4+[S((2,L,SEQ,256),BF),S((2,L,SEQ,640),BF),S((2,L,SEQ,768),BF),S((2,L,SEQ,768),BF),
        S((L,8,D),F32),S((40,D),F32),S((2,1,640),F32),S((2,1,768),F32),S((PATCH_IN,128),F32)]
    st=block_state(); names=tuple(st)
    vm=pl.BlockSpec(memory_space=pltpu.VMEM); anys=pl.BlockSpec(memory_space=pl.ANY); sm=pl.BlockSpec(memory_space=pltpu.SMEM)
    return pl.pallas_call(functools.partial(block_kernel,count_all=count_all,names=names),
        out_shape=outs,in_specs=[sm,sm,vm,vm,vm,anys,vm,vm,vm,vm],out_specs=[anys]*8+[vm]*5,
        scratch_shapes=list(st.values())+[pltpu.SemaphoreType.DMA(())],
        compiler_params=pltpu.CompilerParams(vmem_limit_bytes=62*1024*1024),name="block")(times,base,clean,noise,mod,wall,pe,emb,bh,ball)


MESH = pl.DeviceIdType.MESH
HI = lax.Precision.HIGHEST


def hdot(a, b):
    return lax.dot_general(a, b, (((1,), (0,)), ((), ())), precision=HI, preferred_element_type=F32)


def hndot(a, b):
    return lax.dot_general(a, b, (((1,), (1,)), ((), ())), precision=HI, preferred_element_type=F32)


def htdot(a, b):
    return lax.dot_general(a, b, (((0,), (0,)), ((), ())), precision=HI, preferred_element_type=F32)


def split2(values):
    first = values.astype(BF)
    return first, (values - first.astype(F32)).astype(BF)


def split3(values):
    first, rest = values.astype(BF), values
    rest = rest - first.astype(F32)
    second = rest.astype(BF)
    return first, second, (rest - second.astype(F32)).astype(BF)


def silu_slope_k(values):
    gate = 1.0 / (1.0 + jnp.exp(-values))
    return gate * (1.0 + values * (1.0 - gate))


class Peers:
    def __init__(self, send_sem, recv_sem):
        self.w = lax.axis_index("dp")
        self.t = lax.axis_index("tensor")
        self.n = lax.axis_size("dp")
        self.tn = lax.axis_size("tensor")
        self.c = lax.rem(self.t, 2)
        self.sib = self.t + 1 - 2 * self.c
        self.send_sem, self.recv_sem = send_sem, recv_sem
        self.pending = []

    def barrier(self):
        bar = pltpu.get_barrier_semaphore()
        for i in range(1, self.n):
            pl.semaphore_signal(bar, inc=1, device_id=(lax.rem(self.w + i, self.n), self.t), device_id_type=MESH)
        for i in range(1, self.tn):
            pl.semaphore_signal(bar, inc=1, device_id=(self.w, lax.rem(self.t + i, self.tn)), device_id_type=MESH)

    def ready(self):
        pl.semaphore_wait(pltpu.get_barrier_semaphore(), self.n - 1 + self.tn - 1)

    def copy(self, src, dst, index, device):
        op = pltpu.make_async_remote_copy(
            src_ref=src,
            dst_ref=dst,
            send_sem=self.send_sem.at[index],
            recv_sem=self.recv_sem.at[index],
            device_id=device,
            device_id_type=MESH,
        )
        op.start()
        self.pending.append(op)
        return op

    def dp_push(self, src_of, dst, base):
        ops = []
        for i in range(1, self.n):
            peer = lax.rem(self.w + i, self.n)
            ops.append(self.copy(src_of(peer), dst, base + i - 1, (peer, self.t)))
        return ops

    def tensor_push(self, src, dst, base):
        ops = []
        for i in range(1, self.tn):
            ops.append(self.copy(src, dst, base + i - 1, (self.w, lax.rem(self.t + i, self.tn))))
        return ops

    def core_push(self, src, dst, index):
        return self.copy(src, dst, index, (self.w, self.sib))

    def finish(self):
        for op in self.pending:
            op.wait_send()


def wait_all(ops):
    for op in ops:
        op.wait_recv()


P_TILES = (6, 6, 6, 2, 6)
P_COUNT = 32
Q_COUNT = 40
QKV0, FC0 = 1536, 2112
COLS = 2880


def halves(block):
    high = block.astype(BF).astype(F32)
    return [high, block - high]


def fill(rows, total):
    used = sum(row.shape[0] for row in rows)
    return jnp.concatenate(rows + [jnp.zeros((total - used, rows[0].shape[1]), F32)], axis=0)


AUX = ("cs", "ct", "t1", "a1", "tf", "hot", "wto", "dmod", "small", "dbq", "db1", "hb")


def step_kernel(
    col_ref, row_hbm, smt_ref, bias_ref, times_ref, labels_ref, freq_ref, clean_ref, noise_ref, pe_ref, bh_ref, *rest, names, count_all
):
    outs, aux_out, rest = rest[:8], rest[8 : 8 + len(AUX)], rest[8 + len(AUX) :]
    s = dict(zip(names, rest[: len(names)]))
    aux, rest = dict(zip(AUX, rest[len(names) :])), rest[len(names) + len(AUX) :]
    mod_ref, emb_ref, ball_ref = rest[:3]
    row_ref, pk_ref, pack_ref, bhs, bmod_ref, pkl, ems, eml, a1s, a1l, css, csl, mps, mpl_, mos, mol, bal, local_sem, wsend, wrecv, send_sem, recv_sem = rest[3:]
    wall_ref = s["wall"]
    cs_ref, ct_ref, t1_ref, a1_ref, tf_ref, hot_ref, wto_ref = [aux[name] for name in AUX[:7]]
    net = Peers(send_sem, recv_sem)
    w, t, c, n = net.w, net.t, net.c, net.n
    share = D // n
    half = share // 2
    x, z, y = t // 2, w // 2, lax.rem(w, 2)
    net.barrier()
    rows_in = pltpu.make_async_copy(row_hbm, row_ref, local_sem.at[0])
    rows_in.start()
    sub = lax.broadcasted_iota(jnp.int32, (8, 1), 0)
    when, label = jnp.zeros((8, 1), F32), jnp.zeros((8, 1), jnp.int32)
    for k in range(8):
        when = jnp.where(sub == k, times_ref[k], when)
        label = jnp.where(sub == k, labels_ref[k], label)
    angles = 1000.0 * when * freq_ref[...]
    pk_ref[:, 0:128] = jnp.cos(angles)
    pk_ref[:, 128:256] = jnp.sin(angles)
    pk_ref[:, 256:384] = jnp.where(label == lax.broadcasted_iota(jnp.int32, (8, 128), 1), 1.0, 0.0)
    rows_in.wait()
    wmod_ref = col_ref.at[:, 0:QKV0]
    pack_ref[0, :, 0:576] = col_ref[:, QKV0:FC0]
    pack_ref[0, :, 576:768] = row_ref[:, 0:192].astype(BF)
    pack_ref[1] = col_ref[:, FC0:COLS]
    pack_ref[2] = row_ref[:, 192:960].astype(BF)
    own = []

    def place(q, j, v):
        return wall_ref.at[q, j, pl.ds(pl.multiple_of(share * v, 32), share)]

    for q in range(3):
        op = pltpu.make_async_copy(pack_ref.at[q], place(q, t, w), local_sem.at[q])
        op.start()
        own.append(op)
    pkl[w] = pk_ref[...]
    rest = smt_ref.shape[1]
    emb = jnp.concatenate(
        [smt_ref[:, 0:16], smt_ref[:, rest - 18 : rest - 2], smt_ref[:, 16:17], smt_ref[:, rest - 2 : rest], jnp.zeros((share, 5), F32)],
        axis=1,
    )
    third = share // 3
    emb = jnp.concatenate([emb[0:third], emb[third : 2 * third], emb[2 * third : share], jnp.zeros((third, 8), F32)], axis=1)
    ems[...] = emb.astype(BF)
    eml[w] = ems[...]
    bias = bias_ref[...].astype(BF).astype(F32)
    bmod_ref[...] = bias[:, 0:QKV0]
    bal[t] = jnp.concatenate([bias[:, QKV0:FC0], jnp.zeros((1, 192), F32), bias[:, FC0:COLS]], axis=1)
    net.ready()
    pk_ops = net.dp_push(lambda peer: pk_ref, pkl.at[w], 0)
    em_ops = net.dp_push(lambda peer: ems, eml.at[w], 7)
    ba_ops = net.tensor_push(bal.at[t], bal.at[t], 14)

    zs = [z, z + 1 - 2 * lax.rem(z, 2), lax.rem(z + 2, 4), 3 - z]
    xo = 1 - x
    mine, across = 2 * x + c, 2 * xo + c
    wys = [2 * zs[k] + y for k in range(4)]
    wos = [2 * zs[k] + (1 - y) for k in range(4)]
    to_zs = [(wys[k], t) for k in range(4)]
    wy, wo, to_z = wys.__getitem__, wos.__getitem__, to_zs.__getitem__
    to_x, to_y, to_core = (w, across), (2 * z + (1 - y), t), (w, net.sib)
    sends = []

    def piece_copy(index, q, j, v, device, own_block):
        slot = place(q, j, v)
        return pltpu.make_async_remote_copy(
            src_ref=pack_ref.at[q] if own_block else slot, dst_ref=slot, send_sem=wsend.at[index],
            recv_sem=wrecv.at[q, j, v], device_id=device, device_id_type=MESH,
        )

    def send(q, j, v, device, own_block=False):
        sends.append((len(sends), q, j, v, device, own_block))
        piece_copy(*sends[-1]).start()

    def arrived(q, j, v):
        piece_copy(0, q, j, v, to_core, False).wait_recv()

    def column(q, k):
        if k == 0:
            send(q, mine, w, to_z(1), True)
            send(q, mine, w, to_z(2), True)
        else:
            arrived(q, mine, wy(k))
            if k == 2:
                send(q, mine, wy(2), to_z(1))
        send(q, mine, wy(k), to_x, k == 0)
        send(q, mine, wy(k), to_y, k == 0)
        send(q, mine, wy(k), to_core, k == 0)

    def by_y(q, k):
        return q == 0 and k == 3

    def side(q, k):
        arrived(q, across, wy(k))
        if by_y(q, k):
            send(q, across, wy(k), to_y)
        send(q, across, wy(k), to_core)
        arrived(q, mine, wo(k))
        if not by_y(q, k):
            send(q, mine, wo(k), to_x)
        send(q, mine, wo(k), to_core)

    def corner(q, k):
        arrived(q, across, wo(k))
        send(q, across, wo(k), to_core)

    first_hop, last_hop = {1: to_x}, {1: to_y}

    def level(q, k):
        return (mine, wy(k)), ((across, wy(k)) if q == 1 else (mine, wo(k)))

    def begin(q):
        send(q, mine, w, first_hop[q], True)
        send(q, mine, w, to_z(1), True)
        send(q, mine, w, to_z(2), True)
        send(q, mine, w, last_hop[q], True)
        send(q, mine, w, to_core, True)

    def second(q):
        j, v = level(q, 0)[1]
        arrived(q, j, v)
        for device in (to_z(1), to_z(2), last_hop[q], to_core):
            send(q, j, v, device)

    def along(q, k):
        for j, v in level(q, k):
            arrived(q, j, v)
            if k == 2:
                send(q, j, v, to_z(1))
            send(q, j, v, last_hop[q])
            send(q, j, v, to_core)

    def far(q, k):
        last = (mine, wo(k)) if q == 1 else (across, wy(k))
        for j, v in (last, (across, wo(k))):
            arrived(q, j, v)
            send(q, j, v, to_core)

    def chain0():
        wait_all(pk_ops)
        feats = pkl[...].reshape(8 * n, 384)
        tf_ref[...] = feats[:, 0:FREQ]
        hot_ref[...] = feats[:, FREQ:384]
        small = smt_ref[...].astype(BF).astype(F32)
        t1 = hndot(small[:, 17:273], tf_ref[...]) + small[:, 273:274]
        t1_ref[...] = t1
        act = t1 / (1.0 + jnp.exp(-t1))
        a1s[...] = jnp.concatenate([act[0:half], act[half:share]], axis=1)
        a1l[w] = a1s[...]
        return net.dp_push(lambda peer: a1s, a1l.at[w], 17)

    def chain1(ops):
        wait_all(ops)
        for k in range(n):
            a1_ref[share * k : share * k + half] = a1l[k][:, 0:64]
            a1_ref[share * k + half : share * k + share] = a1l[k][:, 64:128]
        small = smt_ref[...].astype(BF).astype(F32)
        cond = hdot(small[:, 274:1042], a1_ref[...]) + small[:, 1042:1043]
        cond = cond + hndot(small[:, 1043:1075], hot_ref[:, 0:CLASSES])
        ct_ref[...] = cond
        act = cond / (1.0 + jnp.exp(-cond))
        css[...] = jnp.concatenate([act[0:half], act[half:share]], axis=1)
        csl[w] = css[...]
        cs_ops = net.dp_push(lambda peer: css, csl.at[w], 24)
        parts = [tdot(piece, wmod_ref[...]) for piece in split3(act)]
        mps[...] = (parts[0] + parts[1] + parts[2]).reshape(n, 8, QKV0)
        mpl_[w] = mps[w]
        return cs_ops, net.dp_push(lambda peer: mps.at[peer], mpl_.at[w], 31)

    def chain2(ops):
        wait_all(ops)
        total = mpl_[0]
        for k in range(1, n):
            total = total + mpl_[k]
        mos[...] = total + bmod_ref[...]
        mol[t] = mos[...]
        return net.tensor_push(mos, mol.at[t], 38)

    def chain3(ops):
        wait_all(em_ops)
        rows = []
        for k in range(n):
            piece = eml[k].astype(F32)
            rows += [piece[:, 40 * i : 40 * i + 40] for i in range(3)]
        rows = jnp.concatenate(rows, axis=0)
        emb_ref[...] = jnp.concatenate([rows, jnp.zeros((D, 88), F32)], axis=1).T[0:40]
        wait_all(ba_ops)
        ball_ref[...] = bal[...]
        wait_all(ops)
        for lat in range(4):
            for j in range(4):
                for piece in range(2):
                    mod_ref[lat, 2 * j + piece : 2 * j + piece + 1, :] = mol[j, pl.ds(4 * c + lat, 1), D * piece : D * piece + D]

    column(0, 0)
    ops = chain0()
    column(0, 1)
    side(0, 0)
    column(0, 2)
    cs_ops, ops = chain1(ops)
    side(0, 1)
    corner(0, 0)
    column(0, 3)
    side(0, 2)
    begin(1)
    column(2, 0)
    corner(0, 1)
    side(0, 3)
    ops = chain2(ops)
    corner(0, 2)
    corner(0, 3)
    second(1)
    column(2, 1)
    chain3(ops)

    def other_core(q):
        for j in (2 * x + 1 - c, 2 * xo + 1 - c):
            for v in range(n):
                arrived(q, j, v)

    other_core(0)
    own[0].wait()
    plan = (
        (along, 1, 1), (side, 2, 0), (column, 2, 2), (corner, 2, 0), (along, 1, 2), (side, 2, 1), (column, 2, 3), (corner, 2, 1),
        None, (side, 2, 2), None, (along, 1, 3), (side, 2, 3), (corner, 2, 2),
    )
    slots = {i: [functools.partial(*item)] for i, item in enumerate(plan) if item}
    rest = [functools.partial(far, 1, k) for k in range(4)] + [functools.partial(corner, 2, 3)]

    def service(lat, pos):
        for index, todo in slots.items():
            if index % 4 == pos:
                for item in todo:
                    pl.when(lat == index // 4)(item)

    def rows_out():
        wait_all(cs_ops)
        rows = []
        for k in range(n):
            rows += [csl[k][:, 0:64], csl[k][:, 64:128]]
        rows = jnp.concatenate(rows, axis=0)
        a1s_all = jnp.concatenate([rows, jnp.zeros((D, 64), F32)], axis=1).T
        cs_all = a1s_all[0:64].reshape(n, 8, D)
        picked = jnp.zeros((8, D), F32)
        for k in range(n):
            picked = jnp.where(w == k, cs_all[k], picked)
        cs_ref[...] = picked
        wto_ref[...] = smt_ref[:, 274:1042].astype(BF)

    def ready():
        for item in rest:
            item()
        for q in (1, 2):
            other_core(q)
            own[q].wait()

    block = Block(
        s, times_ref, clean_ref, noise_ref, mod_ref, pe_ref, emb_ref, bhs, ball_ref, outs,
        aux["dmod"], aux["small"], aux["hb"], 2 * x, 4 * c, count_all, service,
    )
    bhs[...] = tdot(bh_ref[...].astype(BF), jnp.ones((1, SEQ), BF))
    block.start()
    block.run(ready)
    rows_out()
    for k in range(2):
        aux["dbq"][k] = s["dbq"][2 * x + k]
        aux["db1"][k] = s["db1"][2 * x + k]
    copies = [pltpu.make_async_copy(aux[name], aux_out[i], local_sem.at[3 + i]) for i, name in enumerate(AUX)]
    for op in copies:
        op.start()
    for record in sends:
        piece_copy(*record).wait_send()
    net.finish()
    for op in copies:
        op.wait()


def run_step(col, row, smt, bias, times, labels, freq, clean, noise, pe, bh, n, count_all):
    S = jax.ShapeDtypeStruct
    V = pltpu.VMEM
    DMA = pltpu.SemaphoreType.DMA
    share = D // n
    lat = 8 * n
    half = 4
    any_spec = pl.BlockSpec(memory_space=pl.ANY)
    vm = pl.BlockSpec(memory_space=pltpu.VMEM)
    aux = [
        ((8, D), F32), ((share, lat), F32), ((share, lat), F32), ((D, lat), F32), ((lat, FREQ), F32), ((lat, 128), F32), ((share, D), BF),
        ((half, 8, D), F32), ((40, D), F32), ((2, 1, 640), F32), ((2, 1, D), F32), ((PATCH_IN, 128), F32),
    ]
    outs = [S((half, SEQ, D), BF)] * 4 + [S((2, half, SEQ, width), BF) for width in (256, 640, D, D)]
    outs += [S(*a) for a in aux]
    state = block_state()
    scratch = list(state.values()) + [V(*a) for a in aux] + [
        V((half, 8, D), F32), V((40, D), F32), V((4, 1, QKV0), F32),
        V((share, 960), F32), V((8, 384), F32), V((3, share, D), BF), V((PATCH_IN, SEQ), F32), V((1, QKV0), F32),
        V((n, 8, 384), F32), V((share // 3, 128), BF), V((n, share // 3, 128), BF),
        V((share // 2, 128), F32), V((n, share // 2, 128), F32), V((share // 2, 128), F32), V((n, share // 2, 128), F32),
        V((n, 8, QKV0), F32), V((n, 8, QKV0), F32), V((8, QKV0), F32), V((4, 8, QKV0), F32), V((4, 1, QKV0), F32),
        DMA((3 + len(AUX),)), DMA((120,)), DMA((3, 4, n)), DMA((41,)), DMA((41,)),
    ]
    return pl.pallas_call(
        functools.partial(step_kernel, names=tuple(state), count_all=count_all),
        out_shape=outs,
        in_specs=[vm, any_spec, vm, vm] + [pl.BlockSpec(memory_space=pltpu.SMEM)] * 2 + [vm] * 5,
        out_specs=[any_spec] * len(outs),
        scratch_shapes=scratch,
        compiler_params=pltpu.CompilerParams(collective_id=0, has_side_effects=True, vmem_limit_bytes=62 * 1024 * 1024),
        name="step",
    )(col, row, smt, bias, times, labels, freq, clean, noise, pe, bh)


def gram_schmidt(block):
    rows = lax.broadcasted_iota(jnp.int32, (8, 1), 0)
    for index in range(8):
        row = block[index : index + 1]
        row = row * lax.rsqrt(jnp.sum(row * row, axis=-1, keepdims=True) + TINY)
        inner = jnp.sum(block * row, axis=-1, keepdims=True)
        inner = jnp.where(rows > index, inner, 0.0)
        block = jnp.where(rows == index, row, block - inner * row)
    return block


def grad_kernel(
    a_ref, m_ref, dy_ref, dz_ref, o_ref, dq_ref, du_ref, g_ref, cerr_ref, rerr_ref,
    dmod_ref, small_ref, dbq_ref, db1_ref, hb_ref, right_ref, cs_ref, ct_ref, t1_ref, a1_ref, tf_ref, hot_ref, wmod_ref, wto_ref,
    mcol_ref, mrow_ref, left_out, rightn_out, pst_out, psr_out, pc_out, qst_out, qsn_out, qrs_out, gb_out, gh_out, gsm_out,
    mc, mr, sc, sr, rc, rr, av, mv, dyv, dzv, ov, qv, uv, gv,
    left_ref, rightn_ref, pst_ref, psr_ref, pc_ref, qst_ref, qsn_ref, qrs_ref, gb_ref, gh_ref, gsm_ref,
    dmo, smo, dbo, dbo1, hbo, dm8, dma, dsc, dss, dts, dtl, tks, tkl, px, pland, py, qx, qland, qy,
    load_sem, out_sem, send_sem, recv_sem,
):
    net = Peers(send_sem, recv_sem)
    outs = []

    def emit(*pairs):
        for src, dst in pairs:
            op = pltpu.make_async_copy(src, dst, out_sem.at[len(outs)])
            op.start()
            outs.append(op)

    w, t, c = net.w, net.t, net.c
    n = net.n
    share = D // n
    loads = {}

    def load(name, src, dst, index):
        op = pltpu.make_async_copy(src, dst, load_sem.at[index])
        op.start()
        loads[name] = op

    net.barrier()
    load("q", dq_ref, qv, 9)
    load("a", a_ref, av, 1)
    load("u", du_ref, uv, 0)
    load("m", m_ref, mv, 2)
    def chunk(i, size=256):
        return pl.ds(pl.multiple_of(i * size, size), size)

    def after(i, first):
        return pl.ds(pl.multiple_of(first + 256 * i, 64), 256)

    for name in ("q", "a"):
        loads[name].wait()
    col_ops, row_ops = [], []
    load("g", g_ref, gv, 3)
    load("dz", dz_ref, dzv, 4)
    sc[0:256] = tdot(qv[1 - c, :, 0:256], av[...])
    sc[256:576] = tdot(qv[1 - c, :, 256:640], av[...])[0:320]
    net.ready()
    side = [
        net.core_push(dmod_ref, dmo, 0),
        net.core_push(small_ref, smo, 1),
        net.core_push(dbq_ref.at[1 - c], dbo, 2),
        net.core_push(db1_ref.at[1 - c], dbo1, 9),
        net.core_push(hb_ref, hbo, 10),
    ]

    col_ops.append(net.core_push(sc.at[0:576], rc.at[0:576], 3))
    for name in ("u", "m"):
        loads[name].wait()
    load("o", o_ref, ov, 5)
    load("dy", dy_ref, dyv, 6)
    load("ce", cerr_ref, mc, 7)

    @pl.loop(0, 3)
    def _(i):
        sc[after(i, 576), :] = tdot(uv[1 - c, :, chunk(i)], mv[...])

    col_ops.append(net.core_push(sc.at[576:1344], rc.at[576:1344], 4))
    wait_all(side)
    for lat in range(4):
        for piece in range(2):
            span = slice(D * piece, D * piece + D)
            dm8[pl.ds(4 * c + lat, 1), span] = dmod_ref[lat, pl.ds(2 * t + piece, 1), :]
            dm8[pl.ds(4 * (1 - c) + lat, 1), span] = dmo[lat, pl.ds(2 * t + piece, 1), :]
    dma[w] = dm8[...]
    dm_ops = net.dp_push(lambda peer: dm8, dma.at[w], 16)
    total = small_ref[...] + smo[...]
    for k in range(n):
        tks[k, :, 0:share] = total[:, share * k : share * k + share]
    tkl[w] = tks[w]
    tok_ops = net.dp_push(lambda peer: tks.at[peer], tkl.at[w], 24)
    for name in ("g", "dz", "o", "dy"):
        loads[name].wait()

    @pl.loop(0, 3)
    def _(i):
        sr[after(i, 192), :] = tdot(gv[1 - c, :, chunk(i)], dzv[...])

    sr[0:192, :] = tdot(ov[1 - c], dyv[...])[64:256]
    row_ops.append(net.core_push(sr, rr, 6))
    load("re", rerr_ref, mr, 8)
    loads["ce"].wait()
    dms = split3(dm8[...])
    cs = split3(cs_ref[...])
    left_side = jnp.concatenate([dms[0], dms[1], dms[0], dms[2], dms[1], dms[0]], axis=0)
    right_side = jnp.concatenate([cs[0], cs[0], cs[1], cs[0], cs[1], cs[2]], axis=0)
    for i in range(6):
        mc[256 * i : 256 * i + 256, :] += tdot(left_side[:, 256 * i : 256 * i + 256], right_side)
    wait_all(col_ops)
    mc[QKV0 : QKV0 + 256] += tdot(qv[c, :, 0:256], av[...]) + rc[0:256]
    mc[QKV0 + 256 : FC0] += tdot(qv[c, :, 256:640], av[...])[0:320] + rc[256:576]

    @pl.loop(0, 3)
    def _(i):
        mc[after(i, FC0), :] += tdot(uv[c, :, chunk(i)], mv[...]) + rc[after(i, 576), :]

    out_col = pltpu.make_async_copy(mc, mcol_ref, load_sem.at[0])
    out_col.start()
    loads["re"].wait()
    wait_all(row_ops)

    @pl.loop(0, 3)
    def _(i):
        mr[after(i, 192), :] += tdot(gv[c, :, chunk(i)], dzv[...]) + rr[after(i, 192), :]

    mr[0:192, :] += tdot(ov[c], dyv[...])[64:256] + rr[0:192, :]
    out_row = pltpu.make_async_copy(mr, mrow_ref, load_sem.at[1])
    out_row.start()
    wait_all(dm_ops)
    dmx = dma[...].reshape(8 * n, QKV0)
    part = sum(ndot(wmod_ref[:, 0:QKV0], piece) for piece in split3(dmx))
    dss[...] = part
    dsc[t] = part
    ds_ops = net.tensor_push(dss, dsc.at[t], 32)
    right = right_ref[...]

    def left_part(first, last):
        sides = jnp.concatenate(halves(right[:, first:last]), axis=0).astype(BF)
        high, low = split2(mc[first:last, :])
        got = dot(sides, high) + dot(sides, low)
        return got[0:8] + got[8:16]

    for k, spans in enumerate((((0, 512), (512, 1024), (1024, QKV0)), ((QKV0, FC0),), ((FC0, FC0 + 384), (FC0 + 384, COLS)))):
        got = sum(left_part(*span) for span in spans)
        for i in range(6):
            px[6 * k + i] = got[:, 128 * i : 128 * i + 128]
    row_side = fill(halves(right[:, COLS : COLS + D]) + halves(right[:, COLS + D : COLS + 2 * D]), 128).T.astype(BF)

    def row_chunk(values):
        high, low = split2(values)
        return dot(high, row_side) + dot(low, row_side)

    got = jnp.concatenate([row_chunk(mr[0:192, :]), jnp.zeros((64, 128), F32)], axis=0).T
    for i in range(2):
        px[18 + i] = got[0:8, 128 * i : 128 * i + 128] + got[8:16, 128 * i : 128 * i + 128]
    for i in range(3):
        got = row_chunk(mr[192 + 256 * i : 448 + 256 * i, :]).T
        got = got[16:24] + got[24:32]
        px[20 + 2 * i] = got[:, 0:128]
        px[21 + 2 * i] = got[:, 128:256]
    bias = jnp.concatenate(
        [colsum(dm8[...]), (dbq_ref[c] + dbo[...])[:, 0:576], db1_ref[c] + dbo1[...], jnp.zeros((1, 192), F32)], axis=1
    )
    for i in range(24):
        px[26 + i // 8, i % 8 : i % 8 + 1, :] = bias[:, 128 * i : 128 * i + 128]
    both = hb_ref[...] + hbo[...]
    px[29] = both[0:8]
    px[30] = both[8:16]
    px[31] = jnp.zeros((8, 128), F32)

    def scatter(v, land, per, base):
        own = pl.ds(w * per, per)
        land[w] = v[own]
        return net.dp_push(lambda peer: v.at[pl.ds(peer * per, per)], land.at[w], base)

    def collect(land, v, per, base, ops):
        wait_all(ops)
        own = pl.ds(w * per, per)
        v[own] = sum(land[k] for k in range(1, n)) + land[0]
        return net.dp_push(lambda peer: v.at[own], v.at[own], base)

    ops = scatter(px, pland, P_COUNT // n, 40)
    ops = collect(pland, py, P_COUNT // n, 48, ops)
    wait_all(ds_ops)
    dcond = (dsc[0] + dsc[1] + dsc[2] + dsc[3]) * silu_slope_k(ct_ref[...])
    dtime = sum(tdot(wto_ref[...], piece) for piece in split3(dcond)).reshape(n, 2, share // 2, 8 * n)
    dts[...] = jnp.concatenate([dtime[:, 0], dtime[:, 1]], axis=2)
    dtl[w] = dts[w]
    dt_ops = net.dp_push(lambda peer: dts.at[peer], dtl.at[w], 56)
    wait_all(tok_ops)
    tok = sum(tkl[k] for k in range(1, n)) + tkl[0]
    tok = jnp.concatenate([tok, jnp.zeros((88, 128), F32)], axis=0).T[0:share]
    gsm_ref[:, 0:16] = tok[:, 0:16]
    gsm_ref[:, 16:17] = tok[:, 32:33]
    gsm_ref[:, 1075:1091] = tok[:, 16:32]
    gsm_ref[:, 1091:1093] = tok[:, 33:35]
    wait_all(ops)
    base = 0
    bases = []
    for index, count in enumerate(P_TILES):
        bases.append(gram_schmidt(jnp.concatenate([py[base + k] for k in range(count)], axis=1)))
        base += count
    col_side = fill(halves(bases[0]) + halves(bases[1]) + halves(bases[2]), 128).T.astype(BF)

    def col_chunk(values):
        high, low = split2(values)
        return dot(high, col_side) + dot(low, col_side)

    def put(first, rows, k, tile):
        got = col_chunk(mc[first : first + rows, :])
        if rows % 128:
            got = jnp.concatenate([got, jnp.zeros((128 - rows % 128, 128), F32)], axis=0)
        got = got.T
        got = got[16 * k : 16 * k + 8] + got[16 * k + 8 : 16 * k + 16]
        for i in range(got.shape[1] // 128):
            qx[tile + i] = got[:, 128 * i : 128 * i + 128]

    for i in range(6):
        put(256 * i, 256, 0, 2 * i)
    put(QKV0, 256, 1, 12)
    put(QKV0 + 256, 320, 1, 14)
    for i in range(3):
        put(FC0 + 256 * i, 256, 2, 17 + 2 * i)
    for k, (rows, block) in enumerate(((slice(0, 192), bases[3][:, 0:192]), (slice(192, 960), bases[4]))):
        left = jnp.concatenate(halves(block), axis=0).astype(BF)
        high, low = split2(mr[rows, :])
        got = dot(left, high) + dot(left, low)
        got = got[0:8] + got[8:16]
        for i in range(6):
            qx[23 + 6 * k + i] = got[:, 128 * i : 128 * i + 128]
    for i in range(35, Q_COUNT):
        qx[i] = jnp.zeros((8, 128), F32)
    ops = scatter(qx, qland, Q_COUNT // n, 64)
    gsm_ref[:, 274:1042] = hndot(dcond, a1_ref[...])
    gsm_ref[:, 1042:1043] = jnp.sum(dcond, axis=1, keepdims=True)
    gsm_ref[:, 1043:1075] = hdot(dcond, hot_ref[...])[:, 0:CLASSES]
    offset = 0
    for block, width in zip(bases, (D, D, D, 192, D)):
        left_ref[:, offset : offset + width] = block[:, 0:width]
        offset += width
    gb_ref[...] = jnp.concatenate([py[26 + i // 8, i % 8 : i % 8 + 1, :] for i in range(23)], axis=1)[:, 0:COLS]
    head = jnp.concatenate([py[29], py[30], jnp.zeros((112, 128), F32)], axis=0).T
    gh_ref[...] = head[0:8]
    emit((left_ref, left_out), (gb_ref, gb_out), (gh_ref, gh_out))

    ops = collect(qland, qy, Q_COUNT // n, 72, ops)
    wait_all(dt_ops)
    dtime = sum(dtl[k] for k in range(1, n)) + dtl[0]
    dtime = jnp.concatenate([dtime[:, 0:64], dtime[:, 64:128]], axis=0) * silu_slope_k(t1_ref[...])
    gsm_ref[:, 17:273] = hdot(dtime, tf_ref[...])
    gsm_ref[:, 273:274] = jnp.sum(dtime, axis=1, keepdims=True)

    def left_rows(blocks):
        rows = []
        for block in blocks:
            high, low = halves(block)
            rows += [high, low, high]
        return rows

    def right_rows(blocks):
        rows = []
        for block in blocks:
            high, low = halves(block)
            rows += [high, high, low]
        return rows

    pst_ref[...] = fill(left_rows(bases[:3]), 128).astype(BF)
    proj = jnp.concatenate([bases[3][:, 0:192], jnp.zeros((8, D), F32)], axis=1)
    fc = jnp.concatenate([jnp.zeros((8, 192), F32), bases[4]], axis=1)
    row_stack = fill(left_rows([proj, fc]), 128)
    pc_ref[...] = row_stack.astype(BF)
    row_stack = jnp.concatenate([row_stack, jnp.zeros((128, 64), F32)], axis=1)
    psr_ref[...] = row_stack.T[0:960].astype(BF)
    emit((pst_ref, pst_out), (pc_ref, pc_out), (psr_ref, psr_out), (gsm_ref, gsm_out))
    wait_all(ops)
    qkv = jnp.concatenate([qy[12 + i] for i in range(5)], axis=1)[:, 0:576]
    pieces = [jnp.concatenate([qy[i] for i in range(12)], axis=1), qkv, jnp.concatenate([qy[17 + i] for i in range(6)], axis=1)]
    pad = jnp.zeros((8, 64), F32)
    qc = jnp.concatenate(pieces + [pad], axis=1)
    span = lax.broadcasted_iota(jnp.int32, (8, 2944), 1)
    cuts = [
        jnp.where((span >= first) & (span < last), qc, 0.0) for first, last in ((0, QKV0), (QKV0, FC0), (FC0, COLS))
    ]
    stack = fill(right_rows(cuts), 128)
    qsn_ref[...] = stack.astype(BF)
    qst_ref[...] = stack.T[0:COLS].astype(BF)
    qr = [jnp.concatenate([qy[23 + 6 * k + i] for i in range(6)], axis=1) for k in range(2)]
    qrs_ref[...] = fill(right_rows(qr), 128).astype(BF)
    rightn_ref[:, 0:COLS] = qc[:, 0:COLS]
    rightn_ref[:, COLS : COLS + D] = qr[0]
    rightn_ref[:, COLS + D : COLS + 2 * D] = qr[1]
    emit((qst_ref, qst_out), (qsn_ref, qsn_out), (qrs_ref, qrs_out), (rightn_ref, rightn_out))
    net.finish()
    for op in outs:
        op.wait()
    out_col.wait()
    out_row.wait()


def run_grad(operands, n):
    S = jax.ShapeDtypeStruct
    V = pltpu.VMEM
    rows = operands[0].shape[0]
    lat = 8 * n
    share = D // n
    any_spec = pl.BlockSpec(memory_space=pl.ANY)
    vm = pl.BlockSpec(memory_space=pltpu.VMEM)
    outs = [
        S((COLS, D), F32), S((960, D), F32), S((8, 3264), F32), S((8, 4416), F32),
        S((128, D), BF), S((960, 128), BF), S((128, 960), BF), S((COLS, 128), BF), S((128, 2944), BF), S((128, D), BF),
        S((1, COLS), F32), S((8, 128), F32), S((share, 1093), F32),
    ]
    scratch = [
        V((COLS, D), F32), V((960, D), F32), V((1344, D), F32), V((960, D), F32), V((1344, D), F32), V((960, D), F32),
        V((rows, D), BF), V((rows, D), BF), V((rows, D), BF), V((rows, D), BF),
        V((2, rows, 256), BF), V((2, rows, 640), BF), V((2, rows, D), BF), V((2, rows, D), BF),
        *[V(o.shape, o.dtype) for o in outs[2:]],
        V((4, 8, D), F32), V((40, D), F32), V((1, 640), F32), V((1, D), F32), V((16, 128), F32),
        V((8, QKV0), F32), V((n, 8, QKV0), F32),
        V((4, share, lat), F32), V((share, lat), F32), V((n, share // 2, 128), F32), V((n, share // 2, 128), F32),
        V((n, 40, 128), F32), V((n, 40, 128), F32),
        V((P_COUNT, 8, 128), F32), V((n, P_COUNT // n, 8, 128), F32), V((P_COUNT, 8, 128), F32),
        V((Q_COUNT, 8, 128), F32), V((n, Q_COUNT // n, 8, 128), F32), V((Q_COUNT, 8, 128), F32),
        pltpu.SemaphoreType.DMA((10,)), pltpu.SemaphoreType.DMA((11,)), pltpu.SemaphoreType.DMA((80,)), pltpu.SemaphoreType.DMA((80,)),
    ]
    return pl.pallas_call(
        grad_kernel,
        out_shape=outs,
        in_specs=[any_spec] * 10 + [vm] * 14,
        out_specs=[any_spec] * 13,
        scratch_shapes=scratch,
        compiler_params=pltpu.CompilerParams(collective_id=1, has_side_effects=True, vmem_limit_bytes=60 * 1024 * 1024),
        name="grad",
    )(*operands)


APPLY_IN = (
    "mcol", "mrow", "qst", "psr", "pst", "pc", "qsn", "qrs", "left", "right", "gs", "gb", "gh",
    "cw", "cm", "rw", "rm", "sw", "sm", "bw", "bm", "hw", "hm",
)
APPLY_OUT = ("mcol", "mrow", "cw", "cm", "rw", "rm", "sw", "sm", "bw", "bm", "hw", "hm", "left", "right", "loss")
CUTS = 6


def apply_kernel(w_ref, *refs, n):
    ins = dict(zip(APPLY_IN, refs))
    outs = dict(zip(APPLY_OUT, refs[len(APPLY_IN) :]))
    rest = refs[len(APPLY_IN) + len(APPLY_OUT) :]
    held = [name for name in APPLY_IN if name not in ("left", "right")]
    s = dict(zip(held, rest))
    loss_s, hat_s, sem_in, sem_out = rest[len(held) :]
    share = D // n
    cut = {"mcol": [slice(480 * i, 480 * i + 480) for i in range(CUTS)], "mrow": [slice(480 * i, 480 * i + 480) for i in range(2)]}
    started, finished = {}, []

    def load(name, part=None):
        src, dst = (ins[name], s[name]) if part is None else (ins[name].at[cut[name][part]], s[name].at[cut[name][part]])
        started[name, part] = pltpu.make_async_copy(src, dst, sem_in.at[len(started)])
        started[name, part].start()

    def store(src, dst):
        op = pltpu.make_async_copy(src, dst, sem_out.at[len(finished)])
        op.start()
        finished.append(op)

    for name in ("pst", "qst", "qrs", "pc", "qsn", "psr"):
        load(name)
    for part in range(CUTS):
        load("mcol", part)
        if part == 0:
            for name in ("rw", "rm", "cw", "cm"):
                load(name)
    for part in range(2):
        load("mrow", part)
    for name in ("gs", "sw", "sm", "gb", "bw", "bm", "gh", "hw", "hm"):
        load(name)
    store(ins["left"], outs["left"])
    store(ins["right"], outs["right"])

    def ready(*names):
        for name in names:
            started[name, None].wait()

    def update(weight, moment, grad):
        s[moment][...] = DECAY * s[moment][...] + grad
        s[weight][...] = s[weight][...] - LEARN_RATE * s[moment][...]
        store(s[moment], outs[moment])
        store(s[weight], outs[weight])

    ready("pst", "qst", "qrs", "pc", "qsn")
    place = lax.broadcasted_iota(jnp.int32, (D, 128), 0) == w_ref[0] * share + lax.broadcasted_iota(jnp.int32, (D, 128), 1)
    pick = jnp.where(place, 1.0, 0.0).astype(BF)
    hat_s[...] = tdot(dot(s["pst"][...], pick).astype(BF), s["qsn"][...])[0:share, 0:COLS]
    rows = tdot(dot(s["qrs"][...], pick).astype(BF), s["pc"][...])[0:share]

    def residue(name, part, hat):
        started[name, part].wait()
        span = cut[name][part]
        s[name][span, :] = s[name][span, :] - hat * (1.0 / n)
        store(s[name].at[span], outs[name].at[span])

    def col(part):
        residue("mcol", part, dot(s["qst"][cut["mcol"][part], :], s["pst"][...]))

    def row(part):
        residue("mrow", part, dot(s["psr"][cut["mrow"][part], :], s["qrs"][...]))

    col(0)
    ready("rw", "rm")
    update("rw", "rm", rows)
    col(1)
    ready("cw", "cm")

    @pl.loop(0, share // 8)
    def _(i):
        for r in range(8):
            k = 8 * i + r
            moment = DECAY * s["cm"][k] + hat_s[pl.ds(k, 1), :]
            s["cm"][k] = moment
            s["cw"][k] = s["cw"][k] - LEARN_RATE * moment

    store(s["cm"], outs["cm"])
    store(s["cw"], outs["cw"])
    for part in range(2, CUTS):
        col(part)
    ready("psr")
    for part in range(2):
        row(part)
    ready("gs", "sw", "sm")
    update("sw", "sm", s["gs"][...])
    ready("gb", "bw", "bm", "gh", "hw", "hm")
    update("bw", "bm", s["gb"][...])
    update("hw", "hm", s["gh"][0:1, 0:PATCH_IN])
    loss_s[...] = s["gh"][1:2, 0:1]
    store(loss_s, outs["loss"])
    for op in finished:
        op.wait()


def run_apply(w, operands, n):
    S = jax.ShapeDtypeStruct
    V = pltpu.VMEM
    shapes = {name: operand for name, operand in zip(APPLY_IN, operands)}
    outs = [S(shapes[name].shape, F32) for name in APPLY_OUT[:-1]] + [S((1, 1), F32)]
    held = [V(shapes[name].shape, shapes[name].dtype) for name in APPLY_IN if name not in ("left", "right")]
    any_spec = pl.BlockSpec(memory_space=pl.ANY)
    return pl.pallas_call(
        functools.partial(apply_kernel, n=n),
        out_shape=outs,
        in_specs=[pl.BlockSpec(memory_space=pltpu.SMEM)] + [any_spec] * len(APPLY_IN),
        out_specs=[any_spec] * len(outs),
        scratch_shapes=held + [V((1, 1), F32), V((D // n, COLS), F32), pltpu.SemaphoreType.DMA((32,)), pltpu.SemaphoreType.DMA((32,))],
        compiler_params=pltpu.CompilerParams(vmem_limit_bytes=62 * 1024 * 1024),
        name="apply",
    )(w, *operands)


def position_table():
    quarter = D // 4
    omega = 10000.0 ** (-np.arange(quarter) / quarter)
    place = np.arange(GRID)[:, None] * omega[None, :]
    return jnp.asarray(np.concatenate([np.sin(place), np.cos(place)], axis=1), F32)


def time_features(times):
    half = FREQ // 2
    freqs = jnp.exp(-math.log(10000.0) * jnp.arange(half, dtype=jnp.float32) / half)
    angles = 1000.0 * times[:, None] * freqs[None, :]
    return jnp.concatenate([jnp.cos(angles), jnp.sin(angles)], axis=1)


def small_starts():
    counts = [PATCH_IN, 1, FREQ, 1, D, 1, CLASSES, PATCH_IN, 1, 1]
    starts = [0]
    for amount in counts:
        starts.append(starts[-1] + amount)
    return starts


def cut_parts(array, widths, axis):
    pieces = []
    offset = 0
    for width in widths:
        pieces.append(lax.slice_in_dim(array, offset, offset + width, axis=axis))
        offset = offset + width
    return pieces


def ortho_kernel(x_ref, o_ref):
    count = x_ref.shape[0]
    rows = [x_ref[index] for index in range(count)]
    for index in range(count):
        vector = rows[index]
        vector = vector * lax.rsqrt(jnp.sum(vector * vector, axis=-1, keepdims=True) + TINY)
        o_ref[index] = vector
        for later in range(index + 1, count):
            rows[later] = rows[later] - jnp.sum(rows[later] * vector, axis=-1, keepdims=True) * vector


def orthonormal_all(parts):
    stacked = jnp.stack([jnp.pad(part, ((0, 0), (0, D - part.shape[1]))) for part in parts], axis=1)
    stacked = jnp.pad(stacked, ((0, 0), (0, 8 - len(parts)), (0, 0)))
    out = pl.pallas_call(ortho_kernel, out_shape=jax.ShapeDtypeStruct(stacked.shape, F32), name="ortho")(stacked)
    return [out[:, index, : part.shape[1]] for index, part in enumerate(parts)]


def rounded(values):
    return lax.optimization_barrier(values.astype(BF)).astype(F32)


def silu_slope(values):
    gate = jax.nn.sigmoid(values)
    return gate * (1.0 + values * (1.0 - gate))


def shards_general(
    clean_latents,
    noise_draw,
    timesteps,
    labels,
    col_weights,
    col_moments,
    col_errors,
    row_weights,
    row_moments,
    row_errors,
    bias_weights,
    bias_moments,
    small_weights,
    small_moments,
    head_bias,
    head_moments,
    right_factors,
):
    tensor_size = lax.axis_size("tensor")
    data_size = lax.axis_size("dp")
    tensor_rank = lax.axis_index("tensor")
    data_rank = lax.axis_index("dp")
    batch = clean_latents.shape[0]
    half = batch // 2
    share = D // data_size
    mod_width = 8 * D // tensor_size
    qkv_width = 3 * D // tensor_size
    ffn_width = FF // tensor_size
    proj_rows = D // tensor_size
    count_all = data_size * batch * SEQ * PATCH_IN
    col_widths = [mod_width, qkv_width, ffn_width]
    core = lax.rem(tensor_rank, 2)
    base = tensor_rank - core
    pair = [(index, index + 1 - 2 * (index % 2)) for index in range(tensor_size)]

    def swap(values):
        return lax.ppermute(values, "tensor", pair)

    col_low = col_weights[:, 0, :].astype(BF)
    row_low = row_weights[0].astype(BF).T
    packed = jnp.concatenate(
        [
            col_low[:, mod_width : mod_width + qkv_width],
            row_low[:, :proj_rows],
            col_low[:, mod_width + qkv_width :],
            row_low[:, proj_rows:],
        ],
        axis=1,
    )
    wall = lax.all_gather(lax.all_gather(packed, "dp", axis=0, tiled=True), "tensor", axis=0)
    wall = jnp.stack([wall[:, :, 768 * index : 768 * index + 768] for index in range(3)])
    starts = small_starts()
    small_low = small_weights.astype(BF)
    small_exact = rounded(small_weights)
    picked = jnp.concatenate([small_low[: starts[2]], small_low[starts[7] :]], axis=0)
    emb = lax.all_gather(picked.astype(F32), "dp", axis=1, tiled=True)
    emb = jnp.concatenate([emb[:16], emb[17:33], emb[16:17], emb[33:35], jnp.zeros((5, D), F32)], axis=0)
    w_tin = small_exact[starts[2] : starts[3]]
    b_tin = small_exact[starts[3]]
    w_tout = small_exact[starts[4] : starts[5]]
    b_tout = small_exact[starts[5]]
    table = small_exact[starts[6] : starts[7]]
    bias_exact = rounded(bias_weights[0])
    head_exact = rounded(head_bias)
    w_mod = rounded(col_weights[:, 0, :mod_width])
    bias_all = lax.all_gather(bias_exact, "tensor", axis=0)
    times_all = lax.all_gather(timesteps, "dp", axis=0, tiled=True)
    labels_all = lax.all_gather(labels, "dp", axis=0, tiled=True)
    time_feat = time_features(times_all)
    time_hidden = exact_dot(time_feat, w_tin) + b_tin
    time_act = lax.all_gather(jax.nn.silu(time_hidden), "dp", axis=1, tiled=True)
    onehot = (labels_all[:, None] == jnp.arange(CLASSES, dtype=jnp.int32)[None, :]).astype(F32)
    condition = exact_dot(time_act, w_tout) + b_tout + exact_dot(onehot, table)
    cond_act = jax.nn.silu(condition)
    mod_part = exact_dot(cond_act, w_mod)
    mod_own = lax.psum_scatter(mod_part, "dp", scatter_dimension=0, tiled=True) + bias_exact[:mod_width]
    mod_full = lax.all_gather(mod_own, "tensor", axis=1, tiled=True).reshape(batch, 8, D)
    cond_rows = lax.all_to_all(cond_act, "dp", split_axis=0, concat_axis=1, tiled=True)

    def mine(values):
        return lax.dynamic_slice_in_dim(values, core * half, half, 0)

    ball = jnp.concatenate(
        [
            jnp.pad(bias_all[:, mod_width : mod_width + qkv_width], ((0, 0), (0, 768 - qkv_width))),
            bias_all[:, mod_width + qkv_width :],
        ],
        axis=1,
    )[:, None]
    (a, m, dy, dz, o, dq, du, g, dmod, small, dbq, db1, hb) = run_block(
        base.reshape(1),
        mine(timesteps),
        mine(clean_latents).transpose(0, 2, 1),
        mine(noise_draw).transpose(0, 2, 1),
        mine(mod_full),
        wall,
        position_table(),
        emb,
        head_exact[:, None],
        ball,
        count_all,
    )
    rows = half * SEQ

    def flat(values):
        return values.reshape(rows, values.shape[-1])

    def pick(values, which):
        return lax.dynamic_index_in_dim(values, which, 0, keepdims=False)

    def gradients(which):
        return (
            tdot(flat(a), flat(pick(dq, which))[:, :qkv_width]),
            tdot(flat(m), flat(pick(du, which))),
            tdot(flat(pick(o, which))[:, 64:], flat(dy)),
            tdot(flat(pick(g, which)), flat(dz)),
            pick(dbq, which)[0, :qkv_width],
            pick(db1, which)[0],
        )

    other = swap(gradients(1 - core))
    own = gradients(core)
    g_qkv, g_fc1, g_proj, g_fc2, g_bqkv, g_bfc1 = [left + right for left, right in zip(own, other)]
    dmod_own = dmod.reshape(half, 8 * D)
    dmod_other = swap(dmod_own)
    dmod_group = jnp.where(
        core == 0,
        jnp.concatenate([dmod_own, dmod_other], axis=0),
        jnp.concatenate([dmod_other, dmod_own], axis=0),
    )
    d_mod = lax.dynamic_slice_in_dim(dmod_group, tensor_rank * mod_width, mod_width, 1)
    g_bmod = jnp.sum(d_mod, axis=0)
    g_mod = exact_tdot(cond_rows, d_mod)
    d_mod_all = lax.all_gather(d_mod, "dp", axis=0, tiled=True)
    d_cond = lax.psum(exact_ndot(d_mod_all, w_mod), "tensor") * silu_slope(condition)
    g_table = exact_tdot(onehot, d_cond)
    g_btout = jnp.sum(d_cond, axis=0)
    g_tout = exact_tdot(time_act, d_cond)
    d_time = lax.psum_scatter(exact_ndot(d_cond, w_tout), "dp", scatter_dimension=1, tiled=True)
    d_time = d_time * silu_slope(time_hidden)
    g_btin = jnp.sum(d_time, axis=0)
    g_tin = exact_tdot(time_feat, d_time)
    small_own = lax.psum(lax.psum_scatter(small, "dp", scatter_dimension=1, tiled=True), "tensor") * 0.5
    head_sum, loss_value = lax.psum((hb[:, 0] * 0.5, hb[0, 1] * 0.5), ("dp", "tensor"))
    small_step = jnp.concatenate(
        [
            small_own[:16],
            small_own[32:33],
            g_tin,
            g_btin[None],
            g_tout,
            g_btout[None],
            g_table,
            small_own[16:32],
            small_own[33:34],
            small_own[34:35],
        ],
        axis=0,
    )
    bias_sum = lax.psum(jnp.concatenate([g_bmod, g_bqkv, g_bfc1], axis=0), "dp")
    col_cuts = cut_parts(col_errors[0, 0], col_widths, 1)
    row_cuts = cut_parts(row_errors[0, 0], [proj_rows, ffn_width], 0)
    matrices = [
        g_mod + col_cuts[0],
        g_qkv + col_cuts[1],
        g_fc1 + col_cuts[2],
        g_proj + row_cuts[0],
        g_fc2 + row_cuts[1],
    ]
    right_pieces = cut_parts(right_factors[0], col_widths + [D, D], 1)
    left_local = jnp.concatenate([exact_ndot(right_pieces[i], matrices[i]) for i in range(5)], axis=1)
    left_sum = lax.psum(left_local, "dp")
    bases = orthonormal_all(cut_parts(left_sum, [D, D, D, proj_rows, ffn_width], 1))
    right_local = jnp.concatenate([exact_dot(bases[i], matrices[i]) for i in range(5)], axis=1)
    right_sum = lax.psum(right_local, "dp")
    right_split = cut_parts(right_sum, col_widths + [D, D], 1)
    approx = [exact_tdot(bases[i], right_split[i]) for i in range(5)]
    rest = [matrices[i] - approx[i] / data_size for i in range(5)]
    col_residue = jnp.concatenate(rest[:3], axis=1)[None, None]
    row_residue = jnp.concatenate(rest[3:], axis=0)[None, None]

    def own_columns(values):
        return lax.dynamic_slice_in_dim(values, data_rank * share, share, 1)

    col_step = jnp.concatenate(
        [exact_tdot(own_columns(bases[i]), right_split[i]) for i in range(3)], axis=1
    )[:, None, :]
    row_step = jnp.concatenate(
        [exact_tdot(bases[i], own_columns(right_split[i])) for i in (3, 4)], axis=0
    )[None]
    col_momentum = DECAY * col_moments + col_step
    col_new = col_weights - LEARN_RATE * col_momentum
    row_momentum = DECAY * row_moments + row_step
    row_new = row_weights - LEARN_RATE * row_momentum
    small_momentum = DECAY * small_moments + small_step
    small_new = small_weights - LEARN_RATE * small_momentum
    bias_momentum = DECAY * bias_moments + bias_sum[None]
    bias_new = bias_weights - LEARN_RATE * bias_momentum
    head_momentum = DECAY * head_moments + head_sum
    head_new = head_bias - LEARN_RATE * head_momentum
    left_factors = jnp.concatenate(bases, axis=1)[None]
    right_new = right_sum[None]
    return (
        loss_value,
        col_new,
        col_momentum,
        col_residue,
        row_new,
        row_momentum,
        row_residue,
        bias_new,
        bias_momentum,
        small_new,
        small_momentum,
        head_new,
        head_momentum,
        left_factors,
        right_new,
    )


def shards(
    clean_latents,
    noise_draw,
    timesteps,
    labels,
    col_weights,
    col_moments,
    col_errors,
    row_weights,
    row_moments,
    row_errors,
    bias_weights,
    bias_moments,
    small_weights,
    small_moments,
    head_bias,
    head_moments,
    right_factors,
):
    tensor_size = lax.axis_size("tensor")
    data_size = lax.axis_size("dp")
    tensor_rank = lax.axis_index("tensor")
    data_rank = lax.axis_index("dp")
    batch = clean_latents.shape[0]
    half = batch // 2
    share = D // data_size
    mod_width = 8 * D // tensor_size
    qkv_width = 3 * D // tensor_size
    ffn_width = FF // tensor_size
    proj_rows = D // tensor_size
    count_all = data_size * batch * SEQ * PATCH_IN
    col_widths = [mod_width, qkv_width, ffn_width]
    core = lax.rem(tensor_rank, 2)
    base = tensor_rank - core
    col = col_weights[:, 0]
    col_low = col.astype(BF)
    freq = jnp.asarray(np.exp(-math.log(10000.0) * np.arange(FREQ // 2) / (FREQ // 2))[None], F32)
    small_t = small_weights.T
    a, m, dy, dz, o, dq, du, g, cs, ct, t1, a1, tf, hot, wto, dmod, small, dbq, db1, hb = run_step(
        col_low, row_weights[0].T, small_t, bias_weights, timesteps, labels, freq,
        clean_latents.transpose(0, 2, 1), noise_draw.transpose(0, 2, 1), position_table(), head_bias[None],
        data_size, count_all,
    )
    rows = half * SEQ

    def flat(values):
        return values.reshape(values.shape[:-3] + (rows, values.shape[-1]))

    acts = [flat(values) for values in (a, m, dy, dz, o, dq, du, g)]
    errors = [col_errors[0, 0].T, row_errors[0, 0]]
    mcol, mrow, left_all, right_sum, pst, psr, pc, qst, qsn, qrs, gb, gh, gsm = run_grad(
        acts + errors + [dmod, small, dbq, db1, hb, right_factors[0], cs, ct, t1, a1, tf, hot, col_low, wto], data_size
    )
    cres, rres, col_new, col_momentum, rn, rmn, sn, smn, bias_new, bias_momentum, hn, hmn, left_all, right_sum, loss = run_apply(
        data_rank.reshape(1),
        [mcol, mrow, qst, psr, pst, pc, qsn, qrs, left_all, right_sum, gsm, gb, gh]
        + [col_weights, col_moments, row_weights[0].T, row_moments[0].T, small_t, small_moments.T]
        + [bias_weights, bias_moments, head_bias[None], head_moments[None]],
        data_size,
    )
    loss_value = loss[0, 0]
    col_residue, row_residue = cres.T[None, None], rres[None, None]
    row_new, row_momentum = rn.T[None], rmn.T[None]
    small_new, small_momentum = sn.T, smn.T
    head_new, head_momentum = hn[0], hmn[0]
    left_factors, right_new = left_all[None], right_sum[None]
    return (
        loss_value,
        col_new,
        col_momentum,
        col_residue,
        row_new,
        row_momentum,
        row_residue,
        bias_new,
        bias_momentum,
        small_new,
        small_momentum,
        head_new,
        head_momentum,
        left_factors,
        right_new,
    )


def solution(mesh):
    fits = mesh.shape["dp"] == 8 and mesh.shape["tensor"] == 4
    placed = (
        P("dp", None, None),
        P("dp", None, None),
        P("dp"),
        P("dp"),
        P("dp", "tensor", None),
        P("dp", "tensor", None),
        P("dp", "tensor", None, None),
        P("tensor", None, "dp"),
        P("tensor", None, "dp"),
        P("dp", "tensor", None, None),
        P("tensor", None),
        P("tensor", None),
        P(None, "dp"),
        P(None, "dp"),
        P(),
        P(),
        P("tensor", None, None),
    )
    return jax.shard_map(
        shards if fits else shards_general,
        mesh=mesh,
        in_specs=placed,
        out_specs=(
            P(),
            P("dp", "tensor", None),
            P("dp", "tensor", None),
            P("dp", "tensor", None, None),
            P("tensor", None, "dp"),
            P("tensor", None, "dp"),
            P("dp", "tensor", None, None),
            P("tensor", None),
            P("tensor", None),
            P(None, "dp"),
            P(None, "dp"),
            P(),
            P(),
            P("tensor", None, None),
            P("tensor", None, None),
        ),
        check_vma=False,
    )
```

```python
import functools
import math

import jax
import jax.numpy as jnp
import numpy as np
from jax import lax
from jax.experimental import pallas as pl
from jax.experimental.pallas import tpu as pltpu
from jax.sharding import PartitionSpec as P

D = 768
HEADS = 12
HEAD_DIM = 64
FF = 3072
FREQ = 256
GRID = 16
PATCH_IN = 16
CLASSES = 32
SEQ = 256

EPSILON = 1e-06
TINY = 1e-30
DECAY = 0.9
LEARN_RATE = 100.0
TIME_OFFSET = 0.25
F32 = jnp.float32
BF = jnp.bfloat16
SCALE = 1.0 / math.sqrt(HEAD_DIM)
GELU_C = math.sqrt(2.0 / math.pi)


def exact_dot(left, right):
    return jnp.dot(left, right, precision=lax.Precision.HIGHEST, preferred_element_type=F32)


def exact_tdot(left, right):
    return lax.dot_general(left, right, (((0,), (0,)), ((), ())), precision=lax.Precision.HIGHEST, preferred_element_type=F32)


def exact_ndot(left, right):
    return lax.dot_general(left, right, (((1,), (1,)), ((), ())), precision=lax.Precision.HIGHEST, preferred_element_type=F32)


def dot(a,b): return lax.dot_general(a,b,(((1,),(0,)),((),())),preferred_element_type=F32)
def ndot(a,b): return lax.dot_general(a,b,(((1,),(1,)),((),())),preferred_element_type=F32)
def tdot(a,b): return lax.dot_general(a,b,(((0,),(0,)),((),())),preferred_element_type=F32)

def ln(h):
    c=h-jnp.mean(h,axis=-1,keepdims=True)
    v=jnp.mean(c*c,axis=-1,keepdims=True)
    r=lax.rsqrt(v+EPSILON)
    return c*r,r

def ln_back(dout,xh,r,scale):
    dx=dout*(1.0+scale)
    return r*(dx-jnp.mean(dx,axis=-1,keepdims=True)-xh*jnp.mean(dx*xh,axis=-1,keepdims=True))

def colsum(v): return jnp.sum(v,axis=0,keepdims=True)

UNROLL=dict(af=2,ff=4,fb=4,ab=4)

def block_state():
    V=pltpu.VMEM
    return dict(
        wall=V((3,4,D,D),BF), pe=V((SEQ,D),F32), qkv=V((4,4,SEQ,640),BF), p=V((4,12,SEQ,SEQ),BF),
        xh1=V((4,SEQ,D),F32), y=V((4,SEQ,D),F32), h=V((4,SEQ,D),F32), r1=V((4,SEQ,1),F32),
        xh2=V((SEQ,D),F32), z=V((SEQ,D),F32), r2=V((SEQ,1),F32), slope=V((4,SEQ,D),F32),
        a=V((SEQ,D),BF), m=V((SEQ,D),BF), dz=V((SEQ,D),BF), dy=V((SEQ,D),BF),
        o=V((4,SEQ,256),BF), g=V((4,SEQ,D),BF), du=V((4,SEQ,D),BF), dq=V((4,SEQ,640),BF),
        dbq=V((4,1,640),F32), db1=V((4,1,D),F32), out_sem=pltpu.SemaphoreType.DMA((8,)))

class Block:
    def __init__(self,s,times,clean,noise,mod,pe,emb,bh,ball,outs,dmod,small,hb,base,first,count_all,service):
        self.s=s; self.times=times; self.clean=clean; self.noise=noise; self.mod_ref=mod; self.pe=pe; self.emb=emb; self.bh=bh; self.ball=ball
        self.outs=outs; self.dmod=dmod; self.small=small; self.hb=hb; self.base=base; self.first=first; self.count_all=count_all; self.service=service
        self.lo=lax.broadcasted_iota(jnp.int32,(1,128),1)<64
        self.zero=jnp.zeros((),BF)
    def roll(self,v): return pltpu.roll(v.astype(F32),64,1).astype(BF)
    def out(self,lat,name,index,pair):
        s=self.s
        src=s[name].at[pl.ds(self.base,2)] if pair else s[name]
        dst=self.outs[index].at[:,lat] if pair else self.outs[index].at[lat]
        return pltpu.make_async_copy(src,dst,s["out_sem"].at[index])
    def emit(self,lat,name,index,pair=False): self.out(lat,name,index,pair).start()
    def clear(self,lat,name,index,pair=False):
        @pl.when(lat>0)
        def _(): self.out(lat-1,name,index,pair).wait()
    def last(self):
        for name,index,pair in (("a",0,False),("m",1,False),("dy",2,False),("dz",3,False),("o",4,True),("dq",5,True),("du",6,True),("g",7,True)):
            self.out(3,name,index,pair).wait()
    def start(self):
        s=self.s
        self.small[...]=jnp.zeros_like(self.small); self.hb[...]=jnp.zeros_like(self.hb)
        s["dbq"][...]=jnp.zeros_like(s["dbq"]); s["db1"][...]=jnp.zeros_like(s["db1"])
        for i in range(GRID):
            s["pe"][16*i:16*i+16,0:384]=jnp.broadcast_to(self.pe[i:i+1,:],(16,384))
            s["pe"][16*i:16*i+16,384:768]=self.pe[...]
    def mixed(self,lat):
        place=self.first+lat
        t=self.times[place]
        clean=self.clean[place].astype(F32); noise=self.noise[place].astype(F32)
        return t,clean,noise,(t*clean+(1.0-t)*noise).astype(BF)
    def mod(self,lat,i): return self.mod_ref[lat,i:i+1,:]
    def embed(self,lat):
        s=self.s
        mixed=self.mixed(lat)[3]
        h0=tdot(mixed,self.emb[0:16].astype(BF))+self.emb[32:33]+s["pe"][...]
        s["h"][lat]=h0
        xh,r=ln(h0)
        s["xh1"][lat]=xh; s["r1"][lat]=r
        self.clear(lat,"a",0)
        s["a"][...]=(xh*(1.0+self.mod(lat,1))+self.mod(lat,0)).astype(BF)
        self.emit(lat,"a",0)
        self.clear(lat,"o",4,True)
    def softmax(self,v,lat,idx):
        v=v*SCALE
        e=jnp.exp(v-jnp.max(v,axis=-1,keepdims=True))
        p=(e/jnp.sum(e,axis=-1,keepdims=True)).astype(BF)
        self.s["p"][lat,idx]=p
        return p
    def attend(self,lat,j):
        s=self.s; lo=self.lo; zero=self.zero; wall=s["wall"]
        full=(dot(s["a"][...],wall[0,j])[:,0:640]+self.ball[j,:,0:640]).astype(BF)
        s["qkv"][lat,j]=full
        b0,b1,b2,b3,b4=[full[:,128*i:128*i+128] for i in range(5)]
        p0=self.softmax(ndot(jnp.where(lo,b0,zero),self.roll(b0)),lat,3*j)
        p1=self.softmax(ndot(jnp.where(lo,zero,b1),self.roll(b2)),lat,3*j+1)
        p2=self.softmax(ndot(jnp.where(lo,b3,zero),self.roll(b3)),lat,3*j+2)
        o0=pltpu.roll(dot(p0,b1),64,1)
        s["o"][j,:,0:128]=jnp.where(lo,0.0,o0).astype(BF)
        s["o"][j,:,128:256]=pltpu.roll(jnp.where(lo,dot(p2,b4),dot(p1,b2)),64,1).astype(BF)
    def project(self,lat):
        s=self.s
        self.emit(lat,"o",4,True)
        for n in range(3):
            cols=slice(256*n,256*n+256)
            y=sum(ndot(s["o"][j],s["wall"][0,j,cols,512:768]) for j in range(4))+self.emb[33:34,cols]
            s["y"][lat,:,cols]=y
            s["h"][lat,:,cols]+=self.mod(lat,2)[:,cols]*y
    def attn_fwd(self,lat):
        self.service(lat,0)
        self.embed(lat)
        self.service(lat,1)
        for j in range(2): self.attend(lat,j)
        self.service(lat,2)
        for j in range(2,4): self.attend(lat,j)
        self.service(lat,3)
        self.project(lat)
    def fc_in(self,lat):
        s=self.s
        xh,r=ln(s["h"][lat])
        s["xh2"][...]=xh; s["r2"][...]=r
        self.clear(lat,"m",1)
        s["m"][...]=(xh*(1.0+self.mod(lat,4))+self.mod(lat,3)).astype(BF)
        self.emit(lat,"m",1)
        self.clear(lat,"g",7,True)
    def fc_one(self,lat,j):
        s=self.s
        u=dot(s["m"][...],s["wall"][1,j])+self.ball[j,:,768:1536]
        uu=u*u
        th=jnp.tanh(u*(GELU_C+(GELU_C*0.044715)*uu))
        half=0.5+0.5*th
        s["g"][j]=(u*half).astype(BF)
        s["slope"][j]=half*(1.0+(u-u*th)*(GELU_C+(3.0*0.044715*GELU_C)*uu))
    def fc_fwd(self,lat):
        s=self.s
        self.fc_in(lat)
        u=UNROLL["ff"]
        @pl.loop(0,4//u)
        def _(i):
            for k in range(u): self.fc_one(lat,i*u+k)
        self.emit(lat,"g",7,True)
        for n in range(3):
            cols=slice(256*n,256*n+256)
            z=sum(ndot(s["g"][j],s["wall"][2,j,cols,:]) for j in range(4))+self.emb[34:35,cols]
            s["z"][:,cols]=z
    def head(self,lat):
        s=self.s; mod=lambda i: self.mod(lat,i)
        t,clean,noise,_=self.mixed(lat)
        wh=self.emb[16:32].astype(BF)
        h2=s["h"][lat]+mod(5)*s["z"][...]
        xh,r=ln(h2)
        fi=(xh*(1.0+mod(7))+mod(6)).astype(BF)
        pred=ndot(wh,fi)+self.bh[...]
        diff=pred-(clean-noise)
        weight=1.0/(1.0-t+TIME_OFFSET)
        self.hb[0:1,1:2]+=jnp.sum(colsum(weight*diff*diff),axis=1,keepdims=True)*(1.0/self.count_all)
        dpred=2.0*weight*diff*(1.0/self.count_all)
        self.hb[:,0:1]+=jnp.sum(dpred,axis=1,keepdims=True)
        dpl=dpred.astype(BF)
        self.small[16:32]+=dot(dpl,fi)
        dfi=tdot(dpl,wh)
        self.dmod[lat,6:7]=colsum(dfi); self.dmod[lat,7:8]=colsum(dfi*xh)
        dh=ln_back(dfi,xh,r,mod(7))
        s["h"][lat]=dh
        self.dmod[lat,5:6]=colsum(dh*s["z"][...])
        dzf=dh*mod(5)
        self.small[34:35]+=colsum(dzf)
        self.clear(lat,"dz",3)
        s["dz"][...]=dzf.astype(BF)
        self.emit(lat,"dz",3)
        self.clear(lat,"du",6,True)
    def fc_back_one(self,j):
        s=self.s
        du=dot(s["dz"][...],s["wall"][2,j])*s["slope"][j]
        s["du"][j]=du.astype(BF)
        s["db1"][j]+=colsum(du)
    def fc_bwd(self,lat):
        s=self.s; mod=lambda i: self.mod(lat,i)
        u=UNROLL["fb"]
        @pl.loop(0,4//u)
        def _(i):
            for k in range(u): self.fc_back_one(i*u+k)
        self.emit(lat,"du",6,True)
        for n in range(3):
            cols=slice(256*n,256*n+256)
            s["z"][:,cols]=sum(ndot(s["du"][j],s["wall"][1,j,cols,:]) for j in range(4))
        dm=s["z"][...]
        xh=s["xh2"][...]
        self.dmod[lat,3:4]=colsum(dm); self.dmod[lat,4:5]=colsum(dm*xh)
        dh=s["h"][lat]+ln_back(dm,xh,s["r2"][...],mod(4))
        s["h"][lat]=dh
        self.dmod[lat,2:3]=colsum(dh*s["y"][lat])
        dyf=dh*mod(2)
        self.small[33:34]+=colsum(dyf)
        self.clear(lat,"dy",2)
        s["dy"][...]=dyf.astype(BF)
        self.emit(lat,"dy",2)
        self.clear(lat,"dq",5,True)
    def attend_back(self,lat,j):
        s=self.s; lo=self.lo; zero=self.zero; roll=self.roll
        do=dot(s["dy"][...],s["wall"][0,j,:,512:768])
        r4=pltpu.roll(do[:,0:128],64,1).astype(BF); r5=pltpu.roll(do[:,128:256],64,1).astype(BF)
        do0=jnp.where(lo,r4,zero); do1=jnp.where(lo,zero,r5); do2=jnp.where(lo,r5,zero)
        b0,b1,b2,b3,b4=[s["qkv"][lat,j,:,128*i:128*i+128] for i in range(5)]
        def head(h,doh,v):
            p=s["p"][lat,3*j+h]
            dv=tdot(p,doh)
            dp=ndot(doh,v)
            pf=p.astype(F32)
            t=pf*dp
            ds=(t-pf*jnp.sum(t,axis=-1,keepdims=True)).astype(BF)
            return dv,ds
        dv0,ds0=head(0,do0,b1)
        dv1,ds1=head(1,do1,b2)
        dv2,ds2=head(2,do2,b4)
        rb0=roll(b0); rb3=roll(b3)
        n0=jnp.where(lo,dot(ds0,rb0),tdot(ds0,rb0))*SCALE
        n1=jnp.where(lo,dv0,dot(ds1,roll(b2))*SCALE); n2=jnp.where(lo,tdot(ds1,roll(b1))*SCALE,dv1)
        n3=jnp.where(lo,dot(ds2,rb3),tdot(ds2,rb3))*SCALE
        n4=jnp.where(lo,dv2,0.0)
        for i,v in enumerate((n0,n1,n2,n3,n4)):
            cols=slice(128*i,128*i+128)
            s["dq"][j,:,cols]=v.astype(BF)
            s["dbq"][j,:,cols]+=colsum(v)
    def attn_bwd(self,lat):
        s=self.s; mod=lambda i: self.mod(lat,i)
        u=UNROLL["ab"]
        @pl.loop(0,4//u)
        def _(i):
            for k in range(u): self.attend_back(lat,i*u+k)
        self.emit(lat,"dq",5,True)
        for n in range(3):
            cols=slice(256*n,256*n+256)
            s["z"][:,cols]=sum(ndot(s["dq"][j],s["wall"][0,j,cols,0:640]) for j in range(4))
        da=s["z"][...]
        xh=s["xh1"][lat]
        self.dmod[lat,0:1]=colsum(da); self.dmod[lat,1:2]=colsum(da*xh)
        dh=s["h"][lat]+ln_back(da,xh,s["r1"][lat],mod(1))
        self.small[32:33]+=colsum(dh)
        self.small[0:16]+=dot(self.mixed(lat)[3],dh.astype(BF))

    def run(self,ready=lambda: None):
        @pl.loop(0,4)
        def _(lat): self.attn_fwd(lat)
        ready()
        @pl.loop(0,4)
        def _(lat):
            for phase in (self.fc_fwd,self.head,self.fc_bwd,self.attn_bwd): phase(lat)
        self.last()

def block_kernel(times_ref,base_ref,clean_ref,noise_ref,mod_ref,wall_ref,pe_ref,emb_ref,bh_ref,ball_ref,*rest,count_all,names):
    outs=rest[0:8]; dmod,small,dbq,db1,hb=rest[8:13]
    s=dict(zip(names,rest[13:13+len(names)])); wsem=rest[-1]
    cp=pltpu.make_async_copy(wall_ref,s["wall"],wsem); cp.start()
    base=base_ref[0]
    b=Block(s,times_ref,clean_ref,noise_ref,mod_ref,pe_ref,emb_ref,bh_ref,ball_ref,outs,dmod,small,hb,base,0,count_all,lambda lat,pos: None)
    b.start()
    cp.wait()
    b.run()
    for k in range(2):
        dbq[k]=s["dbq"][base+k]; db1[k]=s["db1"][base+k]

def run_block(base,times,clean,noise,mod,wall,pe,emb,bh,ball,count_all):
    L=clean.shape[0]
    S=jax.ShapeDtypeStruct
    outs=[S((L,SEQ,D),BF)]*4+[S((2,L,SEQ,256),BF),S((2,L,SEQ,640),BF),S((2,L,SEQ,768),BF),S((2,L,SEQ,768),BF),
        S((L,8,D),F32),S((40,D),F32),S((2,1,640),F32),S((2,1,768),F32),S((PATCH_IN,128),F32)]
    st=block_state(); names=tuple(st)
    vm=pl.BlockSpec(memory_space=pltpu.VMEM); anys=pl.BlockSpec(memory_space=pl.ANY); sm=pl.BlockSpec(memory_space=pltpu.SMEM)
    return pl.pallas_call(functools.partial(block_kernel,count_all=count_all,names=names),
        out_shape=outs,in_specs=[sm,sm,vm,vm,vm,anys,vm,vm,vm,vm],out_specs=[anys]*8+[vm]*5,
        scratch_shapes=list(st.values())+[pltpu.SemaphoreType.DMA(())],
        compiler_params=pltpu.CompilerParams(vmem_limit_bytes=62*1024*1024),name="block")(times,base,clean,noise,mod,wall,pe,emb,bh,ball)


MESH = pl.DeviceIdType.MESH
HI = lax.Precision.HIGHEST


def hdot(a, b):
    return lax.dot_general(a, b, (((1,), (0,)), ((), ())), precision=HI, preferred_element_type=F32)


def hndot(a, b):
    return lax.dot_general(a, b, (((1,), (1,)), ((), ())), precision=HI, preferred_element_type=F32)


def htdot(a, b):
    return lax.dot_general(a, b, (((0,), (0,)), ((), ())), precision=HI, preferred_element_type=F32)


def split2(values):
    first = values.astype(BF)
    return first, (values - first.astype(F32)).astype(BF)


def split3(values):
    first, rest = values.astype(BF), values
    rest = rest - first.astype(F32)
    second = rest.astype(BF)
    return first, second, (rest - second.astype(F32)).astype(BF)


def silu_slope_k(values):
    gate = 1.0 / (1.0 + jnp.exp(-values))
    return gate * (1.0 + values * (1.0 - gate))


class Peers:
    def __init__(self, send_sem, recv_sem):
        self.w = lax.axis_index("dp")
        self.t = lax.axis_index("tensor")
        self.n = lax.axis_size("dp")
        self.tn = lax.axis_size("tensor")
        self.c = lax.rem(self.t, 2)
        self.sib = self.t + 1 - 2 * self.c
        self.send_sem, self.recv_sem = send_sem, recv_sem
        self.pending = []

    def barrier(self):
        bar = pltpu.get_barrier_semaphore()
        for i in range(1, self.n):
            pl.semaphore_signal(bar, inc=1, device_id=(lax.rem(self.w + i, self.n), self.t), device_id_type=MESH)
        for i in range(1, self.tn):
            pl.semaphore_signal(bar, inc=1, device_id=(self.w, lax.rem(self.t + i, self.tn)), device_id_type=MESH)

    def ready(self):
        pl.semaphore_wait(pltpu.get_barrier_semaphore(), self.n - 1 + self.tn - 1)

    def copy(self, src, dst, index, device):
        op = pltpu.make_async_remote_copy(
            src_ref=src,
            dst_ref=dst,
            send_sem=self.send_sem.at[index],
            recv_sem=self.recv_sem.at[index],
            device_id=device,
            device_id_type=MESH,
        )
        op.start()
        self.pending.append(op)
        return op

    def dp_push(self, src_of, dst, base):
        ops = []
        for i in range(1, self.n):
            peer = lax.rem(self.w + i, self.n)
            ops.append(self.copy(src_of(peer), dst, base + i - 1, (peer, self.t)))
        return ops

    def tensor_push(self, src, dst, base):
        ops = []
        for i in range(1, self.tn):
            ops.append(self.copy(src, dst, base + i - 1, (self.w, lax.rem(self.t + i, self.tn))))
        return ops

    def core_push(self, src, dst, index):
        return self.copy(src, dst, index, (self.w, self.sib))

    def finish(self):
        for op in self.pending:
            op.wait_send()


def wait_all(ops):
    for op in ops:
        op.wait_recv()


P_TILES = (6, 6, 6, 2, 6)
P_COUNT = 32
Q_COUNT = 40
QKV0, FC0 = 1536, 2112
COLS = 2880


def halves(block):
    high = block.astype(BF).astype(F32)
    return [high, block - high]


def fill(rows, total):
    used = sum(row.shape[0] for row in rows)
    return jnp.concatenate(rows + [jnp.zeros((total - used, rows[0].shape[1]), F32)], axis=0)


AUX = ("cs", "ct", "t1", "a1", "tf", "hot", "wto", "dmod", "small", "dbq", "db1", "hb")


def step_kernel(
    col_ref, row_hbm, smt_ref, bias_ref, times_ref, labels_ref, freq_ref, clean_ref, noise_ref, pe_ref, bh_ref, *rest, names, count_all
):
    outs, aux_out, rest = rest[:8], rest[8 : 8 + len(AUX)], rest[8 + len(AUX) :]
    s = dict(zip(names, rest[: len(names)]))
    aux, rest = dict(zip(AUX, rest[len(names) :])), rest[len(names) + len(AUX) :]
    mod_ref, emb_ref, ball_ref = rest[:3]
    row_ref, pk_ref, pack_ref, bhs, bmod_ref, pkl, ems, eml, a1s, a1l, css, csl, mps, mpl_, mos, mol, bal, local_sem, wsend, wrecv, send_sem, recv_sem = rest[3:]
    wall_ref = s["wall"]
    cs_ref, ct_ref, t1_ref, a1_ref, tf_ref, hot_ref, wto_ref = [aux[name] for name in AUX[:7]]
    net = Peers(send_sem, recv_sem)
    w, t, c, n = net.w, net.t, net.c, net.n
    share = D // n
    half = share // 2
    x, z, y = t // 2, w // 2, lax.rem(w, 2)
    net.barrier()
    rows_in = pltpu.make_async_copy(row_hbm, row_ref, local_sem.at[0])
    rows_in.start()
    sub = lax.broadcasted_iota(jnp.int32, (8, 1), 0)
    when, label = jnp.zeros((8, 1), F32), jnp.zeros((8, 1), jnp.int32)
    for k in range(8):
        when = jnp.where(sub == k, times_ref[k], when)
        label = jnp.where(sub == k, labels_ref[k], label)
    angles = 1000.0 * when * freq_ref[...]
    pk_ref[:, 0:128] = jnp.cos(angles)
    pk_ref[:, 128:256] = jnp.sin(angles)
    pk_ref[:, 256:384] = jnp.where(label == lax.broadcasted_iota(jnp.int32, (8, 128), 1), 1.0, 0.0)
    rows_in.wait()
    wmod_ref = col_ref.at[:, 0:QKV0]
    pack_ref[0, :, 0:576] = col_ref[:, QKV0:FC0]
    pack_ref[0, :, 576:768] = row_ref[:, 0:192].astype(BF)
    pack_ref[1] = col_ref[:, FC0:COLS]
    pack_ref[2] = row_ref[:, 192:960].astype(BF)
    own = []

    def place(q, j, v):
        return wall_ref.at[q, j, pl.ds(pl.multiple_of(share * v, 32), share)]

    for q in range(3):
        op = pltpu.make_async_copy(pack_ref.at[q], place(q, t, w), local_sem.at[q])
        op.start()
        own.append(op)
    pkl[w] = pk_ref[...]
    rest = smt_ref.shape[1]
    emb = jnp.concatenate(
        [smt_ref[:, 0:16], smt_ref[:, rest - 18 : rest - 2], smt_ref[:, 16:17], smt_ref[:, rest - 2 : rest], jnp.zeros((share, 5), F32)],
        axis=1,
    )
    third = share // 3
    emb = jnp.concatenate([emb[0:third], emb[third : 2 * third], emb[2 * third : share], jnp.zeros((third, 8), F32)], axis=1)
    ems[...] = emb.astype(BF)
    eml[w] = ems[...]
    bias = bias_ref[...].astype(BF).astype(F32)
    bmod_ref[...] = bias[:, 0:QKV0]
    bal[t] = jnp.concatenate([bias[:, QKV0:FC0], jnp.zeros((1, 192), F32), bias[:, FC0:COLS]], axis=1)
    net.ready()
    pk_ops = net.dp_push(lambda peer: pk_ref, pkl.at[w], 0)

    zs = [z, z + 1 - 2 * lax.rem(z, 2), lax.rem(z + 2, 4), 3 - z]
    xo = 1 - x
    mine, across = 2 * x + c, 2 * xo + c
    wys = [2 * zs[k] + y for k in range(4)]
    wos = [2 * zs[k] + (1 - y) for k in range(4)]
    to_zs = [(wys[k], t) for k in range(4)]
    wy, wo, to_z = wys.__getitem__, wos.__getitem__, to_zs.__getitem__
    to_x, to_y, to_core = (w, across), (2 * z + (1 - y), t), (w, net.sib)
    sends = []

    def piece_copy(index, q, j, v, device, own_block):
        slot = place(q, j, v)
        return pltpu.make_async_remote_copy(
            src_ref=pack_ref.at[q] if own_block else slot, dst_ref=slot, send_sem=wsend.at[index],
            recv_sem=wrecv.at[q, j, v], device_id=device, device_id_type=MESH,
        )

    def send(q, j, v, device, own_block=False):
        sends.append((len(sends), q, j, v, device, own_block))
        piece_copy(*sends[-1]).start()

    def arrived(q, j, v):
        piece_copy(0, q, j, v, to_core, False).wait_recv()

    def column(q, k):
        if k == 0:
            send(q, mine, w, to_z(1), True)
            send(q, mine, w, to_z(2), True)
        else:
            arrived(q, mine, wy(k))
            if k == 2:
                send(q, mine, wy(2), to_z(1))
        send(q, mine, wy(k), to_x, k == 0)
        send(q, mine, wy(k), to_y, k == 0)
        send(q, mine, wy(k), to_core, k == 0)

    def by_y(q, k):
        return q == 0 and k == 3

    def side(q, k):
        arrived(q, across, wy(k))
        if by_y(q, k):
            send(q, across, wy(k), to_y)
        send(q, across, wy(k), to_core)
        arrived(q, mine, wo(k))
        if not by_y(q, k):
            send(q, mine, wo(k), to_x)
        send(q, mine, wo(k), to_core)

    def corner(q, k):
        arrived(q, across, wo(k))
        send(q, across, wo(k), to_core)

    first_hop, last_hop = {1: to_x}, {1: to_y}

    def level(q, k):
        return (mine, wy(k)), ((across, wy(k)) if q == 1 else (mine, wo(k)))

    def begin(q):
        send(q, mine, w, first_hop[q], True)
        send(q, mine, w, to_z(1), True)
        send(q, mine, w, to_z(2), True)
        send(q, mine, w, last_hop[q], True)
        send(q, mine, w, to_core, True)

    def second(q):
        j, v = level(q, 0)[1]
        arrived(q, j, v)
        for device in (to_z(1), to_z(2), last_hop[q], to_core):
            send(q, j, v, device)

    def along(q, k):
        for j, v in level(q, k):
            arrived(q, j, v)
            if k == 2:
                send(q, j, v, to_z(1))
            send(q, j, v, last_hop[q])
            send(q, j, v, to_core)

    def far(q, k):
        last = (mine, wo(k)) if q == 1 else (across, wy(k))
        for j, v in (last, (across, wo(k))):
            arrived(q, j, v)
            send(q, j, v, to_core)

    def chain0():
        wait_all(pk_ops)
        feats = pkl[...].reshape(8 * n, 384)
        tf_ref[...] = feats[:, 0:FREQ]
        hot_ref[...] = feats[:, FREQ:384]
        small = smt_ref[...].astype(BF).astype(F32)
        t1 = hndot(small[:, 17:273], tf_ref[...]) + small[:, 273:274]
        t1_ref[...] = t1
        act = t1 / (1.0 + jnp.exp(-t1))
        a1s[...] = jnp.concatenate([act[0:half], act[half:share]], axis=1)
        a1l[w] = a1s[...]
        return net.dp_push(lambda peer: a1s, a1l.at[w], 17)

    def chain1(ops):
        wait_all(ops)
        for k in range(n):
            a1_ref[share * k : share * k + half] = a1l[k][:, 0:64]
            a1_ref[share * k + half : share * k + share] = a1l[k][:, 64:128]
        small = smt_ref[...].astype(BF).astype(F32)
        cond = hdot(small[:, 274:1042], a1_ref[...]) + small[:, 1042:1043]
        cond = cond + hndot(small[:, 1043:1075], hot_ref[:, 0:CLASSES])
        ct_ref[...] = cond
        act = cond / (1.0 + jnp.exp(-cond))
        parts = [tdot(piece, wmod_ref[...]) for piece in split3(act)]
        mps[...] = (parts[0] + parts[1] + parts[2]).reshape(n, 8, QKV0)
        mpl_[w] = mps[w]
        mod_ops = net.dp_push(lambda peer: mps.at[peer], mpl_.at[w], 31)
        css[...] = jnp.concatenate([act[0:half], act[half:share]], axis=1)
        csl[w] = css[...]
        return net.dp_push(lambda peer: css, csl.at[w], 24), mod_ops

    def chain2(ops):
        wait_all(ops)
        total = mpl_[0]
        for k in range(1, n):
            total = total + mpl_[k]
        mos[...] = total + bmod_ref[...]
        mol[t] = mos[...]
        return net.tensor_push(mos, mol.at[t], 38)

    def chain3(ops):
        wait_all(em_ops)
        rows = []
        for k in range(n):
            piece = eml[k].astype(F32)
            rows += [piece[:, 40 * i : 40 * i + 40] for i in range(3)]
        rows = jnp.concatenate(rows, axis=0)
        emb_ref[...] = jnp.concatenate([rows, jnp.zeros((D, 88), F32)], axis=1).T[0:40]
        wait_all(ba_ops)
        ball_ref[...] = bal[...]
        wait_all(ops)
        for lat in range(4):
            for j in range(4):
                for piece in range(2):
                    mod_ref[lat, 2 * j + piece : 2 * j + piece + 1, :] = mol[j, pl.ds(4 * c + lat, 1), D * piece : D * piece + D]

    column(0, 0)
    ops = chain0()
    em_ops = net.dp_push(lambda peer: ems, eml.at[w], 7)
    ba_ops = net.tensor_push(bal.at[t], bal.at[t], 14)
    column(0, 1)
    side(0, 0)
    column(0, 2)
    cs_ops, ops = chain1(ops)
    side(0, 1)
    corner(0, 0)
    column(0, 3)
    side(0, 2)
    begin(1)
    column(2, 0)
    corner(0, 1)
    side(0, 3)
    ops = chain2(ops)
    corner(0, 2)
    corner(0, 3)
    second(1)
    column(2, 1)
    chain3(ops)

    def other_core(q):
        for j in (2 * x + 1 - c, 2 * xo + 1 - c):
            for v in range(n):
                arrived(q, j, v)

    other_core(0)
    own[0].wait()
    plan = (
        (along, 1, 1), (side, 2, 0), (column, 2, 2), (corner, 2, 0), (along, 1, 2), (side, 2, 1), (column, 2, 3), (corner, 2, 1),
        None, (side, 2, 2), None, (along, 1, 3), (side, 2, 3), (corner, 2, 2),
    )
    slots = {i: [functools.partial(*item)] for i, item in enumerate(plan) if item}
    rest = [functools.partial(far, 1, k) for k in range(4)] + [functools.partial(corner, 2, 3)]

    def service(lat, pos):
        for index, todo in slots.items():
            if index % 4 == pos:
                for item in todo:
                    pl.when(lat == index // 4)(item)

    def rows_out():
        wait_all(cs_ops)
        rows = []
        for k in range(n):
            rows += [csl[k][:, 0:64], csl[k][:, 64:128]]
        rows = jnp.concatenate(rows, axis=0)
        a1s_all = jnp.concatenate([rows, jnp.zeros((D, 64), F32)], axis=1).T
        cs_all = a1s_all[0:64].reshape(n, 8, D)
        picked = jnp.zeros((8, D), F32)
        for k in range(n):
            picked = jnp.where(w == k, cs_all[k], picked)
        cs_ref[...] = picked
        wto_ref[...] = smt_ref[:, 274:1042].astype(BF)

    def ready():
        for item in rest:
            item()
        for q in (1, 2):
            other_core(q)
            own[q].wait()

    block = Block(
        s, times_ref, clean_ref, noise_ref, mod_ref, pe_ref, emb_ref, bhs, ball_ref, outs,
        aux["dmod"], aux["small"], aux["hb"], 2 * x, 4 * c, count_all, service,
    )
    bhs[...] = tdot(bh_ref[...].astype(BF), jnp.ones((1, SEQ), BF))
    block.start()
    block.run(ready)
    rows_out()
    for k in range(2):
        aux["dbq"][k] = s["dbq"][2 * x + k]
        aux["db1"][k] = s["db1"][2 * x + k]
    copies = [pltpu.make_async_copy(aux[name], aux_out[i], local_sem.at[3 + i]) for i, name in enumerate(AUX)]
    for op in copies:
        op.start()
    for record in sends:
        piece_copy(*record).wait_send()
    net.finish()
    for op in copies:
        op.wait()


def run_step(col, row, smt, bias, times, labels, freq, clean, noise, pe, bh, n, count_all):
    S = jax.ShapeDtypeStruct
    V = pltpu.VMEM
    DMA = pltpu.SemaphoreType.DMA
    share = D // n
    lat = 8 * n
    half = 4
    any_spec = pl.BlockSpec(memory_space=pl.ANY)
    vm = pl.BlockSpec(memory_space=pltpu.VMEM)
    aux = [
        ((8, D), F32), ((share, lat), F32), ((share, lat), F32), ((D, lat), F32), ((lat, FREQ), F32), ((lat, 128), F32), ((share, D), BF),
        ((half, 8, D), F32), ((40, D), F32), ((2, 1, 640), F32), ((2, 1, D), F32), ((PATCH_IN, 128), F32),
    ]
    outs = [S((half, SEQ, D), BF)] * 4 + [S((2, half, SEQ, width), BF) for width in (256, 640, D, D)]
    outs += [S(*a) for a in aux]
    state = block_state()
    scratch = list(state.values()) + [V(*a) for a in aux] + [
        V((half, 8, D), F32), V((40, D), F32), V((4, 1, QKV0), F32),
        V((share, 960), F32), V((8, 384), F32), V((3, share, D), BF), V((PATCH_IN, SEQ), F32), V((1, QKV0), F32),
        V((n, 8, 384), F32), V((share // 3, 128), BF), V((n, share // 3, 128), BF),
        V((share // 2, 128), F32), V((n, share // 2, 128), F32), V((share // 2, 128), F32), V((n, share // 2, 128), F32),
        V((n, 8, QKV0), F32), V((n, 8, QKV0), F32), V((8, QKV0), F32), V((4, 8, QKV0), F32), V((4, 1, QKV0), F32),
        DMA((3 + len(AUX),)), DMA((120,)), DMA((3, 4, n)), DMA((41,)), DMA((41,)),
    ]
    return pl.pallas_call(
        functools.partial(step_kernel, names=tuple(state), count_all=count_all),
        out_shape=outs,
        in_specs=[vm, any_spec, vm, vm] + [pl.BlockSpec(memory_space=pltpu.SMEM)] * 2 + [vm] * 5,
        out_specs=[any_spec] * len(outs),
        scratch_shapes=scratch,
        compiler_params=pltpu.CompilerParams(collective_id=0, has_side_effects=True, vmem_limit_bytes=62 * 1024 * 1024),
        name="step",
    )(col, row, smt, bias, times, labels, freq, clean, noise, pe, bh)


def gram_schmidt(block):
    rows = lax.broadcasted_iota(jnp.int32, (8, 1), 0)
    for index in range(8):
        row = block[index : index + 1]
        row = row * lax.rsqrt(jnp.sum(row * row, axis=-1, keepdims=True) + TINY)
        inner = jnp.sum(block * row, axis=-1, keepdims=True)
        inner = jnp.where(rows > index, inner, 0.0)
        block = jnp.where(rows == index, row, block - inner * row)
    return block


def grad_kernel(
    a_ref, m_ref, dy_ref, dz_ref, o_ref, dq_ref, du_ref, g_ref, cerr_ref, rerr_ref,
    dmod_ref, small_ref, dbq_ref, db1_ref, hb_ref, right_ref, cs_ref, ct_ref, t1_ref, a1_ref, tf_ref, hot_ref, wmod_ref, wto_ref,
    mcol_ref, mrow_ref, left_out, rightn_out, pst_out, psr_out, pc_out, qst_out, qsn_out, qrs_out, gb_out, gh_out, gsm_out,
    mc, mr, sc, sr, rc, rr, av, mv, dyv, dzv, ov, qv, uv, gv,
    left_ref, rightn_ref, pst_ref, psr_ref, pc_ref, qst_ref, qsn_ref, qrs_ref, gb_ref, gh_ref, gsm_ref,
    dmo, smo, dbo, dbo1, hbo, dm8, dma, dsc, dss, dts, dtl, tks, tkl, px, pland, py, qx, qland, qy,
    load_sem, out_sem, send_sem, recv_sem,
):
    net = Peers(send_sem, recv_sem)
    outs = []

    def emit(*pairs):
        for src, dst in pairs:
            op = pltpu.make_async_copy(src, dst, out_sem.at[len(outs)])
            op.start()
            outs.append(op)

    w, t, c = net.w, net.t, net.c
    n = net.n
    share = D // n
    loads = {}

    def load(name, src, dst, index):
        op = pltpu.make_async_copy(src, dst, load_sem.at[index])
        op.start()
        loads[name] = op

    net.barrier()
    load("q", dq_ref, qv, 9)
    load("a", a_ref, av, 1)
    load("u", du_ref, uv, 0)
    load("m", m_ref, mv, 2)
    def chunk(i, size=256):
        return pl.ds(pl.multiple_of(i * size, size), size)

    def after(i, first):
        return pl.ds(pl.multiple_of(first + 256 * i, 64), 256)

    for name in ("q", "a"):
        loads[name].wait()
    col_ops, row_ops = [], []
    load("g", g_ref, gv, 3)
    load("dz", dz_ref, dzv, 4)
    sc[0:256] = tdot(qv[1 - c, :, 0:256], av[...])
    sc[256:576] = tdot(qv[1 - c, :, 256:640], av[...])[0:320]
    net.ready()
    side = [
        net.core_push(dmod_ref, dmo, 0),
        net.core_push(small_ref, smo, 1),
        net.core_push(dbq_ref.at[1 - c], dbo, 2),
        net.core_push(db1_ref.at[1 - c], dbo1, 9),
        net.core_push(hb_ref, hbo, 10),
    ]

    col_ops.append(net.core_push(sc.at[0:576], rc.at[0:576], 3))
    for name in ("u", "m"):
        loads[name].wait()
    load("o", o_ref, ov, 5)
    load("dy", dy_ref, dyv, 6)
    load("ce", cerr_ref, mc, 7)

    @pl.loop(0, 3)
    def _(i):
        sc[after(i, 576), :] = tdot(uv[1 - c, :, chunk(i)], mv[...])

    col_ops.append(net.core_push(sc.at[576:1344], rc.at[576:1344], 4))
    wait_all(side)
    for lat in range(4):
        for piece in range(2):
            span = slice(D * piece, D * piece + D)
            dm8[pl.ds(4 * c + lat, 1), span] = dmod_ref[lat, pl.ds(2 * t + piece, 1), :]
            dm8[pl.ds(4 * (1 - c) + lat, 1), span] = dmo[lat, pl.ds(2 * t + piece, 1), :]
    dma[w] = dm8[...]
    dm_ops = net.dp_push(lambda peer: dm8, dma.at[w], 16)
    total = small_ref[...] + smo[...]
    for k in range(n):
        tks[k, :, 0:share] = total[:, share * k : share * k + share]
    tkl[w] = tks[w]
    tok_ops = net.dp_push(lambda peer: tks.at[peer], tkl.at[w], 24)
    for name in ("g", "dz", "o", "dy"):
        loads[name].wait()

    @pl.loop(0, 3)
    def _(i):
        sr[after(i, 192), :] = tdot(gv[1 - c, :, chunk(i)], dzv[...])

    sr[0:192, :] = tdot(ov[1 - c], dyv[...])[64:256]
    row_ops.append(net.core_push(sr, rr, 6))
    load("re", rerr_ref, mr, 8)
    loads["ce"].wait()
    dms = split3(dm8[...])
    cs = split3(cs_ref[...])
    left_side = jnp.concatenate([dms[0], dms[1], dms[0], dms[2], dms[1], dms[0]], axis=0)
    right_side = jnp.concatenate([cs[0], cs[0], cs[1], cs[0], cs[1], cs[2]], axis=0)
    for i in range(6):
        mc[256 * i : 256 * i + 256, :] += tdot(left_side[:, 256 * i : 256 * i + 256], right_side)
    wait_all(col_ops)
    mc[QKV0 : QKV0 + 256] += tdot(qv[c, :, 0:256], av[...]) + rc[0:256]
    mc[QKV0 + 256 : FC0] += tdot(qv[c, :, 256:640], av[...])[0:320] + rc[256:576]

    @pl.loop(0, 3)
    def _(i):
        mc[after(i, FC0), :] += tdot(uv[c, :, chunk(i)], mv[...]) + rc[after(i, 576), :]

    out_col = pltpu.make_async_copy(mc, mcol_ref, load_sem.at[0])
    out_col.start()
    loads["re"].wait()
    wait_all(row_ops)

    @pl.loop(0, 3)
    def _(i):
        mr[after(i, 192), :] += tdot(gv[c, :, chunk(i)], dzv[...]) + rr[after(i, 192), :]

    mr[0:192, :] += tdot(ov[c], dyv[...])[64:256] + rr[0:192, :]
    out_row = pltpu.make_async_copy(mr, mrow_ref, load_sem.at[1])
    out_row.start()
    wait_all(dm_ops)
    dmx = dma[...].reshape(8 * n, QKV0)
    part = sum(ndot(wmod_ref[:, 0:QKV0], piece) for piece in split3(dmx))
    dss[...] = part
    dsc[t] = part
    ds_ops = net.tensor_push(dss, dsc.at[t], 32)
    right = right_ref[...]

    def left_part(first, last):
        sides = jnp.concatenate(halves(right[:, first:last]), axis=0).astype(BF)
        high, low = split2(mc[first:last, :])
        got = dot(sides, high) + dot(sides, low)
        return got[0:8] + got[8:16]

    for k, spans in enumerate((((0, 512), (512, 1024), (1024, QKV0)), ((QKV0, FC0),), ((FC0, FC0 + 384), (FC0 + 384, COLS)))):
        got = sum(left_part(*span) for span in spans)
        for i in range(6):
            px[6 * k + i] = got[:, 128 * i : 128 * i + 128]
    row_side = fill(halves(right[:, COLS : COLS + D]) + halves(right[:, COLS + D : COLS + 2 * D]), 128).T.astype(BF)

    def row_chunk(values):
        high, low = split2(values)
        return dot(high, row_side) + dot(low, row_side)

    got = jnp.concatenate([row_chunk(mr[0:192, :]), jnp.zeros((64, 128), F32)], axis=0).T
    for i in range(2):
        px[18 + i] = got[0:8, 128 * i : 128 * i + 128] + got[8:16, 128 * i : 128 * i + 128]
    for i in range(3):
        got = row_chunk(mr[192 + 256 * i : 448 + 256 * i, :]).T
        got = got[16:24] + got[24:32]
        px[20 + 2 * i] = got[:, 0:128]
        px[21 + 2 * i] = got[:, 128:256]
    bias = jnp.concatenate(
        [colsum(dm8[...]), (dbq_ref[c] + dbo[...])[:, 0:576], db1_ref[c] + dbo1[...], jnp.zeros((1, 192), F32)], axis=1
    )
    for i in range(24):
        px[26 + i // 8, i % 8 : i % 8 + 1, :] = bias[:, 128 * i : 128 * i + 128]
    both = hb_ref[...] + hbo[...]
    px[29] = both[0:8]
    px[30] = both[8:16]
    px[31] = jnp.zeros((8, 128), F32)

    def scatter(v, land, per, base):
        own = pl.ds(w * per, per)
        land[w] = v[own]
        return net.dp_push(lambda peer: v.at[pl.ds(peer * per, per)], land.at[w], base)

    def collect(land, v, per, base, ops):
        wait_all(ops)
        own = pl.ds(w * per, per)
        v[own] = sum(land[k] for k in range(1, n)) + land[0]
        return net.dp_push(lambda peer: v.at[own], v.at[own], base)

    ops = scatter(px, pland, P_COUNT // n, 40)
    ops = collect(pland, py, P_COUNT // n, 48, ops)
    wait_all(ds_ops)
    dcond = (dsc[0] + dsc[1] + dsc[2] + dsc[3]) * silu_slope_k(ct_ref[...])
    dtime = sum(tdot(wto_ref[...], piece) for piece in split3(dcond)).reshape(n, 2, share // 2, 8 * n)
    dts[...] = jnp.concatenate([dtime[:, 0], dtime[:, 1]], axis=2)
    dtl[w] = dts[w]
    dt_ops = net.dp_push(lambda peer: dts.at[peer], dtl.at[w], 56)
    wait_all(tok_ops)
    tok = sum(tkl[k] for k in range(1, n)) + tkl[0]
    tok = jnp.concatenate([tok, jnp.zeros((88, 128), F32)], axis=0).T[0:share]
    gsm_ref[:, 0:16] = tok[:, 0:16]
    gsm_ref[:, 16:17] = tok[:, 32:33]
    gsm_ref[:, 1075:1091] = tok[:, 16:32]
    gsm_ref[:, 1091:1093] = tok[:, 33:35]
    wait_all(ops)
    base = 0
    bases = []
    for index, count in enumerate(P_TILES):
        bases.append(gram_schmidt(jnp.concatenate([py[base + k] for k in range(count)], axis=1)))
        base += count
    col_side = fill(halves(bases[0]) + halves(bases[1]) + halves(bases[2]), 128).T.astype(BF)

    def col_chunk(values):
        high, low = split2(values)
        return dot(high, col_side) + dot(low, col_side)

    def put(first, rows, k, tile):
        got = col_chunk(mc[first : first + rows, :])
        if rows % 128:
            got = jnp.concatenate([got, jnp.zeros((128 - rows % 128, 128), F32)], axis=0)
        got = got.T
        got = got[16 * k : 16 * k + 8] + got[16 * k + 8 : 16 * k + 16]
        for i in range(got.shape[1] // 128):
            qx[tile + i] = got[:, 128 * i : 128 * i + 128]

    for i in range(6):
        put(256 * i, 256, 0, 2 * i)
    put(QKV0, 256, 1, 12)
    put(QKV0 + 256, 320, 1, 14)
    for i in range(3):
        put(FC0 + 256 * i, 256, 2, 17 + 2 * i)
    for k, (rows, block) in enumerate(((slice(0, 192), bases[3][:, 0:192]), (slice(192, 960), bases[4]))):
        left = jnp.concatenate(halves(block), axis=0).astype(BF)
        high, low = split2(mr[rows, :])
        got = dot(left, high) + dot(left, low)
        got = got[0:8] + got[8:16]
        for i in range(6):
            qx[23 + 6 * k + i] = got[:, 128 * i : 128 * i + 128]
    for i in range(35, Q_COUNT):
        qx[i] = jnp.zeros((8, 128), F32)
    ops = scatter(qx, qland, Q_COUNT // n, 64)
    gsm_ref[:, 274:1042] = hndot(dcond, a1_ref[...])
    gsm_ref[:, 1042:1043] = jnp.sum(dcond, axis=1, keepdims=True)
    gsm_ref[:, 1043:1075] = hdot(dcond, hot_ref[...])[:, 0:CLASSES]
    offset = 0
    for block, width in zip(bases, (D, D, D, 192, D)):
        left_ref[:, offset : offset + width] = block[:, 0:width]
        offset += width
    gb_ref[...] = jnp.concatenate([py[26 + i // 8, i % 8 : i % 8 + 1, :] for i in range(23)], axis=1)[:, 0:COLS]
    head = jnp.concatenate([py[29], py[30], jnp.zeros((112, 128), F32)], axis=0).T
    gh_ref[...] = head[0:8]
    emit((left_ref, left_out), (gb_ref, gb_out), (gh_ref, gh_out))

    ops = collect(qland, qy, Q_COUNT // n, 72, ops)
    wait_all(dt_ops)
    dtime = sum(dtl[k] for k in range(1, n)) + dtl[0]
    dtime = jnp.concatenate([dtime[:, 0:64], dtime[:, 64:128]], axis=0) * silu_slope_k(t1_ref[...])
    gsm_ref[:, 17:273] = hdot(dtime, tf_ref[...])
    gsm_ref[:, 273:274] = jnp.sum(dtime, axis=1, keepdims=True)

    def left_rows(blocks):
        rows = []
        for block in blocks:
            high, low = halves(block)
            rows += [high, low, high]
        return rows

    def right_rows(blocks):
        rows = []
        for block in blocks:
            high, low = halves(block)
            rows += [high, high, low]
        return rows

    pst_ref[...] = fill(left_rows(bases[:3]), 128).astype(BF)
    proj = jnp.concatenate([bases[3][:, 0:192], jnp.zeros((8, D), F32)], axis=1)
    fc = jnp.concatenate([jnp.zeros((8, 192), F32), bases[4]], axis=1)
    row_stack = fill(left_rows([proj, fc]), 128)
    pc_ref[...] = row_stack.astype(BF)
    row_stack = jnp.concatenate([row_stack, jnp.zeros((128, 64), F32)], axis=1)
    psr_ref[...] = row_stack.T[0:960].astype(BF)
    emit((pst_ref, pst_out), (pc_ref, pc_out), (psr_ref, psr_out), (gsm_ref, gsm_out))
    wait_all(ops)
    qkv = jnp.concatenate([qy[12 + i] for i in range(5)], axis=1)[:, 0:576]
    pieces = [jnp.concatenate([qy[i] for i in range(12)], axis=1), qkv, jnp.concatenate([qy[17 + i] for i in range(6)], axis=1)]
    pad = jnp.zeros((8, 64), F32)
    qc = jnp.concatenate(pieces + [pad], axis=1)
    span = lax.broadcasted_iota(jnp.int32, (8, 2944), 1)
    cuts = [
        jnp.where((span >= first) & (span < last), qc, 0.0) for first, last in ((0, QKV0), (QKV0, FC0), (FC0, COLS))
    ]
    stack = fill(right_rows(cuts), 128)
    qsn_ref[...] = stack.astype(BF)
    qst_ref[...] = stack.T[0:COLS].astype(BF)
    qr = [jnp.concatenate([qy[23 + 6 * k + i] for i in range(6)], axis=1) for k in range(2)]
    qrs_ref[...] = fill(right_rows(qr), 128).astype(BF)
    rightn_ref[:, 0:COLS] = qc[:, 0:COLS]
    rightn_ref[:, COLS : COLS + D] = qr[0]
    rightn_ref[:, COLS + D : COLS + 2 * D] = qr[1]
    emit((qst_ref, qst_out), (qsn_ref, qsn_out), (qrs_ref, qrs_out), (rightn_ref, rightn_out))
    net.finish()
    for op in outs:
        op.wait()
    out_col.wait()
    out_row.wait()


def run_grad(operands, n):
    S = jax.ShapeDtypeStruct
    V = pltpu.VMEM
    rows = operands[0].shape[0]
    lat = 8 * n
    share = D // n
    any_spec = pl.BlockSpec(memory_space=pl.ANY)
    vm = pl.BlockSpec(memory_space=pltpu.VMEM)
    outs = [
        S((COLS, D), F32), S((960, D), F32), S((8, 3264), F32), S((8, 4416), F32),
        S((128, D), BF), S((960, 128), BF), S((128, 960), BF), S((COLS, 128), BF), S((128, 2944), BF), S((128, D), BF),
        S((1, COLS), F32), S((8, 128), F32), S((share, 1093), F32),
    ]
    scratch = [
        V((COLS, D), F32), V((960, D), F32), V((1344, D), F32), V((960, D), F32), V((1344, D), F32), V((960, D), F32),
        V((rows, D), BF), V((rows, D), BF), V((rows, D), BF), V((rows, D), BF),
        V((2, rows, 256), BF), V((2, rows, 640), BF), V((2, rows, D), BF), V((2, rows, D), BF),
        *[V(o.shape, o.dtype) for o in outs[2:]],
        V((4, 8, D), F32), V((40, D), F32), V((1, 640), F32), V((1, D), F32), V((16, 128), F32),
        V((8, QKV0), F32), V((n, 8, QKV0), F32),
        V((4, share, lat), F32), V((share, lat), F32), V((n, share // 2, 128), F32), V((n, share // 2, 128), F32),
        V((n, 40, 128), F32), V((n, 40, 128), F32),
        V((P_COUNT, 8, 128), F32), V((n, P_COUNT // n, 8, 128), F32), V((P_COUNT, 8, 128), F32),
        V((Q_COUNT, 8, 128), F32), V((n, Q_COUNT // n, 8, 128), F32), V((Q_COUNT, 8, 128), F32),
        pltpu.SemaphoreType.DMA((10,)), pltpu.SemaphoreType.DMA((11,)), pltpu.SemaphoreType.DMA((80,)), pltpu.SemaphoreType.DMA((80,)),
    ]
    return pl.pallas_call(
        grad_kernel,
        out_shape=outs,
        in_specs=[any_spec] * 10 + [vm] * 14,
        out_specs=[any_spec] * 13,
        scratch_shapes=scratch,
        compiler_params=pltpu.CompilerParams(collective_id=1, has_side_effects=True, vmem_limit_bytes=60 * 1024 * 1024),
        name="grad",
    )(*operands)


APPLY_IN = (
    "mcol", "mrow", "qst", "psr", "pst", "pc", "qsn", "qrs", "left", "right", "gs", "gb", "gh",
    "cw", "cm", "rw", "rm", "sw", "sm", "bw", "bm", "hw", "hm",
)
APPLY_OUT = ("mcol", "mrow", "cw", "cm", "rw", "rm", "sw", "sm", "bw", "bm", "hw", "hm", "left", "right", "loss")
CUTS = 12


def apply_kernel(w_ref, *refs, n):
    ins = dict(zip(APPLY_IN, refs))
    outs = dict(zip(APPLY_OUT, refs[len(APPLY_IN) :]))
    rest = refs[len(APPLY_IN) + len(APPLY_OUT) :]
    held = [name for name in APPLY_IN if name not in ("left", "right")]
    s = dict(zip(held, rest))
    loss_s, hat_s, sem_in, sem_out = rest[len(held) :]
    share = D // n
    cut = {"mcol": [slice(240 * i, 240 * i + 240) for i in range(CUTS)], "mrow": [slice(480 * i, 480 * i + 480) for i in range(2)]}
    started, finished = {}, []

    def load(name, part=None):
        src, dst = (ins[name], s[name]) if part is None else (ins[name].at[cut[name][part]], s[name].at[cut[name][part]])
        started[name, part] = pltpu.make_async_copy(src, dst, sem_in.at[len(started)])
        started[name, part].start()

    def store(src, dst):
        op = pltpu.make_async_copy(src, dst, sem_out.at[len(finished)])
        op.start()
        finished.append(op)

    for name in ("pst", "qst", "qrs", "pc", "qsn", "psr"):
        load(name)
    for part in range(CUTS):
        load("mcol", part)
        if part == 0:
            for name in ("rw", "rm", "cw", "cm"):
                load(name)
    for part in range(2):
        load("mrow", part)
    for name in ("gs", "sw", "sm", "gb", "bw", "bm", "gh", "hw", "hm"):
        load(name)
    store(ins["left"], outs["left"])
    store(ins["right"], outs["right"])

    def ready(*names):
        for name in names:
            started[name, None].wait()

    def update(weight, moment, grad):
        s[moment][...] = DECAY * s[moment][...] + grad
        s[weight][...] = s[weight][...] - LEARN_RATE * s[moment][...]
        store(s[moment], outs[moment])
        store(s[weight], outs[weight])

    ready("pst", "qst", "qrs", "pc", "qsn")
    place = lax.broadcasted_iota(jnp.int32, (D, 128), 0) == w_ref[0] * share + lax.broadcasted_iota(jnp.int32, (D, 128), 1)
    pick = jnp.where(place, 1.0, 0.0).astype(BF)
    hat_s[...] = tdot(dot(s["pst"][...], pick).astype(BF), s["qsn"][...])[0:share, 0:COLS]
    rows = tdot(dot(s["qrs"][...], pick).astype(BF), s["pc"][...])[0:share]

    def residue(name, part, hat):
        started[name, part].wait()
        span = cut[name][part]
        s[name][span, :] = s[name][span, :] - hat * (1.0 / n)
        store(s[name].at[span], outs[name].at[span])

    def col(part):
        residue("mcol", part, dot(s["qst"][cut["mcol"][part], :], s["pst"][...]))

    def row(part):
        residue("mrow", part, dot(s["psr"][cut["mrow"][part], :], s["qrs"][...]))

    col(0)
    ready("rw", "rm")
    update("rw", "rm", rows)
    col(1)
    ready("cw", "cm")

    @pl.loop(0, share // 8)
    def _(i):
        for r in range(8):
            k = 8 * i + r
            moment = DECAY * s["cm"][k] + hat_s[pl.ds(k, 1), :]
            s["cm"][k] = moment
            s["cw"][k] = s["cw"][k] - LEARN_RATE * moment

    store(s["cm"], outs["cm"])
    store(s["cw"], outs["cw"])
    for part in range(2, CUTS):
        col(part)
    ready("psr")
    for part in range(2):
        row(part)
    ready("gs", "sw", "sm")
    update("sw", "sm", s["gs"][...])
    ready("gb", "bw", "bm", "gh", "hw", "hm")
    update("bw", "bm", s["gb"][...])
    update("hw", "hm", s["gh"][0:1, 0:PATCH_IN])
    loss_s[...] = s["gh"][1:2, 0:1]
    store(loss_s, outs["loss"])
    for op in finished:
        op.wait()


def run_apply(w, operands, n):
    S = jax.ShapeDtypeStruct
    V = pltpu.VMEM
    shapes = {name: operand for name, operand in zip(APPLY_IN, operands)}
    outs = [S(shapes[name].shape, F32) for name in APPLY_OUT[:-1]] + [S((1, 1), F32)]
    held = [V(shapes[name].shape, shapes[name].dtype) for name in APPLY_IN if name not in ("left", "right")]
    any_spec = pl.BlockSpec(memory_space=pl.ANY)
    return pl.pallas_call(
        functools.partial(apply_kernel, n=n),
        out_shape=outs,
        in_specs=[pl.BlockSpec(memory_space=pltpu.SMEM)] + [any_spec] * len(APPLY_IN),
        out_specs=[any_spec] * len(outs),
        scratch_shapes=held + [V((1, 1), F32), V((D // n, COLS), F32), pltpu.SemaphoreType.DMA((40,)), pltpu.SemaphoreType.DMA((40,))],
        compiler_params=pltpu.CompilerParams(vmem_limit_bytes=62 * 1024 * 1024),
        name="apply",
    )(w, *operands)


def position_table():
    quarter = D // 4
    omega = 10000.0 ** (-np.arange(quarter) / quarter)
    place = np.arange(GRID)[:, None] * omega[None, :]
    return jnp.asarray(np.concatenate([np.sin(place), np.cos(place)], axis=1), F32)


def time_features(times):
    half = FREQ // 2
    freqs = jnp.exp(-math.log(10000.0) * jnp.arange(half, dtype=jnp.float32) / half)
    angles = 1000.0 * times[:, None] * freqs[None, :]
    return jnp.concatenate([jnp.cos(angles), jnp.sin(angles)], axis=1)


def small_starts():
    counts = [PATCH_IN, 1, FREQ, 1, D, 1, CLASSES, PATCH_IN, 1, 1]
    starts = [0]
    for amount in counts:
        starts.append(starts[-1] + amount)
    return starts


def cut_parts(array, widths, axis):
    pieces = []
    offset = 0
    for width in widths:
        pieces.append(lax.slice_in_dim(array, offset, offset + width, axis=axis))
        offset = offset + width
    return pieces


def ortho_kernel(x_ref, o_ref):
    count = x_ref.shape[0]
    rows = [x_ref[index] for index in range(count)]
    for index in range(count):
        vector = rows[index]
        vector = vector * lax.rsqrt(jnp.sum(vector * vector, axis=-1, keepdims=True) + TINY)
        o_ref[index] = vector
        for later in range(index + 1, count):
            rows[later] = rows[later] - jnp.sum(rows[later] * vector, axis=-1, keepdims=True) * vector


def orthonormal_all(parts):
    stacked = jnp.stack([jnp.pad(part, ((0, 0), (0, D - part.shape[1]))) for part in parts], axis=1)
    stacked = jnp.pad(stacked, ((0, 0), (0, 8 - len(parts)), (0, 0)))
    out = pl.pallas_call(ortho_kernel, out_shape=jax.ShapeDtypeStruct(stacked.shape, F32), name="ortho")(stacked)
    return [out[:, index, : part.shape[1]] for index, part in enumerate(parts)]


def rounded(values):
    return lax.optimization_barrier(values.astype(BF)).astype(F32)


def silu_slope(values):
    gate = jax.nn.sigmoid(values)
    return gate * (1.0 + values * (1.0 - gate))


def shards_general(
    clean_latents,
    noise_draw,
    timesteps,
    labels,
    col_weights,
    col_moments,
    col_errors,
    row_weights,
    row_moments,
    row_errors,
    bias_weights,
    bias_moments,
    small_weights,
    small_moments,
    head_bias,
    head_moments,
    right_factors,
):
    tensor_size = lax.axis_size("tensor")
    data_size = lax.axis_size("dp")
    tensor_rank = lax.axis_index("tensor")
    data_rank = lax.axis_index("dp")
    batch = clean_latents.shape[0]
    half = batch // 2
    share = D // data_size
    mod_width = 8 * D // tensor_size
    qkv_width = 3 * D // tensor_size
    ffn_width = FF // tensor_size
    proj_rows = D // tensor_size
    count_all = data_size * batch * SEQ * PATCH_IN
    col_widths = [mod_width, qkv_width, ffn_width]
    core = lax.rem(tensor_rank, 2)
    base = tensor_rank - core
    pair = [(index, index + 1 - 2 * (index % 2)) for index in range(tensor_size)]

    def swap(values):
        return lax.ppermute(values, "tensor", pair)

    col_low = col_weights[:, 0, :].astype(BF)
    row_low = row_weights[0].astype(BF).T
    packed = jnp.concatenate(
        [
            col_low[:, mod_width : mod_width + qkv_width],
            row_low[:, :proj_rows],
            col_low[:, mod_width + qkv_width :],
            row_low[:, proj_rows:],
        ],
        axis=1,
    )
    wall = lax.all_gather(lax.all_gather(packed, "dp", axis=0, tiled=True), "tensor", axis=0)
    wall = jnp.stack([wall[:, :, 768 * index : 768 * index + 768] for index in range(3)])
    starts = small_starts()
    small_low = small_weights.astype(BF)
    small_exact = rounded(small_weights)
    picked = jnp.concatenate([small_low[: starts[2]], small_low[starts[7] :]], axis=0)
    emb = lax.all_gather(picked.astype(F32), "dp", axis=1, tiled=True)
    emb = jnp.concatenate([emb[:16], emb[17:33], emb[16:17], emb[33:35], jnp.zeros((5, D), F32)], axis=0)
    w_tin = small_exact[starts[2] : starts[3]]
    b_tin = small_exact[starts[3]]
    w_tout = small_exact[starts[4] : starts[5]]
    b_tout = small_exact[starts[5]]
    table = small_exact[starts[6] : starts[7]]
    bias_exact = rounded(bias_weights[0])
    head_exact = rounded(head_bias)
    w_mod = rounded(col_weights[:, 0, :mod_width])
    bias_all = lax.all_gather(bias_exact, "tensor", axis=0)
    times_all = lax.all_gather(timesteps, "dp", axis=0, tiled=True)
    labels_all = lax.all_gather(labels, "dp", axis=0, tiled=True)
    time_feat = time_features(times_all)
    time_hidden = exact_dot(time_feat, w_tin) + b_tin
    time_act = lax.all_gather(jax.nn.silu(time_hidden), "dp", axis=1, tiled=True)
    onehot = (labels_all[:, None] == jnp.arange(CLASSES, dtype=jnp.int32)[None, :]).astype(F32)
    condition = exact_dot(time_act, w_tout) + b_tout + exact_dot(onehot, table)
    cond_act = jax.nn.silu(condition)
    mod_part = exact_dot(cond_act, w_mod)
    mod_own = lax.psum_scatter(mod_part, "dp", scatter_dimension=0, tiled=True) + bias_exact[:mod_width]
    mod_full = lax.all_gather(mod_own, "tensor", axis=1, tiled=True).reshape(batch, 8, D)
    cond_rows = lax.all_to_all(cond_act, "dp", split_axis=0, concat_axis=1, tiled=True)

    def mine(values):
        return lax.dynamic_slice_in_dim(values, core * half, half, 0)

    ball = jnp.concatenate(
        [
            jnp.pad(bias_all[:, mod_width : mod_width + qkv_width], ((0, 0), (0, 768 - qkv_width))),
            bias_all[:, mod_width + qkv_width :],
        ],
        axis=1,
    )[:, None]
    (a, m, dy, dz, o, dq, du, g, dmod, small, dbq, db1, hb) = run_block(
        base.reshape(1),
        mine(timesteps),
        mine(clean_latents).transpose(0, 2, 1),
        mine(noise_draw).transpose(0, 2, 1),
        mine(mod_full),
        wall,
        position_table(),
        emb,
        head_exact[:, None],
        ball,
        count_all,
    )
    rows = half * SEQ

    def flat(values):
        return values.reshape(rows, values.shape[-1])

    def pick(values, which):
        return lax.dynamic_index_in_dim(values, which, 0, keepdims=False)

    def gradients(which):
        return (
            tdot(flat(a), flat(pick(dq, which))[:, :qkv_width]),
            tdot(flat(m), flat(pick(du, which))),
            tdot(flat(pick(o, which))[:, 64:], flat(dy)),
            tdot(flat(pick(g, which)), flat(dz)),
            pick(dbq, which)[0, :qkv_width],
            pick(db1, which)[0],
        )

    other = swap(gradients(1 - core))
    own = gradients(core)
    g_qkv, g_fc1, g_proj, g_fc2, g_bqkv, g_bfc1 = [left + right for left, right in zip(own, other)]
    dmod_own = dmod.reshape(half, 8 * D)
    dmod_other = swap(dmod_own)
    dmod_group = jnp.where(
        core == 0,
        jnp.concatenate([dmod_own, dmod_other], axis=0),
        jnp.concatenate([dmod_other, dmod_own], axis=0),
    )
    d_mod = lax.dynamic_slice_in_dim(dmod_group, tensor_rank * mod_width, mod_width, 1)
    g_bmod = jnp.sum(d_mod, axis=0)
    g_mod = exact_tdot(cond_rows, d_mod)
    d_mod_all = lax.all_gather(d_mod, "dp", axis=0, tiled=True)
    d_cond = lax.psum(exact_ndot(d_mod_all, w_mod), "tensor") * silu_slope(condition)
    g_table = exact_tdot(onehot, d_cond)
    g_btout = jnp.sum(d_cond, axis=0)
    g_tout = exact_tdot(time_act, d_cond)
    d_time = lax.psum_scatter(exact_ndot(d_cond, w_tout), "dp", scatter_dimension=1, tiled=True)
    d_time = d_time * silu_slope(time_hidden)
    g_btin = jnp.sum(d_time, axis=0)
    g_tin = exact_tdot(time_feat, d_time)
    small_own = lax.psum(lax.psum_scatter(small, "dp", scatter_dimension=1, tiled=True), "tensor") * 0.5
    head_sum, loss_value = lax.psum((hb[:, 0] * 0.5, hb[0, 1] * 0.5), ("dp", "tensor"))
    small_step = jnp.concatenate(
        [
            small_own[:16],
            small_own[32:33],
            g_tin,
            g_btin[None],
            g_tout,
            g_btout[None],
            g_table,
            small_own[16:32],
            small_own[33:34],
            small_own[34:35],
        ],
        axis=0,
    )
    bias_sum = lax.psum(jnp.concatenate([g_bmod, g_bqkv, g_bfc1], axis=0), "dp")
    col_cuts = cut_parts(col_errors[0, 0], col_widths, 1)
    row_cuts = cut_parts(row_errors[0, 0], [proj_rows, ffn_width], 0)
    matrices = [
        g_mod + col_cuts[0],
        g_qkv + col_cuts[1],
        g_fc1 + col_cuts[2],
        g_proj + row_cuts[0],
        g_fc2 + row_cuts[1],
    ]
    right_pieces = cut_parts(right_factors[0], col_widths + [D, D], 1)
    left_local = jnp.concatenate([exact_ndot(right_pieces[i], matrices[i]) for i in range(5)], axis=1)
    left_sum = lax.psum(left_local, "dp")
    bases = orthonormal_all(cut_parts(left_sum, [D, D, D, proj_rows, ffn_width], 1))
    right_local = jnp.concatenate([exact_dot(bases[i], matrices[i]) for i in range(5)], axis=1)
    right_sum = lax.psum(right_local, "dp")
    right_split = cut_parts(right_sum, col_widths + [D, D], 1)
    approx = [exact_tdot(bases[i], right_split[i]) for i in range(5)]
    rest = [matrices[i] - approx[i] / data_size for i in range(5)]
    col_residue = jnp.concatenate(rest[:3], axis=1)[None, None]
    row_residue = jnp.concatenate(rest[3:], axis=0)[None, None]

    def own_columns(values):
        return lax.dynamic_slice_in_dim(values, data_rank * share, share, 1)

    col_step = jnp.concatenate(
        [exact_tdot(own_columns(bases[i]), right_split[i]) for i in range(3)], axis=1
    )[:, None, :]
    row_step = jnp.concatenate(
        [exact_tdot(bases[i], own_columns(right_split[i])) for i in (3, 4)], axis=0
    )[None]
    col_momentum = DECAY * col_moments + col_step
    col_new = col_weights - LEARN_RATE * col_momentum
    row_momentum = DECAY * row_moments + row_step
    row_new = row_weights - LEARN_RATE * row_momentum
    small_momentum = DECAY * small_moments + small_step
    small_new = small_weights - LEARN_RATE * small_momentum
    bias_momentum = DECAY * bias_moments + bias_sum[None]
    bias_new = bias_weights - LEARN_RATE * bias_momentum
    head_momentum = DECAY * head_moments + head_sum
    head_new = head_bias - LEARN_RATE * head_momentum
    left_factors = jnp.concatenate(bases, axis=1)[None]
    right_new = right_sum[None]
    return (
        loss_value,
        col_new,
        col_momentum,
        col_residue,
        row_new,
        row_momentum,
        row_residue,
        bias_new,
        bias_momentum,
        small_new,
        small_momentum,
        head_new,
        head_momentum,
        left_factors,
        right_new,
    )


def shards(
    clean_latents,
    noise_draw,
    timesteps,
    labels,
    col_weights,
    col_moments,
    col_errors,
    row_weights,
    row_moments,
    row_errors,
    bias_weights,
    bias_moments,
    small_weights,
    small_moments,
    head_bias,
    head_moments,
    right_factors,
):
    tensor_size = lax.axis_size("tensor")
    data_size = lax.axis_size("dp")
    tensor_rank = lax.axis_index("tensor")
    data_rank = lax.axis_index("dp")
    batch = clean_latents.shape[0]
    half = batch // 2
    share = D // data_size
    mod_width = 8 * D // tensor_size
    qkv_width = 3 * D // tensor_size
    ffn_width = FF // tensor_size
    proj_rows = D // tensor_size
    count_all = data_size * batch * SEQ * PATCH_IN
    col_widths = [mod_width, qkv_width, ffn_width]
    core = lax.rem(tensor_rank, 2)
    base = tensor_rank - core
    col = col_weights[:, 0]
    col_low = col.astype(BF)
    freq = jnp.asarray(np.exp(-math.log(10000.0) * np.arange(FREQ // 2) / (FREQ // 2))[None], F32)
    small_t = small_weights.T
    a, m, dy, dz, o, dq, du, g, cs, ct, t1, a1, tf, hot, wto, dmod, small, dbq, db1, hb = run_step(
        col_low, row_weights[0].T, small_t, bias_weights, timesteps, labels, freq,
        clean_latents.transpose(0, 2, 1), noise_draw.transpose(0, 2, 1), position_table(), head_bias[None],
        data_size, count_all,
    )
    rows = half * SEQ

    def flat(values):
        return values.reshape(values.shape[:-3] + (rows, values.shape[-1]))

    acts = [flat(values) for values in (a, m, dy, dz, o, dq, du, g)]
    errors = [col_errors[0, 0].T, row_errors[0, 0]]
    mcol, mrow, left_all, right_sum, pst, psr, pc, qst, qsn, qrs, gb, gh, gsm = run_grad(
        acts + errors + [dmod, small, dbq, db1, hb, right_factors[0], cs, ct, t1, a1, tf, hot, col_low, wto], data_size
    )
    cres, rres, col_new, col_momentum, rn, rmn, sn, smn, bias_new, bias_momentum, hn, hmn, left_all, right_sum, loss = run_apply(
        data_rank.reshape(1),
        [mcol, mrow, qst, psr, pst, pc, qsn, qrs, left_all, right_sum, gsm, gb, gh]
        + [col_weights, col_moments, row_weights[0].T, row_moments[0].T, small_t, small_moments.T]
        + [bias_weights, bias_moments, head_bias[None], head_moments[None]],
        data_size,
    )
    loss_value = loss[0, 0]
    col_residue, row_residue = cres.T[None, None], rres[None, None]
    row_new, row_momentum = rn.T[None], rmn.T[None]
    small_new, small_momentum = sn.T, smn.T
    head_new, head_momentum = hn[0], hmn[0]
    left_factors, right_new = left_all[None], right_sum[None]
    return (
        loss_value,
        col_new,
        col_momentum,
        col_residue,
        row_new,
        row_momentum,
        row_residue,
        bias_new,
        bias_momentum,
        small_new,
        small_momentum,
        head_new,
        head_momentum,
        left_factors,
        right_new,
    )


def solution(mesh):
    fits = mesh.shape["dp"] == 8 and mesh.shape["tensor"] == 4
    placed = (
        P("dp", None, None),
        P("dp", None, None),
        P("dp"),
        P("dp"),
        P("dp", "tensor", None),
        P("dp", "tensor", None),
        P("dp", "tensor", None, None),
        P("tensor", None, "dp"),
        P("tensor", None, "dp"),
        P("dp", "tensor", None, None),
        P("tensor", None),
        P("tensor", None),
        P(None, "dp"),
        P(None, "dp"),
        P(),
        P(),
        P("tensor", None, None),
    )
    return jax.shard_map(
        shards if fits else shards_general,
        mesh=mesh,
        in_specs=placed,
        out_specs=(
            P(),
            P("dp", "tensor", None),
            P("dp", "tensor", None),
            P("dp", "tensor", None, None),
            P("tensor", None, "dp"),
            P("tensor", None, "dp"),
            P("dp", "tensor", None, None),
            P("tensor", None),
            P("tensor", None),
            P(None, "dp"),
            P(None, "dp"),
            P(),
            P(),
            P("tensor", None, None),
            P("tensor", None, None),
        ),
        check_vma=False,
    )
```
